32 devices in a mesh: dp: 2 (over x), sy: 4 (over z), sx: 4 (over y, core).
Axes of the slice: x: 2, y: 2, z: 4, core: 2. Of those that a mesh axis runs over, the one named last changes fastest.
Arguments:
- features: bfloat16 [2, 64, 256, 768], P('dp', 'sy', 'sx'), may hold values from -100 to 100
- depth_weight: float32 [7, 7, 768], replicated, may hold values from -0.875 to 0.875
- depth_bias: float32 [768], replicated, may hold values from -3 to 3
- reduce_weight: bfloat16 [768, 256], replicated, may hold values from -0.21875 to 0.21875
- reduce_bias: float32 [256], replicated, may hold values from -3 to 3
- class_weight: bfloat16 [10, 256, 256], replicated, may hold values from -0.375 to 0.375
- class_bias: float32 [10], replicated, may hold values from -4 to 4
- labels: int32 [2], P('dp'), may hold values from 0 to 9
Outputs:
- loss: float32 [], replicated
- depth_weight_grad: float32 [7, 7, 768], replicated
- depth_bias_grad: float32 [768], replicated
- reduce_weight_grad: float32 [768, 256], replicated
- reduce_bias_grad: float32 [256], replicated
- class_weight_grad: float32 [10, 256, 256], replicated
- class_bias_grad: float32 [10], replicated
The draws below stay inside these ranges and needn't reach their ends.
All inputs are finite; a program needn't handle non-finite values.
Results may differ from the reference program's by a relative error of at most 0.006.
Values may be sent and summed in bfloat16 or wider, within the bound.
No kernel may reach another device: no remote copies, remote signals or barrier semaphores. Data moves between devices by JAX's collectives and lax.ppermute only.
A program may use at most 64 MiB of HBM per device.

```python
import jax
import jax.numpy as jnp
from jax import lax

CHANNELS = 768
REDUCED = 256
CLASSES = 10
KERNEL = 7
NEWTON_STEPS = 5
IMAGES = 2
ROWS_ALL = 64
COLS_ALL = 256


def draw_features(key, part):
    subkeys = jax.random.split(key, 4)
    shape = (IMAGES, ROWS_ALL, COLS_ALL, CHANNELS)
    channel_scale = jnp.exp(jax.random.uniform(subkeys[1], (IMAGES, 1, 1, CHANNELS), jnp.float32, jnp.log(0.3), jnp.log(3.0)))
    patch_scale = jnp.exp(jax.random.uniform(subkeys[2], (IMAGES, ROWS_ALL // 4, COLS_ALL // 4, 1), jnp.float32, jnp.log(0.6), jnp.log(1.6)))
    patch_scale = jnp.repeat(jnp.repeat(patch_scale, 4, axis=1), 4, axis=2)
    pixel_scale = jax.random.uniform(subkeys[3], (IMAGES, ROWS_ALL, COLS_ALL, 1), jnp.float32, 0.7, 1.4)
    row_place = (jnp.arange(ROWS_ALL, dtype=jnp.float32) / ROWS_ALL).reshape(1, ROWS_ALL, 1, 1)
    col_place = (jnp.arange(COLS_ALL, dtype=jnp.float32) / COLS_ALL).reshape(1, 1, COLS_ALL, 1)
    noise_field = jnp.clip(jax.random.normal(subkeys[0], shape, jnp.float32), -4.0, 4.0)
    row_trend = jnp.power(3.0, row_place) + 0.0 * col_place
    values = noise_field * channel_scale * patch_scale * pixel_scale * row_trend
    return values.astype(jnp.bfloat16)


def gaussian(own_key, shape, spread, reach, held_as=jnp.bfloat16):
    drawn = spread * jax.random.normal(own_key, shape, jnp.float32)
    return jnp.clip(drawn, min=-reach, max=reach).astype(held_as)


def setup_inputs(seed: int = 0) -> dict:
    arg_keys = jax.random.split(jax.random.key(seed), 9)
    return {
        "features": draw_features(jax.random.fold_in(arg_keys[8], 71), 0),
        "depth_weight": gaussian(arg_keys[1], (KERNEL, KERNEL, CHANNELS), (KERNEL * KERNEL) ** -0.5, 0.875, jnp.float32),
        "depth_bias": gaussian(arg_keys[2], (CHANNELS,), 0.5, 3.0, jnp.float32),
        "reduce_weight": gaussian(arg_keys[3], (CHANNELS, REDUCED), CHANNELS ** -0.5, 0.21875),
        "reduce_bias": gaussian(arg_keys[4], (REDUCED,), 0.5, 3.0, jnp.float32),
        "class_weight": gaussian(arg_keys[5], (CLASSES, REDUCED, REDUCED), REDUCED ** -0.5, 0.375),
        "class_bias": gaussian(arg_keys[6], (CLASSES,), 1.0, 4.0, jnp.float32),
        "labels": jax.random.randint(arg_keys[7], (IMAGES,), 0, CLASSES).astype(jnp.int32),
    }


epsilon = 1e-05
loss_scale = 64.0
highest = lax.Precision.HIGHEST

def matrix_root(sigma):
    identity = jnp.eye(sigma.shape[0], dtype=sigma.dtype)
    trace_value = jnp.trace(sigma) + epsilon
    current = sigma / trace_value
    inverse = identity
    for iteration in range(NEWTON_STEPS):
        factor = 0.5 * (3.0 * identity - jnp.dot(inverse, current, precision=highest))
        current = jnp.dot(current, factor, precision=highest)
        inverse = jnp.dot(factor, inverse, precision=highest)
    return jnp.sqrt(trace_value) * current

def taps_conv(padded, tile_rows, tile_cols, depth_weight, depth_bias):
    total = jnp.zeros((tile_rows, tile_cols, padded.shape[2]), depth_weight.dtype) + depth_bias
    for row_tap in range(KERNEL):
        for col_tap in range(KERNEL):
            window = padded[row_tap:row_tap + tile_rows, col_tap:col_tap + tile_cols, :]
            total = total + window.astype(depth_weight.dtype) * depth_weight[row_tap, col_tap]
    return total.astype(jnp.bfloat16)

def forward(flat_conv, reduce_weight, reduce_bias):
    before = jnp.dot(flat_conv, reduce_weight, preferred_element_type=jnp.float32) + reduce_bias
    return (before, jax.nn.silu(before).astype(jnp.bfloat16))

def local_front(image, depth_weight, depth_bias, reduce_weight, reduce_bias):
    half = KERNEL // 2
    padded = jnp.pad(image, ((half, half), (half, half), (0, 0)))
    conv_out = taps_conv(padded, image.shape[0], image.shape[1], depth_weight, depth_bias)
    flat_conv = conv_out.reshape(-1, conv_out.shape[2])
    before, feat = forward(flat_conv, reduce_weight, reduce_bias)
    return (padded, flat_conv, before, feat)

def head(gram, colsum, label, class_weight, class_bias, count, image_count):
    mean_vec = colsum / count
    sigma = gram / count - jnp.outer(mean_vec, mean_vec)
    root, pullback = jax.vjp(matrix_root, sigma)
    weight_full = class_weight.astype(root.dtype)
    logits = jnp.einsum('kij,ij->k', weight_full, root, precision=highest) + class_bias
    onehot = (jnp.arange(logits.shape[0], dtype=jnp.int32) == label).astype(root.dtype)
    loss_part = jnp.sum(jax.nn.softplus(logits)) - jnp.sum(onehot * logits)
    logit_grad = loss_scale * (jax.nn.sigmoid(logits) - onehot) / image_count
    root_grad = jnp.einsum('k,kij->ij', logit_grad, weight_full, precision=highest)
    sigma_grad = pullback(root_grad)[0]
    symmetric = ((sigma_grad + sigma_grad.T) / count).astype(jnp.bfloat16)
    return (loss_part, logit_grad, root, symmetric, mean_vec)

def local_back(padded, flat_conv, before, feat, symmetric, mean_vec, reduce_weight, tile_rows, tile_cols):
    mean_term = jnp.dot(mean_vec, symmetric.astype(mean_vec.dtype), precision=highest)
    feat_grad = jnp.dot(feat, symmetric, preferred_element_type=jnp.float32) - mean_term
    gate = jax.nn.sigmoid(before)
    pre_grad = (feat_grad * gate * (1.0 + before * (1.0 - gate))).astype(jnp.bfloat16)
    weight_grad = lax.dot_general(flat_conv, pre_grad, (((0,), (0,)), ((), ())), preferred_element_type=jnp.float32)
    bias_grad = lax.optimization_barrier(jnp.sum(pre_grad.astype(jnp.float32), axis=0))
    conv_grad = lax.dot_general(pre_grad, reduce_weight, (((1,), (1,)), ((), ())), preferred_element_type=jnp.float32)
    conv_grad = conv_grad.astype(jnp.bfloat16).reshape(tile_rows, tile_cols, -1)
    depth_rows = []
    for row_tap in range(KERNEL):
        depth_cols = []
        for col_tap in range(KERNEL):
            window = padded[row_tap:row_tap + tile_rows, col_tap:col_tap + tile_cols, :]
            depth_cols.append(lax.optimization_barrier(jnp.sum(window.astype(jnp.float32) * conv_grad.astype(jnp.float32), axis=(0, 1))))
        depth_rows.append(jnp.stack(depth_cols))
    depth_grad = jnp.stack(depth_rows)
    depth_bias_grad = lax.optimization_barrier(jnp.sum(conv_grad.astype(jnp.float32), axis=(0, 1)))
    return (weight_grad, bias_grad, depth_grad, depth_bias_grad)

def reference(features, depth_weight, depth_bias, reduce_weight, reduce_bias, class_weight, class_bias, labels):
    count = ROWS_ALL * COLS_ALL

    def first_pass(image):
        padded, flat_conv, before, feat = local_front(image, depth_weight, depth_bias, reduce_weight, reduce_bias)
        gram = lax.dot_general(feat, feat, (((0,), (0,)), ((), ())), preferred_element_type=jnp.float32)
        colsum = lax.optimization_barrier(jnp.sum(feat.astype(jnp.float32), axis=0))
        return (gram, colsum)
    grams, colsums = lax.map(first_pass, features)

    def head_one(packed):
        return head(packed[0], packed[1], packed[2], class_weight, class_bias, count, IMAGES)
    loss_parts, logit_grads, roots, symmetrics, mean_vecs = lax.map(head_one, (grams, colsums, labels))

    def second_pass(packed):
        image, symmetric, mean_vec = packed
        padded, flat_conv, before, feat = local_front(image, depth_weight, depth_bias, reduce_weight, reduce_bias)
        return local_back(padded, flat_conv, before, feat, symmetric, mean_vec, reduce_weight, ROWS_ALL, COLS_ALL)
    weight_grads, bias_grads, depth_grads, depth_bias_grads = lax.map(second_pass, (features, symmetrics, mean_vecs))
    loss = jnp.sum(loss_parts) / IMAGES
    class_weight_grad = jnp.einsum('mk,mij->kij', logit_grads, roots, precision=highest)
    class_bias_grad = lax.optimization_barrier(jnp.sum(logit_grads, axis=0))
    return (loss, lax.optimization_barrier(jnp.sum(depth_grads, axis=0)), lax.optimization_barrier(jnp.sum(depth_bias_grads, axis=0)), lax.optimization_barrier(jnp.sum(weight_grads, axis=0)), lax.optimization_barrier(jnp.sum(bias_grads, axis=0)), class_weight_grad, class_bias_grad)
```

```python
import jax
import jax.numpy as jnp
from jax import lax
from jax.sharding import PartitionSpec as P

KERNEL = 7
NEWTON_STEPS = 5


epsilon = 1e-05
loss_scale = 64.0
highest = lax.Precision.HIGHEST


def with_halo(block, sides, width):
    for axis, dim in sides:
        count = lax.axis_size(axis)
        forward = [(i, i + 1) for i in range(count - 1)]
        backward = [(target, source) for source, target in forward]
        low = lax.ppermute(
            lax.slice_in_dim(block, block.shape[dim] - width, None, axis=dim), axis, forward
        )
        high = lax.ppermute(lax.slice_in_dim(block, 0, width, axis=dim), axis, backward)
        block = jnp.concatenate([low, block, high], axis=dim)
    return block


def others(axis):
    return range(1, lax.axis_size(axis))


def swap(value, axis, shift):
    count = lax.axis_size(axis)
    return lax.ppermute(value, axis, [(i, i ^ shift) for i in range(count)])


def scatter_sum(value, axis):
    count = lax.axis_size(axis)
    here = lax.axis_index(axis)
    pieces = value.reshape((count, value.shape[0] // count) + value.shape[1:])

    def piece(shift):
        return lax.dynamic_index_in_dim(pieces, here ^ shift, 0, keepdims=False)

    arrived = [swap(piece(shift), axis, shift) for shift in others(axis)]
    return sum(arrived, piece(0))


def exchange_sum(value, axis):
    return sum([swap(value, axis, shift) for shift in others(axis)], value)


def gather(value, axis):
    count = lax.axis_size(axis)
    here = lax.axis_index(axis)
    whole = jnp.zeros((count,) + value.shape, value.dtype)
    whole = lax.dynamic_update_index_in_dim(whole, value, here, 0)
    for shift in others(axis):
        whole = lax.dynamic_update_index_in_dim(whole, swap(value, axis, shift), here ^ shift, 0)
    return whole.reshape((count * value.shape[0],) + value.shape[1:])


def image_sum(value):
    value = scatter_sum(scatter_sum(value, "sx"), "sy")
    return gather(gather(value, "sy"), "sx")


def slice_sum(value):
    value = scatter_sum(scatter_sum(value, "sx"), "sy")
    value = exchange_sum(value, "dp")
    return gather(gather(value, "sy"), "sx")


def join_rows(parts, width, multiple):
    flat = jnp.concatenate([part.reshape(-1, width) for part in parts])
    short = -flat.shape[0] % multiple
    return jnp.pad(flat, ((0, short), (0, 0)))


def matrix_root(sigma):
    identity = jnp.eye(sigma.shape[0], dtype=sigma.dtype)
    trace_value = jnp.trace(sigma) + epsilon
    current = sigma / trace_value
    inverse = identity
    for iteration in range(NEWTON_STEPS):
        factor = 0.5 * (3.0 * identity - jnp.dot(inverse, current, precision=highest))
        current = jnp.dot(current, factor, precision=highest)
        inverse = jnp.dot(factor, inverse, precision=highest)
    return jnp.sqrt(trace_value) * current


def taps_conv(padded, tile_rows, tile_cols, depth_weight, depth_bias):
    total = jnp.zeros((tile_rows, tile_cols, padded.shape[2]), depth_weight.dtype) + depth_bias
    for row_tap in range(KERNEL):
        for col_tap in range(KERNEL):
            window = padded[row_tap : row_tap + tile_rows, col_tap : col_tap + tile_cols, :]
            total = total + window.astype(depth_weight.dtype) * depth_weight[row_tap, col_tap]
    return total.astype(jnp.bfloat16)


def body(
    features, depth_weight, depth_bias, reduce_weight, reduce_bias, class_weight, class_bias, labels
):
    tile_rows, tile_cols = (features.shape[1], features.shape[2])
    padded = with_halo(features, (("sy", 1), ("sx", 2)), KERNEL // 2)[0]
    conv_out = taps_conv(padded, tile_rows, tile_cols, depth_weight, depth_bias)
    flat_conv = conv_out.reshape(tile_rows * tile_cols, -1)
    before = jnp.dot(flat_conv, reduce_weight, preferred_element_type=jnp.float32) + reduce_bias
    feat = jax.nn.silu(before).astype(jnp.bfloat16)
    gram = lax.dot_general(feat, feat, (((0,), (0,)), ((), ())), preferred_element_type=jnp.float32)
    colsum = jnp.sum(feat.astype(jnp.float32), axis=0)
    pieces = lax.axis_size("sy") * lax.axis_size("sx")
    width = gram.shape[0]
    joined = image_sum(join_rows([gram, colsum], width, pieces * 8))
    gram, colsum = joined[:width], joined[width]
    count = tile_rows * tile_cols * lax.axis_size("sy") * lax.axis_size("sx")
    image_count = features.shape[0] * lax.axis_size("dp")
    mean_vec = colsum / count
    sigma = gram / count - jnp.outer(mean_vec, mean_vec)
    root, pullback = jax.vjp(matrix_root, sigma)
    weight_full = class_weight.astype(jnp.float32)
    logits = jnp.einsum("kij,ij->k", weight_full, root, precision=highest) + class_bias
    onehot = (jnp.arange(logits.shape[0], dtype=jnp.int32) == labels[0]).astype(jnp.float32)
    loss_part = jnp.sum(jax.nn.softplus(logits)) - jnp.sum(onehot * logits)
    logit_grad = loss_scale * (jax.nn.sigmoid(logits) - onehot) / image_count
    root_grad = jnp.einsum("k,kij->ij", logit_grad, weight_full, precision=highest)
    sigma_grad = pullback(root_grad)[0]
    facts = jnp.concatenate([logit_grad, loss_part[None]])
    sent = join_rows([root, jnp.pad(facts, (0, width - facts.shape[0]))], width, 8)
    class_weight_grad = logit_grad[:, None, None] * root[None, :, :]
    for shift in others("dp"):
        other = swap(sent, "dp", shift)
        other_grad = other[width, : logit_grad.shape[0]]
        class_weight_grad = class_weight_grad + other_grad[:, None, None] * other[None, :width]
        facts = facts + other[width, : facts.shape[0]]
    class_bias_grad = facts[:-1]
    loss = facts[-1] / image_count
    symmetric = ((sigma_grad + sigma_grad.T) / count).astype(jnp.bfloat16)
    mean_term = jnp.dot(mean_vec, symmetric.astype(jnp.float32), precision=highest)
    feat_grad = jnp.dot(feat, symmetric, preferred_element_type=jnp.float32) - mean_term
    gate = jax.nn.sigmoid(before)
    pre_grad = (feat_grad * gate * (1.0 + before * (1.0 - gate))).astype(jnp.bfloat16)
    weight_grad = lax.dot_general(
        flat_conv, pre_grad, (((0,), (0,)), ((), ())), preferred_element_type=jnp.float32
    )
    bias_grad = jnp.sum(pre_grad.astype(jnp.float32), axis=0)
    conv_grad = lax.dot_general(
        pre_grad, reduce_weight, (((1,), (1,)), ((), ())), preferred_element_type=jnp.float32
    )
    conv_grad = conv_grad.astype(jnp.bfloat16).reshape(tile_rows, tile_cols, -1)
    depth_rows = []
    for row_tap in range(KERNEL):
        depth_cols = []
        for col_tap in range(KERNEL):
            window = padded[row_tap : row_tap + tile_rows, col_tap : col_tap + tile_cols, :]
            depth_cols.append(
                jnp.sum(window.astype(jnp.float32) * conv_grad.astype(jnp.float32), axis=(0, 1))
            )
        depth_rows.append(jnp.stack(depth_cols))
    depth_grad = jnp.stack(depth_rows)
    depth_bias_grad = jnp.sum(conv_grad.astype(jnp.float32), axis=(0, 1))
    weight_grad = slice_sum(weight_grad)
    joined = slice_sum(join_rows([depth_grad, depth_bias_grad, bias_grad], width, pieces * 8))
    rows = depth_grad.size // width
    bias_rows = depth_bias_grad.size // width
    depth_grad = joined[:rows].reshape(depth_grad.shape)
    depth_bias_grad = joined[rows : rows + bias_rows].reshape(depth_bias_grad.shape)
    bias_grad = joined[rows + bias_rows]
    return (
        loss,
        depth_grad,
        depth_bias_grad,
        weight_grad,
        bias_grad,
        class_weight_grad,
        class_bias_grad,
    )


def solution(mesh):
    placed = (P("dp", "sy", "sx", None), P(), P(), P(), P(), P(), P(), P("dp"))
    return jax.shard_map(
        body,
        mesh=mesh,
        in_specs=placed,
        out_specs=(P(), P(), P(), P(), P(), P(), P()),
        check_vma=False,
    )
```

```python
import functools

import jax
import jax.numpy as jnp
from jax import lax
from jax.experimental import pallas as pl
from jax.experimental.pallas import tpu as pltpu
from jax.sharding import PartitionSpec as P

KERNEL = 7
HALF = KERNEL // 2
NEWTON_STEPS = 5
LANES = 128
GROUPS = 8
EDGE = 8

epsilon = 1e-05
loss_scale = 64.0
narrow = jnp.bfloat16
wide = jnp.float32


def params(megabytes, grid_axes=0):
    return pltpu.CompilerParams(
        vmem_limit_bytes=megabytes * 1024 * 1024,
        dimension_semantics=("arbitrary",) * grid_axes if grid_axes else None,
    )


def swap(value, axis, shift):
    count = lax.axis_size(axis)
    return lax.ppermute(value, axis, [(i, i ^ shift) for i in range(count)])


def is_upper(axis, shift):
    return (lax.axis_index(axis) & shift) != 0


def halve(value, axis, shift, sent_as):
    upper = is_upper(axis, shift)
    rows = value.shape[0] // 2
    low, high = value[:rows], value[rows:]
    kept = jnp.where(upper, high, low)
    sent = jnp.where(upper, low, high).astype(sent_as)
    return kept + swap(sent, axis, shift).astype(wide)


def unhalve(value, axis, shift):
    upper = is_upper(axis, shift)
    other = swap(value, axis, shift)
    return jnp.concatenate([jnp.where(upper, other, value), jnp.where(upper, value, other)])


def tree_sum(terms):
    while len(terms) > 1:
        terms = [terms[i] + terms[i + 1] for i in range(0, len(terms), 2)]
    return terms[0]


def exchange(value, axis, shift, sent_as):
    sent = value.astype(sent_as)
    return sent.astype(wide) + swap(sent, axis, shift).astype(wide)


def exchange_all(value, axis, sent_as):
    sent = value.astype(sent_as)
    moved = [sent] + [swap(sent, axis, shift) for shift in range(1, lax.axis_size(axis))]
    return tree_sum([part.astype(wide) for part in moved])


def doublings(axis, first=1):
    found = []
    shift = first
    while shift < lax.axis_size(axis):
        found.append(shift)
        shift *= 2
    return found


def next_along(value, axis):
    return lax.ppermute(value, axis, [(i, i + 1) for i in range(lax.axis_size(axis) - 1)])


def back_along(value, axis):
    return lax.ppermute(value, axis, [(i + 1, i) for i in range(lax.axis_size(axis) - 1)])


def spread_columns(source, target):
    for group in range(target.shape[0]):
        target[group] = source[pl.ds(EDGE - HALF + group, GROUPS, stride=GROUPS), :]


def fill_row(wide_row, middle, left, right):
    cols = middle.shape[0]
    wide_row[EDGE : EDGE + cols, :] = middle.astype(wide)
    wide_row[EDGE - HALF : EDGE, :] = left.astype(wide)
    wide_row[EDGE + cols : EDGE + cols + HALF, :] = right.astype(wide)


def spread_weights(weight_ref, spread_ref):
    for tap in range(KERNEL * KERNEL):
        spread_ref[tap] = jnp.broadcast_to(weight_ref[tap : tap + 1, :], spread_ref.shape[1:])


def conv_row(load, spread_ref, bias_ref, steps):
    total = [jnp.broadcast_to(bias_ref[0:1, :], (GROUPS, LANES))] * steps
    for row_tap in range(KERNEL):
        windows = [load(row_tap, group) for group in range(steps + KERNEL - 1)]
        for col_tap in range(KERNEL):
            scale = spread_ref[row_tap * KERNEL + col_tap]
            for step in range(steps):
                total[step] = total[step] + windows[step + col_tap] * scale
    return jnp.concatenate(total, axis=0).astype(narrow)


def reduce_part(tile, first, last, conv_out, reduce_ref, reduce_bias_ref, before, before_out, feat_out):
    product = jnp.dot(conv_out[...], reduce_ref[...], preferred_element_type=wide)

    @pl.when(first)
    def _():
        before[...] = product + reduce_bias_ref[...]

    @pl.when(jnp.logical_not(first))
    def _():
        before[...] += product

    @pl.when(last)
    def _():
        total = before[...]
        before_out[...] = total
        feat_out[...] = (total / (1.0 + jnp.exp(-total))).astype(narrow)


def feat_sums(feat):
    gram = lax.dot_general(feat, feat, (((0,), (0,)), ((), ())), preferred_element_type=wide)
    colsum = jnp.sum(feat.astype(wide), axis=0, keepdims=True)
    return gram, colsum


def inner_kernel(
    block, left, right, weight, bias, reduce_weight, reduce_bias,
    spread_out, conv_out, before_out, feat_out, gram_out, colsum_out,
    wide_row, spread_weight, before,
):
    tile = pl.program_id(0)
    first, last = tile == 0, tile == pl.num_programs(0) - 1
    rows, cols = block.shape[0], block.shape[1]
    steps = cols // GROUPS
    spread_weights(weight, spread_weight)

    def fill(row, _):
        fill_row(wide_row.at[row], block[row], left[row], right[row])
        spread_columns(wide_row.at[row], spread_out.at[0, row])
        return 0

    lax.fori_loop(0, rows, fill, 0)

    def one(index, _):
        def load(row_tap, group):
            return spread_out[0, index + row_tap, group]

        start = pl.multiple_of(index * cols, cols)
        conv_out[pl.ds(start, cols), :] = conv_row(load, spread_weight, bias, steps)
        return 0

    lax.fori_loop(0, rows - 2 * HALF, one, 0)
    reduce_part(
        tile, first, last, conv_out, reduce_weight, reduce_bias, before, before_out, feat_out
    )

    @pl.when(last)
    def _():
        gram_out[...], colsum_out[...] = feat_sums(feat_out[...])


def edge_kernel(
    spread_in, top, bottom, corners_top, corners_bottom, weight, bias, reduce_weight, reduce_bias,
    gram_in, colsum_in,
    spread_top, spread_bottom, conv_out, before_out, feat_out, sums_out,
    wide_row, spread_weight, before,
):
    tile = pl.program_id(0)
    first, last = tile == 0, tile == pl.num_programs(0) - 1
    rows, cols = spread_in.shape[1], top.shape[1]
    steps = cols // GROUPS
    spread_weights(weight, spread_weight)
    for row in range(HALF):
        fill_row(wide_row.at[row], top[row], corners_top[0, row], corners_top[1, row])
        spread_columns(wide_row.at[row], spread_top.at[0, row])
        fill_row(wide_row.at[row + HALF], bottom[row], corners_bottom[0, row], corners_bottom[1, row])
        spread_columns(wide_row.at[row + HALF], spread_bottom.at[0, row])

    def load_from(row):
        def load(row_tap, group):
            place = row + row_tap - HALF
            if place < 0:
                return spread_top[0, place + HALF, group]
            if place >= rows:
                return spread_bottom[0, place - rows, group]
            return spread_in[0, place, group]

        return load

    for index, row in enumerate(edge_rows(rows)):
        conv_out[index * cols : (index + 1) * cols, :] = conv_row(
            load_from(row), spread_weight, bias, steps
        )
    reduce_part(
        tile, first, last, conv_out, reduce_weight, reduce_bias, before, before_out, feat_out
    )

    @pl.when(last)
    def _():
        gram, colsum = feat_sums(feat_out[...])
        gram = gram + gram_in[...]
        colsum = colsum + colsum_in[...]
        width = gram.shape[0]
        half = width // 2
        quarter = half // 2
        sums_out[:half, :] = gram[:half, :]
        sums_out[half : half + quarter, :half] = gram[half : half + quarter, half:]
        sums_out[half : half + quarter, half:] = gram[half + quarter :, half:]
        sums_out[half + quarter :, :] = jnp.broadcast_to(
            colsum, (sums_out.shape[0] - half - quarter, width)
        )


def edge_rows(rows):
    return list(range(HALF)) + list(range(rows - HALF, rows))


def whole_spec(shape):
    return pl.BlockSpec(shape, lambda tile: (0,) * len(shape))


def tile_spec(shape):
    return pl.BlockSpec(shape, lambda tile: (0,) * (len(shape) - 1) + (tile,))


def lead_spec(shape):
    return pl.BlockSpec((1,) + shape[1:], lambda tile: (tile,) + (0,) * (len(shape) - 1))


def row_spec(shape):
    return pl.BlockSpec(shape, lambda tile: (tile, 0))


def shape_of(shape, dtype=wide):
    return jax.ShapeDtypeStruct(shape, dtype)


def conv_inner(block, left, right, weight, bias, reduce_weight, reduce_bias):
    rows, cols, channels = block.shape
    width = reduce_weight.shape[1]
    tiles = channels // LANES
    steps = cols // GROUPS
    pixels = (rows - 2 * HALF) * cols
    spread = (tiles, rows, steps + KERNEL - 1, GROUPS, LANES)
    return pl.pallas_call(
        inner_kernel,
        grid=(tiles,),
        in_specs=[
            tile_spec((rows, cols, LANES)),
            tile_spec((rows, HALF, LANES)),
            tile_spec((rows, HALF, LANES)),
            tile_spec((KERNEL * KERNEL, LANES)),
            tile_spec((1, LANES)),
            row_spec((LANES, width)),
            whole_spec((1, width)),
        ],
        out_specs=[
            lead_spec(spread),
            tile_spec((pixels, LANES)),
            whole_spec((pixels, width)),
            whole_spec((pixels, width)),
            whole_spec((width, width)),
            whole_spec((1, width)),
        ],
        out_shape=[
            shape_of(spread),
            shape_of((pixels, channels), narrow),
            shape_of((pixels, width)),
            shape_of((pixels, width), narrow),
            shape_of((width, width)),
            shape_of((1, width)),
        ],
        scratch_shapes=[
            pltpu.VMEM((rows, cols + 2 * EDGE, LANES), wide),
            pltpu.VMEM((KERNEL * KERNEL, GROUPS, LANES), wide),
            pltpu.VMEM((pixels, width), wide),
        ],
        compiler_params=params(32, 1),
        cost_estimate=pl.CostEstimate(
            flops=2 * KERNEL * KERNEL * pixels * channels,
            bytes_accessed=4 * rows * cols * channels * 2,
            transcendentals=pixels * width,
        ),
        name="conv_inner",
    )(block, left, right, weight, bias, reduce_weight, reduce_bias)


def conv_edge(spread, halos, weight, bias, reduce_weight, reduce_bias, gram, colsum):
    top, bottom, corners_top, corners_bottom = halos
    tiles, rows, groups = spread.shape[:3]
    cols, channels = top.shape[1:]
    width = reduce_weight.shape[1]
    pixels = 2 * HALF * cols
    side = (tiles, HALF, groups, GROUPS, LANES)
    sums_rows = 3 * width // 4 + 2 * GROUPS
    return pl.pallas_call(
        edge_kernel,
        grid=(tiles,),
        in_specs=[
            lead_spec(spread.shape),
            tile_spec((HALF, cols, LANES)),
            tile_spec((HALF, cols, LANES)),
            tile_spec((2, HALF, HALF, LANES)),
            tile_spec((2, HALF, HALF, LANES)),
            tile_spec((KERNEL * KERNEL, LANES)),
            tile_spec((1, LANES)),
            row_spec((LANES, width)),
            whole_spec((1, width)),
            whole_spec((width, width)),
            whole_spec((1, width)),
        ],
        out_specs=[
            lead_spec(side),
            lead_spec(side),
            tile_spec((pixels, LANES)),
            whole_spec((pixels, width)),
            whole_spec((pixels, width)),
            whole_spec((sums_rows, width)),
        ],
        out_shape=[
            shape_of(side),
            shape_of(side),
            shape_of((pixels, channels), narrow),
            shape_of((pixels, width)),
            shape_of((pixels, width), narrow),
            shape_of((sums_rows, width)),
        ],
        scratch_shapes=[
            pltpu.VMEM((2 * HALF, cols + 2 * EDGE, LANES), wide),
            pltpu.VMEM((KERNEL * KERNEL, GROUPS, LANES), wide),
            pltpu.VMEM((pixels, width), wide),
        ],
        compiler_params=params(32, 1),
        cost_estimate=pl.CostEstimate(
            flops=2 * KERNEL * KERNEL * pixels * channels,
            bytes_accessed=4 * rows * cols * channels * 2,
            transcendentals=pixels * width,
        ),
        name="conv_edge",
    )(
        spread, top, bottom, corners_top, corners_bottom,
        weight, bias, reduce_weight, reduce_bias, gram, colsum,
    )


def split(value):
    high = value.astype(narrow)
    return high, (value - high.astype(wide)).astype(narrow)


def product(left, right):
    def dot(a, b):
        return jnp.dot(a, b, preferred_element_type=wide)

    return dot(left[0], right[0]) + (dot(left[0], right[1]) + dot(left[1], right[0]))


def square_root(current):
    size = current.shape[0]
    row = lax.broadcasted_iota(jnp.int32, (size, size), 0)
    col = lax.broadcasted_iota(jnp.int32, (size, size), 1)
    triple = jnp.where(row == col, 3.0, 0.0)
    factor = split(0.5 * (triple - current))
    current = split(current)
    trail = [(current, None, factor)]
    inverse = factor
    current = split(product(current, factor))
    for step in range(1, NEWTON_STEPS):
        factor = split(0.5 * (triple - product(inverse, current)))
        trail.append((current, inverse, factor))
        last = step == NEWTON_STEPS - 1
        if not last:
            inverse = split(product(factor, inverse))
        current = product(current, factor)
        if not last:
            current = split(current)
    return current, trail


def square_root_change(change, trail):
    first, _, factor = trail[0]
    move = split(change)
    factor_move = split(-0.5 * change)
    change = product(move, factor) + product(first, factor_move)
    inverse_move = factor_move
    for step in range(1, NEWTON_STEPS):
        current, inverse, factor = trail[step]
        move = split(change)
        factor_move = split(
            -0.5 * (product(inverse_move, current) + product(inverse, move))
        )
        change = product(move, factor) + product(current, factor_move)
        if step < NEWTON_STEPS - 1:
            inverse_move = split(product(factor_move, inverse) + product(factor, inverse_move))
    return change


def head_kernel(
    flags, own, other, class_weight, class_bias, feat_inner, feat_edge, gate_inner, gate_edge,
    conv_turned, reduce_turned,
    root_out, facts_out, weight_grad_out, bias_grad_out, conv_inner_out, conv_edge_out,
    sums, root_grad_ref, pre, *, count, image_count,
):
    width = root_out.shape[0]
    half = width // 2
    quarter = half // 2
    rows = own.shape[0]
    upper = flags[0] != 0
    mine, theirs = own[...], other[...]
    sums[:rows, :] = jnp.where(upper, theirs, mine)
    sums[rows:, :] = jnp.where(upper, mine, theirs)
    low = jnp.concatenate(
        [sums[half : half + quarter, :half], sums[half : half + quarter, half:]], axis=0
    )
    cross = sums[:half, half:]
    gram = jnp.concatenate(
        [sums[:half, :], jnp.concatenate([cross.T, low], axis=1)], axis=0
    )
    mean_row = sums[half + quarter : half + quarter + 1, :] / count
    mean_col = jnp.broadcast_to(mean_row, (width, width)).T
    sigma = gram / count - mean_col * mean_row
    row = lax.broadcasted_iota(jnp.int32, (width, width), 0)
    col = lax.broadcasted_iota(jnp.int32, (width, width), 1)
    diagonal = row == col
    trace_value = jnp.sum(jnp.where(diagonal, sigma, 0.0), keepdims=True) + epsilon
    root_scale = jnp.sqrt(trace_value)
    unit, trail = square_root(sigma / trace_value)
    root = root_scale * unit
    root_out[...] = root

    classes = class_weight.shape[0]
    slots = class_bias.shape[0]
    place = lax.broadcasted_iota(jnp.int32, (slots, 1), 0)
    partial = [
        jnp.sum(class_weight[index].astype(wide) * root, axis=0, keepdims=True)
        for index in range(classes)
    ]
    partial.append(jnp.zeros((slots - classes, width), wide))
    logits = jnp.sum(jnp.concatenate(partial, axis=0), axis=1, keepdims=True) + class_bias[...]
    onehot = jnp.where(place == flags[1], 1.0, 0.0)
    soft = jnp.maximum(logits, 0.0) + jnp.log(1.0 + jnp.exp(-jnp.abs(logits)))
    share = 1.0 / (1.0 + jnp.exp(-logits))
    used = place < classes
    loss_part = jnp.sum(jnp.where(used, soft - onehot * logits, 0.0), keepdims=True)
    logit_grad = jnp.where(used, loss_scale * (share - onehot) / image_count, 0.0)
    facts_out[...] = jnp.broadcast_to(
        jnp.where(place == classes, loss_part, logit_grad), facts_out.shape
    )

    root_grad = jnp.zeros((width, width), wide)
    for index in range(classes):
        root_grad = root_grad + class_weight[index].astype(wide) * logit_grad[index : index + 1, :]
    root_grad = root_grad + root_grad.T
    change = square_root_change(root_scale * root_grad, trail)
    trace_grad = jnp.sum(root_grad * unit, keepdims=True) / (2.0 * root_scale) - jnp.sum(
        change * sigma, keepdims=True
    ) / (trace_value * trace_value)
    symmetric = (
        (change / trace_value + jnp.where(diagonal, trace_grad, 0.0)) / count
    ).astype(narrow)
    mean_term = jnp.sum(mean_col * symmetric.astype(wide), axis=0, keepdims=True)

    inner = feat_inner.shape[0]
    for feat, gate, start in ((feat_inner, gate_inner, 0), (feat_edge, gate_edge, inner)):
        grad = jnp.dot(feat[...], symmetric, preferred_element_type=wide) - mean_term
        pre[start : start + feat.shape[0], :] = (grad * gate[...]).astype(narrow)
    pre_grad = pre[...]
    bias_grad_out[...] = jnp.sum(pre_grad.astype(wide), axis=0, keepdims=True)
    weight_grad_out[...] = jnp.dot(conv_turned[...], pre_grad, preferred_element_type=wide)
    for out, start in ((conv_inner_out, 0), (conv_edge_out, inner)):
        out[...] = jnp.dot(
            pre[start : start + out.shape[0], :], reduce_turned[...], preferred_element_type=wide
        ).astype(narrow)


def head(flags, own, other, class_weight, class_bias, prepared, count, image_count):
    feat_inner, feat_edge, gate_inner, gate_edge, conv_turned, reduce_turned = prepared
    width, channels = reduce_turned.shape
    inner, edge = feat_inner.shape[0], feat_edge.shape[0]
    slots = class_bias.shape[0]
    in_vmem = pl.BlockSpec(memory_space=pltpu.VMEM)
    return pl.pallas_call(
        functools.partial(head_kernel, count=count, image_count=image_count),
        in_specs=[pl.BlockSpec(memory_space=pltpu.SMEM)] + [in_vmem] * 10,
        out_specs=[in_vmem] * 6,
        out_shape=[
            shape_of((width, width)),
            shape_of((slots, width)),
            shape_of((channels, width)),
            shape_of((1, width)),
            shape_of((inner, channels), narrow),
            shape_of((edge, channels), narrow),
        ],
        scratch_shapes=[
            pltpu.VMEM((2 * own.shape[0], width), wide),
            pltpu.VMEM((width, width), wide),
            pltpu.VMEM((inner + edge, width), narrow),
        ],
        compiler_params=params(48),
        cost_estimate=pl.CostEstimate(
            flops=200 * 2 * width**3, bytes_accessed=8 * 1024 * 1024, transcendentals=0
        ),
        name="head",
    )(
        flags, own, other, class_weight, class_bias,
        feat_inner, feat_edge, gate_inner, gate_edge, conv_turned, reduce_turned,
    )


def prepare_kernel(
    before_inner, before_edge, conv_inner_in, conv_edge_in, reduce_weight,
    gate_inner, gate_edge, conv_turned, reduce_turned,
):
    for before, gate in ((before_inner, gate_inner), (before_edge, gate_edge)):
        value = before[...]
        share = 1.0 / (1.0 + jnp.exp(-value))
        gate[...] = share * (1.0 + value * (1.0 - share))
    inner = conv_inner_in.shape[0]
    conv_turned[:, :inner] = conv_inner_in[...].T
    conv_turned[:, inner:] = conv_edge_in[...].T
    reduce_turned[...] = reduce_weight[...].T


def prepare(before_inner, before_edge, conv_in, conv_ed, reduce_weight):
    in_vmem = pl.BlockSpec(memory_space=pltpu.VMEM)
    channels, width = reduce_weight.shape
    inner, edge = before_inner.shape[0], before_edge.shape[0]
    return pl.pallas_call(
        prepare_kernel,
        in_specs=[in_vmem] * 5,
        out_specs=[in_vmem] * 4,
        out_shape=[
            shape_of((inner, width)),
            shape_of((edge, width)),
            shape_of((channels, inner + edge), narrow),
            shape_of((width, channels), narrow),
        ],
        compiler_params=params(32),
        cost_estimate=pl.CostEstimate(
            flops=10**9, bytes_accessed=6 * 1024 * 1024, transcendentals=(inner + edge) * width
        ),
        name="prepare",
    )(before_inner, before_edge, conv_in, conv_ed, reduce_weight)


def taps_kernel(spread_in, spread_top, spread_bottom, grad_inner, grad_edge, out, grads):
    rows = spread_in.shape[1]
    steps = grads.shape[1]
    cols = steps * GROUPS
    order = edge_rows(rows)
    for row in range(rows):
        if row in order:
            source, place = grad_edge, order.index(row)
        else:
            source, place = grad_inner, row - HALF
        values = source[place * cols : (place + 1) * cols, :].astype(wide)
        for step in range(steps):
            grads[row, step] = values[step * GROUPS : (step + 1) * GROUPS, :]

    def load(place, group):
        if place < 0:
            return spread_top[0, place + HALF, group]
        if place >= rows:
            return spread_bottom[0, place - rows, group]
        return spread_in[0, place, group]

    for first in range(0, KERNEL, 2):
        row_taps = [tap for tap in (first, first + 1) if tap < KERNEL]
        total = {
            (row_tap, col_tap): jnp.zeros((GROUPS, LANES), wide)
            for row_tap in row_taps
            for col_tap in range(KERNEL)
        }
        for place in range(first - HALF, rows + row_taps[-1] - HALF):
            windows = [load(place, group) for group in range(steps + KERNEL - 1)]
            for row_tap in row_taps:
                row = place - row_tap + HALF
                if not 0 <= row < rows:
                    continue
                for step in range(steps):
                    grad = grads[row, step]
                    for col_tap in range(KERNEL):
                        total[row_tap, col_tap] += windows[step + col_tap] * grad
        for (row_tap, col_tap), value in total.items():
            tap = row_tap * KERNEL + col_tap
            out[tap : tap + 1, :] = jnp.sum(value, axis=0, keepdims=True)
    total = [jnp.zeros((GROUPS, LANES), wide) for _ in range(KERNEL)]
    for index in range(rows * steps):
        slot = index % KERNEL
        total[slot] = total[slot] + grads[index // steps, index % steps]
    taps = KERNEL * KERNEL
    out[taps : taps + 1, :] = jnp.sum(sum(total), axis=0, keepdims=True)
    out[taps + 1 :, :] = jnp.zeros((out.shape[0] - taps - 1, LANES), wide)


def tap_grads(spread, spread_top, spread_bottom, grad_inner, grad_edge, first, many):
    tiles, rows, groups = spread.shape[:3]
    steps = groups - KERNEL + 1
    side = spread_top.shape

    def from_lead(shape):
        return pl.BlockSpec((1,) + shape[1:], lambda tile: (tile + first,) + (0,) * (len(shape) - 1))

    def from_tile(shape):
        return pl.BlockSpec((shape[0], LANES), lambda tile: (0, tile + first))

    return pl.pallas_call(
        taps_kernel,
        grid=(many,),
        in_specs=[
            from_lead(spread.shape),
            from_lead(side),
            from_lead(side),
            from_tile(grad_inner.shape),
            from_tile(grad_edge.shape),
        ],
        out_specs=pl.BlockSpec((KERNEL * KERNEL + 15, LANES), lambda tile: (0, tile)),
        out_shape=shape_of((KERNEL * KERNEL + 15, many * LANES)),
        scratch_shapes=[pltpu.VMEM((rows, steps, GROUPS, LANES), wide)],
        compiler_params=params(32, 1),
        cost_estimate=pl.CostEstimate(
            flops=2 * KERNEL * KERNEL * rows * steps * GROUPS * many * LANES,
            bytes_accessed=8 * 1024 * 1024 * many // tiles,
            transcendentals=0,
        ),
        name="tap_grads",
    )(spread, spread_top, spread_bottom, grad_inner, grad_edge)


def body(
    features, depth_weight, depth_bias, reduce_weight, reduce_bias, class_weight, class_bias, labels
):
    block = features[0]
    rows, cols, channels = block.shape
    width = reduce_weight.shape[1]
    classes = class_bias.shape[0]
    count = rows * cols * lax.axis_size("sy") * lax.axis_size("sx")
    image_count = features.shape[0] * lax.axis_size("dp")

    left = next_along(block[:, cols - HALF :], "sx")
    right = back_along(block[:, :HALF], "sx")
    top = next_along(block[rows - HALF :], "sy")
    bottom = back_along(block[:HALF], "sy")
    corners_top = next_along(jnp.stack([left[rows - HALF :], right[rows - HALF :]]), "sy")
    corners_bottom = back_along(jnp.stack([left[:HALF], right[:HALF]]), "sy")

    flat_weight = depth_weight.reshape(KERNEL * KERNEL, channels)
    flat_bias = depth_bias[None]
    reduce_row = reduce_bias[None]
    spread, conv_in, before_in, feat_in, gram, colsum = conv_inner(
        block, left, right, flat_weight, flat_bias, reduce_weight, reduce_row
    )
    spread_top, spread_bottom, conv_ed, before_ed, feat_ed, sums = conv_edge(
        spread,
        (top, bottom, corners_top, corners_bottom),
        flat_weight,
        flat_bias,
        reduce_weight,
        reduce_row,
        gram,
        colsum,
    )

    sums = halve(sums, "sx", 1, wide)
    gate_in, gate_ed, conv_turned, reduce_turned = prepare(
        before_in, before_ed, conv_in, conv_ed, reduce_weight
    )
    for shift in doublings("sx", 2):
        sums = exchange(sums, "sx", shift, wide)
    for shift in doublings("sy"):
        sums = exchange(sums, "sy", shift, wide)
    other = swap(sums, "sx", 1)

    flags = jnp.stack([is_upper("sx", 1).astype(jnp.int32), labels[0]])
    bias_column = jnp.pad(class_bias, (0, -classes % (2 * GROUPS)))[:, None]
    root, facts, weight_grad, bias_grad, conv_grad_in, conv_grad_ed = head(
        flags,
        sums,
        other,
        class_weight,
        bias_column,
        (feat_in, feat_ed, gate_in, gate_ed, conv_turned, reduce_turned),
        count,
        image_count,
    )

    sent = jnp.concatenate([root, facts])
    known = [sent] + [swap(sent, "dp", shift) for shift in range(1, lax.axis_size("dp"))]
    class_weight_grad = tree_sum(
        [part[width : width + classes, 0][:, None, None] * part[None, :width] for part in known]
    )
    totals = tree_sum([part[width:, 0] for part in known])
    class_bias_grad = totals[:classes]
    loss = totals[classes] / image_count

    tiles = channels // LANES
    many = tiles // 3 if tiles % 3 == 0 else tiles
    parts = [
        tap_grads(spread, spread_top, spread_bottom, conv_grad_in, conv_grad_ed, first, many)
        for first in range(0, tiles, many)
    ]
    weight_grad = halve(weight_grad, "sx", 1, wide)
    for shift in doublings("sx", 2):
        weight_grad = halve(weight_grad, "sx", shift, narrow)
    for shift in doublings("dp"):
        weight_grad = exchange(weight_grad, "dp", shift, narrow)
    weight_grad = exchange_all(weight_grad, "sy", narrow)
    for shift in reversed(doublings("sx")):
        weight_grad = unhalve(weight_grad, "sx", shift)

    taps = KERNEL * KERNEL
    small = jnp.concatenate(parts, axis=1)
    row = jnp.arange(small.shape[0])[:, None]
    small = jnp.where(row == taps + 1, jnp.pad(bias_grad, ((0, 0), (0, channels - width))), small)
    small = halve(small, "sx", 1, wide)
    for shift in doublings("sx", 2):
        small = exchange(small, "sx", shift, narrow)
    for shift in doublings("dp"):
        small = exchange(small, "dp", shift, narrow)
    small = exchange_all(small, "sy", narrow)
    small = unhalve(small, "sx", 1)
    return (
        loss,
        small[:taps].reshape(depth_weight.shape),
        small[taps],
        weight_grad,
        small[taps + 1, :width],
        class_weight_grad,
        class_bias_grad,
    )


def solution(mesh):
    placed = (P("dp", "sy", "sx", None), P(), P(), P(), P(), P(), P(), P("dp"))
    return jax.shard_map(
        body,
        mesh=mesh,
        in_specs=placed,
        out_specs=(P(), P(), P(), P(), P(), P(), P()),
        check_vma=False,
    )
```

```python
import functools

import jax
import jax.numpy as jnp
from jax import lax
from jax.experimental import pallas as pl
from jax.experimental.pallas import tpu as pltpu
from jax.sharding import PartitionSpec as P

KERNEL = 7
HALF = KERNEL // 2
NEWTON_STEPS = 5
LANES = 128
GROUPS = 8
EDGE = 8

epsilon = 1e-05
loss_scale = 64.0
narrow = jnp.bfloat16
wide = jnp.float32


def params(megabytes, grid_axes=0):
    return pltpu.CompilerParams(
        vmem_limit_bytes=megabytes * 1024 * 1024,
        dimension_semantics=("arbitrary",) * grid_axes if grid_axes else None,
    )


def swap(value, axis, shift):
    count = lax.axis_size(axis)
    return lax.ppermute(value, axis, [(i, i ^ shift) for i in range(count)])


def is_upper(axis, shift):
    return (lax.axis_index(axis) & shift) != 0


def halve(value, axis, shift, sent_as):
    upper = is_upper(axis, shift)
    rows = value.shape[0] // 2
    low, high = value[:rows], value[rows:]
    kept = jnp.where(upper, high, low)
    sent = jnp.where(upper, low, high).astype(sent_as)
    return kept + swap(sent, axis, shift).astype(wide)


def unhalve(value, axis, shift):
    upper = is_upper(axis, shift)
    other = swap(value, axis, shift)
    return jnp.concatenate([jnp.where(upper, other, value), jnp.where(upper, value, other)])


def tree_sum(terms):
    while len(terms) > 1:
        terms = [terms[i] + terms[i + 1] for i in range(0, len(terms), 2)]
    return terms[0]


def exchange(value, axis, shift, sent_as):
    sent = value.astype(sent_as)
    return sent.astype(wide) + swap(sent, axis, shift).astype(wide)


def exchange_all(value, axis, sent_as):
    sent = value.astype(sent_as)
    moved = [sent] + [swap(sent, axis, shift) for shift in range(1, lax.axis_size(axis))]
    return tree_sum([part.astype(wide) for part in moved])


def doublings(axis, first=1):
    found = []
    shift = first
    while shift < lax.axis_size(axis):
        found.append(shift)
        shift *= 2
    return found


def next_along(value, axis):
    return lax.ppermute(value, axis, [(i, i + 1) for i in range(lax.axis_size(axis) - 1)])


def back_along(value, axis):
    return lax.ppermute(value, axis, [(i + 1, i) for i in range(lax.axis_size(axis) - 1)])


def spread_columns(source, target):
    for group in range(target.shape[0]):
        target[group] = source[pl.ds(EDGE - HALF + group, GROUPS, stride=GROUPS), :]


def fill_row(wide_row, middle, left, right):
    cols = middle.shape[0]
    wide_row[EDGE : EDGE + cols, :] = middle.astype(wide)
    wide_row[EDGE - HALF : EDGE, :] = left.astype(wide)
    wide_row[EDGE + cols : EDGE + cols + HALF, :] = right.astype(wide)


def spread_weights(weight_ref, spread_ref):
    for row_tap in range(KERNEL):
        for col_tap in range(KERNEL):
            scale = weight_ref[row_tap, col_tap : col_tap + 1, :]
            spread_ref[row_tap * KERNEL + col_tap] = jnp.broadcast_to(scale, spread_ref.shape[1:])


def conv_row(load, spread_ref, bias_ref, steps):
    total = [jnp.broadcast_to(bias_ref[0:1, :], (GROUPS, LANES))] * steps
    for row_tap in range(KERNEL):
        windows = [load(row_tap, group) for group in range(steps + KERNEL - 1)]
        for col_tap in range(KERNEL):
            scale = spread_ref[row_tap * KERNEL + col_tap]
            for step in range(steps):
                total[step] = total[step] + windows[step + col_tap] * scale
    return jnp.concatenate(total, axis=0).astype(narrow)


def reduce_part(tile, first, last, conv_out, reduce_ref, reduce_bias_ref, before, before_out, feat_out):
    product = jnp.dot(conv_out[...], reduce_ref[...], preferred_element_type=wide)

    @pl.when(first)
    def _():
        before[...] = product + reduce_bias_ref[...]

    @pl.when(jnp.logical_not(first))
    def _():
        before[...] += product

    @pl.when(last)
    def _():
        total = before[...]
        before_out[...] = total
        feat_out[...] = (total / (1.0 + jnp.exp(-total))).astype(narrow)


def feat_sums(feat):
    gram = lax.dot_general(feat, feat, (((0,), (0,)), ((), ())), preferred_element_type=wide)
    colsum = jnp.sum(feat.astype(wide), axis=0, keepdims=True)
    return gram, colsum


def inner_kernel(
    block, left, right, weight, bias, reduce_weight, reduce_bias,
    spread_out, conv_out, before_out, feat_out, gram_out, colsum_out,
    wide_row, spread_weight, before,
):
    tile = pl.program_id(0)
    first, last = tile == 0, tile == pl.num_programs(0) - 1
    rows, cols = block.shape[0], block.shape[1]
    steps = cols // GROUPS
    spread_weights(weight, spread_weight)

    def fill(row, _):
        fill_row(wide_row.at[row], block[row], left[row], right[row])
        spread_columns(wide_row.at[row], spread_out.at[0, row])
        return 0

    lax.fori_loop(0, rows, fill, 0)

    def one(index, _):
        def load(row_tap, group):
            return spread_out[0, index + row_tap, group]

        start = pl.multiple_of(index * cols, cols)
        conv_out[pl.ds(start, cols), :] = conv_row(load, spread_weight, bias, steps)
        return 0

    lax.fori_loop(0, rows - 2 * HALF, one, 0)
    reduce_part(
        tile, first, last, conv_out, reduce_weight, reduce_bias, before, before_out, feat_out
    )

    @pl.when(last)
    def _():
        gram_out[...], colsum_out[...] = feat_sums(feat_out[...])


def edge_kernel(
    spread_in, top, bottom, weight, bias, reduce_weight, reduce_bias, gram_in, colsum_in,
    spread_top, spread_bottom, conv_out, before_out, feat_out, sums_out,
    wide_row, corners, spread_weight, before,
):
    tile = pl.program_id(0)
    first, last = tile == 0, tile == pl.num_programs(0) - 1
    rows, cols = spread_in.shape[1], wide_row.shape[1] - 2 * EDGE
    steps = cols // GROUPS
    spread_weights(weight, spread_weight)
    for side, (strip, spread) in enumerate(((top, spread_top), (bottom, spread_bottom))):
        corners[side] = strip[HALF * cols :, :].astype(wide)
        for row in range(HALF):
            place = wide_row.at[side * HALF + row]
            left = corners[side, row * HALF : (row + 1) * HALF, :]
            right = corners[side, (HALF + row) * HALF : (HALF + row + 1) * HALF, :]
            fill_row(place, strip[row * cols : (row + 1) * cols, :], left, right)
            spread_columns(place, spread.at[0, row])

    def load_from(row):
        def load(row_tap, group):
            place = row + row_tap - HALF
            if place < 0:
                return spread_top[0, place + HALF, group]
            if place >= rows:
                return spread_bottom[0, place - rows, group]
            return spread_in[0, place, group]

        return load

    for index, row in enumerate(edge_rows(rows)):
        conv_out[index * cols : (index + 1) * cols, :] = conv_row(
            load_from(row), spread_weight, bias, steps
        )
    reduce_part(
        tile, first, last, conv_out, reduce_weight, reduce_bias, before, before_out, feat_out
    )

    @pl.when(last)
    def _():
        gram, colsum = feat_sums(feat_out[...])
        gram = gram + gram_in[...]
        colsum = colsum + colsum_in[...]
        width = gram.shape[0]
        half = width // 2
        quarter = half // 2
        sums_out[:half, :] = gram[:half, :]
        sums_out[half : half + quarter, :half] = gram[half : half + quarter, half:]
        sums_out[half : half + quarter, half:] = gram[half + quarter :, half:]
        sums_out[half + quarter :, :] = jnp.broadcast_to(
            colsum, (sums_out.shape[0] - half - quarter, width)
        )


def edge_rows(rows):
    return list(range(HALF)) + list(range(rows - HALF, rows))


def whole_spec(shape):
    return pl.BlockSpec(shape, lambda tile: (0,) * len(shape))


def tile_spec(shape):
    return pl.BlockSpec(shape, lambda tile: (0,) * (len(shape) - 1) + (tile,))


def lead_spec(shape):
    return pl.BlockSpec((1,) + shape[1:], lambda tile: (tile,) + (0,) * (len(shape) - 1))


def row_spec(shape):
    return pl.BlockSpec(shape, lambda tile: (tile, 0))


def shape_of(shape, dtype=wide):
    return jax.ShapeDtypeStruct(shape, dtype)


def conv_inner(block, left, right, weight, bias, reduce_weight, reduce_bias):
    rows, cols, channels = block.shape
    width = reduce_weight.shape[1]
    tiles = channels // LANES
    steps = cols // GROUPS
    pixels = (rows - 2 * HALF) * cols
    spread = (tiles, rows, steps + KERNEL - 1, GROUPS, LANES)
    return pl.pallas_call(
        inner_kernel,
        grid=(tiles,),
        in_specs=[
            tile_spec((rows, cols, LANES)),
            tile_spec((rows, HALF, LANES)),
            tile_spec((rows, HALF, LANES)),
            tile_spec((KERNEL, KERNEL, LANES)),
            tile_spec((1, LANES)),
            row_spec((LANES, width)),
            whole_spec((1, width)),
        ],
        out_specs=[
            lead_spec(spread),
            tile_spec((pixels, LANES)),
            whole_spec((pixels, width)),
            whole_spec((pixels, width)),
            whole_spec((width, width)),
            whole_spec((1, width)),
        ],
        out_shape=[
            shape_of(spread),
            shape_of((pixels, channels), narrow),
            shape_of((pixels, width)),
            shape_of((pixels, width), narrow),
            shape_of((width, width)),
            shape_of((1, width)),
        ],
        scratch_shapes=[
            pltpu.VMEM((rows, cols + 2 * EDGE, LANES), wide),
            pltpu.VMEM((KERNEL * KERNEL, GROUPS, LANES), wide),
            pltpu.VMEM((pixels, width), wide),
        ],
        compiler_params=params(56, 1),
        cost_estimate=pl.CostEstimate(
            flops=2 * KERNEL * KERNEL * pixels * channels,
            bytes_accessed=4 * rows * cols * channels * 2,
            transcendentals=pixels * width,
        ),
        name="conv_inner",
    )(block, left, right, weight, bias, reduce_weight, reduce_bias)


def conv_edge(spread, halos, weight, bias, reduce_weight, reduce_bias, gram, colsum):
    top, bottom = halos
    tiles, rows, groups = spread.shape[:3]
    cols, channels = (groups - KERNEL + 1) * GROUPS, top.shape[1]
    width = reduce_weight.shape[1]
    pixels = 2 * HALF * cols
    side = (tiles, HALF, groups, GROUPS, LANES)
    sums_rows = 3 * width // 4 + 2 * GROUPS
    return pl.pallas_call(
        edge_kernel,
        grid=(tiles,),
        in_specs=[
            lead_spec(spread.shape),
            tile_spec((top.shape[0], LANES)),
            tile_spec((top.shape[0], LANES)),
            tile_spec((KERNEL, KERNEL, LANES)),
            tile_spec((1, LANES)),
            row_spec((LANES, width)),
            whole_spec((1, width)),
            whole_spec((width, width)),
            whole_spec((1, width)),
        ],
        out_specs=[
            lead_spec(side),
            lead_spec(side),
            tile_spec((pixels, LANES)),
            whole_spec((pixels, width)),
            whole_spec((pixels, width)),
            whole_spec((sums_rows, width)),
        ],
        out_shape=[
            shape_of(side),
            shape_of(side),
            shape_of((pixels, channels), narrow),
            shape_of((pixels, width)),
            shape_of((pixels, width), narrow),
            shape_of((sums_rows, width)),
        ],
        scratch_shapes=[
            pltpu.VMEM((2 * HALF, cols + 2 * EDGE, LANES), wide),
            pltpu.VMEM((2, top.shape[0] - HALF * cols, LANES), wide),
            pltpu.VMEM((KERNEL * KERNEL, GROUPS, LANES), wide),
            pltpu.VMEM((pixels, width), wide),
        ],
        compiler_params=params(56, 1),
        cost_estimate=pl.CostEstimate(
            flops=2 * KERNEL * KERNEL * pixels * channels,
            bytes_accessed=4 * rows * cols * channels * 2,
            transcendentals=pixels * width,
        ),
        name="conv_edge",
    )(
        spread, top, bottom, weight, bias, reduce_weight, reduce_bias, gram, colsum,
    )


def split(value):
    high = value.astype(narrow)
    return high, (value - high.astype(wide)).astype(narrow)


def product(left, right):
    def dot(a, b):
        return jnp.dot(a, b, preferred_element_type=wide)

    return dot(left[0], right[0]) + (dot(left[0], right[1]) + dot(left[1], right[0]))


def square_root(current):
    size = current.shape[0]
    row = lax.broadcasted_iota(jnp.int32, (size, size), 0)
    col = lax.broadcasted_iota(jnp.int32, (size, size), 1)
    triple = jnp.where(row == col, 3.0, 0.0)
    factor = split(0.5 * (triple - current))
    current = split(current)
    trail = [(current, None, factor)]
    inverse = factor
    current = split(product(current, factor))
    for step in range(1, NEWTON_STEPS):
        factor = split(0.5 * (triple - product(inverse, current)))
        trail.append((current, inverse, factor))
        last = step == NEWTON_STEPS - 1
        if not last:
            inverse = split(product(factor, inverse))
        current = product(current, factor)
        if not last:
            current = split(current)
    return current, trail


def square_root_change(change, trail):
    first, _, factor = trail[0]
    move = split(change)
    factor_move = split(-0.5 * change)
    change = product(move, factor) + product(first, factor_move)
    inverse_move = factor_move
    for step in range(1, NEWTON_STEPS):
        current, inverse, factor = trail[step]
        move = split(change)
        factor_move = split(
            -0.5 * (product(inverse_move, current) + product(inverse, move))
        )
        change = product(move, factor) + product(current, factor_move)
        if step < NEWTON_STEPS - 1:
            inverse_move = split(product(factor_move, inverse) + product(factor, inverse_move))
    return change


def head_kernel(
    flags, own, other, class_bias, *refs, count, image_count,
):
    stored, refs = refs[:7], refs[7:]
    root_out, facts_out, weight_grad_out, bias_grad_out, conv_inner_out, conv_edge_out = refs[:6]
    held, (sums, pre, arrived) = refs[6:13], refs[13:]
    copies = [
        pltpu.make_async_copy(source, target, arrived.at[index])
        for index, (source, target) in enumerate(zip(stored, held))
    ]
    for copy in copies:
        copy.start()
    class_weight, feat_inner, feat_edge, gate_inner, gate_edge, conv_turned, reduce_turned = held
    width = root_out.shape[0]
    half = width // 2
    quarter = half // 2
    rows = own.shape[0]
    upper = flags[0] != 0
    mine, theirs = own[...], other[...]
    sums[:rows, :] = jnp.where(upper, theirs, mine)
    sums[rows:, :] = jnp.where(upper, mine, theirs)
    low = jnp.concatenate(
        [sums[half : half + quarter, :half], sums[half : half + quarter, half:]], axis=0
    )
    cross = sums[:half, half:]
    gram = jnp.concatenate(
        [sums[:half, :], jnp.concatenate([cross.T, low], axis=1)], axis=0
    )
    mean_row = sums[half + quarter : half + quarter + 1, :] / count
    mean_col = jnp.broadcast_to(mean_row, (width, width)).T
    sigma = gram / count - mean_col * mean_row
    row = lax.broadcasted_iota(jnp.int32, (width, width), 0)
    col = lax.broadcasted_iota(jnp.int32, (width, width), 1)
    diagonal = row == col
    trace_value = jnp.sum(jnp.where(diagonal, sigma, 0.0), keepdims=True) + epsilon
    root_scale = jnp.sqrt(trace_value)
    unit, trail = square_root(sigma / trace_value)
    root = root_scale * unit
    root_out[...] = root

    copies[0].wait()
    classes = class_weight.shape[0]
    slots = class_bias.shape[0]
    place = lax.broadcasted_iota(jnp.int32, (slots, 1), 0)
    partial = [
        jnp.sum(class_weight[index].astype(wide) * root, axis=0, keepdims=True)
        for index in range(classes)
    ]
    partial.append(jnp.zeros((slots - classes, width), wide))
    logits = jnp.sum(jnp.concatenate(partial, axis=0), axis=1, keepdims=True) + class_bias[...]
    onehot = jnp.where(place == flags[1], 1.0, 0.0)
    soft = jnp.maximum(logits, 0.0) + jnp.log(1.0 + jnp.exp(-jnp.abs(logits)))
    share = 1.0 / (1.0 + jnp.exp(-logits))
    used = place < classes
    loss_part = jnp.sum(jnp.where(used, soft - onehot * logits, 0.0), keepdims=True)
    logit_grad = jnp.where(used, loss_scale * (share - onehot) / image_count, 0.0)
    facts_out[...] = jnp.broadcast_to(
        jnp.where(place == classes, loss_part, logit_grad), facts_out.shape
    )

    root_grad = jnp.zeros((width, width), wide)
    for index in range(classes):
        root_grad = root_grad + class_weight[index].astype(wide) * logit_grad[index : index + 1, :]
    root_grad = root_grad + root_grad.T
    change = square_root_change(root_scale * root_grad, trail)
    trace_grad = jnp.sum(root_grad * unit, keepdims=True) / (2.0 * root_scale) - jnp.sum(
        change * sigma, keepdims=True
    ) / (trace_value * trace_value)
    symmetric = (
        (change / trace_value + jnp.where(diagonal, trace_grad, 0.0)) / count
    ).astype(narrow)
    mean_term = jnp.sum(mean_col * symmetric.astype(wide), axis=0, keepdims=True)

    for copy in copies[1:]:
        copy.wait()
    inner = feat_inner.shape[0]
    for feat, gate, start in ((feat_inner, gate_inner, 0), (feat_edge, gate_edge, inner)):
        grad = jnp.dot(feat[...], symmetric, preferred_element_type=wide) - mean_term
        pre[start : start + feat.shape[0], :] = (grad * gate[...]).astype(narrow)
    pre_grad = pre[...]
    bias_grad_out[...] = jnp.sum(pre_grad.astype(wide), axis=0, keepdims=True)
    weight_grad_out[...] = jnp.dot(conv_turned[...], pre_grad, preferred_element_type=wide)
    for out, start in ((conv_inner_out, 0), (conv_edge_out, inner)):
        out[...] = jnp.dot(
            pre[start : start + out.shape[0], :], reduce_turned[...], preferred_element_type=wide
        ).astype(narrow)


def head(flags, own, other, class_weight, class_bias, prepared, count, image_count):
    feat_inner, feat_edge, gate_inner, gate_edge, conv_turned, reduce_turned = prepared
    width, channels = reduce_turned.shape
    inner, edge = feat_inner.shape[0], feat_edge.shape[0]
    slots = class_bias.shape[0]
    stored = (class_weight,) + tuple(prepared)
    in_vmem = pl.BlockSpec(memory_space=pltpu.VMEM)
    return pl.pallas_call(
        functools.partial(head_kernel, count=count, image_count=image_count),
        in_specs=[pl.BlockSpec(memory_space=pltpu.SMEM)]
        + [in_vmem] * 3
        + [pl.BlockSpec(memory_space=pltpu.HBM)] * len(stored),
        out_specs=[in_vmem] * 6,
        out_shape=[
            shape_of((width, width)),
            shape_of((slots, width)),
            shape_of((channels, width)),
            shape_of((1, width)),
            shape_of((inner, channels), narrow),
            shape_of((edge, channels), narrow),
        ],
        scratch_shapes=[pltpu.VMEM(part.shape, part.dtype) for part in stored]
        + [
            pltpu.VMEM((2 * own.shape[0], width), wide),
            pltpu.VMEM((inner + edge, width), narrow),
            pltpu.SemaphoreType.DMA((len(stored),)),
        ],
        compiler_params=params(56),
        cost_estimate=pl.CostEstimate(
            flops=200 * 2 * width**3, bytes_accessed=8 * 1024 * 1024, transcendentals=0
        ),
        name="head",
    )(
        flags, own, other, class_bias, *stored
    )


def prepare_kernel(
    before_inner, before_edge, conv_inner_in, conv_edge_in, reduce_weight,
    gate_inner, gate_edge, conv_turned, reduce_turned,
):
    for before, gate in ((before_inner, gate_inner), (before_edge, gate_edge)):
        value = before[...]
        share = 1.0 / (1.0 + jnp.exp(-value))
        gate[...] = share * (1.0 + value * (1.0 - share))
    inner = conv_inner_in.shape[0]
    conv_turned[:, :inner] = conv_inner_in[...].T
    conv_turned[:, inner:] = conv_edge_in[...].T
    reduce_turned[...] = reduce_weight[...].T


def prepare(before_inner, before_edge, conv_in, conv_ed, reduce_weight):
    in_vmem = pl.BlockSpec(memory_space=pltpu.VMEM)
    channels, width = reduce_weight.shape
    inner, edge = before_inner.shape[0], before_edge.shape[0]
    return pl.pallas_call(
        prepare_kernel,
        in_specs=[in_vmem] * 5,
        out_specs=[in_vmem] * 4,
        out_shape=[
            shape_of((inner, width)),
            shape_of((edge, width)),
            shape_of((channels, inner + edge), narrow),
            shape_of((width, channels), narrow),
        ],
        compiler_params=params(56),
        cost_estimate=pl.CostEstimate(
            flops=10**9, bytes_accessed=6 * 1024 * 1024, transcendentals=(inner + edge) * width
        ),
        name="prepare",
    )(before_inner, before_edge, conv_in, conv_ed, reduce_weight)


def taps_kernel(spread_in, spread_top, spread_bottom, grad_inner, grad_edge, out, grads):
    rows = spread_in.shape[1]
    steps = grads.shape[1]
    cols = steps * GROUPS
    order = edge_rows(rows)
    for row in range(rows):
        if row in order:
            source, place = grad_edge, order.index(row)
        else:
            source, place = grad_inner, row - HALF
        values = source[place * cols : (place + 1) * cols, :].astype(wide)
        for step in range(steps):
            grads[row, step] = values[step * GROUPS : (step + 1) * GROUPS, :]

    def load(place, group):
        if place < 0:
            return spread_top[0, place + HALF, group]
        if place >= rows:
            return spread_bottom[0, place - rows, group]
        return spread_in[0, place, group]

    for first in range(0, KERNEL, 2):
        row_taps = [tap for tap in (first, first + 1) if tap < KERNEL]
        total = {
            (row_tap, col_tap): jnp.zeros((GROUPS, LANES), wide)
            for row_tap in row_taps
            for col_tap in range(KERNEL)
        }
        for place in range(first - HALF, rows + row_taps[-1] - HALF):
            windows = [load(place, group) for group in range(steps + KERNEL - 1)]
            for row_tap in row_taps:
                row = place - row_tap + HALF
                if not 0 <= row < rows:
                    continue
                for step in range(steps):
                    grad = grads[row, step]
                    for col_tap in range(KERNEL):
                        total[row_tap, col_tap] += windows[step + col_tap] * grad
        for (row_tap, col_tap), value in total.items():
            tap = row_tap * KERNEL + col_tap
            out[tap : tap + 1, :] = jnp.sum(value, axis=0, keepdims=True)
    total = [jnp.zeros((GROUPS, LANES), wide) for _ in range(KERNEL)]
    for index in range(rows * steps):
        slot = index % KERNEL
        total[slot] = total[slot] + grads[index // steps, index % steps]
    taps = KERNEL * KERNEL
    out[taps : taps + 1, :] = jnp.sum(sum(total), axis=0, keepdims=True)
    out[taps + 1 :, :] = jnp.zeros((out.shape[0] - taps - 1, LANES), wide)


def tap_grads(spread, spread_top, spread_bottom, grad_inner, grad_edge, first, many):
    tiles, rows, groups = spread.shape[:3]
    steps = groups - KERNEL + 1
    side = spread_top.shape

    def from_lead(shape):
        return pl.BlockSpec((1,) + shape[1:], lambda tile: (tile + first,) + (0,) * (len(shape) - 1))

    def from_tile(shape):
        return pl.BlockSpec((shape[0], LANES), lambda tile: (0, tile + first))

    return pl.pallas_call(
        taps_kernel,
        grid=(many,),
        in_specs=[
            from_lead(spread.shape),
            from_lead(side),
            from_lead(side),
            from_tile(grad_inner.shape),
            from_tile(grad_edge.shape),
        ],
        out_specs=pl.BlockSpec((KERNEL * KERNEL + 15, LANES), lambda tile: (0, tile)),
        out_shape=shape_of((KERNEL * KERNEL + 15, many * LANES)),
        scratch_shapes=[pltpu.VMEM((rows, steps, GROUPS, LANES), wide)],
        compiler_params=params(56, 1),
        cost_estimate=pl.CostEstimate(
            flops=2 * KERNEL * KERNEL * rows * steps * GROUPS * many * LANES,
            bytes_accessed=8 * 1024 * 1024 * many // tiles,
            transcendentals=0,
        ),
        name="tap_grads",
    )(spread, spread_top, spread_bottom, grad_inner, grad_edge)


def edge_strip(block, left, right, rows):
    channels = block.shape[2]
    parts = [part[rows].reshape(-1, channels) for part in (block, left, right)]
    short = -(2 * HALF * HALF) % 16
    return jnp.concatenate(parts + [jnp.zeros((short, channels), block.dtype)])


def body(
    features, depth_weight, depth_bias, reduce_weight, reduce_bias, class_weight, class_bias, labels
):
    block = features[0]
    rows, cols, channels = block.shape
    width = reduce_weight.shape[1]
    classes = class_bias.shape[0]
    count = rows * cols * lax.axis_size("sy") * lax.axis_size("sx")
    image_count = features.shape[0] * lax.axis_size("dp")

    left = next_along(block[:, cols - HALF :], "sx")
    right = back_along(block[:, :HALF], "sx")
    low, high, left, right = lax.optimization_barrier(
        (
            edge_strip(block, left, right, slice(rows - HALF, rows)),
            edge_strip(block, left, right, slice(0, HALF)),
            left,
            right,
        )
    )
    top = next_along(low, "sy")
    bottom = back_along(high, "sy")

    flat_bias = depth_bias[None]
    reduce_row = reduce_bias[None]
    spread, conv_in, before_in, feat_in, gram, colsum = conv_inner(
        block, left, right, depth_weight, flat_bias, reduce_weight, reduce_row
    )
    spread_top, spread_bottom, conv_ed, before_ed, feat_ed, sums = conv_edge(
        spread,
        (top, bottom),
        depth_weight,
        flat_bias,
        reduce_weight,
        reduce_row,
        gram,
        colsum,
    )

    sums = halve(sums, "sx", 1, wide)
    sums, before_in, before_ed, conv_in, conv_ed = lax.optimization_barrier(
        (sums, before_in, before_ed, conv_in, conv_ed)
    )
    gate_in, gate_ed, conv_turned, reduce_turned = prepare(
        before_in, before_ed, conv_in, conv_ed, reduce_weight
    )
    for shift in doublings("sx", 2):
        sums = exchange(sums, "sx", shift, wide)
    for shift in doublings("sy"):
        sums = exchange(sums, "sy", shift, wide)
    other = swap(sums, "sx", 1)

    flags = jnp.stack([is_upper("sx", 1).astype(jnp.int32), labels[0]])
    bias_column = jnp.pad(class_bias, (0, -classes % (2 * GROUPS)))[:, None]
    root, facts, weight_grad, bias_grad, conv_grad_in, conv_grad_ed = head(
        flags,
        sums,
        other,
        class_weight,
        bias_column,
        (feat_in, feat_ed, gate_in, gate_ed, conv_turned, reduce_turned),
        count,
        image_count,
    )

    sent = jnp.concatenate([root, facts])
    known = [sent] + [swap(sent, "dp", shift) for shift in range(1, lax.axis_size("dp"))]
    class_weight_grad = tree_sum(
        [part[width : width + classes, 0][:, None, None] * part[None, :width] for part in known]
    )
    totals = tree_sum([part[width:, 0] for part in known])
    class_bias_grad = totals[:classes]
    loss = totals[classes] / image_count

    tiles = channels // LANES
    many = tiles // 3 if tiles % 3 == 0 else tiles
    turns = list(range(0, tiles, many))
    parts = []

    def beside(sums):
        nonlocal conv_grad_in, conv_grad_ed
        if not turns:
            return sums
        sums, conv_grad_in, conv_grad_ed, *parts[:] = lax.optimization_barrier(
            (sums, conv_grad_in, conv_grad_ed, *parts)
        )
        parts.append(
            tap_grads(
                spread, spread_top, spread_bottom, conv_grad_in, conv_grad_ed, turns.pop(0), many
            )
        )
        return sums

    weight_grad = halve(weight_grad, "sx", 1, wide)
    for shift in doublings("sx", 2):
        weight_grad = halve(beside(weight_grad), "sx", shift, narrow)
    for shift in doublings("dp"):
        weight_grad = exchange(beside(weight_grad), "dp", shift, narrow)
    weight_grad = exchange_all(beside(weight_grad), "sy", narrow)
    while turns:
        weight_grad = beside(weight_grad)
    for shift in reversed(doublings("sx")):
        weight_grad = unhalve(weight_grad, "sx", shift)

    taps = KERNEL * KERNEL
    small = jnp.concatenate(parts, axis=1)
    row = jnp.arange(small.shape[0])[:, None]
    small = jnp.where(row == taps + 1, jnp.pad(bias_grad, ((0, 0), (0, channels - width))), small)
    small = halve(small, "sx", 1, wide)
    for shift in doublings("sx", 2):
        small = exchange(small, "sx", shift, narrow)
    for shift in doublings("dp"):
        small = exchange(small, "dp", shift, narrow)
    small = exchange_all(small, "sy", narrow)
    small = unhalve(small, "sx", 1)
    return (
        loss,
        small[:taps].reshape(depth_weight.shape),
        small[taps],
        weight_grad,
        small[taps + 1, :width],
        class_weight_grad,
        class_bias_grad,
    )


def solution(mesh):
    placed = (P("dp", "sy", "sx", None), P(), P(), P(), P(), P(), P(), P("dp"))
    return jax.shard_map(
        body,
        mesh=mesh,
        in_specs=placed,
        out_specs=(P(), P(), P(), P(), P(), P(), P()),
        check_vma=False,
    )
```

```python
import functools

import jax
import jax.numpy as jnp
from jax import lax
from jax.experimental import pallas as pl
from jax.experimental.pallas import tpu as pltpu
from jax.sharding import PartitionSpec as P

KERNEL = 7
HALF = KERNEL // 2
NEWTON_STEPS = 5
LANES = 128
GROUPS = 8
EDGE = 8

epsilon = 1e-05
loss_scale = 64.0
narrow = jnp.bfloat16
wide = jnp.float32


def params(megabytes):
    return pltpu.CompilerParams(vmem_limit_bytes=megabytes * 1024 * 1024)


def swap(value, axis, shift):
    count = lax.axis_size(axis)
    return lax.ppermute(value, axis, [(i, i ^ shift) for i in range(count)])


def is_upper(axis, shift):
    return (lax.axis_index(axis) & shift) != 0


def halve(value, axis, shift, sent_as):
    upper = is_upper(axis, shift)
    rows = value.shape[0] // 2
    low, high = value[:rows], value[rows:]
    kept = jnp.where(upper, high, low)
    sent = jnp.where(upper, low, high).astype(sent_as)
    return kept + swap(sent, axis, shift).astype(wide)


def unhalve(value, axis, shift):
    upper = is_upper(axis, shift)
    other = swap(value, axis, shift)
    return jnp.concatenate([jnp.where(upper, other, value), jnp.where(upper, value, other)])


def tree_sum(terms):
    while len(terms) > 1:
        terms = [terms[i] + terms[i + 1] for i in range(0, len(terms), 2)]
    return terms[0]


def exchange(value, axis, shift, sent_as):
    sent = value.astype(sent_as)
    return sent.astype(wide) + swap(sent, axis, shift).astype(wide)


def exchange_all(value, axis, sent_as):
    sent = value.astype(sent_as)
    moved = [sent] + [swap(sent, axis, shift) for shift in range(1, lax.axis_size(axis))]
    return tree_sum([part.astype(wide) for part in moved])


def doublings(axis, first=1):
    found = []
    shift = first
    while shift < lax.axis_size(axis):
        found.append(shift)
        shift *= 2
    return found


def next_along(value, axis):
    return lax.ppermute(value, axis, [(i, i + 1) for i in range(lax.axis_size(axis) - 1)])


def back_along(value, axis):
    return lax.ppermute(value, axis, [(i + 1, i) for i in range(lax.axis_size(axis) - 1)])


def spread_columns(source, target):
    for group in range(target.shape[0]):
        target[group] = source[pl.ds(EDGE - HALF + group, GROUPS, stride=GROUPS), :]


def fill_row(wide_row, middle, left, right):
    cols = middle.shape[0]
    wide_row[EDGE : EDGE + cols, :] = middle.astype(wide)
    wide_row[EDGE - HALF : EDGE, :] = left.astype(wide)
    wide_row[EDGE + cols : EDGE + cols + HALF, :] = right.astype(wide)


def lanes_of(tile):
    return pl.ds(pl.multiple_of(tile * LANES, LANES), LANES)


def spread_weights(weight_ref, spread_ref, lanes):
    for row_tap in range(KERNEL):
        for col_tap in range(KERNEL):
            scale = weight_ref[row_tap, col_tap : col_tap + 1, lanes]
            spread_ref[row_tap * KERNEL + col_tap] = jnp.broadcast_to(scale, spread_ref.shape[1:])


def conv_row(load, spread_ref, bias, steps):
    total = [bias] * steps
    for row_tap in range(KERNEL):
        windows = [load(row_tap, group) for group in range(steps + KERNEL - 1)]
        for col_tap in range(KERNEL):
            scale = spread_ref[row_tap * KERNEL + col_tap]
            for step in range(steps):
                total[step] = total[step] + windows[step + col_tap] * scale
    return jnp.concatenate(total, axis=0).astype(narrow)


def reduce_part(conv_out, reduce_ref, reduce_bias_ref, before_out, feat_out):
    before = jnp.dot(conv_out[...], reduce_ref[...], preferred_element_type=wide)
    before = before + reduce_bias_ref[...]
    before_out[...] = before
    feat_out[...] = (before / (1.0 + jnp.exp(-before))).astype(narrow)
    feat = feat_out[...]
    gram = lax.dot_general(feat, feat, (((0,), (0,)), ((), ())), preferred_element_type=wide)
    return gram, jnp.sum(feat.astype(wide), axis=0, keepdims=True)


def inner_kernel(
    block, left, right, weight, bias, reduce_weight, reduce_bias,
    spread_out, conv_out, before_out, feat_out, gram_out, colsum_out,
    wide_row, spread_weight,
):
    rows, cols = block.shape[0], block.shape[1]
    steps = cols // GROUPS

    def one_tile(tile, _):
        lanes = lanes_of(tile)
        spread_weights(weight, spread_weight, lanes)
        start_value = jnp.broadcast_to(bias[0:1, lanes], (GROUPS, LANES))

        def fill(row, _):
            place = wide_row.at[row]
            fill_row(place, block[row, :, lanes], left[row, :, lanes], right[row, :, lanes])
            spread_columns(place, spread_out.at[tile, row])
            return 0

        lax.fori_loop(0, rows, fill, 0)

        def one_row(index, _):
            def load(row_tap, group):
                return spread_out[tile, index + row_tap, group]

            start = pl.multiple_of(index * cols, cols)
            conv_out[pl.ds(start, cols), lanes] = conv_row(load, spread_weight, start_value, steps)
            return 0

        lax.fori_loop(0, rows - 2 * HALF, one_row, 0)
        return 0

    lax.fori_loop(0, spread_out.shape[0], one_tile, 0)
    gram_out[...], colsum_out[...] = reduce_part(
        conv_out, reduce_weight, reduce_bias, before_out, feat_out
    )


def edge_kernel(
    flag, spread_in, top, bottom, weight, bias, reduce_weight, reduce_bias, gram_in, colsum_in,
    spread_top, spread_bottom, conv_out, before_out, feat_out, kept_out, sent_out,
    wide_row, corners, spread_weight, sums,
):
    rows, cols = spread_in.shape[1], wide_row.shape[1] - 2 * EDGE
    steps = cols // GROUPS

    def one_tile(tile, _):
        lanes = lanes_of(tile)
        spread_weights(weight, spread_weight, lanes)
        start_value = jnp.broadcast_to(bias[0:1, lanes], (GROUPS, LANES))
        for side, (strip, spread) in enumerate(((top, spread_top), (bottom, spread_bottom))):
            corners[side] = strip[HALF * cols :, lanes].astype(wide)
            for row in range(HALF):
                place = wide_row.at[side * HALF + row]
                left = corners[side, row * HALF : (row + 1) * HALF, :]
                right = corners[side, (HALF + row) * HALF : (HALF + row + 1) * HALF, :]
                fill_row(place, strip[row * cols : (row + 1) * cols, lanes], left, right)
                spread_columns(place, spread.at[tile, row])

        def load_from(row):
            def load(row_tap, group):
                place = row + row_tap - HALF
                if place < 0:
                    return spread_top[tile, place + HALF, group]
                if place >= rows:
                    return spread_bottom[tile, place - rows, group]
                return spread_in[tile, place, group]

            return load

        for index, row in enumerate(edge_rows(rows)):
            conv_out[index * cols : (index + 1) * cols, lanes] = conv_row(
                load_from(row), spread_weight, start_value, steps
            )
        return 0

    lax.fori_loop(0, spread_in.shape[0], one_tile, 0)
    gram, colsum = reduce_part(conv_out, reduce_weight, reduce_bias, before_out, feat_out)
    gram = gram + gram_in[...]
    colsum = colsum + colsum_in[...]
    width = gram.shape[0]
    half = width // 2
    quarter = half // 2
    sums[:half, :] = gram[:half, :]
    sums[half : half + quarter, :half] = gram[half : half + quarter, half:]
    sums[half : half + quarter, half:] = gram[half + quarter :, half:]
    sums[half + quarter :, :] = jnp.broadcast_to(
        colsum, (sums.shape[0] - half - quarter, width)
    )
    part = kept_out.shape[0]
    keep_or_send(flag[0] != 0, sums[:part, :], sums[part:, :], kept_out, sent_out)


def keep_or_send(upper, low, high, kept_out, sent_out):
    kept_out[...] = jnp.where(upper, high, low)
    sent_out[...] = jnp.where(upper, low, high).astype(sent_out.dtype)


def edge_rows(rows):
    return list(range(HALF)) + list(range(rows - HALF, rows))


def shape_of(shape, dtype=wide):
    return jax.ShapeDtypeStruct(shape, dtype)


in_vmem = pl.BlockSpec(memory_space=pltpu.VMEM)
in_smem = pl.BlockSpec(memory_space=pltpu.SMEM)


def cost(microseconds):
    return pl.CostEstimate(
        flops=microseconds * 10**9, bytes_accessed=microseconds * 10**6, transcendentals=0
    )


def conv_inner(block, left, right, weight, bias, reduce_weight, reduce_bias):
    rows, cols, channels = block.shape
    width = reduce_weight.shape[1]
    tiles = channels // LANES
    steps = cols // GROUPS
    pixels = (rows - 2 * HALF) * cols
    return pl.pallas_call(
        inner_kernel,
        in_specs=[in_vmem] * 7,
        out_specs=[in_vmem] * 6,
        out_shape=[
            shape_of((tiles, rows, steps + KERNEL - 1, GROUPS, LANES)),
            shape_of((pixels, channels), narrow),
            shape_of((pixels, width)),
            shape_of((pixels, width), narrow),
            shape_of((width, width)),
            shape_of((1, width)),
        ],
        scratch_shapes=[
            pltpu.VMEM((rows, cols + 2 * EDGE, LANES), wide),
            pltpu.VMEM((KERNEL * KERNEL, GROUPS, LANES), wide),
        ],
        compiler_params=params(24),
        cost_estimate=cost(10),
        name="conv_inner",
    )(block, left, right, weight, bias, reduce_weight, reduce_bias)


def conv_edge(flag, spread, top, bottom, weight, bias, reduce_weight, reduce_bias, gram, colsum):
    tiles, rows, groups = spread.shape[:3]
    cols, channels = (groups - KERNEL + 1) * GROUPS, top.shape[1]
    width = reduce_weight.shape[1]
    pixels = 2 * HALF * cols
    side = (tiles, HALF, groups, GROUPS, LANES)
    sums_rows = 3 * width // 4 + 2 * GROUPS
    return pl.pallas_call(
        edge_kernel,
        in_specs=[in_smem] + [in_vmem] * 9,
        out_specs=[in_vmem] * 7,
        out_shape=[
            shape_of(side),
            shape_of(side),
            shape_of((pixels, channels), narrow),
            shape_of((pixels, width)),
            shape_of((pixels, width), narrow),
            shape_of((sums_rows // 2, width)),
            shape_of((sums_rows // 2, width)),
        ],
        scratch_shapes=[
            pltpu.VMEM((2 * HALF, cols + 2 * EDGE, LANES), wide),
            pltpu.VMEM((2, top.shape[0] - HALF * cols, LANES), wide),
            pltpu.VMEM((KERNEL * KERNEL, GROUPS, LANES), wide),
            pltpu.VMEM((sums_rows, width), wide),
        ],
        compiler_params=params(24),
        cost_estimate=cost(6),
        name="conv_edge",
    )(flag, spread, top, bottom, weight, bias, reduce_weight, reduce_bias, gram, colsum)


def split(value):
    high = value.astype(narrow)
    return high, (value - high.astype(wide)).astype(narrow)


def product(left, right):
    def dot(a, b):
        return jnp.dot(a, b, preferred_element_type=wide)

    return dot(left[0], right[0]) + (dot(left[0], right[1]) + dot(left[1], right[0]))


def square_root(current):
    size = current.shape[0]
    row = lax.broadcasted_iota(jnp.int32, (size, size), 0)
    col = lax.broadcasted_iota(jnp.int32, (size, size), 1)
    triple = jnp.where(row == col, 3.0, 0.0)
    factor = split(0.5 * (triple - current))
    current = split(current)
    trail = [(current, None, factor)]
    inverse = factor
    current = split(product(current, factor))
    for step in range(1, NEWTON_STEPS):
        factor = split(0.5 * (triple - product(inverse, current)))
        trail.append((current, inverse, factor))
        last = step == NEWTON_STEPS - 1
        if not last:
            inverse = split(product(factor, inverse))
        current = product(current, factor)
        if not last:
            current = split(current)
    return current, trail


def square_root_change(change, trail):
    first, _, factor = trail[0]
    move = split(change)
    factor_move = split(-0.5 * change)
    change = product(move, factor) + product(first, factor_move)
    inverse_move = factor_move
    for step in range(1, NEWTON_STEPS):
        current, inverse, factor = trail[step]
        move = split(change)
        factor_move = split(
            -0.5 * (product(inverse_move, current) + product(inverse, move))
        )
        change = product(move, factor) + product(current, factor_move)
        if step < NEWTON_STEPS - 1:
            inverse_move = split(product(factor_move, inverse) + product(factor, inverse_move))
    return change


def head_kernel(
    flag, label, class_bias, own, other, class_weight,
    feat_inner, feat_edge, gate_inner, gate_edge, conv_turned, reduce_turned,
    root_out, kept_out, sent_out, bias_grad_out, conv_inner_out, conv_edge_out,
    sums, pre, *, count, image_count,
):
    width = root_out.shape[1]
    half = width // 2
    quarter = half // 2
    rows = own.shape[0]
    upper = flag[0] != 0
    mine, theirs = own[...], other[...]
    sums[:rows, :] = jnp.where(upper, theirs, mine)
    sums[rows:, :] = jnp.where(upper, mine, theirs)
    low = jnp.concatenate(
        [sums[half : half + quarter, :half], sums[half : half + quarter, half:]], axis=0
    )
    cross = sums[:half, half:]
    gram = jnp.concatenate(
        [sums[:half, :], jnp.concatenate([cross.T, low], axis=1)], axis=0
    )
    mean_row = sums[half + quarter : half + quarter + 1, :] / count
    mean_col = jnp.broadcast_to(mean_row, (width, width)).T
    sigma = gram / count - mean_col * mean_row
    row = lax.broadcasted_iota(jnp.int32, (width, width), 0)
    col = lax.broadcasted_iota(jnp.int32, (width, width), 1)
    diagonal = row == col
    trace_value = jnp.sum(jnp.where(diagonal, sigma, 0.0), keepdims=True) + epsilon
    root_scale = jnp.sqrt(trace_value)
    unit, trail = square_root(sigma / trace_value)
    root = root_scale * unit
    root_out[:width, :] = root

    classes = class_weight.shape[0]
    slots = root_out.shape[0] - width
    place = lax.broadcasted_iota(jnp.int32, (slots, 1), 0)
    bias = jnp.zeros((slots, 1), wide)
    for index in range(classes):
        bias = jnp.where(place == index, class_bias[index], bias)
    partial = [
        jnp.sum(class_weight[index].astype(wide) * root, axis=0, keepdims=True)
        for index in range(classes)
    ]
    partial.append(jnp.zeros((slots - classes, width), wide))
    logits = jnp.sum(jnp.concatenate(partial, axis=0), axis=1, keepdims=True) + bias
    onehot = jnp.where(place == label[0], 1.0, 0.0)
    soft = jnp.maximum(logits, 0.0) + jnp.log(1.0 + jnp.exp(-jnp.abs(logits)))
    share = 1.0 / (1.0 + jnp.exp(-logits))
    used = place < classes
    loss_part = jnp.sum(jnp.where(used, soft - onehot * logits, 0.0), keepdims=True)
    logit_grad = jnp.where(used, loss_scale * (share - onehot) / image_count, 0.0)
    root_out[width:, :] = jnp.broadcast_to(
        jnp.where(place == classes, loss_part, logit_grad), (slots, width)
    )

    root_grad = jnp.zeros((width, width), wide)
    for index in range(classes):
        root_grad = root_grad + class_weight[index].astype(wide) * logit_grad[index : index + 1, :]
    root_grad = root_grad + root_grad.T
    change = square_root_change(root_scale * root_grad, trail)
    trace_grad = jnp.sum(root_grad * unit, keepdims=True) / (2.0 * root_scale) - jnp.sum(
        change * sigma, keepdims=True
    ) / (trace_value * trace_value)
    symmetric = (
        (change / trace_value + jnp.where(diagonal, trace_grad, 0.0)) / count
    ).astype(narrow)
    mean_term = jnp.sum(mean_col * symmetric.astype(wide), axis=0, keepdims=True)

    inner = feat_inner.shape[0]
    for feat, gate, start in ((feat_inner, gate_inner, 0), (feat_edge, gate_edge, inner)):
        grad = jnp.dot(feat[...], symmetric, preferred_element_type=wide) - mean_term
        pre[start : start + feat.shape[0], :] = (grad * gate[...]).astype(narrow)
    pre_grad = pre[...]
    bias_grad_out[...] = jnp.sum(pre_grad.astype(wide), axis=0, keepdims=True)
    weight_grad = jnp.dot(conv_turned[...], pre_grad, preferred_element_type=wide)
    part = kept_out.shape[0]
    keep_or_send(upper, weight_grad[:part, :], weight_grad[part:, :], kept_out, sent_out)
    for out, start in ((conv_inner_out, 0), (conv_edge_out, inner)):
        out[...] = jnp.dot(
            pre[start : start + out.shape[0], :], reduce_turned[...], preferred_element_type=wide
        ).astype(narrow)


def head(flag, label, class_bias, own, other, class_weight, prepared, count, image_count):
    feat_inner, feat_edge, gate_inner, gate_edge, conv_turned, reduce_turned = prepared
    width, channels = reduce_turned.shape
    inner, edge = feat_inner.shape[0], feat_edge.shape[0]
    slots = -(-(class_weight.shape[0] + 1) // GROUPS) * GROUPS
    return pl.pallas_call(
        functools.partial(head_kernel, count=count, image_count=image_count),
        in_specs=[in_smem] * 3 + [in_vmem] * 9,
        out_specs=[in_vmem] * 6,
        out_shape=[
            shape_of((width + slots, width)),
            shape_of((channels // 2, width)),
            shape_of((channels // 2, width)),
            shape_of((1, width)),
            shape_of((inner, channels), narrow),
            shape_of((edge, channels), narrow),
        ],
        scratch_shapes=[
            pltpu.VMEM((2 * own.shape[0], width), wide),
            pltpu.VMEM((inner + edge, width), narrow),
        ],
        compiler_params=params(24),
        cost_estimate=cost(10),
        name="head",
    )(
        flag, label, class_bias, own, other, class_weight,
        feat_inner, feat_edge, gate_inner, gate_edge, conv_turned, reduce_turned,
    )


def prepare_kernel(
    before_inner, before_edge, conv_inner_in, conv_edge_in, reduce_weight,
    gate_inner, gate_edge, conv_turned, reduce_turned,
):
    for before, gate in ((before_inner, gate_inner), (before_edge, gate_edge)):
        value = before[...]
        share = 1.0 / (1.0 + jnp.exp(-value))
        gate[...] = share * (1.0 + value * (1.0 - share))
    inner = conv_inner_in.shape[0]
    conv_turned[:, :inner] = conv_inner_in[...].T
    conv_turned[:, inner:] = conv_edge_in[...].T
    reduce_turned[...] = reduce_weight[...].T


def prepare(before_inner, before_edge, conv_in, conv_ed, reduce_weight):
    channels, width = reduce_weight.shape
    inner, edge = before_inner.shape[0], before_edge.shape[0]
    return pl.pallas_call(
        prepare_kernel,
        in_specs=[in_vmem] * 5,
        out_specs=[in_vmem] * 4,
        out_shape=[
            shape_of((inner, width)),
            shape_of((edge, width)),
            shape_of((channels, inner + edge), narrow),
            shape_of((width, channels), narrow),
        ],
        compiler_params=params(16),
        cost_estimate=cost(1),
        name="prepare",
    )(before_inner, before_edge, conv_in, conv_ed, reduce_weight)


def taps_kernel(
    flag, spread_in, spread_top, spread_bottom, grad_inner, grad_edge, bias_grad, *refs,
    first, many,
):
    kept_out, sent_out, grads, out = refs[-4:]
    rows = spread_in.shape[1]
    steps = grads.shape[1]
    cols = steps * GROUPS
    order = edge_rows(rows)
    taps = KERNEL * KERNEL
    part = kept_out.shape[0]
    upper = flag[0] != 0
    out[taps:, :] = jnp.zeros((out.shape[0] - taps, LANES), wide)

    def one_tile(tile, _):
        lanes = lanes_of(tile)

        for row in range(rows):
            if row in order:
                source, place = grad_edge, order.index(row)
            else:
                source, place = grad_inner, row - HALF
            values = source[place * cols : (place + 1) * cols, lanes].astype(wide)
            for step in range(steps):
                grads[row, step] = values[step * GROUPS : (step + 1) * GROUPS, :]

        def load(place, group):
            if place < 0:
                return spread_top[tile, place + HALF, group]
            if place >= rows:
                return spread_bottom[tile, place - rows, group]
            return spread_in[tile, place, group]

        for begin in range(0, KERNEL, 2):
            row_taps = [tap for tap in (begin, begin + 1) if tap < KERNEL]
            total = {
                (row_tap, col_tap): jnp.zeros((GROUPS, LANES), wide)
                for row_tap in row_taps
                for col_tap in range(KERNEL)
            }
            for place in range(begin - HALF, rows + row_taps[-1] - HALF):
                windows = [load(place, group) for group in range(steps + KERNEL - 1)]
                for row_tap in row_taps:
                    row = place - row_tap + HALF
                    if not 0 <= row < rows:
                        continue
                    for step in range(steps):
                        grad = grads[row, step]
                        for col_tap in range(KERNEL):
                            total[row_tap, col_tap] += windows[step + col_tap] * grad
            for (row_tap, col_tap), value in total.items():
                tap = row_tap * KERNEL + col_tap
                out[tap : tap + 1, :] = jnp.sum(value, axis=0, keepdims=True)
        total = [jnp.zeros((GROUPS, LANES), wide) for _ in range(KERNEL)]
        for index in range(rows * steps):
            slot = index % KERNEL
            total[slot] = total[slot] + grads[index // steps, index % steps]
        out[taps : taps + 1, :] = jnp.sum(sum(total), axis=0, keepdims=True)
        low, high = out[:part, :], out[part:, :]
        kept_out[:, lanes] = jnp.where(upper, high, low)
        sent_out[:, lanes] = jnp.where(upper, low, high)
        return 0

    lax.fori_loop(first, first + many, one_tile, 0)
    if first == 0:
        width = bias_grad.shape[1]
        place = taps + 1 - part
        row = jnp.broadcast_to(bias_grad[...], (1, width))

        @pl.when(upper)
        def _():
            kept_out[place : place + 1, :width] = row

        @pl.when(jnp.logical_not(upper))
        def _():
            sent_out[place : place + 1, :width] = row


def tap_grads(flag, spreads, grads, bias_grad, filled, first, many):
    tiles, rows, groups = spreads[0].shape[:3]
    steps = groups - KERNEL + 1
    taps_rows = -(-(KERNEL * KERNEL + 2) // 32) * 32
    part = (taps_rows // 2, tiles * LANES)
    return pl.pallas_call(
        functools.partial(taps_kernel, first=first, many=many),
        in_specs=[in_smem] + [in_vmem] * (6 + len(filled)),
        out_specs=[in_vmem] * 2,
        out_shape=[shape_of(part), shape_of(part)],
        input_output_aliases={7 + index: index for index in range(len(filled))},
        scratch_shapes=[
            pltpu.VMEM((rows, steps, GROUPS, LANES), wide),
            pltpu.VMEM((taps_rows, LANES), wide),
        ],
        compiler_params=params(16),
        cost_estimate=cost(5),
        name="tap_grads",
    )(flag, *spreads, *grads, bias_grad, *filled)


def edge_strip(block, left, right, rows):
    channels = block.shape[2]
    parts = [part[rows].reshape(-1, channels) for part in (block, left, right)]
    short = -(2 * HALF * HALF) % 16
    return jnp.concatenate(parts + [jnp.zeros((short, channels), block.dtype)])


def body(
    features, depth_weight, depth_bias, reduce_weight, reduce_bias, class_weight, class_bias, labels
):
    together = lax.optimization_barrier
    block = features[0]
    rows, cols, channels = block.shape
    width = reduce_weight.shape[1]
    classes = class_bias.shape[0]
    count = rows * cols * lax.axis_size("sy") * lax.axis_size("sx")
    image_count = features.shape[0] * lax.axis_size("dp")

    flag = is_upper("sx", 1).astype(jnp.int32)[None]
    bias_row = depth_bias[None]
    reduce_row = reduce_bias[None]
    left = next_along(block[:, cols - HALF :], "sx")
    right = back_along(block[:, :HALF], "sx")
    low, high, left, right, flag, bias_row, reduce_row = together(
        (
            edge_strip(block, left, right, slice(rows - HALF, rows)),
            edge_strip(block, left, right, slice(0, HALF)),
            left,
            right,
            flag,
            bias_row,
            reduce_row,
        )
    )
    top = next_along(low, "sy")
    bottom = back_along(high, "sy")
    spread, conv_in, before_in, feat_in, gram, colsum = conv_inner(
        block, left, right, depth_weight, bias_row, reduce_weight, reduce_row
    )
    spread_top, spread_bottom, conv_ed, before_ed, feat_ed, kept, sent = conv_edge(
        flag, spread, top, bottom, depth_weight, bias_row, reduce_weight, reduce_row, gram, colsum
    )

    sums = kept + swap(sent, "sx", 1)
    sums, before_in, before_ed, conv_in, conv_ed = together(
        (sums, before_in, before_ed, conv_in, conv_ed)
    )
    gate_in, gate_ed, conv_turned, reduce_turned = prepare(
        before_in, before_ed, conv_in, conv_ed, reduce_weight
    )
    for shift in doublings("sx", 2):
        sums = exchange(sums, "sx", shift, wide)
    sums, gate_in, gate_ed, conv_turned, reduce_turned = together(
        (sums, gate_in, gate_ed, conv_turned, reduce_turned)
    )
    for shift in doublings("sy"):
        sums = exchange(sums, "sy", shift, wide)
    other = swap(sums, "sx", 1)

    root, kept, sent, bias_grad, *grads = head(
        flag,
        labels,
        class_bias,
        sums,
        other,
        class_weight,
        (feat_in, feat_ed, gate_in, gate_ed, conv_turned, reduce_turned),
        count,
        image_count,
    )

    known = [root] + [swap(root, "dp", shift) for shift in range(1, lax.axis_size("dp"))]
    spreads = (spread, spread_top, spread_bottom)
    tiles = channels // LANES
    many = tiles // 3 if tiles % 3 == 0 else tiles
    turns = list(range(0, tiles, many))
    filled = []

    def beside(sums):
        if turns:
            sums, grads[:], filled[:] = together((sums, grads, filled))
            filled[:] = tap_grads(flag, spreads, grads, bias_grad, filled, turns.pop(0), many)
        return sums

    sums = kept + swap(sent, "sx", 1)
    for shift in doublings("sx", 2):
        sums = halve(beside(sums), "sx", shift, narrow)
    for shift in doublings("dp"):
        sums = exchange(beside(sums), "dp", shift, narrow)
    sums = exchange_all(beside(sums), "sy", narrow)
    while turns:
        sums = beside(sums)

    sums, (kept, sent), known = together((sums, filled, known))
    small = kept + swap(sent, "sx", 1)
    class_weight_grad = tree_sum(
        [part[width : width + classes, 0][:, None, None] * part[None, :width] for part in known]
    )
    totals = tree_sum([part[width:, 0] for part in known])
    class_bias_grad = totals[:classes]
    loss = totals[classes] / image_count
    small, sums = together((small, sums))
    for shift in reversed(doublings("sx", 2)):
        sums = unhalve(sums, "sx", shift)
    for shift in doublings("sx", 2):
        small = exchange(small, "sx", shift, narrow)
    for shift in doublings("dp"):
        small = exchange(small, "dp", shift, narrow)
    small, sums = together((small, sums))
    weight_grad = unhalve(sums, "sx", 1)
    small = exchange_all(small, "sy", narrow)
    small = unhalve(small, "sx", 1)

    taps = KERNEL * KERNEL
    return (
        loss,
        small[:taps].reshape(depth_weight.shape),
        small[taps],
        weight_grad,
        small[taps + 1, :width],
        class_weight_grad,
        class_bias_grad,
    )


def solution(mesh):
    placed = (P("dp", "sy", "sx", None), P(), P(), P(), P(), P(), P(), P("dp"))
    return jax.shard_map(
        body,
        mesh=mesh,
        in_specs=placed,
        out_specs=(P(), P(), P(), P(), P(), P(), P()),
        check_vma=False,
    )
```

```python
import functools

import jax
import jax.numpy as jnp
from jax import lax
from jax.experimental import pallas as pl
from jax.experimental.pallas import tpu as pltpu
from jax.sharding import PartitionSpec as P

KERNEL = 7
HALF = KERNEL // 2
NEWTON_STEPS = 5
LANES = 128
GROUPS = 8
EDGE = 8

epsilon = 1e-05
loss_scale = 64.0
narrow = jnp.bfloat16
wide = jnp.float32


def params(megabytes):
    return pltpu.CompilerParams(vmem_limit_bytes=megabytes * 1024 * 1024)


def swap(value, axis, shift):
    count = lax.axis_size(axis)
    return lax.ppermute(value, axis, [(i, i ^ shift) for i in range(count)])


def is_upper(axis, shift):
    return (lax.axis_index(axis) & shift) != 0


def halve(value, axis, shift, upper, sent_as):
    rows = value.shape[0] // 2
    low, high = value[:rows], value[rows:]
    kept = jnp.where(upper, high, low)
    sent = jnp.where(upper, low, high).astype(sent_as)
    return kept + swap(sent, axis, shift).astype(wide)


def unhalve(value, axis, shift, upper):
    other = swap(value, axis, shift)
    return jnp.concatenate([jnp.where(upper, other, value), jnp.where(upper, value, other)])


def tree_sum(terms):
    while len(terms) > 1:
        terms = [terms[i] + terms[i + 1] for i in range(0, len(terms), 2)]
    return terms[0]


def exchange(value, axis, shift, sent_as):
    sent = value.astype(sent_as)
    return sent.astype(wide) + swap(sent, axis, shift).astype(wide)


def exchange_all(value, axis, sent_as):
    sent = value.astype(sent_as)
    moved = [sent] + [swap(sent, axis, shift) for shift in range(1, lax.axis_size(axis))]
    return tree_sum([part.astype(wide) for part in moved])


def doublings(axis, first=1):
    found = []
    shift = first
    while shift < lax.axis_size(axis):
        found.append(shift)
        shift *= 2
    return found


def next_along(value, axis):
    return lax.ppermute(value, axis, [(i, i + 1) for i in range(lax.axis_size(axis) - 1)])


def back_along(value, axis):
    return lax.ppermute(value, axis, [(i + 1, i) for i in range(lax.axis_size(axis) - 1)])


def spread_columns(source, target):
    for group in range(target.shape[0]):
        target[group] = source[pl.ds(EDGE - HALF + group, GROUPS, stride=GROUPS), :]


def fill_row(wide_row, middle, left, right):
    cols = middle.shape[0]
    wide_row[EDGE : EDGE + cols, :] = middle.astype(wide)
    wide_row[EDGE - HALF : EDGE, :] = left.astype(wide)
    wide_row[EDGE + cols : EDGE + cols + HALF, :] = right.astype(wide)


def lanes_of(tile):
    return pl.ds(pl.multiple_of(tile * LANES, LANES), LANES)


def spread_weights(weight_ref, spread_ref, lanes):
    for row_tap in range(KERNEL):
        for col_tap in range(KERNEL):
            scale = weight_ref[row_tap, col_tap : col_tap + 1, lanes]
            spread_ref[row_tap * KERNEL + col_tap] = jnp.broadcast_to(scale, spread_ref.shape[1:])


def conv_rows(load, spread_ref, bias, steps, count):
    total = [[bias] * steps for _ in range(count)]
    for place in range(KERNEL + count - 1):
        windows = [load(place, group) for group in range(steps + KERNEL - 1)]
        for row in range(count):
            row_tap = place - row
            if not 0 <= row_tap < KERNEL:
                continue
            for col_tap in range(KERNEL):
                scale = spread_ref[row_tap * KERNEL + col_tap]
                for step in range(steps):
                    total[row][step] = total[row][step] + windows[step + col_tap] * scale
    return jnp.concatenate([part for row in total for part in row], axis=0).astype(narrow)


def reduce_part(conv_out, reduce_ref, reduce_bias_ref, before_out, feat_out):
    before = jnp.dot(conv_out[...], reduce_ref[...], preferred_element_type=wide)
    before = before + reduce_bias_ref[...]
    before_out[...] = before
    feat_out[...] = (before / (1.0 + jnp.exp(-before))).astype(narrow)
    feat = feat_out[...]
    gram = lax.dot_general(feat, feat, (((0,), (0,)), ((), ())), preferred_element_type=wide)
    return gram, jnp.sum(feat.astype(wide), axis=0, keepdims=True)


def inner_kernel(
    block, left, right, weight, bias, reduce_weight, reduce_bias,
    spread_out, conv_out, before_out, feat_out, gram_out, colsum_out,
    wide_row, spread_weight,
):
    rows, cols = block.shape[0], block.shape[1]
    steps = cols // GROUPS
    inner = rows - 2 * HALF
    at_once = 2 if inner % 2 == 0 else 1

    def one_tile(tile, _):
        lanes = lanes_of(tile)
        spread_weights(weight, spread_weight, lanes)
        start_value = jnp.broadcast_to(bias[0:1, lanes], (GROUPS, LANES))

        def fill(row, _):
            place = wide_row.at[row]
            fill_row(place, block[row, :, lanes], left[row, :, lanes], right[row, :, lanes])
            spread_columns(place, spread_out.at[tile, row])
            return 0

        lax.fori_loop(0, rows, fill, 0)

        def one_row(index, _):
            def load(row_tap, group):
                return spread_out[tile, index + row_tap, group]

            start = pl.multiple_of(index * cols, at_once * cols)
            conv_out[pl.ds(start, at_once * cols), lanes] = conv_rows(
                load, spread_weight, start_value, steps, at_once
            )
            return 0

        lax.fori_loop(0, inner // at_once, lambda turn, _: one_row(turn * at_once, 0), 0)
        return 0

    lax.fori_loop(0, spread_out.shape[0], one_tile, 0)
    gram_out[...], colsum_out[...] = reduce_part(
        conv_out, reduce_weight, reduce_bias, before_out, feat_out
    )


def edge_kernel(
    flag, spread_in, top, bottom, weight, bias, reduce_weight, reduce_bias, gram_in, colsum_in,
    spread_top, spread_bottom, conv_out, before_out, feat_out, kept_out, sent_out,
    wide_row, corners, spread_weight, sums,
):
    rows, cols = spread_in.shape[1], wide_row.shape[1] - 2 * EDGE
    steps = cols // GROUPS

    def one_tile(tile, _):
        lanes = lanes_of(tile)
        spread_weights(weight, spread_weight, lanes)
        start_value = jnp.broadcast_to(bias[0:1, lanes], (GROUPS, LANES))
        for side, (strip, spread) in enumerate(((top, spread_top), (bottom, spread_bottom))):
            corners[side] = strip[HALF * cols :, lanes].astype(wide)
            for row in range(HALF):
                place = wide_row.at[side * HALF + row]
                left = corners[side, row * HALF : (row + 1) * HALF, :]
                right = corners[side, (HALF + row) * HALF : (HALF + row + 1) * HALF, :]
                fill_row(place, strip[row * cols : (row + 1) * cols, lanes], left, right)
                spread_columns(place, spread.at[tile, row])

        def load_from(row):
            def load(row_tap, group):
                place = row + row_tap - HALF
                if place < 0:
                    return spread_top[tile, place + HALF, group]
                if place >= rows:
                    return spread_bottom[tile, place - rows, group]
                return spread_in[tile, place, group]

            return load

        for side, row in enumerate((0, rows - HALF)):
            start = side * HALF * cols
            conv_out[start : start + HALF * cols, lanes] = conv_rows(
                load_from(row), spread_weight, start_value, steps, HALF
            )
        return 0

    lax.fori_loop(0, spread_in.shape[0], one_tile, 0)
    gram, colsum = reduce_part(conv_out, reduce_weight, reduce_bias, before_out, feat_out)
    gram = gram + gram_in[...]
    colsum = colsum + colsum_in[...]
    width = gram.shape[0]
    half = width // 2
    quarter = half // 2
    sums[:half, :] = gram[:half, :]
    sums[half : half + quarter, :half] = gram[half : half + quarter, half:]
    sums[half : half + quarter, half:] = gram[half + quarter :, half:]
    sums[half + quarter :, :] = jnp.broadcast_to(
        colsum, (sums.shape[0] - half - quarter, width)
    )
    part = kept_out.shape[0]
    keep_or_send(flag[0] != 0, sums[:part, :], sums[part:, :], kept_out, sent_out)


def keep_or_send(upper, low, high, kept_out, sent_out):
    kept_out[...] = jnp.where(upper, high, low)
    sent_out[...] = jnp.where(upper, low, high).astype(sent_out.dtype)


def edge_rows(rows):
    return list(range(HALF)) + list(range(rows - HALF, rows))


def shape_of(shape, dtype=wide):
    return jax.ShapeDtypeStruct(shape, dtype)


in_vmem = pl.BlockSpec(memory_space=pltpu.VMEM)
in_smem = pl.BlockSpec(memory_space=pltpu.SMEM)


def cost(microseconds):
    return pl.CostEstimate(
        flops=microseconds * 10**9, bytes_accessed=microseconds * 10**6, transcendentals=0
    )


def conv_inner(block, left, right, weight, bias, reduce_weight, reduce_bias):
    rows, cols, channels = block.shape
    width = reduce_weight.shape[1]
    tiles = channels // LANES
    steps = cols // GROUPS
    pixels = (rows - 2 * HALF) * cols
    return pl.pallas_call(
        inner_kernel,
        in_specs=[in_vmem] * 7,
        out_specs=[in_vmem] * 6,
        out_shape=[
            shape_of((tiles, rows, steps + KERNEL - 1, GROUPS, LANES)),
            shape_of((pixels, channels), narrow),
            shape_of((pixels, width)),
            shape_of((pixels, width), narrow),
            shape_of((width, width)),
            shape_of((1, width)),
        ],
        scratch_shapes=[
            pltpu.VMEM((rows, cols + 2 * EDGE, LANES), wide),
            pltpu.VMEM((KERNEL * KERNEL, GROUPS, LANES), wide),
        ],
        compiler_params=params(24),
        cost_estimate=cost(10),
        name="conv_inner",
    )(block, left, right, weight, bias, reduce_weight, reduce_bias)


def conv_edge(flag, spread, top, bottom, weight, bias, reduce_weight, reduce_bias, gram, colsum):
    tiles, rows, groups = spread.shape[:3]
    cols, channels = (groups - KERNEL + 1) * GROUPS, top.shape[1]
    width = reduce_weight.shape[1]
    pixels = 2 * HALF * cols
    side = (tiles, HALF, groups, GROUPS, LANES)
    sums_rows = 3 * width // 4 + 2 * GROUPS
    return pl.pallas_call(
        edge_kernel,
        in_specs=[in_smem] + [in_vmem] * 9,
        out_specs=[in_vmem] * 7,
        out_shape=[
            shape_of(side),
            shape_of(side),
            shape_of((pixels, channels), narrow),
            shape_of((pixels, width)),
            shape_of((pixels, width), narrow),
            shape_of((sums_rows // 2, width)),
            shape_of((sums_rows // 2, width)),
        ],
        scratch_shapes=[
            pltpu.VMEM((2 * HALF, cols + 2 * EDGE, LANES), wide),
            pltpu.VMEM((2, top.shape[0] - HALF * cols, LANES), wide),
            pltpu.VMEM((KERNEL * KERNEL, GROUPS, LANES), wide),
            pltpu.VMEM((sums_rows, width), wide),
        ],
        compiler_params=params(24),
        cost_estimate=cost(6),
        name="conv_edge",
    )(flag, spread, top, bottom, weight, bias, reduce_weight, reduce_bias, gram, colsum)


def split(value):
    high = value.astype(narrow)
    return high, (value - high.astype(wide)).astype(narrow)


def product(left, right):
    def dot(a, b):
        return jnp.dot(a, b, preferred_element_type=wide)

    return dot(left[0], right[0]) + (dot(left[0], right[1]) + dot(left[1], right[0]))


def square_root(current):
    size = current.shape[0]
    row = lax.broadcasted_iota(jnp.int32, (size, size), 0)
    col = lax.broadcasted_iota(jnp.int32, (size, size), 1)
    triple = jnp.where(row == col, 3.0, 0.0)
    factor = split(0.5 * (triple - current))
    current = split(current)
    trail = [(current, None, factor)]
    inverse = factor
    current = split(product(current, factor))
    for step in range(1, NEWTON_STEPS):
        factor = split(0.5 * (triple - product(inverse, current)))
        trail.append((current, inverse, factor))
        last = step == NEWTON_STEPS - 1
        if not last:
            inverse = split(product(factor, inverse))
        current = product(current, factor)
        if not last:
            current = split(current)
    return current, trail


def square_root_change(change, trail):
    first, _, factor = trail[0]
    move = split(change)
    factor_move = split(-0.5 * change)
    change = product(move, factor) + product(first, factor_move)
    inverse_move = factor_move
    for step in range(1, NEWTON_STEPS):
        current, inverse, factor = trail[step]
        move = split(change)
        factor_move = split(
            -0.5 * (product(inverse_move, current) + product(inverse, move))
        )
        change = product(move, factor) + product(current, factor_move)
        if step < NEWTON_STEPS - 1:
            inverse_move = split(product(factor_move, inverse) + product(factor, inverse_move))
    return change


def head_kernel(
    flag, label, class_bias, own, other, class_weight,
    feat_inner, feat_edge, gate_inner, gate_edge, conv_turned, reduce_turned,
    root_out, kept_out, sent_out, bias_grad_out, conv_inner_out, conv_edge_out,
    sums, pre, *, count, image_count,
):
    width = root_out.shape[1]
    half = width // 2
    quarter = half // 2
    rows = own.shape[0]
    upper = flag[0] != 0
    mine, theirs = own[...], other[...]
    sums[:rows, :] = jnp.where(upper, theirs, mine)
    sums[rows:, :] = jnp.where(upper, mine, theirs)
    low = jnp.concatenate(
        [sums[half : half + quarter, :half], sums[half : half + quarter, half:]], axis=0
    )
    cross = sums[:half, half:]
    gram = jnp.concatenate(
        [sums[:half, :], jnp.concatenate([cross.T, low], axis=1)], axis=0
    )
    mean_row = sums[half + quarter : half + quarter + 1, :] / count
    mean_col = jnp.broadcast_to(mean_row, (width, width)).T
    sigma = gram / count - mean_col * mean_row
    row = lax.broadcasted_iota(jnp.int32, (width, width), 0)
    col = lax.broadcasted_iota(jnp.int32, (width, width), 1)
    diagonal = row == col
    trace_value = jnp.sum(jnp.where(diagonal, sigma, 0.0), keepdims=True) + epsilon
    root_scale = jnp.sqrt(trace_value)
    unit, trail = square_root(sigma / trace_value)
    root = root_scale * unit
    root_out[:width, :] = root

    classes = class_weight.shape[0]
    slots = root_out.shape[0] - width
    place = lax.broadcasted_iota(jnp.int32, (slots, 1), 0)
    bias = jnp.zeros((slots, 1), wide)
    for index in range(classes):
        bias = jnp.where(place == index, class_bias[index], bias)
    partial = [
        jnp.sum(class_weight[index].astype(wide) * root, axis=0, keepdims=True)
        for index in range(classes)
    ]
    partial.append(jnp.zeros((slots - classes, width), wide))
    logits = jnp.sum(jnp.concatenate(partial, axis=0), axis=1, keepdims=True) + bias
    onehot = jnp.where(place == label[0], 1.0, 0.0)
    soft = jnp.maximum(logits, 0.0) + jnp.log(1.0 + jnp.exp(-jnp.abs(logits)))
    share = 1.0 / (1.0 + jnp.exp(-logits))
    used = place < classes
    loss_part = jnp.sum(jnp.where(used, soft - onehot * logits, 0.0), keepdims=True)
    logit_grad = jnp.where(used, loss_scale * (share - onehot) / image_count, 0.0)
    root_out[width:, :] = jnp.broadcast_to(
        jnp.where(place == classes, loss_part, logit_grad), (slots, width)
    )

    root_grad = jnp.zeros((width, width), wide)
    for index in range(classes):
        root_grad = root_grad + class_weight[index].astype(wide) * logit_grad[index : index + 1, :]
    root_grad = root_grad + root_grad.T
    change = square_root_change(root_scale * root_grad, trail)
    trace_grad = jnp.sum(root_grad * unit, keepdims=True) / (2.0 * root_scale) - jnp.sum(
        change * sigma, keepdims=True
    ) / (trace_value * trace_value)
    symmetric = (
        (change / trace_value + jnp.where(diagonal, trace_grad, 0.0)) / count
    ).astype(narrow)
    mean_term = jnp.sum(mean_col * symmetric.astype(wide), axis=0, keepdims=True)

    inner = feat_inner.shape[0]
    for feat, gate, start in ((feat_inner, gate_inner, 0), (feat_edge, gate_edge, inner)):
        grad = jnp.dot(feat[...], symmetric, preferred_element_type=wide) - mean_term
        pre[start : start + feat.shape[0], :] = (grad * gate[...]).astype(narrow)
    pre_grad = pre[...]
    bias_grad_out[...] = jnp.sum(pre_grad.astype(wide), axis=0, keepdims=True)
    weight_grad = jnp.dot(conv_turned[...], pre_grad, preferred_element_type=wide)
    part = kept_out.shape[0]
    keep_or_send(upper, weight_grad[:part, :], weight_grad[part:, :], kept_out, sent_out)
    for out, start in ((conv_inner_out, 0), (conv_edge_out, inner)):
        out[...] = jnp.dot(
            pre[start : start + out.shape[0], :], reduce_turned[...], preferred_element_type=wide
        ).astype(narrow)


def head(flag, label, class_bias, own, other, class_weight, prepared, count, image_count):
    feat_inner, feat_edge, gate_inner, gate_edge, conv_turned, reduce_turned = prepared
    width, channels = reduce_turned.shape
    inner, edge = feat_inner.shape[0], feat_edge.shape[0]
    slots = -(-(class_weight.shape[0] + 1) // GROUPS) * GROUPS
    return pl.pallas_call(
        functools.partial(head_kernel, count=count, image_count=image_count),
        in_specs=[in_smem] * 3 + [in_vmem] * 9,
        out_specs=[in_vmem] * 6,
        out_shape=[
            shape_of((width + slots, width)),
            shape_of((channels // 2, width)),
            shape_of((channels // 2, width)),
            shape_of((1, width)),
            shape_of((inner, channels), narrow),
            shape_of((edge, channels), narrow),
        ],
        scratch_shapes=[
            pltpu.VMEM((2 * own.shape[0], width), wide),
            pltpu.VMEM((inner + edge, width), narrow),
        ],
        compiler_params=params(24),
        cost_estimate=cost(10),
        name="head",
    )(
        flag, label, class_bias, own, other, class_weight,
        feat_inner, feat_edge, gate_inner, gate_edge, conv_turned, reduce_turned,
    )


def prepare_kernel(
    before_inner, before_edge, conv_inner_in, conv_edge_in, reduce_weight,
    gate_inner, gate_edge, conv_turned, reduce_turned,
):
    for before, gate in ((before_inner, gate_inner), (before_edge, gate_edge)):
        value = before[...]
        share = 1.0 / (1.0 + jnp.exp(-value))
        gate[...] = share * (1.0 + value * (1.0 - share))
    inner = conv_inner_in.shape[0]
    conv_turned[:, :inner] = conv_inner_in[...].T
    conv_turned[:, inner:] = conv_edge_in[...].T
    reduce_turned[...] = reduce_weight[...].T


def prepare(before_inner, before_edge, conv_in, conv_ed, reduce_weight):
    channels, width = reduce_weight.shape
    inner, edge = before_inner.shape[0], before_edge.shape[0]
    return pl.pallas_call(
        prepare_kernel,
        in_specs=[in_vmem] * 5,
        out_specs=[in_vmem] * 4,
        out_shape=[
            shape_of((inner, width)),
            shape_of((edge, width)),
            shape_of((channels, inner + edge), narrow),
            shape_of((width, channels), narrow),
        ],
        compiler_params=params(16),
        cost_estimate=cost(1),
        name="prepare",
    )(before_inner, before_edge, conv_in, conv_ed, reduce_weight)


def taps_kernel(
    flag, spread_in, spread_top, spread_bottom, grad_inner, grad_edge, bias_grad, *refs,
    first, many,
):
    kept_out, sent_out, grads, out = refs[-4:]
    rows = spread_in.shape[1]
    steps = grads.shape[1]
    cols = steps * GROUPS
    order = edge_rows(rows)
    taps = KERNEL * KERNEL
    part = kept_out.shape[0]
    upper = flag[0] != 0
    out[taps:, :] = jnp.zeros((out.shape[0] - taps, LANES), wide)

    def one_tile(tile, _):
        lanes = lanes_of(tile)

        for row in range(rows):
            if row in order:
                source, place = grad_edge, order.index(row)
            else:
                source, place = grad_inner, row - HALF
            values = source[place * cols : (place + 1) * cols, lanes].astype(wide)
            for step in range(steps):
                grads[row, step] = values[step * GROUPS : (step + 1) * GROUPS, :]

        def load(place, group):
            if place < 0:
                return spread_top[tile, place + HALF, group]
            if place >= rows:
                return spread_bottom[tile, place - rows, group]
            return spread_in[tile, place, group]

        for begin in range(0, KERNEL, 2):
            row_taps = [tap for tap in (begin, begin + 1) if tap < KERNEL]
            total = {
                (row_tap, col_tap): jnp.zeros((GROUPS, LANES), wide)
                for row_tap in row_taps
                for col_tap in range(KERNEL)
            }
            for place in range(begin - HALF, rows + row_taps[-1] - HALF):
                windows = [load(place, group) for group in range(steps + KERNEL - 1)]
                for row_tap in row_taps:
                    row = place - row_tap + HALF
                    if not 0 <= row < rows:
                        continue
                    for step in range(steps):
                        grad = grads[row, step]
                        for col_tap in range(KERNEL):
                            total[row_tap, col_tap] += windows[step + col_tap] * grad
            for (row_tap, col_tap), value in total.items():
                tap = row_tap * KERNEL + col_tap
                out[tap : tap + 1, :] = jnp.sum(value, axis=0, keepdims=True)
        total = [jnp.zeros((GROUPS, LANES), wide) for _ in range(KERNEL)]
        for index in range(rows * steps):
            slot = index % KERNEL
            total[slot] = total[slot] + grads[index // steps, index % steps]
        out[taps : taps + 1, :] = jnp.sum(sum(total), axis=0, keepdims=True)
        low, high = out[:part, :], out[part:, :]
        kept_out[:, lanes] = jnp.where(upper, high, low)
        sent_out[:, lanes] = jnp.where(upper, low, high)
        return 0

    lax.fori_loop(first, first + many, one_tile, 0)
    if first == 0:
        width = bias_grad.shape[1]
        place = taps + 1 - part
        row = jnp.broadcast_to(bias_grad[...], (1, width))

        @pl.when(upper)
        def _():
            kept_out[place : place + 1, :width] = row

        @pl.when(jnp.logical_not(upper))
        def _():
            sent_out[place : place + 1, :width] = row


def tap_grads(flag, spreads, grads, bias_grad, filled, first, many):
    tiles, rows, groups = spreads[0].shape[:3]
    steps = groups - KERNEL + 1
    taps_rows = -(-(KERNEL * KERNEL + 2) // 32) * 32
    part = (taps_rows // 2, tiles * LANES)
    return pl.pallas_call(
        functools.partial(taps_kernel, first=first, many=many),
        in_specs=[in_smem] + [in_vmem] * (6 + len(filled)),
        out_specs=[in_vmem] * 2,
        out_shape=[shape_of(part), shape_of(part)],
        input_output_aliases={7 + index: index for index in range(len(filled))},
        scratch_shapes=[
            pltpu.VMEM((rows, steps, GROUPS, LANES), wide),
            pltpu.VMEM((taps_rows, LANES), wide),
        ],
        compiler_params=params(16),
        cost_estimate=cost(5),
        name="tap_grads",
    )(flag, *spreads, *grads, bias_grad, *filled)


def finish_kernel(flag, own, other, depth_out, depth_bias_out, bias_out, sums):
    part = own.shape[0]
    upper = flag[0] != 0
    sums[:part, :] = jnp.where(upper, other[...], own[...])
    sums[part:, :] = jnp.where(upper, own[...], other[...])
    for row_tap in range(KERNEL):
        depth_out[row_tap] = sums[row_tap * KERNEL : (row_tap + 1) * KERNEL, :]
    taps = KERNEL * KERNEL
    depth_bias_out[...] = sums[taps : taps + 1, :]
    bias_out[...] = sums[taps + 1 : taps + 2, : bias_out.shape[1]]


def finish(flag, own, other, width):
    part, channels = own.shape
    return pl.pallas_call(
        finish_kernel,
        in_specs=[in_smem] + [in_vmem] * 2,
        out_specs=[in_vmem] * 3,
        out_shape=[
            shape_of((KERNEL, KERNEL, channels)),
            shape_of((1, channels)),
            shape_of((1, width)),
        ],
        scratch_shapes=[pltpu.VMEM((2 * part, channels), wide)],
        compiler_params=params(8),
        cost_estimate=cost(1),
        name="finish",
    )(flag, own, other)


def edge_strip(block, left, right, rows):
    channels = block.shape[2]
    parts = [part[rows].reshape(-1, channels) for part in (block, left, right)]
    short = -(2 * HALF * HALF) % 16
    return jnp.concatenate(parts + [jnp.zeros((short, channels), block.dtype)])


def body(
    features, depth_weight, depth_bias, reduce_weight, reduce_bias, class_weight, class_bias, labels
):
    together = lax.optimization_barrier
    block = features[0]
    rows, cols, channels = block.shape
    width = reduce_weight.shape[1]
    classes = class_bias.shape[0]
    count = rows * cols * lax.axis_size("sy") * lax.axis_size("sx")
    image_count = features.shape[0] * lax.axis_size("dp")

    flag = is_upper("sx", 1).astype(jnp.int32)[None]
    uppers = [is_upper("sx", shift) for shift in doublings("sx")]
    bias_row = depth_bias[None]
    reduce_row = reduce_bias[None]
    left = next_along(block[:, cols - HALF :], "sx")
    right = back_along(block[:, :HALF], "sx")
    low, high, left, right, flag, uppers, bias_row, reduce_row = together(
        (
            edge_strip(block, left, right, slice(rows - HALF, rows)),
            edge_strip(block, left, right, slice(0, HALF)),
            left,
            right,
            flag,
            uppers,
            bias_row,
            reduce_row,
        )
    )
    uppers = dict(zip(doublings("sx"), uppers))
    top = next_along(low, "sy")
    bottom = back_along(high, "sy")
    spread, conv_in, before_in, feat_in, gram, colsum = conv_inner(
        block, left, right, depth_weight, bias_row, reduce_weight, reduce_row
    )
    spread_top, spread_bottom, conv_ed, before_ed, feat_ed, kept, sent = conv_edge(
        flag, spread, top, bottom, depth_weight, bias_row, reduce_weight, reduce_row, gram, colsum
    )

    sums = kept + swap(sent, "sx", 1)
    sums, before_in, before_ed, conv_in, conv_ed = together(
        (sums, before_in, before_ed, conv_in, conv_ed)
    )
    gate_in, gate_ed, conv_turned, reduce_turned = prepare(
        before_in, before_ed, conv_in, conv_ed, reduce_weight
    )
    for shift in doublings("sx", 2):
        sums = exchange(sums, "sx", shift, wide)
    sums, gate_in, gate_ed, conv_turned, reduce_turned = together(
        (sums, gate_in, gate_ed, conv_turned, reduce_turned)
    )
    for shift in doublings("sy"):
        sums = exchange(sums, "sy", shift, wide)
    other = swap(sums, "sx", 1)

    root, kept, sent, bias_grad, *grads = head(
        flag,
        labels,
        class_bias,
        sums,
        other,
        class_weight,
        (feat_in, feat_ed, gate_in, gate_ed, conv_turned, reduce_turned),
        count,
        image_count,
    )

    known = [root] + [swap(root, "dp", shift) for shift in range(1, lax.axis_size("dp"))]
    spreads = (spread, spread_top, spread_bottom)
    tiles = channels // LANES
    many = tiles // 3 if tiles % 3 == 0 else tiles
    turns = list(range(0, tiles, many))
    filled = []

    def beside(sums):
        if turns:
            sums, grads[:], filled[:] = together((sums, grads, filled))
            filled[:] = tap_grads(flag, spreads, grads, bias_grad, filled, turns.pop(0), many)
        return sums

    sums = kept + swap(sent, "sx", 1)
    for shift in doublings("sx", 2):
        sums = halve(beside(sums), "sx", shift, uppers[shift], narrow)
    for shift in doublings("dp"):
        sums = exchange(beside(sums), "dp", shift, narrow)
    sums = exchange_all(beside(sums), "sy", narrow)
    while turns:
        sums = beside(sums)

    sums, (kept, sent), known = together((sums, filled, known))
    small = kept + swap(sent, "sx", 1)
    class_weight_grad = tree_sum(
        [part[width : width + classes, 0][:, None, None] * part[None, :width] for part in known]
    )
    totals = tree_sum([part[width:, 0] for part in known])
    class_bias_grad = totals[:classes]
    loss = totals[classes] / image_count
    small, sums = together((small, sums))
    for shift in reversed(doublings("sx", 2)):
        sums = unhalve(sums, "sx", shift, uppers[shift])
    for shift in doublings("sx", 2):
        small = exchange(small, "sx", shift, narrow)
    for shift in doublings("dp"):
        small = exchange(small, "dp", shift, narrow)
    small, sums = together((small, sums))
    weight_grad = unhalve(sums, "sx", 1, uppers[1])
    small = exchange_all(small, "sy", narrow)
    small, weight_grad, class_weight_grad, class_bias_grad, loss = together(
        (small, weight_grad, class_weight_grad, class_bias_grad, loss)
    )
    depth_grad, depth_bias_grad, bias_grad = finish(flag, small, swap(small, "sx", 1), width)
    return (
        loss,
        depth_grad,
        depth_bias_grad[0],
        weight_grad,
        bias_grad[0],
        class_weight_grad,
        class_bias_grad,
    )


def solution(mesh):
    placed = (P("dp", "sy", "sx", None), P(), P(), P(), P(), P(), P(), P("dp"))
    return jax.shard_map(
        body,
        mesh=mesh,
        in_specs=placed,
        out_specs=(P(), P(), P(), P(), P(), P(), P()),
        check_vma=False,
    )
```

```python
import functools

import jax
import jax.numpy as jnp
from jax import lax
from jax.experimental import pallas as pl
from jax.experimental.pallas import tpu as pltpu
from jax.sharding import PartitionSpec as P

KERNEL = 7
HALF = KERNEL // 2
NEWTON_STEPS = 5
LANES = 128
GROUPS = 8
EDGE = 8

epsilon = 1e-05
loss_scale = 64.0
narrow = jnp.bfloat16
wide = jnp.float32


def params(megabytes):
    return pltpu.CompilerParams(vmem_limit_bytes=megabytes * 1024 * 1024)


def swap(value, axis, shift):
    count = lax.axis_size(axis)
    return lax.ppermute(value, axis, [(i, i ^ shift) for i in range(count)])


def is_upper(axis, shift):
    return (lax.axis_index(axis) & shift) != 0


def halve(value, axis, shift, upper, sent_as):
    rows = value.shape[0] // 2
    low, high = value[:rows], value[rows:]
    kept = jnp.where(upper, high, low)
    sent = jnp.where(upper, low, high).astype(sent_as)
    return kept + swap(sent, axis, shift).astype(wide)


def unhalve(value, axis, shift, upper):
    other = swap(value, axis, shift)
    return jnp.concatenate([jnp.where(upper, other, value), jnp.where(upper, value, other)])


def tree_sum(terms):
    while len(terms) > 1:
        terms = [terms[i] + terms[i + 1] for i in range(0, len(terms), 2)]
    return terms[0]


def exchange(value, axis, shift, sent_as):
    sent = value.astype(sent_as)
    return sent.astype(wide) + swap(sent, axis, shift).astype(wide)


def exchange_all(value, axis, sent_as):
    sent = value.astype(sent_as)
    moved = [sent] + [swap(sent, axis, shift) for shift in range(1, lax.axis_size(axis))]
    return tree_sum([part.astype(wide) for part in moved])


def exchange_square(value, axes, shifts, sent_as):
    counts = [lax.axis_size(axis) for axis in axes]
    sent = value.astype(sent_as)
    moved = [sent]
    for first, second in ((0, 1), (1, 0), (1, 1)):
        pairs = [
            (i * counts[1] + j, (i ^ (first * shifts[0])) * counts[1] + (j ^ (second * shifts[1])))
            for i in range(counts[0])
            for j in range(counts[1])
        ]
        moved.append(lax.ppermute(sent, axes, pairs))
    return tree_sum([part.astype(wide) for part in moved])


def doublings(axis, first=1):
    found = []
    shift = first
    while shift < lax.axis_size(axis):
        found.append(shift)
        shift *= 2
    return found


def pair_up(first, second):
    many = min(len(first), len(second))
    return list(zip(second, first)), first[many:], second[many:]


def next_along(value, axis):
    return lax.ppermute(value, axis, [(i, i + 1) for i in range(lax.axis_size(axis) - 1)])


def back_along(value, axis):
    return lax.ppermute(value, axis, [(i + 1, i) for i in range(lax.axis_size(axis) - 1)])


def spread_columns(source, target):
    for group in range(target.shape[0]):
        target[group] = source[pl.ds(EDGE - HALF + group, GROUPS, stride=GROUPS), :]


def fill_row(wide_row, middle, left, right):
    cols = middle.shape[0]
    wide_row[EDGE : EDGE + cols, :] = middle.astype(wide)
    wide_row[EDGE - HALF : EDGE, :] = left.astype(wide)
    wide_row[EDGE + cols : EDGE + cols + HALF, :] = right.astype(wide)


def lanes_of(tile):
    return pl.ds(pl.multiple_of(tile * LANES, LANES), LANES)


def spread_weights(weight_ref, spread_ref, lanes):
    for row_tap in range(KERNEL):
        for col_tap in range(KERNEL):
            scale = weight_ref[row_tap, col_tap : col_tap + 1, lanes]
            spread_ref[row_tap * KERNEL + col_tap] = jnp.broadcast_to(scale, spread_ref.shape[1:])


def conv_rows(load, spread_ref, bias, steps, count):
    total = [[bias] * steps for _ in range(count)]
    for place in range(KERNEL + count - 1):
        windows = [load(place, group) for group in range(steps + KERNEL - 1)]
        for row in range(count):
            row_tap = place - row
            if not 0 <= row_tap < KERNEL:
                continue
            for col_tap in range(KERNEL):
                scale = spread_ref[row_tap * KERNEL + col_tap]
                for step in range(steps):
                    total[row][step] = total[row][step] + windows[step + col_tap] * scale
    return jnp.concatenate([part for row in total for part in row], axis=0).astype(narrow)


def reduce_part(conv_out, reduce_ref, reduce_bias_ref, before_out, feat_out):
    before = jnp.dot(conv_out[...], reduce_ref[...], preferred_element_type=wide)
    before = before + reduce_bias_ref[...]
    before_out[...] = before
    feat_out[...] = (before / (1.0 + jnp.exp(-before))).astype(narrow)
    feat = feat_out[...]
    gram = lax.dot_general(feat, feat, (((0,), (0,)), ((), ())), preferred_element_type=wide)
    return gram, jnp.sum(feat.astype(wide), axis=0, keepdims=True)


def inner_kernel(
    block, left, right, weight, bias, reduce_weight, reduce_bias,
    spread_out, conv_out, before_out, feat_out, gram_out, colsum_out,
    wide_row, spread_weight,
):
    rows, cols = block.shape[0], block.shape[1]
    steps = cols // GROUPS
    inner = rows - 2 * HALF
    at_once = 2 if inner % 2 == 0 else 1

    def one_tile(tile, _):
        lanes = lanes_of(tile)
        spread_weights(weight, spread_weight, lanes)
        start_value = jnp.broadcast_to(bias[0:1, lanes], (GROUPS, LANES))

        def fill(row, _):
            place = wide_row.at[row]
            fill_row(place, block[row, :, lanes], left[row, :, lanes], right[row, :, lanes])
            spread_columns(place, spread_out.at[tile, row])
            return 0

        lax.fori_loop(0, rows, fill, 0)

        def one_row(index, _):
            def load(row_tap, group):
                return spread_out[tile, index + row_tap, group]

            start = pl.multiple_of(index * cols, at_once * cols)
            conv_out[pl.ds(start, at_once * cols), lanes] = conv_rows(
                load, spread_weight, start_value, steps, at_once
            )
            return 0

        lax.fori_loop(0, inner // at_once, lambda turn, _: one_row(turn * at_once, 0), 0)
        return 0

    lax.fori_loop(0, spread_out.shape[0], one_tile, 0)
    gram_out[...], colsum_out[...] = reduce_part(
        conv_out, reduce_weight, reduce_bias, before_out, feat_out
    )


def edge_kernel(
    flag, spread_in, top, bottom, weight, bias, reduce_weight, reduce_bias, gram_in, colsum_in,
    spread_top, spread_bottom, conv_out, before_out, feat_out, kept_out, sent_out,
    wide_row, corners, spread_weight, sums,
):
    rows, cols = spread_in.shape[1], wide_row.shape[1] - 2 * EDGE
    steps = cols // GROUPS

    def one_tile(tile, _):
        lanes = lanes_of(tile)
        spread_weights(weight, spread_weight, lanes)
        start_value = jnp.broadcast_to(bias[0:1, lanes], (GROUPS, LANES))
        for side, (strip, spread) in enumerate(((top, spread_top), (bottom, spread_bottom))):
            corners[side] = strip[HALF * cols :, lanes].astype(wide)
            for row in range(HALF):
                place = wide_row.at[side * HALF + row]
                left = corners[side, row * HALF : (row + 1) * HALF, :]
                right = corners[side, (HALF + row) * HALF : (HALF + row + 1) * HALF, :]
                fill_row(place, strip[row * cols : (row + 1) * cols, lanes], left, right)
                spread_columns(place, spread.at[tile, row])

        def load_from(row):
            def load(row_tap, group):
                place = row + row_tap - HALF
                if place < 0:
                    return spread_top[tile, place + HALF, group]
                if place >= rows:
                    return spread_bottom[tile, place - rows, group]
                return spread_in[tile, place, group]

            return load

        for side, row in enumerate((0, rows - HALF)):
            start = side * HALF * cols
            conv_out[start : start + HALF * cols, lanes] = conv_rows(
                load_from(row), spread_weight, start_value, steps, HALF
            )
        return 0

    lax.fori_loop(0, spread_in.shape[0], one_tile, 0)
    gram, colsum = reduce_part(conv_out, reduce_weight, reduce_bias, before_out, feat_out)
    gram = gram + gram_in[...]
    colsum = colsum + colsum_in[...]
    width = gram.shape[0]
    half = width // 2
    quarter = half // 2
    sums[:half, :] = gram[:half, :]
    sums[half : half + quarter, :half] = gram[half : half + quarter, half:]
    sums[half : half + quarter, half:] = gram[half + quarter :, half:]
    sums[half + quarter :, :] = jnp.broadcast_to(
        colsum, (sums.shape[0] - half - quarter, width)
    )
    part = kept_out.shape[0]
    keep_or_send(flag[0] != 0, sums[:part, :], sums[part:, :], kept_out, sent_out)


def keep_or_send(upper, low, high, kept_out, sent_out):
    kept_out[...] = jnp.where(upper, high, low)
    sent_out[...] = jnp.where(upper, low, high).astype(sent_out.dtype)


def edge_rows(rows):
    return list(range(HALF)) + list(range(rows - HALF, rows))


def shape_of(shape, dtype=wide):
    return jax.ShapeDtypeStruct(shape, dtype)


in_vmem = pl.BlockSpec(memory_space=pltpu.VMEM)
in_smem = pl.BlockSpec(memory_space=pltpu.SMEM)


def cost(microseconds):
    return pl.CostEstimate(
        flops=microseconds * 10**9, bytes_accessed=microseconds * 10**6, transcendentals=0
    )


def conv_inner(block, left, right, weight, bias, reduce_weight, reduce_bias):
    rows, cols, channels = block.shape
    width = reduce_weight.shape[1]
    tiles = channels // LANES
    steps = cols // GROUPS
    pixels = (rows - 2 * HALF) * cols
    return pl.pallas_call(
        inner_kernel,
        in_specs=[in_vmem] * 7,
        out_specs=[in_vmem] * 6,
        out_shape=[
            shape_of((tiles, rows, steps + KERNEL - 1, GROUPS, LANES)),
            shape_of((pixels, channels), narrow),
            shape_of((pixels, width)),
            shape_of((pixels, width), narrow),
            shape_of((width, width)),
            shape_of((1, width)),
        ],
        scratch_shapes=[
            pltpu.VMEM((rows, cols + 2 * EDGE, LANES), wide),
            pltpu.VMEM((KERNEL * KERNEL, GROUPS, LANES), wide),
        ],
        compiler_params=params(24),
        cost_estimate=cost(10),
        name="conv_inner",
    )(block, left, right, weight, bias, reduce_weight, reduce_bias)


def conv_edge(flag, spread, top, bottom, weight, bias, reduce_weight, reduce_bias, gram, colsum):
    tiles, rows, groups = spread.shape[:3]
    cols, channels = (groups - KERNEL + 1) * GROUPS, top.shape[1]
    width = reduce_weight.shape[1]
    pixels = 2 * HALF * cols
    side = (tiles, HALF, groups, GROUPS, LANES)
    sums_rows = 3 * width // 4 + 2 * GROUPS
    return pl.pallas_call(
        edge_kernel,
        in_specs=[in_smem] + [in_vmem] * 9,
        out_specs=[in_vmem] * 7,
        out_shape=[
            shape_of(side),
            shape_of(side),
            shape_of((pixels, channels), narrow),
            shape_of((pixels, width)),
            shape_of((pixels, width), narrow),
            shape_of((sums_rows // 2, width)),
            shape_of((sums_rows // 2, width)),
        ],
        scratch_shapes=[
            pltpu.VMEM((2 * HALF, cols + 2 * EDGE, LANES), wide),
            pltpu.VMEM((2, top.shape[0] - HALF * cols, LANES), wide),
            pltpu.VMEM((KERNEL * KERNEL, GROUPS, LANES), wide),
            pltpu.VMEM((sums_rows, width), wide),
        ],
        compiler_params=params(24),
        cost_estimate=cost(6),
        name="conv_edge",
    )(flag, spread, top, bottom, weight, bias, reduce_weight, reduce_bias, gram, colsum)


def split(value):
    high = value.astype(narrow)
    return high, (value - high.astype(wide)).astype(narrow)


def product(left, right):
    def dot(a, b):
        return jnp.dot(a, b, preferred_element_type=wide)

    return dot(left[0], right[0]) + (dot(left[0], right[1]) + dot(left[1], right[0]))


def square_root(current):
    size = current.shape[0]
    row = lax.broadcasted_iota(jnp.int32, (size, size), 0)
    col = lax.broadcasted_iota(jnp.int32, (size, size), 1)
    triple = jnp.where(row == col, 3.0, 0.0)
    factor = split(0.5 * (triple - current))
    current = split(current)
    trail = [(current, None, factor)]
    inverse = factor
    current = split(product(current, factor))
    for step in range(1, NEWTON_STEPS):
        factor = split(0.5 * (triple - product(inverse, current)))
        trail.append((current, inverse, factor))
        last = step == NEWTON_STEPS - 1
        if not last:
            inverse = split(product(factor, inverse))
        current = product(current, factor)
        if not last:
            current = split(current)
    return current, trail


def square_root_change(change, trail):
    first, _, factor = trail[0]
    move = split(change)
    factor_move = split(-0.5 * change)
    change = product(move, factor) + product(first, factor_move)
    inverse_move = factor_move
    for step in range(1, NEWTON_STEPS):
        current, inverse, factor = trail[step]
        move = split(change)
        factor_move = split(
            -0.5 * (product(inverse_move, current) + product(inverse, move))
        )
        change = product(move, factor) + product(current, factor_move)
        if step < NEWTON_STEPS - 1:
            inverse_move = split(product(factor_move, inverse) + product(factor, inverse_move))
    return change


def head_kernel(
    flag, label, class_bias, own, other, class_weight,
    feat_inner, feat_edge, gate_inner, gate_edge, conv_turned, reduce_turned,
    root_out, kept_out, sent_out, bias_grad_out, conv_inner_out, conv_edge_out,
    sums, pre, *, count, image_count,
):
    width = root_out.shape[1]
    half = width // 2
    quarter = half // 2
    rows = own.shape[0]
    upper = flag[0] != 0
    mine, theirs = own[...], other[...]
    sums[:rows, :] = jnp.where(upper, theirs, mine)
    sums[rows:, :] = jnp.where(upper, mine, theirs)
    low = jnp.concatenate(
        [sums[half : half + quarter, :half], sums[half : half + quarter, half:]], axis=0
    )
    cross = sums[:half, half:]
    gram = jnp.concatenate(
        [sums[:half, :], jnp.concatenate([cross.T, low], axis=1)], axis=0
    )
    mean_row = sums[half + quarter : half + quarter + 1, :] / count
    mean_col = jnp.broadcast_to(mean_row, (width, width)).T
    sigma = gram / count - mean_col * mean_row
    row = lax.broadcasted_iota(jnp.int32, (width, width), 0)
    col = lax.broadcasted_iota(jnp.int32, (width, width), 1)
    diagonal = row == col
    trace_value = jnp.sum(jnp.where(diagonal, sigma, 0.0), keepdims=True) + epsilon
    root_scale = jnp.sqrt(trace_value)
    unit, trail = square_root(sigma / trace_value)
    root = root_scale * unit
    root_out[:width, :] = root

    classes = class_weight.shape[0]
    slots = root_out.shape[0] - width
    place = lax.broadcasted_iota(jnp.int32, (slots, 1), 0)
    bias = jnp.zeros((slots, 1), wide)
    for index in range(classes):
        bias = jnp.where(place == index, class_bias[index], bias)
    partial = [
        jnp.sum(class_weight[index].astype(wide) * root, axis=0, keepdims=True)
        for index in range(classes)
    ]
    partial.append(jnp.zeros((slots - classes, width), wide))
    logits = jnp.sum(jnp.concatenate(partial, axis=0), axis=1, keepdims=True) + bias
    onehot = jnp.where(place == label[0], 1.0, 0.0)
    soft = jnp.maximum(logits, 0.0) + jnp.log(1.0 + jnp.exp(-jnp.abs(logits)))
    share = 1.0 / (1.0 + jnp.exp(-logits))
    used = place < classes
    loss_part = jnp.sum(jnp.where(used, soft - onehot * logits, 0.0), keepdims=True)
    logit_grad = jnp.where(used, loss_scale * (share - onehot) / image_count, 0.0)
    root_out[width:, :] = jnp.broadcast_to(
        jnp.where(place == classes, loss_part, logit_grad), (slots, width)
    )

    root_grad = jnp.zeros((width, width), wide)
    for index in range(classes):
        root_grad = root_grad + class_weight[index].astype(wide) * logit_grad[index : index + 1, :]
    root_grad = root_grad + root_grad.T
    change = square_root_change(root_scale * root_grad, trail)
    trace_grad = jnp.sum(root_grad * unit, keepdims=True) / (2.0 * root_scale) - jnp.sum(
        change * sigma, keepdims=True
    ) / (trace_value * trace_value)
    symmetric = (
        (change / trace_value + jnp.where(diagonal, trace_grad, 0.0)) / count
    ).astype(narrow)
    mean_term = jnp.sum(mean_col * symmetric.astype(wide), axis=0, keepdims=True)

    inner = feat_inner.shape[0]
    for feat, gate, start in ((feat_inner, gate_inner, 0), (feat_edge, gate_edge, inner)):
        grad = jnp.dot(feat[...], symmetric, preferred_element_type=wide) - mean_term
        pre[start : start + feat.shape[0], :] = (grad * gate[...]).astype(narrow)
    pre_grad = pre[...]
    bias_grad_out[...] = jnp.sum(pre_grad.astype(wide), axis=0, keepdims=True)
    weight_grad = jnp.dot(conv_turned[...], pre_grad, preferred_element_type=wide)
    part = kept_out.shape[0]
    keep_or_send(upper, weight_grad[:part, :], weight_grad[part:, :], kept_out, sent_out)
    for out, start in ((conv_inner_out, 0), (conv_edge_out, inner)):
        out[...] = jnp.dot(
            pre[start : start + out.shape[0], :], reduce_turned[...], preferred_element_type=wide
        ).astype(narrow)


def head(flag, label, class_bias, own, other, class_weight, prepared, count, image_count):
    feat_inner, feat_edge, gate_inner, gate_edge, conv_turned, reduce_turned = prepared
    width, channels = reduce_turned.shape
    inner, edge = feat_inner.shape[0], feat_edge.shape[0]
    slots = -(-(class_weight.shape[0] + 1) // GROUPS) * GROUPS
    return pl.pallas_call(
        functools.partial(head_kernel, count=count, image_count=image_count),
        in_specs=[in_smem] * 3 + [in_vmem] * 9,
        out_specs=[in_vmem] * 6,
        out_shape=[
            shape_of((width + slots, width)),
            shape_of((channels // 2, width)),
            shape_of((channels // 2, width)),
            shape_of((1, width)),
            shape_of((inner, channels), narrow),
            shape_of((edge, channels), narrow),
        ],
        scratch_shapes=[
            pltpu.VMEM((2 * own.shape[0], width), wide),
            pltpu.VMEM((inner + edge, width), narrow),
        ],
        compiler_params=params(24),
        cost_estimate=cost(10),
        name="head",
    )(
        flag, label, class_bias, own, other, class_weight,
        feat_inner, feat_edge, gate_inner, gate_edge, conv_turned, reduce_turned,
    )


def prepare_kernel(
    before_inner, before_edge, conv_inner_in, conv_edge_in, reduce_weight,
    gate_inner, gate_edge, conv_turned, reduce_turned,
):
    for before, gate in ((before_inner, gate_inner), (before_edge, gate_edge)):
        value = before[...]
        share = 1.0 / (1.0 + jnp.exp(-value))
        gate[...] = share * (1.0 + value * (1.0 - share))
    inner = conv_inner_in.shape[0]
    conv_turned[:, :inner] = conv_inner_in[...].T
    conv_turned[:, inner:] = conv_edge_in[...].T
    reduce_turned[...] = reduce_weight[...].T


def prepare(before_inner, before_edge, conv_in, conv_ed, reduce_weight):
    channels, width = reduce_weight.shape
    inner, edge = before_inner.shape[0], before_edge.shape[0]
    return pl.pallas_call(
        prepare_kernel,
        in_specs=[in_vmem] * 5,
        out_specs=[in_vmem] * 4,
        out_shape=[
            shape_of((inner, width)),
            shape_of((edge, width)),
            shape_of((channels, inner + edge), narrow),
            shape_of((width, channels), narrow),
        ],
        compiler_params=params(16),
        cost_estimate=cost(1),
        name="prepare",
    )(before_inner, before_edge, conv_in, conv_ed, reduce_weight)


def taps_kernel(
    flag, spread_in, spread_top, spread_bottom, grad_inner, grad_edge, bias_grad, *refs,
    first, many,
):
    kept_out, sent_out, grads, out = refs[-4:]
    rows = spread_in.shape[1]
    steps = grads.shape[1]
    cols = steps * GROUPS
    order = edge_rows(rows)
    taps = KERNEL * KERNEL
    part = kept_out.shape[0]
    upper = flag[0] != 0
    out[taps:, :] = jnp.zeros((out.shape[0] - taps, LANES), wide)

    def one_tile(tile, _):
        lanes = lanes_of(tile)

        for row in range(rows):
            if row in order:
                source, place = grad_edge, order.index(row)
            else:
                source, place = grad_inner, row - HALF
            values = source[place * cols : (place + 1) * cols, lanes].astype(wide)
            for step in range(steps):
                grads[row, step] = values[step * GROUPS : (step + 1) * GROUPS, :]

        def load(place, group):
            if place < 0:
                return spread_top[tile, place + HALF, group]
            if place >= rows:
                return spread_bottom[tile, place - rows, group]
            return spread_in[tile, place, group]

        for begin in range(0, KERNEL, 2):
            row_taps = [tap for tap in (begin, begin + 1) if tap < KERNEL]
            total = {
                (row_tap, col_tap): jnp.zeros((GROUPS, LANES), wide)
                for row_tap in row_taps
                for col_tap in range(KERNEL)
            }
            for place in range(begin - HALF, rows + row_taps[-1] - HALF):
                windows = [load(place, group) for group in range(steps + KERNEL - 1)]
                for row_tap in row_taps:
                    row = place - row_tap + HALF
                    if not 0 <= row < rows:
                        continue
                    for step in range(steps):
                        grad = grads[row, step]
                        for col_tap in range(KERNEL):
                            total[row_tap, col_tap] += windows[step + col_tap] * grad
            for (row_tap, col_tap), value in total.items():
                tap = row_tap * KERNEL + col_tap
                out[tap : tap + 1, :] = jnp.sum(value, axis=0, keepdims=True)
        total = [jnp.zeros((GROUPS, LANES), wide) for _ in range(KERNEL)]
        for index in range(rows * steps):
            slot = index % KERNEL
            total[slot] = total[slot] + grads[index // steps, index % steps]
        out[taps : taps + 1, :] = jnp.sum(sum(total), axis=0, keepdims=True)
        low, high = out[:part, :], out[part:, :]
        kept_out[:, lanes] = jnp.where(upper, high, low)
        sent_out[:, lanes] = jnp.where(upper, low, high)
        return 0

    lax.fori_loop(first, first + many, one_tile, 0)
    if first == 0:
        width = bias_grad.shape[1]
        place = taps + 1 - part
        row = jnp.broadcast_to(bias_grad[...], (1, width))

        @pl.when(upper)
        def _():
            kept_out[place : place + 1, :width] = row

        @pl.when(jnp.logical_not(upper))
        def _():
            sent_out[place : place + 1, :width] = row


def tap_grads(flag, spreads, grads, bias_grad, filled, first, many):
    tiles, rows, groups = spreads[0].shape[:3]
    steps = groups - KERNEL + 1
    taps_rows = -(-(KERNEL * KERNEL + 2) // 32) * 32
    part = (taps_rows // 2, tiles * LANES)
    return pl.pallas_call(
        functools.partial(taps_kernel, first=first, many=many),
        in_specs=[in_smem] + [in_vmem] * (6 + len(filled)),
        out_specs=[in_vmem] * 2,
        out_shape=[shape_of(part), shape_of(part)],
        input_output_aliases={7 + index: index for index in range(len(filled))},
        scratch_shapes=[
            pltpu.VMEM((rows, steps, GROUPS, LANES), wide),
            pltpu.VMEM((taps_rows, LANES), wide),
        ],
        compiler_params=params(16),
        cost_estimate=cost(5),
        name="tap_grads",
    )(flag, *spreads, *grads, bias_grad, *filled)


def finish_kernel(flag, own, other, depth_out, depth_bias_out, bias_out, sums):
    part = own.shape[0]
    upper = flag[0] != 0
    sums[:part, :] = jnp.where(upper, other[...], own[...])
    sums[part:, :] = jnp.where(upper, own[...], other[...])
    for row_tap in range(KERNEL):
        depth_out[row_tap] = sums[row_tap * KERNEL : (row_tap + 1) * KERNEL, :]
    taps = KERNEL * KERNEL
    depth_bias_out[...] = sums[taps, :]
    bias_out[...] = sums[taps + 1, : bias_out.shape[0]]


def finish(flag, own, other, width):
    part, channels = own.shape
    return pl.pallas_call(
        finish_kernel,
        in_specs=[in_smem] + [in_vmem] * 2,
        out_specs=[in_vmem] * 3,
        out_shape=[
            shape_of((KERNEL, KERNEL, channels)),
            shape_of((channels,)),
            shape_of((width,)),
        ],
        scratch_shapes=[pltpu.VMEM((2 * part, channels), wide)],
        compiler_params=params(8),
        cost_estimate=cost(1),
        name="finish",
    )(flag, own, other)


def edge_strip(block, left, right, rows):
    channels = block.shape[2]
    parts = [part[rows].reshape(-1, channels) for part in (block, left, right)]
    short = -(2 * HALF * HALF) % 16
    return jnp.concatenate(parts + [jnp.zeros((short, channels), block.dtype)])


def body(
    features, depth_weight, depth_bias, reduce_weight, reduce_bias, class_weight, class_bias, labels
):
    together = lax.optimization_barrier
    block = features[0]
    rows, cols, channels = block.shape
    width = reduce_weight.shape[1]
    classes = class_bias.shape[0]
    count = rows * cols * lax.axis_size("sy") * lax.axis_size("sx")
    image_count = features.shape[0] * lax.axis_size("dp")

    flag = is_upper("sx", 1).astype(jnp.int32)[None]
    uppers = [is_upper("sx", shift) for shift in doublings("sx")]
    bias_row = depth_bias[None]
    reduce_row = reduce_bias[None]
    left = next_along(block[:, cols - HALF :], "sx")
    right = back_along(block[:, :HALF], "sx")
    low, high, left, right, flag, uppers, bias_row, reduce_row = together(
        (
            edge_strip(block, left, right, slice(rows - HALF, rows)),
            edge_strip(block, left, right, slice(0, HALF)),
            left,
            right,
            flag,
            uppers,
            bias_row,
            reduce_row,
        )
    )
    uppers = dict(zip(doublings("sx"), uppers))
    top = next_along(low, "sy")
    bottom = back_along(high, "sy")
    spread, conv_in, before_in, feat_in, gram, colsum = conv_inner(
        block, left, right, depth_weight, bias_row, reduce_weight, reduce_row
    )
    spread_top, spread_bottom, conv_ed, before_ed, feat_ed, kept, sent = conv_edge(
        flag, spread, top, bottom, depth_weight, bias_row, reduce_weight, reduce_row, gram, colsum
    )

    sums = kept + swap(sent, "sx", 1)
    sums, before_in, before_ed, conv_in, conv_ed = together(
        (sums, before_in, before_ed, conv_in, conv_ed)
    )
    gate_in, gate_ed, conv_turned, reduce_turned = prepare(
        before_in, before_ed, conv_in, conv_ed, reduce_weight
    )
    for shift in doublings("sx", 2):
        sums = exchange(sums, "sx", shift, wide)
    sums, gate_in, gate_ed, conv_turned, reduce_turned = together(
        (sums, gate_in, gate_ed, conv_turned, reduce_turned)
    )
    for shift in doublings("sy"):
        sums = exchange(sums, "sy", shift, wide)
    other = swap(sums, "sx", 1)

    root, kept, sent, bias_grad, *grads = head(
        flag,
        labels,
        class_bias,
        sums,
        other,
        class_weight,
        (feat_in, feat_ed, gate_in, gate_ed, conv_turned, reduce_turned),
        count,
        image_count,
    )

    known = [root] + [swap(root, "dp", shift) for shift in range(1, lax.axis_size("dp"))]
    spreads = (spread, spread_top, spread_bottom)
    tiles = channels // LANES
    many = tiles // 3 if tiles % 3 == 0 else tiles
    turns = list(range(0, tiles, many))
    filled = []

    def beside(sums):
        if turns:
            sums, grads[:], filled[:] = together((sums, grads, filled))
            filled[:] = tap_grads(flag, spreads, grads, bias_grad, filled, turns.pop(0), many)
        return sums

    sums = kept + swap(sent, "sx", 1)
    for shift in doublings("sx", 2):
        sums = halve(beside(sums), "sx", shift, uppers[shift], narrow)
    for shift in doublings("dp"):
        sums = exchange(beside(sums), "dp", shift, narrow)
    sums = exchange_all(beside(sums), "sy", narrow).astype(narrow)
    while turns:
        sums = beside(sums)

    sums, (kept, sent), known = together((sums, filled, known))
    small = kept + swap(sent, "sx", 1)
    class_weight_grad = tree_sum(
        [part[width : width + classes, 0][:, None, None] * part[None, :width] for part in known]
    )
    totals = tree_sum([part[width:, 0] for part in known])
    class_bias_grad = totals[:classes]
    loss = totals[classes] / image_count
    small, sums = together((small, sums))
    for shift in reversed(doublings("sx", 2)):
        sums = unhalve(sums, "sx", shift, uppers[shift])
    squares, left_x, left_dp = pair_up(doublings("sx", 2), doublings("dp"))
    for pair in squares:
        small = exchange_square(small, ("dp", "sx"), pair, narrow)
    for shift in left_x:
        small = exchange(small, "sx", shift, narrow)
    for shift in left_dp:
        small = exchange(small, "dp", shift, narrow)
    small, sums = together((small, sums))
    weight_grad = unhalve(sums, "sx", 1, uppers[1]).astype(wide)
    small = exchange_all(small, "sy", narrow)
    depth_grad, depth_bias_grad, bias_grad = finish(flag, small, swap(small, "sx", 1), width)
    return (
        loss,
        depth_grad,
        depth_bias_grad,
        weight_grad,
        bias_grad,
        class_weight_grad,
        class_bias_grad,
    )


def solution(mesh):
    placed = (P("dp", "sy", "sx", None), P(), P(), P(), P(), P(), P(), P("dp"))
    return jax.shard_map(
        body,
        mesh=mesh,
        in_specs=placed,
        out_specs=(P(), P(), P(), P(), P(), P(), P()),
        check_vma=False,
    )
```

```python
import functools

import jax
import jax.numpy as jnp
from jax import lax
from jax.experimental import pallas as pl
from jax.experimental.pallas import tpu as pltpu
from jax.sharding import PartitionSpec as P

KERNEL = 7
HALF = KERNEL // 2
NEWTON_STEPS = 5
LANES = 128
GROUPS = 8
EDGE = 8
TAPS_ROWS = 64

epsilon = 1e-05
loss_scale = 64.0
narrow = jnp.bfloat16
wide = jnp.float32


def params(megabytes):
    return pltpu.CompilerParams(vmem_limit_bytes=megabytes * 1024 * 1024)


def swap(value, axis, shift):
    count = lax.axis_size(axis)
    return lax.ppermute(value, axis, [(i, i ^ shift) for i in range(count)])


def is_upper(axis, shift):
    return (lax.axis_index(axis) & shift) != 0


def tree_sum(terms):
    while len(terms) > 1:
        terms = [terms[i] + terms[i + 1] for i in range(0, len(terms), 2)]
    return terms[0]


def exchange(value, axis, shift, sent_as):
    sent = value.astype(sent_as)
    return sent.astype(wide) + swap(sent, axis, shift).astype(wide)


def exchange_all(value, axis, sent_as):
    sent = value.astype(sent_as)
    moved = [sent] + [swap(sent, axis, shift) for shift in range(1, lax.axis_size(axis))]
    return tree_sum([part.astype(wide) for part in moved])


def square_pairs(axes, shifts):
    counts = [lax.axis_size(axis) for axis in axes]
    return {
        2 * first + second: [
            (i * counts[1] + j, (i ^ (first * shifts[0])) * counts[1] + (j ^ (second * shifts[1])))
            for i in range(counts[0])
            for j in range(counts[1])
        ]
        for first, second in ((0, 1), (1, 0), (1, 1))
    }


def square_scatter(value, axes, pairs, places, sent_as):
    pieces = value.reshape((4, value.shape[0] // 4) + value.shape[1:])

    def piece(turn):
        return lax.dynamic_index_in_dim(pieces, places[turn], 0, keepdims=False)

    moved = [
        lax.ppermute(piece(turn).astype(sent_as), axes, pairs[turn]).astype(wide)
        for turn in (1, 2, 3)
    ]
    return tree_sum([piece(0)] + moved)


def square_gather(value, axes, pairs, places):
    whole = jnp.zeros((4,) + value.shape, value.dtype)
    for turn in range(4):
        part = lax.ppermute(value, axes, pairs[turn]) if turn else value
        whole = lax.dynamic_update_index_in_dim(whole, part, places[turn], 0)
    return whole.reshape((-1,) + value.shape[1:])


def doublings(axis, first=1):
    found = []
    shift = first
    while shift < lax.axis_size(axis):
        found.append(shift)
        shift *= 2
    return found


def next_along(value, axis):
    return lax.ppermute(value, axis, [(i, i + 1) for i in range(lax.axis_size(axis) - 1)])


def back_along(value, axis):
    return lax.ppermute(value, axis, [(i + 1, i) for i in range(lax.axis_size(axis) - 1)])


def spread_columns(source, target):
    for group in range(target.shape[0]):
        target[group] = source[pl.ds(EDGE - HALF + group, GROUPS, stride=GROUPS), :]


def fill_row(wide_row, middle, left, right):
    cols = middle.shape[0]
    wide_row[EDGE : EDGE + cols, :] = middle.astype(wide)
    wide_row[EDGE - HALF : EDGE, :] = left.astype(wide)
    wide_row[EDGE + cols : EDGE + cols + HALF, :] = right.astype(wide)


def lanes_of(tile):
    return pl.ds(pl.multiple_of(tile * LANES, LANES), LANES)


def spread_weights(weight_ref, spread_ref, lanes):
    for row_tap in range(KERNEL):
        for col_tap in range(KERNEL):
            scale = weight_ref[row_tap, col_tap : col_tap + 1, lanes]
            spread_ref[row_tap * KERNEL + col_tap] = jnp.broadcast_to(scale, spread_ref.shape[1:])


def conv_rows(load, spread_ref, bias, steps, count):
    total = [[bias] * steps for _ in range(count)]
    for place in range(KERNEL + count - 1):
        windows = [load(place, group) for group in range(steps + KERNEL - 1)]
        for row in range(count):
            row_tap = place - row
            if not 0 <= row_tap < KERNEL:
                continue
            for col_tap in range(KERNEL):
                scale = spread_ref[row_tap * KERNEL + col_tap]
                for step in range(steps):
                    total[row][step] = total[row][step] + windows[step + col_tap] * scale
    return jnp.concatenate([part for row in total for part in row], axis=0).astype(narrow)


def reduce_part(conv_out, reduce_ref, reduce_bias_ref, before_out, feat_out):
    before = jnp.dot(conv_out[...], reduce_ref[...], preferred_element_type=wide)
    before = before + reduce_bias_ref[...]
    before_out[...] = before
    feat_out[...] = (before / (1.0 + jnp.exp(-before))).astype(narrow)
    feat = feat_out[...]
    gram = lax.dot_general(feat, feat, (((0,), (0,)), ((), ())), preferred_element_type=wide)
    return gram, jnp.sum(feat.astype(wide), axis=0, keepdims=True)


def inner_kernel(
    block, left, right, weight, bias, reduce_weight, reduce_bias,
    spread_out, conv_out, before_out, feat_out, gram_out, colsum_out,
    wide_row, spread_weight,
):
    rows, cols = block.shape[0], block.shape[1]
    steps = cols // GROUPS
    inner = rows - 2 * HALF
    at_once = 2 if inner % 2 == 0 else 1

    def one_tile(tile, _):
        lanes = lanes_of(tile)
        spread_weights(weight, spread_weight, lanes)
        start_value = jnp.broadcast_to(bias[0:1, lanes], (GROUPS, LANES))

        def fill(row, _):
            place = wide_row.at[row]
            fill_row(place, block[row, :, lanes], left[row, :, lanes], right[row, :, lanes])
            spread_columns(place, spread_out.at[tile, row])
            return 0

        lax.fori_loop(0, rows, fill, 0)

        def one_row(index, _):
            def load(row_tap, group):
                return spread_out[tile, index + row_tap, group]

            start = pl.multiple_of(index * cols, at_once * cols)
            conv_out[pl.ds(start, at_once * cols), lanes] = conv_rows(
                load, spread_weight, start_value, steps, at_once
            )
            return 0

        lax.fori_loop(0, inner // at_once, lambda turn, _: one_row(turn * at_once, 0), 0)
        return 0

    lax.fori_loop(0, spread_out.shape[0], one_tile, 0)
    gram_out[...], colsum_out[...] = reduce_part(
        conv_out, reduce_weight, reduce_bias, before_out, feat_out
    )


def edge_kernel(
    flag, spread_in, top, bottom, weight, bias, reduce_weight, reduce_bias, gram_in, colsum_in,
    spread_top, spread_bottom, conv_out, before_out, feat_out, kept_out, sent_out,
    wide_row, corners, spread_weight, sums,
):
    rows, cols = spread_in.shape[1], wide_row.shape[1] - 2 * EDGE
    steps = cols // GROUPS

    def one_tile(tile, _):
        lanes = lanes_of(tile)
        spread_weights(weight, spread_weight, lanes)
        start_value = jnp.broadcast_to(bias[0:1, lanes], (GROUPS, LANES))
        for side, (strip, spread) in enumerate(((top, spread_top), (bottom, spread_bottom))):
            corners[side] = strip[HALF * cols :, lanes].astype(wide)
            for row in range(HALF):
                place = wide_row.at[side * HALF + row]
                left = corners[side, row * HALF : (row + 1) * HALF, :]
                right = corners[side, (HALF + row) * HALF : (HALF + row + 1) * HALF, :]
                fill_row(place, strip[row * cols : (row + 1) * cols, lanes], left, right)
                spread_columns(place, spread.at[tile, row])

        def load_from(row):
            def load(row_tap, group):
                place = row + row_tap - HALF
                if place < 0:
                    return spread_top[tile, place + HALF, group]
                if place >= rows:
                    return spread_bottom[tile, place - rows, group]
                return spread_in[tile, place, group]

            return load

        for side, row in enumerate((0, rows - HALF)):
            start = side * HALF * cols
            conv_out[start : start + HALF * cols, lanes] = conv_rows(
                load_from(row), spread_weight, start_value, steps, HALF
            )
        return 0

    lax.fori_loop(0, spread_in.shape[0], one_tile, 0)
    gram, colsum = reduce_part(conv_out, reduce_weight, reduce_bias, before_out, feat_out)
    gram = gram + gram_in[...]
    colsum = colsum + colsum_in[...]
    width = gram.shape[0]
    half = width // 2
    quarter = half // 2
    sums[:half, :] = gram[:half, :]
    sums[half : half + quarter, :half] = gram[half : half + quarter, half:]
    sums[half : half + quarter, half:] = gram[half + quarter :, half:]
    sums[half + quarter :, :] = jnp.broadcast_to(
        colsum, (sums.shape[0] - half - quarter, width)
    )
    part = kept_out.shape[0]
    keep_or_send(flag[0] != 0, sums[:part, :], sums[part:, :], kept_out, sent_out)


def keep_or_send(upper, low, high, kept_out, sent_out):
    kept_out[...] = jnp.where(upper, high, low)
    sent_out[...] = jnp.where(upper, low, high).astype(sent_out.dtype)


def edge_rows(rows):
    return list(range(HALF)) + list(range(rows - HALF, rows))


def shape_of(shape, dtype=wide):
    return jax.ShapeDtypeStruct(shape, dtype)


in_vmem = pl.BlockSpec(memory_space=pltpu.VMEM)
in_smem = pl.BlockSpec(memory_space=pltpu.SMEM)


def cost(microseconds):
    return pl.CostEstimate(
        flops=microseconds * 10**9, bytes_accessed=microseconds * 10**6, transcendentals=0
    )


def conv_inner(block, left, right, weight, bias, reduce_weight, reduce_bias):
    rows, cols, channels = block.shape
    width = reduce_weight.shape[1]
    tiles = channels // LANES
    steps = cols // GROUPS
    pixels = (rows - 2 * HALF) * cols
    return pl.pallas_call(
        inner_kernel,
        in_specs=[in_vmem] * 7,
        out_specs=[in_vmem] * 6,
        out_shape=[
            shape_of((tiles, rows, steps + KERNEL - 1, GROUPS, LANES)),
            shape_of((pixels, channels), narrow),
            shape_of((pixels, width)),
            shape_of((pixels, width), narrow),
            shape_of((width, width)),
            shape_of((1, width)),
        ],
        scratch_shapes=[
            pltpu.VMEM((rows, cols + 2 * EDGE, LANES), wide),
            pltpu.VMEM((KERNEL * KERNEL, GROUPS, LANES), wide),
        ],
        compiler_params=params(24),
        cost_estimate=cost(10),
        name="conv_inner",
    )(block, left, right, weight, bias, reduce_weight, reduce_bias)


def conv_edge(flag, spread, top, bottom, weight, bias, reduce_weight, reduce_bias, gram, colsum):
    tiles, rows, groups = spread.shape[:3]
    cols, channels = (groups - KERNEL + 1) * GROUPS, top.shape[1]
    width = reduce_weight.shape[1]
    pixels = 2 * HALF * cols
    side = (tiles, HALF, groups, GROUPS, LANES)
    sums_rows = 3 * width // 4 + 2 * GROUPS
    return pl.pallas_call(
        edge_kernel,
        in_specs=[in_smem] + [in_vmem] * 9,
        out_specs=[in_vmem] * 7,
        out_shape=[
            shape_of(side),
            shape_of(side),
            shape_of((pixels, channels), narrow),
            shape_of((pixels, width)),
            shape_of((pixels, width), narrow),
            shape_of((sums_rows // 2, width)),
            shape_of((sums_rows // 2, width)),
        ],
        scratch_shapes=[
            pltpu.VMEM((2 * HALF, cols + 2 * EDGE, LANES), wide),
            pltpu.VMEM((2, top.shape[0] - HALF * cols, LANES), wide),
            pltpu.VMEM((KERNEL * KERNEL, GROUPS, LANES), wide),
            pltpu.VMEM((sums_rows, width), wide),
        ],
        compiler_params=params(24),
        cost_estimate=cost(6),
        name="conv_edge",
    )(flag, spread, top, bottom, weight, bias, reduce_weight, reduce_bias, gram, colsum)


def split(value):
    high = value.astype(narrow)
    return high, (value - high.astype(wide)).astype(narrow)


def product(left, right):
    def dot(a, b):
        return jnp.dot(a, b, preferred_element_type=wide)

    return dot(left[0], right[0]) + (dot(left[0], right[1]) + dot(left[1], right[0]))


def square_root(current):
    size = current.shape[0]
    row = lax.broadcasted_iota(jnp.int32, (size, size), 0)
    col = lax.broadcasted_iota(jnp.int32, (size, size), 1)
    triple = jnp.where(row == col, 3.0, 0.0)
    factor = split(0.5 * (triple - current))
    current = split(current)
    trail = [(current, None, factor)]
    inverse = factor
    current = split(product(current, factor))
    for step in range(1, NEWTON_STEPS):
        factor = split(0.5 * (triple - product(inverse, current)))
        trail.append((current, inverse, factor))
        last = step == NEWTON_STEPS - 1
        if not last:
            inverse = split(product(factor, inverse))
        current = product(current, factor)
        if not last:
            current = split(current)
    return current, trail


def square_root_change(change, trail):
    first, _, factor = trail[0]
    move = split(change)
    factor_move = split(-0.5 * change)
    change = product(move, factor) + product(first, factor_move)
    inverse_move = factor_move
    for step in range(1, NEWTON_STEPS):
        current, inverse, factor = trail[step]
        move = split(change)
        factor_move = split(
            -0.5 * (product(inverse_move, current) + product(inverse, move))
        )
        change = product(move, factor) + product(current, factor_move)
        if step < NEWTON_STEPS - 1:
            inverse_move = split(product(factor_move, inverse) + product(factor, inverse_move))
    return change


def head_kernel(
    flag, label, class_bias, own, other, class_weight,
    feat_inner, feat_edge, gate_inner, gate_edge, conv_turned, reduce_turned,
    root_out, payload, conv_inner_out, conv_edge_out,
    sums, pre, *, count, image_count,
):
    width = root_out.shape[1]
    half = width // 2
    quarter = half // 2
    rows = own.shape[0]
    upper = flag[0] != 0
    mine, theirs = own[...], other[...]
    sums[:rows, :] = jnp.where(upper, theirs, mine)
    sums[rows:, :] = jnp.where(upper, mine, theirs)
    low = jnp.concatenate(
        [sums[half : half + quarter, :half], sums[half : half + quarter, half:]], axis=0
    )
    cross = sums[:half, half:]
    gram = jnp.concatenate(
        [sums[:half, :], jnp.concatenate([cross.T, low], axis=1)], axis=0
    )
    mean_row = sums[half + quarter : half + quarter + 1, :] / count
    mean_col = jnp.broadcast_to(mean_row, (width, width)).T
    sigma = gram / count - mean_col * mean_row
    row = lax.broadcasted_iota(jnp.int32, (width, width), 0)
    col = lax.broadcasted_iota(jnp.int32, (width, width), 1)
    diagonal = row == col
    trace_value = jnp.sum(jnp.where(diagonal, sigma, 0.0), keepdims=True) + epsilon
    root_scale = jnp.sqrt(trace_value)
    unit, trail = square_root(sigma / trace_value)
    root = root_scale * unit
    root_out[:width, :] = root

    classes = class_weight.shape[0]
    slots = root_out.shape[0] - width
    place = lax.broadcasted_iota(jnp.int32, (slots, 1), 0)
    bias = jnp.zeros((slots, 1), wide)
    for index in range(classes):
        bias = jnp.where(place == index, class_bias[index], bias)
    partial = [
        jnp.sum(class_weight[index].astype(wide) * root, axis=0, keepdims=True)
        for index in range(classes)
    ]
    partial.append(jnp.zeros((slots - classes, width), wide))
    logits = jnp.sum(jnp.concatenate(partial, axis=0), axis=1, keepdims=True) + bias
    onehot = jnp.where(place == label[0], 1.0, 0.0)
    soft = jnp.maximum(logits, 0.0) + jnp.log(1.0 + jnp.exp(-jnp.abs(logits)))
    share = 1.0 / (1.0 + jnp.exp(-logits))
    used = place < classes
    loss_part = jnp.sum(jnp.where(used, soft - onehot * logits, 0.0), keepdims=True)
    logit_grad = jnp.where(used, loss_scale * (share - onehot) / image_count, 0.0)
    root_out[width:, :] = jnp.broadcast_to(
        jnp.where(place == classes, loss_part, logit_grad), (slots, width)
    )

    root_grad = jnp.zeros((width, width), wide)
    for index in range(classes):
        root_grad = root_grad + class_weight[index].astype(wide) * logit_grad[index : index + 1, :]
    root_grad = root_grad + root_grad.T
    change = square_root_change(root_scale * root_grad, trail)
    trace_grad = jnp.sum(root_grad * unit, keepdims=True) / (2.0 * root_scale) - jnp.sum(
        change * sigma, keepdims=True
    ) / (trace_value * trace_value)
    symmetric = (
        (change / trace_value + jnp.where(diagonal, trace_grad, 0.0)) / count
    ).astype(narrow)
    mean_term = jnp.sum(mean_col * symmetric.astype(wide), axis=0, keepdims=True)

    inner = feat_inner.shape[0]
    for feat, gate, start in ((feat_inner, gate_inner, 0), (feat_edge, gate_edge, inner)):
        grad = jnp.dot(feat[...], symmetric, preferred_element_type=wide) - mean_term
        pre[start : start + feat.shape[0], :] = (grad * gate[...]).astype(narrow)
    pre_grad = pre[...]
    payload[width:, :] = jnp.zeros((payload.shape[0] - width, payload.shape[1]), wide)
    taps = KERNEL * KERNEL
    payload[width + taps + 1 : width + taps + 2, :width] = jnp.sum(
        pre_grad.astype(wide), axis=0, keepdims=True
    )
    for first in range(0, conv_turned.shape[0], width):
        payload[:width, first : first + width] = jnp.dot(
            conv_turned[first : first + width, :], pre_grad, preferred_element_type=wide
        )
    for out, start in ((conv_inner_out, 0), (conv_edge_out, inner)):
        out[...] = jnp.dot(
            pre[start : start + out.shape[0], :], reduce_turned[...], preferred_element_type=wide
        ).astype(narrow)


def head(flag, label, class_bias, own, other, class_weight, prepared, count, image_count):
    feat_inner, feat_edge, gate_inner, gate_edge, conv_turned, reduce_turned = prepared
    width, channels = reduce_turned.shape
    inner, edge = feat_inner.shape[0], feat_edge.shape[0]
    slots = -(-(class_weight.shape[0] + 1) // GROUPS) * GROUPS
    return pl.pallas_call(
        functools.partial(head_kernel, count=count, image_count=image_count),
        in_specs=[in_smem] * 3 + [in_vmem] * 9,
        out_specs=[in_vmem] * 4,
        out_shape=[
            shape_of((width + slots, width)),
            shape_of((width + TAPS_ROWS, channels)),
            shape_of((inner, channels), narrow),
            shape_of((edge, channels), narrow),
        ],
        scratch_shapes=[
            pltpu.VMEM((2 * own.shape[0], width), wide),
            pltpu.VMEM((inner + edge, width), narrow),
        ],
        compiler_params=params(24),
        cost_estimate=cost(10),
        name="head",
    )(
        flag, label, class_bias, own, other, class_weight,
        feat_inner, feat_edge, gate_inner, gate_edge, conv_turned, reduce_turned,
    )


def prepare_kernel(
    before_inner, before_edge, conv_inner_in, conv_edge_in, reduce_weight,
    gate_inner, gate_edge, conv_turned, reduce_turned,
):
    for before, gate in ((before_inner, gate_inner), (before_edge, gate_edge)):
        value = before[...]
        share = 1.0 / (1.0 + jnp.exp(-value))
        gate[...] = share * (1.0 + value * (1.0 - share))
    inner = conv_inner_in.shape[0]
    conv_turned[:, :inner] = conv_inner_in[...].T
    conv_turned[:, inner:] = conv_edge_in[...].T
    reduce_turned[...] = reduce_weight[...].T


def prepare(before_inner, before_edge, conv_in, conv_ed, reduce_weight):
    channels, width = reduce_weight.shape
    inner, edge = before_inner.shape[0], before_edge.shape[0]
    return pl.pallas_call(
        prepare_kernel,
        in_specs=[in_vmem] * 5,
        out_specs=[in_vmem] * 4,
        out_shape=[
            shape_of((inner, width)),
            shape_of((edge, width)),
            shape_of((channels, inner + edge), narrow),
            shape_of((width, channels), narrow),
        ],
        compiler_params=params(16),
        cost_estimate=cost(1),
        name="prepare",
    )(before_inner, before_edge, conv_in, conv_ed, reduce_weight)


def taps_kernel(
    spread_in, spread_top, spread_bottom, grad_inner, grad_edge, payload_in, payload, grads, *,
    first, last,
):
    rows = spread_in.shape[1]
    steps = grads.shape[1]
    cols = steps * GROUPS
    order = edge_rows(rows)
    taps = KERNEL * KERNEL
    base = payload.shape[0] - TAPS_ROWS

    def one_tile(tile, _):
        lanes = lanes_of(tile)

        for row in range(rows):
            if row in order:
                source, place = grad_edge, order.index(row)
            else:
                source, place = grad_inner, row - HALF
            values = source[place * cols : (place + 1) * cols, lanes].astype(wide)
            for step in range(steps):
                grads[row, step] = values[step * GROUPS : (step + 1) * GROUPS, :]

        def load(place, group):
            if place < 0:
                return spread_top[tile, place + HALF, group]
            if place >= rows:
                return spread_bottom[tile, place - rows, group]
            return spread_in[tile, place, group]

        for begin in range(0, KERNEL, 2):
            row_taps = [tap for tap in (begin, begin + 1) if tap < KERNEL]
            total = {
                (row_tap, col_tap): jnp.zeros((GROUPS, LANES), wide)
                for row_tap in row_taps
                for col_tap in range(KERNEL)
            }
            for place in range(begin - HALF, rows + row_taps[-1] - HALF):
                windows = [load(place, group) for group in range(steps + KERNEL - 1)]
                for row_tap in row_taps:
                    row = place - row_tap + HALF
                    if not 0 <= row < rows:
                        continue
                    for step in range(steps):
                        grad = grads[row, step]
                        for col_tap in range(KERNEL):
                            total[row_tap, col_tap] += windows[step + col_tap] * grad
            for (row_tap, col_tap), value in total.items():
                tap = row_tap * KERNEL + col_tap
                payload[base + tap : base + tap + 1, lanes] = jnp.sum(value, axis=0, keepdims=True)
        total = [jnp.zeros((GROUPS, LANES), wide) for _ in range(KERNEL)]
        for index in range(rows * steps):
            slot = index % KERNEL
            total[slot] = total[slot] + grads[index // steps, index % steps]
        payload[base + taps : base + taps + 1, lanes] = jnp.sum(sum(total), axis=0, keepdims=True)
        return 0

    lax.fori_loop(first, last, one_tile, 0)


def tap_grads(spreads, grads, payload, first, last):
    rows, groups = spreads[0].shape[1:3]
    steps = groups - KERNEL + 1
    return pl.pallas_call(
        functools.partial(taps_kernel, first=first, last=last),
        in_specs=[in_vmem] * 6,
        out_specs=in_vmem,
        out_shape=shape_of(payload.shape),
        input_output_aliases={5: 0},
        scratch_shapes=[pltpu.VMEM((rows, steps, GROUPS, LANES), wide)],
        compiler_params=params(16),
        cost_estimate=cost(2 * (last - first)),
        name="tap_grads",
    )(*spreads, *grads, payload)


def finish_kernel(
    flag, own, other, weight_out, depth_out, depth_bias_out, bias_out, payload,
):
    part = own.shape[0]
    upper = flag[0] != 0
    mine, theirs = own[...].astype(wide), other[...].astype(wide)
    payload[:part, :] = jnp.where(upper, theirs, mine)
    payload[part:, :] = jnp.where(upper, mine, theirs)
    width = weight_out.shape[1]
    for first in range(0, weight_out.shape[0], width):
        weight_out[first : first + width, :] = payload[:width, first : first + width]
    for row_tap in range(KERNEL):
        start = width + row_tap * KERNEL
        depth_out[row_tap] = payload[start : start + KERNEL, :]
    taps = KERNEL * KERNEL
    depth_bias_out[...] = payload[width + taps, :]
    bias_out[...] = payload[width + taps + 1, :width]


def finish(flag, own, other, width):
    part, channels = own.shape
    return pl.pallas_call(
        finish_kernel,
        in_specs=[in_smem] + [in_vmem] * 2,
        out_specs=[in_vmem] * 4,
        out_shape=[
            shape_of((channels, width)),
            shape_of((KERNEL, KERNEL, channels)),
            shape_of((channels,)),
            shape_of((width,)),
        ],
        scratch_shapes=[pltpu.VMEM((2 * part, channels), wide)],
        compiler_params=params(8),
        cost_estimate=cost(1),
        name="finish",
    )(flag, own, other)


def edge_strip(block, left, right, rows):
    channels = block.shape[2]
    parts = [part[rows].reshape(-1, channels) for part in (block, left, right)]
    short = -(2 * HALF * HALF) % 16
    return jnp.concatenate(parts + [jnp.zeros((short, channels), block.dtype)])


def body(
    features, depth_weight, depth_bias, reduce_weight, reduce_bias, class_weight, class_bias, labels
):
    together = lax.optimization_barrier
    block = features[0]
    rows, cols, channels = block.shape
    width = reduce_weight.shape[1]
    classes = class_bias.shape[0]
    count = rows * cols * lax.axis_size("sy") * lax.axis_size("sx")
    image_count = features.shape[0] * lax.axis_size("dp")

    flag = is_upper("sx", 1).astype(jnp.int32)[None]
    upper = is_upper("sx", 1)
    corner = 2 * (lax.axis_index("dp") & 1) + ((lax.axis_index("sx") & 2) >> 1)
    places = [corner ^ turn for turn in range(4)]
    bias_row = depth_bias[None]
    reduce_row = reduce_bias[None]
    left = next_along(block[:, cols - HALF :], "sx")
    right = back_along(block[:, :HALF], "sx")
    low, high, left, right, flag, upper, places, bias_row, reduce_row = together(
        (
            edge_strip(block, left, right, slice(rows - HALF, rows)),
            edge_strip(block, left, right, slice(0, HALF)),
            left,
            right,
            flag,
            upper,
            places,
            bias_row,
            reduce_row,
        )
    )
    top = next_along(low, "sy")
    bottom = back_along(high, "sy")
    spread, conv_in, before_in, feat_in, gram, colsum = conv_inner(
        block, left, right, depth_weight, bias_row, reduce_weight, reduce_row
    )
    spread_top, spread_bottom, conv_ed, before_ed, feat_ed, kept, sent = conv_edge(
        flag, spread, top, bottom, depth_weight, bias_row, reduce_weight, reduce_row, gram, colsum
    )

    sums = kept + swap(sent, "sx", 1)
    sums, before_in, before_ed, conv_in, conv_ed = together(
        (sums, before_in, before_ed, conv_in, conv_ed)
    )
    gate_in, gate_ed, conv_turned, reduce_turned = prepare(
        before_in, before_ed, conv_in, conv_ed, reduce_weight
    )
    for shift in doublings("sx", 2):
        sums = exchange(sums, "sx", shift, wide)
    sums, gate_in, gate_ed, conv_turned, reduce_turned = together(
        (sums, gate_in, gate_ed, conv_turned, reduce_turned)
    )
    for shift in doublings("sy"):
        sums = exchange(sums, "sy", shift, wide)
    other = swap(sums, "sx", 1)

    root, payload, *grads = head(
        flag,
        labels,
        class_bias,
        sums,
        other,
        class_weight,
        (feat_in, feat_ed, gate_in, gate_ed, conv_turned, reduce_turned),
        count,
        image_count,
    )
    known = [root] + [swap(root, "dp", shift) for shift in range(1, lax.axis_size("dp"))]
    spreads = (spread, spread_top, spread_bottom)
    tiles = channels // LANES
    payload = tap_grads(spreads, grads, payload, 0, tiles // 2)
    payload, known = together((payload, known))
    payload = tap_grads(spreads, grads, payload, tiles // 2, tiles)

    part = payload.shape[0] // 2
    low, high = payload[:part], payload[part:]
    kept, sent = jnp.where(upper, high, low), jnp.where(upper, low, high)
    payload = kept + swap(sent.astype(narrow), "sx", 1).astype(wide)
    axes = ("dp", "sx")
    pairs = square_pairs(axes, (1, 2))
    payload = square_scatter(payload, axes, pairs, places, narrow)
    class_weight_grad = tree_sum(
        [part[width : width + classes, 0][:, None, None] * part[None, :width] for part in known]
    )
    totals = tree_sum([part[width:, 0] for part in known])
    class_bias_grad = totals[:classes]
    loss = totals[classes] / image_count
    for shift in doublings("dp", 2):
        payload = exchange(payload, "dp", shift, narrow)
    payload = exchange_all(payload, "sy", narrow).astype(narrow)
    payload, class_weight_grad, class_bias_grad, loss = together(
        (payload, class_weight_grad, class_bias_grad, loss)
    )
    payload = square_gather(payload, axes, pairs, places)
    weight_grad, depth_grad, depth_bias_grad, bias_grad = finish(
        flag, payload, swap(payload, "sx", 1), width
    )
    return (
        loss,
        depth_grad,
        depth_bias_grad,
        weight_grad,
        bias_grad,
        class_weight_grad,
        class_bias_grad,
    )


def solution(mesh):
    placed = (P("dp", "sy", "sx", None), P(), P(), P(), P(), P(), P(), P("dp"))
    return jax.shard_map(
        body,
        mesh=mesh,
        in_specs=placed,
        out_specs=(P(), P(), P(), P(), P(), P(), P()),
        check_vma=False,
    )
```

```python
import functools

import jax
import jax.numpy as jnp
from jax import lax
from jax.experimental import pallas as pl
from jax.experimental.pallas import tpu as pltpu
from jax.sharding import PartitionSpec as P

KERNEL = 7
HALF = KERNEL // 2
NEWTON_STEPS = 5
LANES = 128
GROUPS = 8
EDGE = 8
TAPS_ROWS = 64

epsilon = 1e-05
loss_scale = 64.0
narrow = jnp.bfloat16
wide = jnp.float32


def params(megabytes):
    return pltpu.CompilerParams(vmem_limit_bytes=megabytes * 1024 * 1024)


def swap(value, axis, shift):
    count = lax.axis_size(axis)
    return lax.ppermute(value, axis, [(i, i ^ shift) for i in range(count)])


def is_upper(axis, shift):
    return (lax.axis_index(axis) & shift) != 0


def tree_sum(terms):
    while len(terms) > 1:
        terms = [terms[i] + terms[i + 1] for i in range(0, len(terms), 2)]
    return terms[0]


def exchange(value, axis, shift, sent_as):
    sent = value.astype(sent_as)
    return sent.astype(wide) + swap(sent, axis, shift).astype(wide)


def exchange_all(value, axis, sent_as):
    sent = value.astype(sent_as)
    moved = [sent] + [swap(sent, axis, shift) for shift in range(1, lax.axis_size(axis))]
    return tree_sum([part.astype(wide) for part in moved])


def square_pairs(axes, shifts):
    counts = [lax.axis_size(axis) for axis in axes]
    return {
        2 * first + second: [
            (i * counts[1] + j, (i ^ (first * shifts[0])) * counts[1] + (j ^ (second * shifts[1])))
            for i in range(counts[0])
            for j in range(counts[1])
        ]
        for first, second in ((0, 1), (1, 0), (1, 1))
    }


def square_scatter(value, axes, pairs, places, sent_as):
    pieces = value.reshape((4, value.shape[0] // 4) + value.shape[1:])

    def piece(turn):
        starts = (places[turn],) + (0,) * value.ndim
        sizes = (1,) + pieces.shape[1:]
        return lax.dynamic_slice(pieces, starts, sizes, allow_negative_indices=False)[0]

    moved = [
        lax.ppermute(piece(turn).astype(sent_as), axes, pairs[turn]).astype(wide)
        for turn in (1, 2, 3)
    ]
    return tree_sum([piece(0)] + moved)


def square_gather(value, axes, pairs, places):
    whole = jnp.zeros((4,) + value.shape, value.dtype)
    for turn in range(4):
        part = lax.ppermute(value, axes, pairs[turn]) if turn else value
        starts = (places[turn],) + (0,) * value.ndim
        whole = lax.dynamic_update_slice(whole, part[None], starts, allow_negative_indices=False)
    return whole.reshape((-1,) + value.shape[1:])


def doublings(axis, first=1):
    found = []
    shift = first
    while shift < lax.axis_size(axis):
        found.append(shift)
        shift *= 2
    return found


def next_along(value, axis):
    return lax.ppermute(value, axis, [(i, i + 1) for i in range(lax.axis_size(axis) - 1)])


def back_along(value, axis):
    return lax.ppermute(value, axis, [(i + 1, i) for i in range(lax.axis_size(axis) - 1)])


def spread_columns(source, target):
    for group in range(target.shape[0]):
        target[group] = source[pl.ds(EDGE - HALF + group, GROUPS, stride=GROUPS), :]


def fill_row(wide_row, middle, left, right):
    cols = middle.shape[0]
    wide_row[EDGE : EDGE + cols, :] = middle.astype(wide)
    wide_row[EDGE - HALF : EDGE, :] = left.astype(wide)
    wide_row[EDGE + cols : EDGE + cols + HALF, :] = right.astype(wide)


def lanes_of(tile):
    return pl.ds(pl.multiple_of(tile * LANES, LANES), LANES)


def spread_weights(weight_ref, spread_ref, lanes):
    for row_tap in range(KERNEL):
        for col_tap in range(KERNEL):
            scale = weight_ref[row_tap, col_tap : col_tap + 1, lanes]
            spread_ref[row_tap * KERNEL + col_tap] = jnp.broadcast_to(scale, spread_ref.shape[1:])


def conv_rows(load, spread_ref, bias, steps, count):
    total = [[bias] * steps for _ in range(count)]
    for place in range(KERNEL + count - 1):
        windows = [load(place, group) for group in range(steps + KERNEL - 1)]
        for row in range(count):
            row_tap = place - row
            if not 0 <= row_tap < KERNEL:
                continue
            for col_tap in range(KERNEL):
                scale = spread_ref[row_tap * KERNEL + col_tap]
                for step in range(steps):
                    total[row][step] = total[row][step] + windows[step + col_tap] * scale
    return jnp.concatenate([part for row in total for part in row], axis=0).astype(narrow)


def reduce_part(conv_out, reduce_ref, reduce_bias_ref, before_out, feat_out):
    before = jnp.dot(conv_out[...], reduce_ref[...], preferred_element_type=wide)
    before = before + reduce_bias_ref[...]
    before_out[...] = before
    feat_out[...] = (before / (1.0 + jnp.exp(-before))).astype(narrow)
    feat = feat_out[...]
    gram = lax.dot_general(feat, feat, (((0,), (0,)), ((), ())), preferred_element_type=wide)
    return gram, jnp.sum(feat.astype(wide), axis=0, keepdims=True)


def inner_kernel(
    block, left, right, weight, bias, reduce_weight, reduce_bias,
    spread_out, conv_out, before_out, feat_out, gram_out, colsum_out,
    wide_row, spread_weight,
):
    rows, cols = block.shape[0], block.shape[1]
    steps = cols // GROUPS
    inner = rows - 2 * HALF
    at_once = 2 if inner % 2 == 0 else 1

    def one_tile(tile, _):
        lanes = lanes_of(tile)
        spread_weights(weight, spread_weight, lanes)
        start_value = jnp.broadcast_to(bias[0:1, lanes], (GROUPS, LANES))

        def fill(row, _):
            place = wide_row.at[row]
            fill_row(place, block[row, :, lanes], left[row, :, lanes], right[row, :, lanes])
            spread_columns(place, spread_out.at[tile, row])
            return 0

        lax.fori_loop(0, rows, fill, 0)

        def one_row(index, _):
            def load(row_tap, group):
                return spread_out[tile, index + row_tap, group]

            start = pl.multiple_of(index * cols, at_once * cols)
            conv_out[pl.ds(start, at_once * cols), lanes] = conv_rows(
                load, spread_weight, start_value, steps, at_once
            )
            return 0

        lax.fori_loop(0, inner // at_once, lambda turn, _: one_row(turn * at_once, 0), 0)
        return 0

    lax.fori_loop(0, spread_out.shape[0], one_tile, 0)
    gram_out[...], colsum_out[...] = reduce_part(
        conv_out, reduce_weight, reduce_bias, before_out, feat_out
    )


def edge_kernel(
    flag, spread_in, top, bottom, weight, bias, reduce_weight, reduce_bias, gram_in, colsum_in,
    spread_top, spread_bottom, conv_out, before_out, feat_out, kept_out, sent_out,
    wide_row, corners, spread_weight, sums,
):
    rows, cols = spread_in.shape[1], wide_row.shape[1] - 2 * EDGE
    steps = cols // GROUPS

    def one_tile(tile, _):
        lanes = lanes_of(tile)
        spread_weights(weight, spread_weight, lanes)
        start_value = jnp.broadcast_to(bias[0:1, lanes], (GROUPS, LANES))
        for side, (strip, spread) in enumerate(((top, spread_top), (bottom, spread_bottom))):
            corners[side] = strip[HALF * cols :, lanes].astype(wide)
            for row in range(HALF):
                place = wide_row.at[side * HALF + row]
                left = corners[side, row * HALF : (row + 1) * HALF, :]
                right = corners[side, (HALF + row) * HALF : (HALF + row + 1) * HALF, :]
                fill_row(place, strip[row * cols : (row + 1) * cols, lanes], left, right)
                spread_columns(place, spread.at[tile, row])

        def load_from(row):
            def load(row_tap, group):
                place = row + row_tap - HALF
                if place < 0:
                    return spread_top[tile, place + HALF, group]
                if place >= rows:
                    return spread_bottom[tile, place - rows, group]
                return spread_in[tile, place, group]

            return load

        for side, row in enumerate((0, rows - HALF)):
            start = side * HALF * cols
            conv_out[start : start + HALF * cols, lanes] = conv_rows(
                load_from(row), spread_weight, start_value, steps, HALF
            )
        return 0

    lax.fori_loop(0, spread_in.shape[0], one_tile, 0)
    gram, colsum = reduce_part(conv_out, reduce_weight, reduce_bias, before_out, feat_out)
    gram = gram + gram_in[...]
    colsum = colsum + colsum_in[...]
    width = gram.shape[0]
    half = width // 2
    quarter = half // 2
    sums[:half, :] = gram[:half, :]
    sums[half : half + quarter, :half] = gram[half : half + quarter, half:]
    sums[half : half + quarter, half:] = gram[half + quarter :, half:]
    sums[half + quarter :, :] = jnp.broadcast_to(
        colsum, (sums.shape[0] - half - quarter, width)
    )
    part = kept_out.shape[0]
    keep_or_send(flag[0] != 0, sums[:part, :], sums[part:, :], kept_out, sent_out)


def keep_or_send(upper, low, high, kept_out, sent_out):
    kept_out[...] = jnp.where(upper, high, low)
    sent_out[...] = jnp.where(upper, low, high).astype(sent_out.dtype)


def edge_rows(rows):
    return list(range(HALF)) + list(range(rows - HALF, rows))


def shape_of(shape, dtype=wide):
    return jax.ShapeDtypeStruct(shape, dtype)


in_vmem = pl.BlockSpec(memory_space=pltpu.VMEM)
in_smem = pl.BlockSpec(memory_space=pltpu.SMEM)


def cost(microseconds):
    return pl.CostEstimate(
        flops=microseconds * 10**9, bytes_accessed=microseconds * 10**6, transcendentals=0
    )


def conv_inner(block, left, right, weight, bias, reduce_weight, reduce_bias):
    rows, cols, channels = block.shape
    width = reduce_weight.shape[1]
    tiles = channels // LANES
    steps = cols // GROUPS
    pixels = (rows - 2 * HALF) * cols
    return pl.pallas_call(
        inner_kernel,
        in_specs=[in_vmem] * 7,
        out_specs=[in_vmem] * 6,
        out_shape=[
            shape_of((tiles, rows, steps + KERNEL - 1, GROUPS, LANES)),
            shape_of((pixels, channels), narrow),
            shape_of((pixels, width)),
            shape_of((pixels, width), narrow),
            shape_of((width, width)),
            shape_of((1, width)),
        ],
        scratch_shapes=[
            pltpu.VMEM((rows, cols + 2 * EDGE, LANES), wide),
            pltpu.VMEM((KERNEL * KERNEL, GROUPS, LANES), wide),
        ],
        compiler_params=params(24),
        cost_estimate=cost(10),
        name="conv_inner",
    )(block, left, right, weight, bias, reduce_weight, reduce_bias)


def conv_edge(flag, spread, top, bottom, weight, bias, reduce_weight, reduce_bias, gram, colsum):
    tiles, rows, groups = spread.shape[:3]
    cols, channels = (groups - KERNEL + 1) * GROUPS, top.shape[1]
    width = reduce_weight.shape[1]
    pixels = 2 * HALF * cols
    side = (tiles, HALF, groups, GROUPS, LANES)
    sums_rows = 3 * width // 4 + 2 * GROUPS
    return pl.pallas_call(
        edge_kernel,
        in_specs=[in_smem] + [in_vmem] * 9,
        out_specs=[in_vmem] * 7,
        out_shape=[
            shape_of(side),
            shape_of(side),
            shape_of((pixels, channels), narrow),
            shape_of((pixels, width)),
            shape_of((pixels, width), narrow),
            shape_of((sums_rows // 2, width)),
            shape_of((sums_rows // 2, width)),
        ],
        scratch_shapes=[
            pltpu.VMEM((2 * HALF, cols + 2 * EDGE, LANES), wide),
            pltpu.VMEM((2, top.shape[0] - HALF * cols, LANES), wide),
            pltpu.VMEM((KERNEL * KERNEL, GROUPS, LANES), wide),
            pltpu.VMEM((sums_rows, width), wide),
        ],
        compiler_params=params(24),
        cost_estimate=cost(6),
        name="conv_edge",
    )(flag, spread, top, bottom, weight, bias, reduce_weight, reduce_bias, gram, colsum)


def split(value):
    high = value.astype(narrow)
    return high, (value - high.astype(wide)).astype(narrow)


def product(left, right):
    def dot(a, b):
        return jnp.dot(a, b, preferred_element_type=wide)

    return dot(left[0], right[0]) + (dot(left[0], right[1]) + dot(left[1], right[0]))


def square_root(current):
    size = current.shape[0]
    row = lax.broadcasted_iota(jnp.int32, (size, size), 0)
    col = lax.broadcasted_iota(jnp.int32, (size, size), 1)
    triple = jnp.where(row == col, 3.0, 0.0)
    factor = split(0.5 * (triple - current))
    current = split(current)
    trail = [(current, None, factor)]
    inverse = factor
    current = split(product(current, factor))
    for step in range(1, NEWTON_STEPS):
        factor = split(0.5 * (triple - product(inverse, current)))
        trail.append((current, inverse, factor))
        last = step == NEWTON_STEPS - 1
        if not last:
            inverse = split(product(factor, inverse))
        current = product(current, factor)
        if not last:
            current = split(current)
    return current, trail


def square_root_change(change, trail):
    first, _, factor = trail[0]
    move = split(change)
    factor_move = split(-0.5 * change)
    change = product(move, factor) + product(first, factor_move)
    inverse_move = factor_move
    for step in range(1, NEWTON_STEPS):
        current, inverse, factor = trail[step]
        move = split(change)
        factor_move = split(
            -0.5 * (product(inverse_move, current) + product(inverse, move))
        )
        change = product(move, factor) + product(current, factor_move)
        if step < NEWTON_STEPS - 1:
            inverse_move = split(product(factor_move, inverse) + product(factor, inverse_move))
    return change


def head_kernel(
    flag, label, class_bias, own, other, class_weight,
    feat_inner, feat_edge, gate_inner, gate_edge, conv_turned, reduce_turned,
    root_out, payload, conv_inner_out, conv_edge_out,
    sums, pre, *, count, image_count,
):
    width = root_out.shape[1]
    half = width // 2
    quarter = half // 2
    rows = own.shape[0]
    upper = flag[0] != 0
    mine, theirs = own[...], other[...]
    sums[:rows, :] = jnp.where(upper, theirs, mine)
    sums[rows:, :] = jnp.where(upper, mine, theirs)
    low = jnp.concatenate(
        [sums[half : half + quarter, :half], sums[half : half + quarter, half:]], axis=0
    )
    cross = sums[:half, half:]
    gram = jnp.concatenate(
        [sums[:half, :], jnp.concatenate([cross.T, low], axis=1)], axis=0
    )
    mean_row = sums[half + quarter : half + quarter + 1, :] / count
    mean_col = jnp.broadcast_to(mean_row, (width, width)).T
    sigma = gram / count - mean_col * mean_row
    row = lax.broadcasted_iota(jnp.int32, (width, width), 0)
    col = lax.broadcasted_iota(jnp.int32, (width, width), 1)
    diagonal = row == col
    trace_value = jnp.sum(jnp.where(diagonal, sigma, 0.0), keepdims=True) + epsilon
    root_scale = jnp.sqrt(trace_value)
    unit, trail = square_root(sigma / trace_value)
    root = root_scale * unit
    root_out[:width, :] = root

    classes = class_weight.shape[0]
    slots = root_out.shape[0] - width
    place = lax.broadcasted_iota(jnp.int32, (slots, 1), 0)
    bias = jnp.zeros((slots, 1), wide)
    for index in range(classes):
        bias = jnp.where(place == index, class_bias[index], bias)
    partial = [
        jnp.sum(class_weight[index].astype(wide) * root, axis=0, keepdims=True)
        for index in range(classes)
    ]
    partial.append(jnp.zeros((slots - classes, width), wide))
    logits = jnp.sum(jnp.concatenate(partial, axis=0), axis=1, keepdims=True) + bias
    onehot = jnp.where(place == label[0], 1.0, 0.0)
    soft = jnp.maximum(logits, 0.0) + jnp.log(1.0 + jnp.exp(-jnp.abs(logits)))
    share = 1.0 / (1.0 + jnp.exp(-logits))
    used = place < classes
    loss_part = jnp.sum(jnp.where(used, soft - onehot * logits, 0.0), keepdims=True)
    logit_grad = jnp.where(used, loss_scale * (share - onehot) / image_count, 0.0)
    root_out[width:, :] = jnp.broadcast_to(
        jnp.where(place == classes, loss_part, logit_grad), (slots, width)
    )

    root_grad = jnp.zeros((width, width), wide)
    for index in range(classes):
        root_grad = root_grad + class_weight[index].astype(wide) * logit_grad[index : index + 1, :]
    root_grad = root_grad + root_grad.T
    change = square_root_change(root_scale * root_grad, trail)
    trace_grad = jnp.sum(root_grad * unit, keepdims=True) / (2.0 * root_scale) - jnp.sum(
        change * sigma, keepdims=True
    ) / (trace_value * trace_value)
    symmetric = (
        (change / trace_value + jnp.where(diagonal, trace_grad, 0.0)) / count
    ).astype(narrow)
    mean_term = jnp.sum(mean_col * symmetric.astype(wide), axis=0, keepdims=True)

    inner = feat_inner.shape[0]
    for feat, gate, start in ((feat_inner, gate_inner, 0), (feat_edge, gate_edge, inner)):
        grad = jnp.dot(feat[...], symmetric, preferred_element_type=wide) - mean_term
        pre[start : start + feat.shape[0], :] = (grad * gate[...]).astype(narrow)
    pre_grad = pre[...]
    payload[width:, :] = jnp.zeros((payload.shape[0] - width, payload.shape[1]), wide)
    taps = KERNEL * KERNEL
    payload[width + taps + 1 : width + taps + 2, :width] = jnp.sum(
        pre_grad.astype(wide), axis=0, keepdims=True
    )
    for first in range(0, conv_turned.shape[0], width):
        payload[:width, first : first + width] = jnp.dot(
            conv_turned[first : first + width, :], pre_grad, preferred_element_type=wide
        )
    for out, start in ((conv_inner_out, 0), (conv_edge_out, inner)):
        out[...] = jnp.dot(
            pre[start : start + out.shape[0], :], reduce_turned[...], preferred_element_type=wide
        ).astype(narrow)


def head(flag, label, class_bias, own, other, class_weight, prepared, count, image_count):
    feat_inner, feat_edge, gate_inner, gate_edge, conv_turned, reduce_turned = prepared
    width, channels = reduce_turned.shape
    inner, edge = feat_inner.shape[0], feat_edge.shape[0]
    slots = -(-(class_weight.shape[0] + 1) // GROUPS) * GROUPS
    return pl.pallas_call(
        functools.partial(head_kernel, count=count, image_count=image_count),
        in_specs=[in_smem] * 3 + [in_vmem] * 9,
        out_specs=[in_vmem] * 4,
        out_shape=[
            shape_of((width + slots, width)),
            shape_of((width + TAPS_ROWS, channels)),
            shape_of((inner, channels), narrow),
            shape_of((edge, channels), narrow),
        ],
        scratch_shapes=[
            pltpu.VMEM((2 * own.shape[0], width), wide),
            pltpu.VMEM((inner + edge, width), narrow),
        ],
        compiler_params=params(24),
        cost_estimate=cost(10),
        name="head",
    )(
        flag, label, class_bias, own, other, class_weight,
        feat_inner, feat_edge, gate_inner, gate_edge, conv_turned, reduce_turned,
    )


def prepare_kernel(
    before_inner, before_edge, conv_inner_in, conv_edge_in, reduce_weight,
    gate_inner, gate_edge, conv_turned, reduce_turned,
):
    for before, gate in ((before_inner, gate_inner), (before_edge, gate_edge)):
        value = before[...]
        share = 1.0 / (1.0 + jnp.exp(-value))
        gate[...] = share * (1.0 + value * (1.0 - share))
    inner = conv_inner_in.shape[0]
    conv_turned[:, :inner] = conv_inner_in[...].T
    conv_turned[:, inner:] = conv_edge_in[...].T
    reduce_turned[...] = reduce_weight[...].T


def prepare(before_inner, before_edge, conv_in, conv_ed, reduce_weight):
    channels, width = reduce_weight.shape
    inner, edge = before_inner.shape[0], before_edge.shape[0]
    return pl.pallas_call(
        prepare_kernel,
        in_specs=[in_vmem] * 5,
        out_specs=[in_vmem] * 4,
        out_shape=[
            shape_of((inner, width)),
            shape_of((edge, width)),
            shape_of((channels, inner + edge), narrow),
            shape_of((width, channels), narrow),
        ],
        compiler_params=params(16),
        cost_estimate=cost(1),
        name="prepare",
    )(before_inner, before_edge, conv_in, conv_ed, reduce_weight)


def taps_kernel(
    spread_in, spread_top, spread_bottom, grad_inner, grad_edge, payload_in, payload, grads, out, *,
    first, last,
):
    rows = spread_in.shape[1]
    steps = grads.shape[1]
    cols = steps * GROUPS
    order = edge_rows(rows)
    taps = KERNEL * KERNEL
    base = payload.shape[0] - TAPS_ROWS

    def one_tile(tile, _):
        lanes = lanes_of(tile)

        for row in range(rows):
            if row in order:
                source, place = grad_edge, order.index(row)
            else:
                source, place = grad_inner, row - HALF
            values = source[place * cols : (place + 1) * cols, lanes].astype(wide)
            for step in range(steps):
                grads[row, step] = values[step * GROUPS : (step + 1) * GROUPS, :]

        def load(place, group):
            if place < 0:
                return spread_top[tile, place + HALF, group]
            if place >= rows:
                return spread_bottom[tile, place - rows, group]
            return spread_in[tile, place, group]

        for begin in range(0, KERNEL, 2):
            row_taps = [tap for tap in (begin, begin + 1) if tap < KERNEL]
            total = {
                (row_tap, col_tap): jnp.zeros((GROUPS, LANES), wide)
                for row_tap in row_taps
                for col_tap in range(KERNEL)
            }
            for place in range(begin - HALF, rows + row_taps[-1] - HALF):
                windows = [load(place, group) for group in range(steps + KERNEL - 1)]
                for row_tap in row_taps:
                    row = place - row_tap + HALF
                    if not 0 <= row < rows:
                        continue
                    for step in range(steps):
                        grad = grads[row, step]
                        for col_tap in range(KERNEL):
                            total[row_tap, col_tap] += windows[step + col_tap] * grad
            for (row_tap, col_tap), value in total.items():
                tap = row_tap * KERNEL + col_tap
                out[tap : tap + 1, :] = jnp.sum(value, axis=0, keepdims=True)
        total = [jnp.zeros((GROUPS, LANES), wide) for _ in range(KERNEL)]
        for index in range(rows * steps):
            slot = index % KERNEL
            total[slot] = total[slot] + grads[index // steps, index % steps]
        out[taps : taps + 1, :] = jnp.sum(sum(total), axis=0, keepdims=True)
        payload[pl.ds(base, taps + 1), lanes] = out[: taps + 1, :]
        return 0

    lax.fori_loop(first, last, one_tile, 0)


def tap_grads(spreads, grads, payload, first, last):
    rows, groups = spreads[0].shape[1:3]
    steps = groups - KERNEL + 1
    return pl.pallas_call(
        functools.partial(taps_kernel, first=first, last=last),
        in_specs=[in_vmem] * 6,
        out_specs=in_vmem,
        out_shape=shape_of(payload.shape),
        input_output_aliases={5: 0},
        scratch_shapes=[
            pltpu.VMEM((rows, steps, GROUPS, LANES), wide),
            pltpu.VMEM((TAPS_ROWS, LANES), wide),
        ],
        compiler_params=params(16),
        cost_estimate=cost(2 * (last - first)),
        name="tap_grads",
    )(*spreads, *grads, payload)


def finish_kernel(
    flag, own, other, weight_out, depth_out, depth_bias_out, bias_out, payload,
):
    part = own.shape[0]
    upper = flag[0] != 0
    mine, theirs = own[...].astype(wide), other[...].astype(wide)
    payload[:part, :] = jnp.where(upper, theirs, mine)
    payload[part:, :] = jnp.where(upper, mine, theirs)
    width = weight_out.shape[1]
    for first in range(0, weight_out.shape[0], width):
        weight_out[first : first + width, :] = payload[:width, first : first + width]
    for row_tap in range(KERNEL):
        start = width + row_tap * KERNEL
        depth_out[row_tap] = payload[start : start + KERNEL, :]
    taps = KERNEL * KERNEL
    depth_bias_out[...] = payload[width + taps, :]
    bias_out[...] = payload[width + taps + 1, :width]


def finish(flag, own, other, width):
    part, channels = own.shape
    return pl.pallas_call(
        finish_kernel,
        in_specs=[in_smem] + [in_vmem] * 2,
        out_specs=[in_vmem] * 4,
        out_shape=[
            shape_of((channels, width)),
            shape_of((KERNEL, KERNEL, channels)),
            shape_of((channels,)),
            shape_of((width,)),
        ],
        scratch_shapes=[pltpu.VMEM((2 * part, channels), wide)],
        compiler_params=params(8),
        cost_estimate=cost(1),
        name="finish",
    )(flag, own, other)


def edge_strip(block, left, right, rows):
    channels = block.shape[2]
    parts = [part[rows].reshape(-1, channels) for part in (block, left, right)]
    short = -(2 * HALF * HALF) % 16
    return jnp.concatenate(parts + [jnp.zeros((short, channels), block.dtype)])


def body(
    features, depth_weight, depth_bias, reduce_weight, reduce_bias, class_weight, class_bias, labels
):
    together = lax.optimization_barrier
    block = features[0]
    rows, cols, channels = block.shape
    width = reduce_weight.shape[1]
    classes = class_bias.shape[0]
    count = rows * cols * lax.axis_size("sy") * lax.axis_size("sx")
    image_count = features.shape[0] * lax.axis_size("dp")

    flag = is_upper("sx", 1).astype(jnp.int32)[None]
    upper = is_upper("sx", 1)
    corner = 2 * (lax.axis_index("dp") & 1) + ((lax.axis_index("sx") & 2) >> 1)
    places = [corner ^ turn for turn in range(4)]
    bias_row = depth_bias[None]
    reduce_row = reduce_bias[None]
    left = next_along(block[:, cols - HALF :], "sx")
    right = back_along(block[:, :HALF], "sx")
    low, high, left, right, flag, upper, places, bias_row, reduce_row = together(
        (
            edge_strip(block, left, right, slice(rows - HALF, rows)),
            edge_strip(block, left, right, slice(0, HALF)),
            left,
            right,
            flag,
            upper,
            places,
            bias_row,
            reduce_row,
        )
    )
    top = next_along(low, "sy")
    bottom = back_along(high, "sy")
    spread, conv_in, before_in, feat_in, gram, colsum = conv_inner(
        block, left, right, depth_weight, bias_row, reduce_weight, reduce_row
    )
    spread_top, spread_bottom, conv_ed, before_ed, feat_ed, kept, sent = conv_edge(
        flag, spread, top, bottom, depth_weight, bias_row, reduce_weight, reduce_row, gram, colsum
    )

    sums = kept + swap(sent, "sx", 1)
    sums, before_in, before_ed, conv_in, conv_ed = together(
        (sums, before_in, before_ed, conv_in, conv_ed)
    )
    gate_in, gate_ed, conv_turned, reduce_turned = prepare(
        before_in, before_ed, conv_in, conv_ed, reduce_weight
    )
    for shift in doublings("sx", 2):
        sums = exchange(sums, "sx", shift, wide)
    sums, gate_in, gate_ed, conv_turned, reduce_turned = together(
        (sums, gate_in, gate_ed, conv_turned, reduce_turned)
    )
    for shift in doublings("sy"):
        sums = exchange(sums, "sy", shift, wide)
    other = swap(sums, "sx", 1)

    root, payload, *grads = head(
        flag,
        labels,
        class_bias,
        sums,
        other,
        class_weight,
        (feat_in, feat_ed, gate_in, gate_ed, conv_turned, reduce_turned),
        count,
        image_count,
    )
    known = [root] + [swap(root, "dp", shift) for shift in range(1, lax.axis_size("dp"))]
    spreads = (spread, spread_top, spread_bottom)
    tiles = channels // LANES
    payload = tap_grads(spreads, grads, payload, 0, tiles // 2)
    payload, known = together((payload, known))
    payload = tap_grads(spreads, grads, payload, tiles // 2, tiles)

    part = payload.shape[0] // 2
    low, high = payload[:part], payload[part:]
    kept, sent = jnp.where(upper, high, low), jnp.where(upper, low, high)
    payload = kept + swap(sent.astype(narrow), "sx", 1).astype(wide)
    axes = ("dp", "sx")
    pairs = square_pairs(axes, (1, 2))
    payload = square_scatter(payload, axes, pairs, places, narrow)
    payload, known = together((payload, known))
    class_weight_grad = tree_sum(
        [part[width : width + classes, 0][:, None, None] * part[None, :width] for part in known]
    )
    totals = tree_sum([part[width:, 0] for part in known])
    class_bias_grad = totals[:classes]
    loss = totals[classes] / image_count
    for shift in doublings("dp", 2):
        payload = exchange(payload, "dp", shift, narrow)
    payload = exchange_all(payload, "sy", narrow).astype(narrow)
    payload, class_weight_grad, class_bias_grad, loss = together(
        (payload, class_weight_grad, class_bias_grad, loss)
    )
    payload = square_gather(payload, axes, pairs, places)
    weight_grad, depth_grad, depth_bias_grad, bias_grad = finish(
        flag, payload, swap(payload, "sx", 1), width
    )
    return (
        loss,
        depth_grad,
        depth_bias_grad,
        weight_grad,
        bias_grad,
        class_weight_grad,
        class_bias_grad,
    )


def solution(mesh):
    placed = (P("dp", "sy", "sx", None), P(), P(), P(), P(), P(), P(), P("dp"))
    return jax.shard_map(
        body,
        mesh=mesh,
        in_specs=placed,
        out_specs=(P(), P(), P(), P(), P(), P(), P()),
        check_vma=False,
    )
```

```python
import functools

import jax
import jax.numpy as jnp
from jax import lax
from jax.experimental import pallas as pl
from jax.experimental.pallas import tpu as pltpu
from jax.sharding import PartitionSpec as P

KERNEL = 7
HALF = KERNEL // 2
NEWTON_STEPS = 5
LANES = 128
GROUPS = 8
EDGE = 8
TAPS_ROWS = 64
SIDE = 4
FILL_ROWS = 4
PARTS = (4, 3, 4)

epsilon = 1e-05
loss_scale = 64.0
narrow = jnp.bfloat16
wide = jnp.float32


def params(megabytes):
    return pltpu.CompilerParams(vmem_limit_bytes=megabytes * 1024 * 1024)


def swap(value, axis, shift):
    count = lax.axis_size(axis)
    return lax.ppermute(value, axis, [(i, i ^ shift) for i in range(count)])


def is_upper(axis, shift):
    return (lax.axis_index(axis) & shift) != 0


def tree_sum(terms):
    while len(terms) > 1:
        terms = [terms[i] + terms[i + 1] for i in range(0, len(terms), 2)]
    return terms[0]


def exchange(value, axis, shift, sent_as):
    sent = value.astype(sent_as)
    return sent.astype(wide) + swap(sent, axis, shift).astype(wide)


def exchange_all(value, axis, sent_as):
    sent = value.astype(sent_as)
    moved = [sent] + [swap(sent, axis, shift) for shift in range(1, lax.axis_size(axis))]
    return tree_sum([part.astype(wide) for part in moved])


def square_pairs(axes, shifts):
    counts = [lax.axis_size(axis) for axis in axes]
    return {
        2 * first + second: [
            (i * counts[1] + j, (i ^ (first * shifts[0])) * counts[1] + (j ^ (second * shifts[1])))
            for i in range(counts[0])
            for j in range(counts[1])
        ]
        for first, second in ((0, 1), (1, 0), (1, 1))
    }


def square_scatter(value, axes, pairs, places, sent_as):
    pieces = value.reshape((4, value.shape[0] // 4) + value.shape[1:])

    def piece(turn):
        starts = (places[turn],) + (0,) * value.ndim
        sizes = (1,) + pieces.shape[1:]
        return lax.dynamic_slice(pieces, starts, sizes, allow_negative_indices=False)[0]

    moved = [
        lax.ppermute(piece(turn).astype(sent_as), axes, pairs[turn]).astype(wide)
        for turn in (1, 2, 3)
    ]
    return tree_sum([piece(0)] + moved)


def square_gather(value, axes, pairs, places):
    whole = jnp.zeros((4,) + value.shape, value.dtype)
    for turn in range(4):
        part = lax.ppermute(value, axes, pairs[turn]) if turn else value
        starts = (places[turn],) + (0,) * value.ndim
        whole = lax.dynamic_update_slice(whole, part[None], starts, allow_negative_indices=False)
    return whole.reshape((-1,) + value.shape[1:])


def doublings(axis, first=1):
    found = []
    shift = first
    while shift < lax.axis_size(axis):
        found.append(shift)
        shift *= 2
    return found


def next_along(value, axis):
    return lax.ppermute(value, axis, [(i, i + 1) for i in range(lax.axis_size(axis) - 1)])


def back_along(value, axis):
    return lax.ppermute(value, axis, [(i + 1, i) for i in range(lax.axis_size(axis) - 1)])


def spread_columns(source, target):
    for group in range(target.shape[0]):
        target[group] = source[pl.ds(EDGE - HALF + group, GROUPS, stride=GROUPS), :]


def fill_row(wide_row, middle, left, right):
    cols = middle.shape[0]
    wide_row[EDGE : EDGE + cols, :] = middle.astype(wide)
    wide_row[EDGE - HALF : EDGE, :] = left.astype(wide)
    wide_row[EDGE + cols : EDGE + cols + HALF, :] = right.astype(wide)


def lanes_of(tile):
    return pl.ds(pl.multiple_of(tile * LANES, LANES), LANES)


def part_starts():
    starts, total = {}, 0
    for row_part in range(3):
        for col_part in range(3):
            starts[row_part, col_part] = total
            total += PARTS[row_part] * PARTS[col_part]
    return starts, total


FILTERS, PRODUCTS = part_starts()


def part_taps(taps):
    even, odd = taps[0::2], taps[1::2]
    both = [a + b for a, b in zip(even, odd)] + even[len(odd) :]
    return even, odd, both


def spread_weights(weight_ref, filters, lanes):
    rows = []
    for row_tap in range(KERNEL):
        row = [weight_ref[row_tap, tap : tap + 1, lanes] for tap in range(KERNEL)]
        rows.append([jnp.broadcast_to(tap, (GROUPS, LANES)) for tap in row])
    columns = [part_taps([rows[tap][col] for tap in range(KERNEL)]) for col in range(KERNEL)]
    for row_part, many in enumerate(PARTS):
        for row in range(many):
            line = [columns[col][row_part][row] for col in range(KERNEL)]
            for col_part, taps in enumerate(part_taps(line)):
                start = FILTERS[row_part, col_part] + row * PARTS[col_part]
                for col, value in enumerate(taps):
                    filters[start + col] = value


def fill_parts(load, parts, row_pairs, groups):
    for pair in range(row_pairs):
        for group in range(groups):
            middle = load(2 * pair + 1, group)
            parts[0, pair, group] = load(2 * pair, group) - middle
            if pair < row_pairs - 1:
                parts[1, pair, group] = load(2 * pair + 2, group) - middle


def part_line(load, parts, row_part, col_part, pair, many):
    def value(group):
        return load(2 * pair + 1, group) if row_part == 2 else parts[row_part, pair, group]

    first = (0, 2, 1)[col_part]
    line = [value(2 * col + first) for col in range(many)]
    if col_part < 2:
        line = [side - value(2 * col + 1) for col, side in enumerate(line)]
    return line


def conv_rows(load, filters, bias, steps, count, parts, products):
    row_pairs, col_pairs = count // 2, steps // 2
    fill_parts(load, parts, row_pairs + 3, 2 * col_pairs + 6)
    for row_part in range(3):
        for col_part in range(3):
            start = FILTERS[row_part, col_part]
            many_rows, many_cols = PARTS[row_part], PARTS[col_part]
            total = [[None] * col_pairs for _ in range(row_pairs)]
            for place in range(row_pairs + many_rows - 1):
                line = part_line(
                    load, parts, row_part, col_part, place, col_pairs + many_cols - 1
                )
                for row in range(row_pairs):
                    tap_row = place - row
                    if not 0 <= tap_row < many_rows:
                        continue
                    for tap_col in range(many_cols):
                        scale = filters[start + tap_row * many_cols + tap_col]
                        for col in range(col_pairs):
                            term = line[col + tap_col] * scale
                            old = total[row][col]
                            total[row][col] = term if old is None else old + term
            for row in range(row_pairs):
                for col in range(col_pairs):
                    products[3 * row_part + col_part, row, col] = total[row][col]
    found = []
    for row in range(row_pairs):
        lines = [[], []]
        for col in range(col_pairs):
            values = [products[part, row, col] for part in range(9)]
            shared = [values[6] + values[8] + bias, values[7] + values[8] + bias]
            for row_part in range(2):
                for col_part in range(2):
                    own = values[3 * row_part + col_part] + values[3 * row_part + 2]
                    lines[row_part].append(own + shared[col_part])
        found += lines[0] + lines[1]
    return jnp.concatenate(found, axis=0).astype(narrow)


def parts_scratch(count, steps):
    row_pairs, col_pairs = count // 2, steps // 2
    return [
        pltpu.VMEM((PRODUCTS, GROUPS, LANES), wide),
        pltpu.VMEM((2, row_pairs + 3, 2 * col_pairs + 6, GROUPS, LANES), wide),
        pltpu.VMEM((9, row_pairs, col_pairs, GROUPS, LANES), wide),
    ]


def reduce_part(conv_out, reduce_ref, reduce_bias_ref, before_out, feat_out):
    before = jnp.dot(conv_out[...], reduce_ref[...], preferred_element_type=wide)
    before = before + reduce_bias_ref[...]
    before_out[...] = before
    feat_out[...] = (before / (1.0 + jnp.exp(-before))).astype(narrow)
    feat = feat_out[...]
    gram = lax.dot_general(feat, feat, (((0,), (0,)), ((), ())), preferred_element_type=wide)
    return gram, jnp.sum(feat.astype(wide), axis=0, keepdims=True)


def inner_kernel(
    block, left, right, weight, bias, reduce_weight, reduce_bias,
    spread_out, conv_out, before_out, feat_out, gram_out, colsum_out,
    wide_row, filters, parts, products,
):
    rows, cols = block.shape[0], block.shape[1]
    steps = cols // GROUPS

    def one_tile(tile, _):
        lanes = lanes_of(tile)
        spread_weights(weight, filters, lanes)
        start_value = jnp.broadcast_to(bias[0:1, lanes], (GROUPS, LANES))

        def fill(turn, _):
            for row in range(FILL_ROWS):
                row = turn * FILL_ROWS + row
                place = wide_row.at[row]
                fill_row(place, block[row, :, lanes], left[row, :, lanes], right[row, :, lanes])
                spread_columns(place, spread_out.at[tile, row])
            return 0

        lax.fori_loop(0, rows // FILL_ROWS, fill, 0)

        def load(row, group):
            return spread_out[tile, row + SIDE - HALF, group]

        conv_out[:, lanes] = conv_rows(
            load, filters, start_value, steps, rows - 2 * SIDE, parts, products
        )
        return 0

    lax.fori_loop(0, spread_out.shape[0], one_tile, 0)
    gram_out[...], colsum_out[...] = reduce_part(
        conv_out, reduce_weight, reduce_bias, before_out, feat_out
    )


def edge_kernel(
    flag, spread_in, top, bottom, weight, bias, reduce_weight, reduce_bias, gram_in, colsum_in,
    spread_top, spread_bottom, conv_out, before_out, feat_out, kept_out, sent_out,
    wide_row, corners, filters, parts, products, sums,
):
    rows, cols = spread_in.shape[1], wide_row.shape[1] - 2 * EDGE
    steps = cols // GROUPS

    def one_tile(tile, _):
        lanes = lanes_of(tile)
        spread_weights(weight, filters, lanes)
        start_value = jnp.broadcast_to(bias[0:1, lanes], (GROUPS, LANES))
        for side, (strip, spread) in enumerate(((top, spread_top), (bottom, spread_bottom))):
            corners[side] = strip[HALF * cols :, lanes].astype(wide)
            for row in range(HALF):
                place = wide_row.at[side * HALF + row]
                left = corners[side, row * HALF : (row + 1) * HALF, :]
                right = corners[side, (HALF + row) * HALF : (HALF + row + 1) * HALF, :]
                fill_row(place, strip[row * cols : (row + 1) * cols, lanes], left, right)
                spread_columns(place, spread.at[tile, row])

        def load_from(row):
            def load(row_tap, group):
                place = row + row_tap - HALF
                if place < 0:
                    return spread_top[tile, place + HALF, group]
                if place >= rows:
                    return spread_bottom[tile, place - rows, group]
                return spread_in[tile, place, group]

            return load

        for side, row in enumerate((0, rows - SIDE)):
            start = side * SIDE * cols
            conv_out[start : start + SIDE * cols, lanes] = conv_rows(
                load_from(row), filters, start_value, steps, SIDE, parts.at[side], products.at[side]
            )
        return 0

    lax.fori_loop(0, spread_in.shape[0], one_tile, 0)
    gram, colsum = reduce_part(conv_out, reduce_weight, reduce_bias, before_out, feat_out)
    gram = gram + gram_in[...]
    colsum = colsum + colsum_in[...]
    width = gram.shape[0]
    half = width // 2
    quarter = half // 2
    sums[:half, :] = gram[:half, :]
    sums[half : half + quarter, :half] = gram[half : half + quarter, half:]
    sums[half : half + quarter, half:] = gram[half + quarter :, half:]
    sums[half + quarter :, :] = jnp.broadcast_to(
        colsum, (sums.shape[0] - half - quarter, width)
    )
    part = kept_out.shape[0]
    keep_or_send(flag[0] != 0, sums[:part, :], sums[part:, :], kept_out, sent_out)


def keep_or_send(upper, low, high, kept_out, sent_out):
    kept_out[...] = jnp.where(upper, high, low)
    sent_out[...] = jnp.where(upper, low, high).astype(sent_out.dtype)


def edge_rows(rows):
    return list(range(SIDE)) + list(range(rows - SIDE, rows))


def shape_of(shape, dtype=wide):
    return jax.ShapeDtypeStruct(shape, dtype)


in_vmem = pl.BlockSpec(memory_space=pltpu.VMEM)
in_smem = pl.BlockSpec(memory_space=pltpu.SMEM)


def cost(microseconds):
    return pl.CostEstimate(
        flops=microseconds * 10**9, bytes_accessed=microseconds * 10**6, transcendentals=0
    )


def conv_inner(block, left, right, weight, bias, reduce_weight, reduce_bias):
    rows, cols, channels = block.shape
    width = reduce_weight.shape[1]
    tiles = channels // LANES
    steps = cols // GROUPS
    pixels = (rows - 2 * SIDE) * cols
    return pl.pallas_call(
        inner_kernel,
        in_specs=[in_vmem] * 7,
        out_specs=[in_vmem] * 6,
        out_shape=[
            shape_of((tiles, rows, steps + KERNEL - 1, GROUPS, LANES)),
            shape_of((pixels, channels), narrow),
            shape_of((pixels, width)),
            shape_of((pixels, width), narrow),
            shape_of((width, width)),
            shape_of((1, width)),
        ],
        scratch_shapes=[
            pltpu.VMEM((rows, cols + 2 * EDGE, LANES), wide),
            *parts_scratch(rows - 2 * SIDE, steps),
        ],
        compiler_params=params(24),
        cost_estimate=cost(10),
        name="conv_inner",
    )(block, left, right, weight, bias, reduce_weight, reduce_bias)


def conv_edge(flag, spread, top, bottom, weight, bias, reduce_weight, reduce_bias, gram, colsum):
    tiles, rows, groups = spread.shape[:3]
    cols, channels = (groups - KERNEL + 1) * GROUPS, top.shape[1]
    width = reduce_weight.shape[1]
    pixels = 2 * SIDE * cols
    filters, parts, products = parts_scratch(SIDE, cols // GROUPS)
    side = (tiles, HALF, groups, GROUPS, LANES)
    sums_rows = 3 * width // 4 + 2 * GROUPS
    return pl.pallas_call(
        edge_kernel,
        in_specs=[in_smem] + [in_vmem] * 9,
        out_specs=[in_vmem] * 7,
        out_shape=[
            shape_of(side),
            shape_of(side),
            shape_of((pixels, channels), narrow),
            shape_of((pixels, width)),
            shape_of((pixels, width), narrow),
            shape_of((sums_rows // 2, width)),
            shape_of((sums_rows // 2, width)),
        ],
        scratch_shapes=[
            pltpu.VMEM((2 * HALF, cols + 2 * EDGE, LANES), wide),
            pltpu.VMEM((2, top.shape[0] - HALF * cols, LANES), wide),
            filters,
            pltpu.VMEM((2,) + parts.shape, wide),
            pltpu.VMEM((2,) + products.shape, wide),
            pltpu.VMEM((sums_rows, width), wide),
        ],
        compiler_params=params(24),
        cost_estimate=cost(6),
        name="conv_edge",
    )(flag, spread, top, bottom, weight, bias, reduce_weight, reduce_bias, gram, colsum)


def split(value):
    high = value.astype(narrow)
    return high, (value - high.astype(wide)).astype(narrow)


def product(left, right):
    def dot(a, b):
        return jnp.dot(a, b, preferred_element_type=wide)

    return dot(left[0], right[0]) + (dot(left[0], right[1]) + dot(left[1], right[0]))


def square_root(current):
    size = current.shape[0]
    row = lax.broadcasted_iota(jnp.int32, (size, size), 0)
    col = lax.broadcasted_iota(jnp.int32, (size, size), 1)
    triple = jnp.where(row == col, 3.0, 0.0)
    factor = split(0.5 * (triple - current))
    current = split(current)
    trail = [(current, None, factor)]
    inverse = factor
    current = split(product(current, factor))
    for step in range(1, NEWTON_STEPS):
        factor = split(0.5 * (triple - product(inverse, current)))
        trail.append((current, inverse, factor))
        last = step == NEWTON_STEPS - 1
        if not last:
            inverse = split(product(factor, inverse))
        current = product(current, factor)
        if not last:
            current = split(current)
    return current, trail


def square_root_change(change, trail):
    first, _, factor = trail[0]
    move = split(change)
    factor_move = split(-0.5 * change)
    change = product(move, factor) + product(first, factor_move)
    inverse_move = factor_move
    for step in range(1, NEWTON_STEPS):
        current, inverse, factor = trail[step]
        move = split(change)
        factor_move = split(
            -0.5 * (product(inverse_move, current) + product(inverse, move))
        )
        change = product(move, factor) + product(current, factor_move)
        if step < NEWTON_STEPS - 1:
            inverse_move = split(product(factor_move, inverse) + product(factor, inverse_move))
    return change


def head_kernel(
    flag, label, class_bias, own, other, class_weight,
    feat_inner, feat_edge, gate_inner, gate_edge, conv_turned, reduce_turned,
    root_out, payload, conv_inner_out, conv_edge_out,
    sums, pre, *, count, image_count,
):
    width = root_out.shape[1]
    half = width // 2
    quarter = half // 2
    rows = own.shape[0]
    upper = flag[0] != 0
    mine, theirs = own[...], other[...]
    sums[:rows, :] = jnp.where(upper, theirs, mine)
    sums[rows:, :] = jnp.where(upper, mine, theirs)
    low = jnp.concatenate(
        [sums[half : half + quarter, :half], sums[half : half + quarter, half:]], axis=0
    )
    cross = sums[:half, half:]
    gram = jnp.concatenate(
        [sums[:half, :], jnp.concatenate([cross.T, low], axis=1)], axis=0
    )
    mean_row = sums[half + quarter : half + quarter + 1, :] / count
    mean_col = jnp.broadcast_to(mean_row, (width, width)).T
    sigma = gram / count - mean_col * mean_row
    row = lax.broadcasted_iota(jnp.int32, (width, width), 0)
    col = lax.broadcasted_iota(jnp.int32, (width, width), 1)
    diagonal = row == col
    trace_value = jnp.sum(jnp.where(diagonal, sigma, 0.0), keepdims=True) + epsilon
    root_scale = jnp.sqrt(trace_value)
    unit, trail = square_root(sigma / trace_value)
    root = root_scale * unit
    root_out[:width, :] = root

    classes = class_weight.shape[0]
    slots = root_out.shape[0] - width
    place = lax.broadcasted_iota(jnp.int32, (slots, 1), 0)
    bias = jnp.zeros((slots, 1), wide)
    for index in range(classes):
        bias = jnp.where(place == index, class_bias[index], bias)
    partial = [
        jnp.sum(class_weight[index].astype(wide) * root, axis=0, keepdims=True)
        for index in range(classes)
    ]
    partial.append(jnp.zeros((slots - classes, width), wide))
    logits = jnp.sum(jnp.concatenate(partial, axis=0), axis=1, keepdims=True) + bias
    onehot = jnp.where(place == label[0], 1.0, 0.0)
    soft = jnp.maximum(logits, 0.0) + jnp.log(1.0 + jnp.exp(-jnp.abs(logits)))
    share = 1.0 / (1.0 + jnp.exp(-logits))
    used = place < classes
    loss_part = jnp.sum(jnp.where(used, soft - onehot * logits, 0.0), keepdims=True)
    logit_grad = jnp.where(used, loss_scale * (share - onehot) / image_count, 0.0)
    root_out[width:, :] = jnp.broadcast_to(
        jnp.where(place == classes, loss_part, logit_grad), (slots, width)
    )

    root_grad = jnp.zeros((width, width), wide)
    for index in range(classes):
        root_grad = root_grad + class_weight[index].astype(wide) * logit_grad[index : index + 1, :]
    root_grad = root_grad + root_grad.T
    change = square_root_change(root_scale * root_grad, trail)
    trace_grad = jnp.sum(root_grad * unit, keepdims=True) / (2.0 * root_scale) - jnp.sum(
        change * sigma, keepdims=True
    ) / (trace_value * trace_value)
    symmetric = (
        (change / trace_value + jnp.where(diagonal, trace_grad, 0.0)) / count
    ).astype(narrow)
    mean_term = jnp.sum(mean_col * symmetric.astype(wide), axis=0, keepdims=True)

    inner = feat_inner.shape[0]
    for feat, gate, start in ((feat_inner, gate_inner, 0), (feat_edge, gate_edge, inner)):
        grad = jnp.dot(feat[...], symmetric, preferred_element_type=wide) - mean_term
        pre[start : start + feat.shape[0], :] = (grad * gate[...]).astype(narrow)
    pre_grad = pre[...]
    payload[width:, :] = jnp.zeros((payload.shape[0] - width, payload.shape[1]), wide)
    taps = KERNEL * KERNEL
    payload[width + taps + 1 : width + taps + 2, :width] = jnp.sum(
        pre_grad.astype(wide), axis=0, keepdims=True
    )
    for first in range(0, conv_turned.shape[0], width):
        payload[:width, first : first + width] = jnp.dot(
            conv_turned[first : first + width, :], pre_grad, preferred_element_type=wide
        )
    for out, start in ((conv_inner_out, 0), (conv_edge_out, inner)):
        out[...] = jnp.dot(
            pre[start : start + out.shape[0], :], reduce_turned[...], preferred_element_type=wide
        ).astype(narrow)


def head(flag, label, class_bias, own, other, class_weight, prepared, count, image_count):
    feat_inner, feat_edge, gate_inner, gate_edge, conv_turned, reduce_turned = prepared
    width, channels = reduce_turned.shape
    inner, edge = feat_inner.shape[0], feat_edge.shape[0]
    slots = -(-(class_weight.shape[0] + 1) // GROUPS) * GROUPS
    return pl.pallas_call(
        functools.partial(head_kernel, count=count, image_count=image_count),
        in_specs=[in_smem] * 3 + [in_vmem] * 9,
        out_specs=[in_vmem] * 4,
        out_shape=[
            shape_of((width + slots, width)),
            shape_of((width + TAPS_ROWS, channels)),
            shape_of((inner, channels), narrow),
            shape_of((edge, channels), narrow),
        ],
        scratch_shapes=[
            pltpu.VMEM((2 * own.shape[0], width), wide),
            pltpu.VMEM((inner + edge, width), narrow),
        ],
        compiler_params=params(24),
        cost_estimate=cost(10),
        name="head",
    )(
        flag, label, class_bias, own, other, class_weight,
        feat_inner, feat_edge, gate_inner, gate_edge, conv_turned, reduce_turned,
    )


def prepare_kernel(
    before_inner, before_edge, conv_inner_in, conv_edge_in, reduce_weight,
    gate_inner, gate_edge, conv_turned, reduce_turned,
):
    for before, gate in ((before_inner, gate_inner), (before_edge, gate_edge)):
        value = before[...]
        share = 1.0 / (1.0 + jnp.exp(-value))
        gate[...] = share * (1.0 + value * (1.0 - share))
    inner = conv_inner_in.shape[0]
    conv_turned[:, :inner] = conv_inner_in[...].T
    conv_turned[:, inner:] = conv_edge_in[...].T
    reduce_turned[...] = reduce_weight[...].T


def prepare(before_inner, before_edge, conv_in, conv_ed, reduce_weight):
    channels, width = reduce_weight.shape
    inner, edge = before_inner.shape[0], before_edge.shape[0]
    return pl.pallas_call(
        prepare_kernel,
        in_specs=[in_vmem] * 5,
        out_specs=[in_vmem] * 4,
        out_shape=[
            shape_of((inner, width)),
            shape_of((edge, width)),
            shape_of((channels, inner + edge), narrow),
            shape_of((width, channels), narrow),
        ],
        compiler_params=params(16),
        cost_estimate=cost(1),
        name="prepare",
    )(before_inner, before_edge, conv_in, conv_ed, reduce_weight)


def taps_kernel(
    spread_in, spread_top, spread_bottom, grad_inner, grad_edge, payload_in, payload,
    parts, grads, products, out, *, first, last,
):
    rows = spread_in.shape[1]
    row_pairs, col_pairs = grads.shape[1:3]
    steps = 2 * col_pairs
    cols = steps * GROUPS
    order = edge_rows(rows)
    taps = KERNEL * KERNEL
    base = payload.shape[0] - TAPS_ROWS

    def one_tile(tile, _):
        lanes = lanes_of(tile)

        def grad_row(row):
            if row in order:
                source, place = grad_edge, order.index(row)
            else:
                source, place = grad_inner, row - SIDE
            values = source[place * cols : (place + 1) * cols, lanes].astype(wide)
            return [values[step * GROUPS : (step + 1) * GROUPS, :] for step in range(steps)]

        for pair in range(row_pairs):
            even, odd = grad_row(2 * pair), grad_row(2 * pair + 1)
            both = [a + b for a, b in zip(even, odd)]
            for row_part, line in enumerate((even, odd, both)):
                for col in range(col_pairs):
                    grads[3 * row_part, pair, col] = line[2 * col]
                    grads[3 * row_part + 1, pair, col] = line[2 * col + 1]
                    grads[3 * row_part + 2, pair, col] = line[2 * col] + line[2 * col + 1]

        def load(place, group):
            place = place - HALF
            if place < 0:
                return spread_top[tile, place + HALF, group]
            if place >= rows:
                return spread_bottom[tile, place - rows, group]
            return spread_in[tile, place, group]

        fill_parts(load, parts, row_pairs + 3, 2 * col_pairs + 6)
        for row_part in range(3):
            for col_part in range(3):
                part = 3 * row_part + col_part
                start = FILTERS[row_part, col_part]
                many_rows, many_cols = PARTS[row_part], PARTS[col_part]
                total = {}
                for place in range(row_pairs + many_rows - 1):
                    line = part_line(
                        load, parts, row_part, col_part, place, col_pairs + many_cols - 1
                    )
                    for tap_row in range(many_rows):
                        row = place - tap_row
                        if not 0 <= row < row_pairs:
                            continue
                        for col in range(col_pairs):
                            grad = grads[part, row, col]
                            for tap_col in range(many_cols):
                                term = line[col + tap_col] * grad
                                tap = tap_row * many_cols + tap_col
                                total[tap] = total[tap] + term if tap in total else term
                for tap, value in total.items():
                    products[start + tap] = value

        for row_tap in range(KERNEL):
            for col_tap in range(KERNEL):
                place = (row_tap // 2, col_tap // 2)
                found = None
                for row_part in (row_tap % 2, 2):
                    for col_part in (col_tap % 2, 2):
                        start = FILTERS[row_part, col_part]
                        value = products[start + place[0] * PARTS[col_part] + place[1]]
                        found = value if found is None else found + value
                tap = row_tap * KERNEL + col_tap
                out[tap : tap + 1, :] = jnp.sum(found, axis=0, keepdims=True)
        found = [
            sum(grads[8, pair, col] for col in range(1, col_pairs)) + grads[8, pair, 0]
            for pair in range(row_pairs)
        ]
        out[taps : taps + 1, :] = jnp.sum(sum(found[1:], found[0]), axis=0, keepdims=True)
        payload[pl.ds(base, taps + 1), lanes] = out[: taps + 1, :]
        return 0

    lax.fori_loop(first, last, one_tile, 0)


def tap_grads(spreads, grads, payload, first, last):
    rows, groups = spreads[0].shape[1:3]
    row_pairs, col_pairs = rows // 2, (groups - KERNEL + 1) // 2
    return pl.pallas_call(
        functools.partial(taps_kernel, first=first, last=last),
        in_specs=[in_vmem] * 6,
        out_specs=in_vmem,
        out_shape=shape_of(payload.shape),
        input_output_aliases={5: 0},
        scratch_shapes=[
            pltpu.VMEM((2, row_pairs + 3, 2 * col_pairs + 6, GROUPS, LANES), wide),
            pltpu.VMEM((9, row_pairs, col_pairs, GROUPS, LANES), wide),
            pltpu.VMEM((PRODUCTS, GROUPS, LANES), wide),
            pltpu.VMEM((TAPS_ROWS, LANES), wide),
        ],
        compiler_params=params(16),
        cost_estimate=cost(2 * (last - first)),
        name="tap_grads",
    )(*spreads, *grads, payload)


def finish_kernel(
    flag, own, other, weight_out, depth_out, depth_bias_out, bias_out, payload,
):
    part = own.shape[0]
    upper = flag[0] != 0
    mine, theirs = own[...].astype(wide), other[...].astype(wide)
    payload[:part, :] = jnp.where(upper, theirs, mine)
    payload[part:, :] = jnp.where(upper, mine, theirs)
    width = weight_out.shape[1]
    for first in range(0, weight_out.shape[0], width):
        weight_out[first : first + width, :] = payload[:width, first : first + width]
    for row_tap in range(KERNEL):
        start = width + row_tap * KERNEL
        depth_out[row_tap] = payload[start : start + KERNEL, :]
    taps = KERNEL * KERNEL
    depth_bias_out[...] = payload[width + taps, :]
    bias_out[...] = payload[width + taps + 1, :width]


def finish(flag, own, other, width):
    part, channels = own.shape
    return pl.pallas_call(
        finish_kernel,
        in_specs=[in_smem] + [in_vmem] * 2,
        out_specs=[in_vmem] * 4,
        out_shape=[
            shape_of((channels, width)),
            shape_of((KERNEL, KERNEL, channels)),
            shape_of((channels,)),
            shape_of((width,)),
        ],
        scratch_shapes=[pltpu.VMEM((2 * part, channels), wide)],
        compiler_params=params(8),
        cost_estimate=cost(1),
        name="finish",
    )(flag, own, other)


def edge_strip(block, left, right, rows):
    channels = block.shape[2]
    parts = [part[rows].reshape(-1, channels) for part in (block, left, right)]
    short = -(2 * HALF * HALF) % 16
    return jnp.concatenate(parts + [jnp.zeros((short, channels), block.dtype)])


def body(
    features, depth_weight, depth_bias, reduce_weight, reduce_bias, class_weight, class_bias, labels
):
    together = lax.optimization_barrier
    block = features[0]
    rows, cols, channels = block.shape
    width = reduce_weight.shape[1]
    classes = class_bias.shape[0]
    count = rows * cols * lax.axis_size("sy") * lax.axis_size("sx")
    image_count = features.shape[0] * lax.axis_size("dp")

    flag = is_upper("sx", 1).astype(jnp.int32)[None]
    upper = is_upper("sx", 1)
    corner = 2 * (lax.axis_index("dp") & 1) + ((lax.axis_index("sx") & 2) >> 1)
    places = [corner ^ turn for turn in range(4)]
    bias_row = depth_bias[None]
    reduce_row = reduce_bias[None]
    left = next_along(block[:, cols - HALF :], "sx")
    right = back_along(block[:, :HALF], "sx")
    low, high, left, right, flag, upper, places, bias_row, reduce_row = together(
        (
            edge_strip(block, left, right, slice(rows - HALF, rows)),
            edge_strip(block, left, right, slice(0, HALF)),
            left,
            right,
            flag,
            upper,
            places,
            bias_row,
            reduce_row,
        )
    )
    top = next_along(low, "sy")
    bottom = back_along(high, "sy")
    spread, conv_in, before_in, feat_in, gram, colsum = conv_inner(
        block, left, right, depth_weight, bias_row, reduce_weight, reduce_row
    )
    spread_top, spread_bottom, conv_ed, before_ed, feat_ed, kept, sent = conv_edge(
        flag, spread, top, bottom, depth_weight, bias_row, reduce_weight, reduce_row, gram, colsum
    )

    sums = kept + swap(sent, "sx", 1)
    sums, before_in, before_ed, conv_in, conv_ed = together(
        (sums, before_in, before_ed, conv_in, conv_ed)
    )
    gate_in, gate_ed, conv_turned, reduce_turned = prepare(
        before_in, before_ed, conv_in, conv_ed, reduce_weight
    )
    for shift in doublings("sx", 2):
        sums = exchange(sums, "sx", shift, wide)
    sums, gate_in, gate_ed, conv_turned, reduce_turned = together(
        (sums, gate_in, gate_ed, conv_turned, reduce_turned)
    )
    for shift in doublings("sy"):
        sums = exchange(sums, "sy", shift, wide)
    other = swap(sums, "sx", 1)

    root, payload, *grads = head(
        flag,
        labels,
        class_bias,
        sums,
        other,
        class_weight,
        (feat_in, feat_ed, gate_in, gate_ed, conv_turned, reduce_turned),
        count,
        image_count,
    )
    known = [root] + [swap(root, "dp", shift) for shift in range(1, lax.axis_size("dp"))]
    spreads = (spread, spread_top, spread_bottom)
    tiles = channels // LANES
    payload = tap_grads(spreads, grads, payload, 0, tiles - 1)
    payload, known = together((payload, known))
    payload = tap_grads(spreads, grads, payload, tiles - 1, tiles)

    part = payload.shape[0] // 2
    low, high = payload[:part], payload[part:]
    kept, sent = jnp.where(upper, high, low), jnp.where(upper, low, high)
    payload = kept + swap(sent.astype(narrow), "sx", 1).astype(wide)
    axes = ("dp", "sx")
    pairs = square_pairs(axes, (1, 2))
    payload = square_scatter(payload, axes, pairs, places, narrow)
    for shift in doublings("dp", 2):
        payload = exchange(payload, "dp", shift, narrow)
    payload = exchange_all(payload, "sy", narrow).astype(narrow)
    payload, known = together((payload, known))
    class_weight_grad = tree_sum(
        [part[width : width + classes, 0][:, None, None] * part[None, :width] for part in known]
    )
    totals = tree_sum([part[width:, 0] for part in known])
    class_bias_grad = totals[:classes]
    loss = totals[classes] / image_count
    payload = square_gather(payload, axes, pairs, places)
    other, class_weight_grad, class_bias_grad, loss = together(
        (swap(payload, "sx", 1), class_weight_grad, class_bias_grad, loss)
    )
    weight_grad, depth_grad, depth_bias_grad, bias_grad = finish(flag, payload, other, width)
    return (
        loss,
        depth_grad,
        depth_bias_grad,
        weight_grad,
        bias_grad,
        class_weight_grad,
        class_bias_grad,
    )


def solution(mesh):
    placed = (P("dp", "sy", "sx", None), P(), P(), P(), P(), P(), P(), P("dp"))
    return jax.shard_map(
        body,
        mesh=mesh,
        in_specs=placed,
        out_specs=(P(), P(), P(), P(), P(), P(), P()),
        check_vma=False,
    )
```

```python
import functools

import jax
import jax.numpy as jnp
from jax import lax
from jax.experimental import pallas as pl
from jax.experimental.pallas import tpu as pltpu
from jax.sharding import PartitionSpec as P

KERNEL = 7
HALF = KERNEL // 2
NEWTON_STEPS = 5
LANES = 128
GROUPS = 8
EDGE = 8
TAPS_ROWS = 64
SIDE = 4
FILL_ROWS = 4
PARTS = (4, 3, 4)

epsilon = 1e-05
loss_scale = 64.0
narrow = jnp.bfloat16
wide = jnp.float32


def params(megabytes):
    return pltpu.CompilerParams(vmem_limit_bytes=megabytes * 1024 * 1024)


def swap(value, axis, shift):
    count = lax.axis_size(axis)
    return lax.ppermute(value, axis, [(i, i ^ shift) for i in range(count)])


def is_upper(axis, shift):
    return (lax.axis_index(axis) & shift) != 0


def tree_sum(terms):
    while len(terms) > 1:
        terms = [terms[i] + terms[i + 1] for i in range(0, len(terms), 2)]
    return terms[0]


def exchange(value, axis, shift, sent_as):
    sent = value.astype(sent_as)
    return sent.astype(wide) + swap(sent, axis, shift).astype(wide)


def exchange_all(value, axis, sent_as):
    sent = value.astype(sent_as)
    moved = [sent] + [swap(sent, axis, shift) for shift in range(1, lax.axis_size(axis))]
    return tree_sum([part.astype(wide) for part in moved])


def square_pairs(axes, shifts):
    counts = [lax.axis_size(axis) for axis in axes]
    return {
        2 * first + second: [
            (i * counts[1] + j, (i ^ (first * shifts[0])) * counts[1] + (j ^ (second * shifts[1])))
            for i in range(counts[0])
            for j in range(counts[1])
        ]
        for first, second in ((0, 1), (1, 0), (1, 1))
    }


def square_scatter(value, axes, pairs, places, sent_as):
    pieces = value.reshape((4, value.shape[0] // 4) + value.shape[1:])

    def piece(turn):
        starts = (places[turn],) + (0,) * value.ndim
        sizes = (1,) + pieces.shape[1:]
        return lax.dynamic_slice(pieces, starts, sizes, allow_negative_indices=False)[0]

    moved = [
        lax.ppermute(piece(turn).astype(sent_as), axes, pairs[turn]).astype(wide)
        for turn in (1, 2, 3)
    ]
    return tree_sum([piece(0)] + moved)


def square_gather(value, axes, pairs, places):
    whole = jnp.zeros((4,) + value.shape, value.dtype)
    for turn in range(4):
        part = lax.ppermute(value, axes, pairs[turn]) if turn else value
        starts = (places[turn],) + (0,) * value.ndim
        whole = lax.dynamic_update_slice(whole, part[None], starts, allow_negative_indices=False)
    return whole.reshape((-1,) + value.shape[1:])


def doublings(axis, first=1):
    found = []
    shift = first
    while shift < lax.axis_size(axis):
        found.append(shift)
        shift *= 2
    return found


def next_along(value, axis):
    return lax.ppermute(value, axis, [(i, i + 1) for i in range(lax.axis_size(axis) - 1)])


def back_along(value, axis):
    return lax.ppermute(value, axis, [(i + 1, i) for i in range(lax.axis_size(axis) - 1)])


def spread_columns(source, target):
    for group in range(target.shape[0]):
        target[group] = source[pl.ds(EDGE - HALF + group, GROUPS, stride=GROUPS), :]


def fill_row(wide_row, middle, left, right):
    cols = middle.shape[0]
    wide_row[EDGE : EDGE + cols, :] = middle.astype(wide)
    wide_row[EDGE - HALF : EDGE, :] = left.astype(wide)
    wide_row[EDGE + cols : EDGE + cols + HALF, :] = right.astype(wide)


def lanes_of(tile):
    return pl.ds(pl.multiple_of(tile * LANES, LANES), LANES)


def part_starts():
    starts, total = {}, 0
    for row_part in range(3):
        for col_part in range(3):
            starts[row_part, col_part] = total
            total += PARTS[row_part] * PARTS[col_part]
    return starts, total


FILTERS, PRODUCTS = part_starts()


def part_taps(taps):
    even, odd = taps[0::2], taps[1::2]
    both = [a + b for a, b in zip(even, odd)] + even[len(odd) :]
    return even, odd, both


def spread_weights(weight_ref, filters, tile, lanes):
    rows = []
    for row_tap in range(KERNEL):
        row = [weight_ref[row_tap, tap : tap + 1, lanes] for tap in range(KERNEL)]
        rows.append([jnp.broadcast_to(tap, (GROUPS, LANES)) for tap in row])
    columns = [part_taps([rows[tap][col] for tap in range(KERNEL)]) for col in range(KERNEL)]
    for row_part, many in enumerate(PARTS):
        for row in range(many):
            line = [columns[col][row_part][row] for col in range(KERNEL)]
            for col_part, taps in enumerate(part_taps(line)):
                start = FILTERS[row_part, col_part] + row * PARTS[col_part]
                for col, value in enumerate(taps):
                    filters[tile, start + col] = value


def fill_parts(load, parts, row_pairs, groups):
    for pair in range(row_pairs):
        for group in range(groups):
            middle = load(2 * pair + 1, group)
            parts[0, pair, group] = load(2 * pair, group) - middle
            if pair < row_pairs - 1:
                parts[1, pair, group] = load(2 * pair + 2, group) - middle


def part_line(load, parts, row_part, col_part, pair, many):
    def value(group):
        return load(2 * pair + 1, group) if row_part == 2 else parts[row_part, pair, group]

    first = (0, 2, 1)[col_part]
    line = [value(2 * col + first) for col in range(many)]
    if col_part < 2:
        line = [side - value(2 * col + 1) for col, side in enumerate(line)]
    return line


def conv_rows(load, filters, tile, bias, steps, count, parts, products):
    row_pairs, col_pairs = count // 2, steps // 2
    fill_parts(load, parts, row_pairs + 3, 2 * col_pairs + 6)
    for row_part in range(3):
        for col_part in range(3):
            start = FILTERS[row_part, col_part]
            many_rows, many_cols = PARTS[row_part], PARTS[col_part]
            total = [[None] * col_pairs for _ in range(row_pairs)]
            for place in range(row_pairs + many_rows - 1):
                line = part_line(
                    load, parts, row_part, col_part, place, col_pairs + many_cols - 1
                )
                for row in range(row_pairs):
                    tap_row = place - row
                    if not 0 <= tap_row < many_rows:
                        continue
                    for tap_col in range(many_cols):
                        scale = filters[tile, start + tap_row * many_cols + tap_col]
                        for col in range(col_pairs):
                            term = line[col + tap_col] * scale
                            old = total[row][col]
                            total[row][col] = term if old is None else old + term
            for row in range(row_pairs):
                for col in range(col_pairs):
                    products[3 * row_part + col_part, row, col] = total[row][col]
    found = []
    for row in range(row_pairs):
        lines = [[], []]
        for col in range(col_pairs):
            values = [products[part, row, col] for part in range(9)]
            shared = [values[6] + values[8] + bias, values[7] + values[8] + bias]
            for row_part in range(2):
                for col_part in range(2):
                    own = values[3 * row_part + col_part] + values[3 * row_part + 2]
                    lines[row_part].append(own + shared[col_part])
        found += lines[0] + lines[1]
    return jnp.concatenate(found, axis=0).astype(narrow)


def parts_scratch(count, steps):
    row_pairs, col_pairs = count // 2, steps // 2
    return [
        pltpu.VMEM((2, row_pairs + 3, 2 * col_pairs + 6, GROUPS, LANES), wide),
        pltpu.VMEM((9, row_pairs, col_pairs, GROUPS, LANES), wide),
    ]


def reduce_part(conv_out, reduce_ref, reduce_bias_ref, before_out, feat_out):
    before = jnp.dot(conv_out[...], reduce_ref[...], preferred_element_type=wide)
    before = before + reduce_bias_ref[...]
    before_out[...] = before
    feat_out[...] = (before / (1.0 + jnp.exp(-before))).astype(narrow)
    feat = feat_out[...]
    gram = lax.dot_general(feat, feat, (((0,), (0,)), ((), ())), preferred_element_type=wide)
    return gram, jnp.sum(feat.astype(wide), axis=0, keepdims=True)


def spread_kernel(block, weight, spread_out, filters, wide_row):
    rows, cols = block.shape[0], block.shape[1]

    def one_tile(tile, _):
        lanes = lanes_of(tile)
        spread_weights(weight, filters, tile, lanes)

        def fill(turn, _):
            for row in range(FILL_ROWS):
                row = turn * FILL_ROWS + row
                place = wide_row.at[row]
                nothing = jnp.zeros((HALF, LANES), wide)
                fill_row(place, block[row, :, lanes], nothing, nothing)
                spread_columns(place, spread_out.at[tile, row])
            return 0

        lax.fori_loop(0, rows // FILL_ROWS, fill, 0)
        return 0

    lax.fori_loop(0, spread_out.shape[0], one_tile, 0)


def inner_kernel(
    spread_in, left, right, filters, bias, reduce_weight, reduce_bias,
    spread_out, conv_out, before_out, feat_out, gram_out, colsum_out,
    parts, products,
):
    rows, groups = spread_out.shape[1:3]
    steps = groups - KERNEL + 1

    def one_tile(tile, _):
        lanes = lanes_of(tile)
        start_value = jnp.broadcast_to(bias[0:1, lanes], (GROUPS, LANES))
        for row in range(rows):
            start, end = left[row, :, lanes].astype(wide), right[row, :, lanes].astype(wide)
            for col in range(HALF):
                spread_out[tile, row, col, 0:1, :] = start[col : col + 1, :]
                group = groups - HALF + col
                spread_out[tile, row, group, GROUPS - 1 : GROUPS, :] = end[col : col + 1, :]

        def load(row, group):
            return spread_out[tile, row + SIDE - HALF, group]

        conv_out[:, lanes] = conv_rows(
            load, filters, tile, start_value, steps, rows - 2 * SIDE, parts, products
        )
        return 0

    lax.fori_loop(0, spread_out.shape[0], one_tile, 0)
    gram_out[...], colsum_out[...] = reduce_part(
        conv_out, reduce_weight, reduce_bias, before_out, feat_out
    )


def edge_kernel(
    flag, spread_in, top, bottom, corners_top, corners_bottom, filters, bias, reduce_weight,
    reduce_bias, gram_in, colsum_in,
    spread_top, spread_bottom, conv_out, before_out, feat_out, kept_out, sent_out,
    wide_row, parts, products, sums,
):
    rows, cols = spread_in.shape[1], wide_row.shape[1] - 2 * EDGE
    steps = cols // GROUPS

    def one_tile(tile, _):
        lanes = lanes_of(tile)
        start_value = jnp.broadcast_to(bias[0:1, lanes], (GROUPS, LANES))
        sides = ((top, corners_top, spread_top), (bottom, corners_bottom, spread_bottom))
        for side, (strip, ends, spread) in enumerate(sides):
            for row in range(HALF):
                place = wide_row.at[side * HALF + row]
                left, right = ends[0, row, :, lanes], ends[1, row, :, lanes]
                fill_row(place, strip[row, :, lanes], left, right)
                spread_columns(place, spread.at[tile, row])

        def load_from(row):
            def load(row_tap, group):
                place = row + row_tap - HALF
                if place < 0:
                    return spread_top[tile, place + HALF, group]
                if place >= rows:
                    return spread_bottom[tile, place - rows, group]
                return spread_in[tile, place, group]

            return load

        for side, row in enumerate((0, rows - SIDE)):
            start = side * SIDE * cols
            conv_out[start : start + SIDE * cols, lanes] = conv_rows(
                load_from(row), filters, tile, start_value, steps, SIDE,
                parts.at[side], products.at[side],
            )
        return 0

    lax.fori_loop(0, spread_in.shape[0], one_tile, 0)
    gram, colsum = reduce_part(conv_out, reduce_weight, reduce_bias, before_out, feat_out)
    gram = gram + gram_in[...]
    colsum = colsum + colsum_in[...]
    half = gram.shape[0] // 2
    row = lax.broadcasted_iota(jnp.int32, (half, half), 0)
    col = lax.broadcasted_iota(jnp.int32, (half, half), 1)
    last_block = gram[half:, half:]
    diagonal = jnp.sum(jnp.where(row == col, last_block, 0.0), axis=0, keepdims=True)
    sums[:half, :half] = gram[:half, half:]
    sums[:half, half:] = jnp.where(row <= col, gram[:half, :half], last_block)
    sums[half : half + GROUPS, :] = jnp.broadcast_to(colsum, (GROUPS, 2 * half))
    sums[half + GROUPS :, :half] = jnp.broadcast_to(diagonal, (GROUPS, half))
    sums[half + GROUPS :, half:] = jnp.zeros((GROUPS, half), wide)
    part = kept_out.shape[0]
    keep_or_send(flag[0] != 0, sums[:part, :], sums[part:, :], kept_out, sent_out)


def keep_or_send(upper, low, high, kept_out, sent_out):
    kept_out[...] = jnp.where(upper, high, low)
    sent_out[...] = jnp.where(upper, low, high).astype(sent_out.dtype)


def edge_rows(rows):
    return list(range(SIDE)) + list(range(rows - SIDE, rows))


def shape_of(shape, dtype=wide):
    return jax.ShapeDtypeStruct(shape, dtype)


in_vmem = pl.BlockSpec(memory_space=pltpu.VMEM)
in_smem = pl.BlockSpec(memory_space=pltpu.SMEM)


def cost(microseconds):
    return pl.CostEstimate(
        flops=microseconds * 10**9, bytes_accessed=microseconds * 10**6, transcendentals=0
    )


def spread_block(block, weight):
    rows, cols, channels = block.shape
    tiles = channels // LANES
    return pl.pallas_call(
        spread_kernel,
        in_specs=[in_vmem] * 2,
        out_specs=[in_vmem] * 2,
        out_shape=[
            shape_of((tiles, rows, cols // GROUPS + KERNEL - 1, GROUPS, LANES)),
            shape_of((tiles, PRODUCTS, GROUPS, LANES)),
        ],
        scratch_shapes=[pltpu.VMEM((rows, cols + 2 * EDGE, LANES), wide)],
        compiler_params=params(8),
        cost_estimate=cost(2),
        name="spread_block",
    )(block, weight)


def conv_inner(spread, left, right, filters, bias, reduce_weight, reduce_bias):
    tiles, rows, groups = spread.shape[:3]
    channels, width = reduce_weight.shape
    steps = groups - KERNEL + 1
    pixels = (rows - 2 * SIDE) * steps * GROUPS
    return pl.pallas_call(
        inner_kernel,
        in_specs=[in_vmem] * 7,
        out_specs=[in_vmem] * 6,
        out_shape=[
            shape_of(spread.shape),
            shape_of((pixels, channels), narrow),
            shape_of((pixels, width)),
            shape_of((pixels, width), narrow),
            shape_of((width, width)),
            shape_of((1, width)),
        ],
        input_output_aliases={0: 0},
        scratch_shapes=parts_scratch(rows - 2 * SIDE, steps),
        compiler_params=params(24),
        cost_estimate=cost(10),
        name="conv_inner",
    )(spread, left, right, filters, bias, reduce_weight, reduce_bias)


def conv_edge(flag, spread, halos, filters, bias, reduce_weight, reduce_bias, gram, colsum):
    tiles, rows, groups = spread.shape[:3]
    cols = (groups - KERNEL + 1) * GROUPS
    channels, width = reduce_weight.shape
    pixels = 2 * SIDE * cols
    parts, products = parts_scratch(SIDE, cols // GROUPS)
    side = (tiles, HALF, groups, GROUPS, LANES)
    sums_rows = width // 2 + 2 * GROUPS
    return pl.pallas_call(
        edge_kernel,
        in_specs=[in_smem] + [in_vmem] * 11,
        out_specs=[in_vmem] * 7,
        out_shape=[
            shape_of(side),
            shape_of(side),
            shape_of((pixels, channels), narrow),
            shape_of((pixels, width)),
            shape_of((pixels, width), narrow),
            shape_of((sums_rows // 2, width)),
            shape_of((sums_rows // 2, width)),
        ],
        scratch_shapes=[
            pltpu.VMEM((2 * HALF, cols + 2 * EDGE, LANES), wide),
            pltpu.VMEM((2,) + parts.shape, wide),
            pltpu.VMEM((2,) + products.shape, wide),
            pltpu.VMEM((sums_rows, width), wide),
        ],
        compiler_params=params(24),
        cost_estimate=cost(6),
        name="conv_edge",
    )(flag, spread, *halos, filters, bias, reduce_weight, reduce_bias, gram, colsum)


def split(value):
    high = value.astype(narrow)
    return high, (value - high.astype(wide)).astype(narrow)


def product(left, right):
    def dot(a, b):
        return jnp.dot(a, b, preferred_element_type=wide)

    return dot(left[0], right[0]) + (dot(left[0], right[1]) + dot(left[1], right[0]))


def square_root(current):
    size = current.shape[0]
    row = lax.broadcasted_iota(jnp.int32, (size, size), 0)
    col = lax.broadcasted_iota(jnp.int32, (size, size), 1)
    triple = jnp.where(row == col, 3.0, 0.0)
    factor = split(0.5 * (triple - current))
    current = split(current)
    trail = [(current, None, factor)]
    inverse = factor
    current = split(product(current, factor))
    for step in range(1, NEWTON_STEPS):
        factor = split(0.5 * (triple - product(inverse, current)))
        trail.append((current, inverse, factor))
        last = step == NEWTON_STEPS - 1
        if not last:
            inverse = split(product(factor, inverse))
        current = product(current, factor)
        if not last:
            current = split(current)
    return current, trail


def square_root_change(change, trail):
    first, _, factor = trail[0]
    move = split(change)
    factor_move = split(-0.5 * change)
    change = product(move, factor) + product(first, factor_move)
    inverse_move = factor_move
    for step in range(1, NEWTON_STEPS):
        current, inverse, factor = trail[step]
        move = split(change)
        factor_move = split(
            -0.5 * (product(inverse_move, current) + product(inverse, move))
        )
        change = product(move, factor) + product(current, factor_move)
        if step < NEWTON_STEPS - 1:
            inverse_move = split(product(factor_move, inverse) + product(factor, inverse_move))
    return change


def head_kernel(
    flag, label, class_bias, own, other, class_weight,
    feat_inner, feat_edge, gate_inner, gate_edge, conv_turned, reduce_turned,
    root_out, payload, conv_inner_out, conv_edge_out,
    sums, pre, *, count, image_count,
):
    width = root_out.shape[1]
    half = width // 2
    rows = own.shape[0]
    upper = flag[0] != 0
    mine, theirs = own[...], other[...]
    sums[:rows, :] = jnp.where(upper, theirs, mine)
    sums[rows:, :] = jnp.where(upper, mine, theirs)
    row = lax.broadcasted_iota(jnp.int32, (half, half), 0)
    col = lax.broadcasted_iota(jnp.int32, (half, half), 1)
    cross, mixed = sums[:half, :half], sums[:half, half:]
    turned = mixed.T
    first = jnp.where(row <= col, mixed, turned)
    diagonal = jnp.broadcast_to(sums[half + GROUPS : half + GROUPS + 1, :half], (half, half))
    last = jnp.where(row == col, diagonal, jnp.where(row > col, mixed, turned))
    gram = jnp.concatenate(
        [
            jnp.concatenate([first, cross], axis=1),
            jnp.concatenate([cross.T, last], axis=1),
        ],
        axis=0,
    )
    mean_row = sums[half : half + 1, :] / count
    mean_col = jnp.broadcast_to(mean_row, (width, width)).T
    sigma = gram / count - mean_col * mean_row
    row = lax.broadcasted_iota(jnp.int32, (width, width), 0)
    col = lax.broadcasted_iota(jnp.int32, (width, width), 1)
    diagonal = row == col
    trace_value = jnp.sum(jnp.where(diagonal, sigma, 0.0), keepdims=True) + epsilon
    root_scale = jnp.sqrt(trace_value)
    unit, trail = square_root(sigma / trace_value)
    root = root_scale * unit
    root_out[:width, :] = root

    classes = class_weight.shape[0]
    slots = root_out.shape[0] - width
    place = lax.broadcasted_iota(jnp.int32, (slots, 1), 0)
    bias = jnp.zeros((slots, 1), wide)
    for index in range(classes):
        bias = jnp.where(place == index, class_bias[index], bias)
    partial = [
        jnp.sum(class_weight[index].astype(wide) * root, axis=0, keepdims=True)
        for index in range(classes)
    ]
    partial.append(jnp.zeros((slots - classes, width), wide))
    logits = jnp.sum(jnp.concatenate(partial, axis=0), axis=1, keepdims=True) + bias
    onehot = jnp.where(place == label[0], 1.0, 0.0)
    soft = jnp.maximum(logits, 0.0) + jnp.log(1.0 + jnp.exp(-jnp.abs(logits)))
    share = 1.0 / (1.0 + jnp.exp(-logits))
    used = place < classes
    loss_part = jnp.sum(jnp.where(used, soft - onehot * logits, 0.0), keepdims=True)
    logit_grad = jnp.where(used, loss_scale * (share - onehot) / image_count, 0.0)
    root_out[width:, :] = jnp.broadcast_to(
        jnp.where(place == classes, loss_part, logit_grad), (slots, width)
    )

    root_grad = jnp.zeros((width, width), wide)
    for index in range(classes):
        root_grad = root_grad + class_weight[index].astype(wide) * logit_grad[index : index + 1, :]
    root_grad = root_grad + root_grad.T
    change = square_root_change(root_scale * root_grad, trail)
    trace_grad = jnp.sum(root_grad * unit, keepdims=True) / (2.0 * root_scale) - jnp.sum(
        change * sigma, keepdims=True
    ) / (trace_value * trace_value)
    symmetric = (
        (change / trace_value + jnp.where(diagonal, trace_grad, 0.0)) / count
    ).astype(narrow)
    mean_term = jnp.sum(mean_col * symmetric.astype(wide), axis=0, keepdims=True)

    inner = feat_inner.shape[0]
    for feat, gate, start in ((feat_inner, gate_inner, 0), (feat_edge, gate_edge, inner)):
        grad = jnp.dot(feat[...], symmetric, preferred_element_type=wide) - mean_term
        pre[start : start + feat.shape[0], :] = (grad * gate[...]).astype(narrow)
    pre_grad = pre[...]
    payload[width:, :] = jnp.zeros((payload.shape[0] - width, payload.shape[1]), wide)
    taps = KERNEL * KERNEL
    payload[width + taps + 1 : width + taps + 2, :width] = jnp.sum(
        pre_grad.astype(wide), axis=0, keepdims=True
    )
    for first in range(0, conv_turned.shape[0], width):
        payload[:width, first : first + width] = jnp.dot(
            conv_turned[first : first + width, :], pre_grad, preferred_element_type=wide
        )
    for out, start in ((conv_inner_out, 0), (conv_edge_out, inner)):
        out[...] = jnp.dot(
            pre[start : start + out.shape[0], :], reduce_turned[...], preferred_element_type=wide
        ).astype(narrow)


def head(flag, label, class_bias, own, other, class_weight, prepared, count, image_count):
    feat_inner, feat_edge, gate_inner, gate_edge, conv_turned, reduce_turned = prepared
    width, channels = reduce_turned.shape
    inner, edge = feat_inner.shape[0], feat_edge.shape[0]
    slots = -(-(class_weight.shape[0] + 1) // GROUPS) * GROUPS
    return pl.pallas_call(
        functools.partial(head_kernel, count=count, image_count=image_count),
        in_specs=[in_smem] * 3 + [in_vmem] * 9,
        out_specs=[in_vmem] * 4,
        out_shape=[
            shape_of((width + slots, width)),
            shape_of((width + TAPS_ROWS, channels)),
            shape_of((inner, channels), narrow),
            shape_of((edge, channels), narrow),
        ],
        scratch_shapes=[
            pltpu.VMEM((2 * own.shape[0], width), wide),
            pltpu.VMEM((inner + edge, width), narrow),
        ],
        compiler_params=params(24),
        cost_estimate=cost(10),
        name="head",
    )(
        flag, label, class_bias, own, other, class_weight,
        feat_inner, feat_edge, gate_inner, gate_edge, conv_turned, reduce_turned,
    )


def prepare_kernel(
    before_inner, before_edge, conv_inner_in, conv_edge_in, reduce_weight,
    gate_inner, gate_edge, conv_turned, reduce_turned,
):
    for before, gate in ((before_inner, gate_inner), (before_edge, gate_edge)):
        value = before[...]
        share = 1.0 / (1.0 + jnp.exp(-value))
        gate[...] = share * (1.0 + value * (1.0 - share))
    inner = conv_inner_in.shape[0]
    conv_turned[:, :inner] = conv_inner_in[...].T
    conv_turned[:, inner:] = conv_edge_in[...].T
    reduce_turned[...] = reduce_weight[...].T


def prepare(before_inner, before_edge, conv_in, conv_ed, reduce_weight):
    channels, width = reduce_weight.shape
    inner, edge = before_inner.shape[0], before_edge.shape[0]
    return pl.pallas_call(
        prepare_kernel,
        in_specs=[in_vmem] * 5,
        out_specs=[in_vmem] * 4,
        out_shape=[
            shape_of((inner, width)),
            shape_of((edge, width)),
            shape_of((channels, inner + edge), narrow),
            shape_of((width, channels), narrow),
        ],
        compiler_params=params(16),
        cost_estimate=cost(1),
        name="prepare",
    )(before_inner, before_edge, conv_in, conv_ed, reduce_weight)


def taps_kernel(
    spread_in, spread_top, spread_bottom, grad_inner, grad_edge, payload_in, payload,
    parts, grads, products, out, *, first, last,
):
    rows = spread_in.shape[1]
    row_pairs, col_pairs = grads.shape[1:3]
    steps = 2 * col_pairs
    cols = steps * GROUPS
    order = edge_rows(rows)
    taps = KERNEL * KERNEL
    base = payload.shape[0] - TAPS_ROWS

    def one_tile(tile, _):
        lanes = lanes_of(tile)

        def grad_row(row):
            if row in order:
                source, place = grad_edge, order.index(row)
            else:
                source, place = grad_inner, row - SIDE
            values = source[place * cols : (place + 1) * cols, lanes].astype(wide)
            return [values[step * GROUPS : (step + 1) * GROUPS, :] for step in range(steps)]

        for pair in range(row_pairs):
            even, odd = grad_row(2 * pair), grad_row(2 * pair + 1)
            both = [a + b for a, b in zip(even, odd)]
            for row_part, line in enumerate((even, odd, both)):
                for col in range(col_pairs):
                    grads[3 * row_part, pair, col] = line[2 * col]
                    grads[3 * row_part + 1, pair, col] = line[2 * col + 1]
                    grads[3 * row_part + 2, pair, col] = line[2 * col] + line[2 * col + 1]

        def load(place, group):
            place = place - HALF
            if place < 0:
                return spread_top[tile, place + HALF, group]
            if place >= rows:
                return spread_bottom[tile, place - rows, group]
            return spread_in[tile, place, group]

        fill_parts(load, parts, row_pairs + 3, 2 * col_pairs + 6)
        for row_part in range(3):
            for col_part in range(3):
                part = 3 * row_part + col_part
                start = FILTERS[row_part, col_part]
                many_rows, many_cols = PARTS[row_part], PARTS[col_part]
                total = {}
                for place in range(row_pairs + many_rows - 1):
                    line = part_line(
                        load, parts, row_part, col_part, place, col_pairs + many_cols - 1
                    )
                    for tap_row in range(many_rows):
                        row = place - tap_row
                        if not 0 <= row < row_pairs:
                            continue
                        for col in range(col_pairs):
                            grad = grads[part, row, col]
                            for tap_col in range(many_cols):
                                term = line[col + tap_col] * grad
                                tap = tap_row * many_cols + tap_col
                                total[tap] = total[tap] + term if tap in total else term
                for tap, value in total.items():
                    products[start + tap] = value

        for row_tap in range(KERNEL):
            for col_tap in range(KERNEL):
                place = (row_tap // 2, col_tap // 2)
                found = None
                for row_part in (row_tap % 2, 2):
                    for col_part in (col_tap % 2, 2):
                        start = FILTERS[row_part, col_part]
                        value = products[start + place[0] * PARTS[col_part] + place[1]]
                        found = value if found is None else found + value
                tap = row_tap * KERNEL + col_tap
                out[tap : tap + 1, :] = jnp.sum(found, axis=0, keepdims=True)
        found = [
            sum(grads[8, pair, col] for col in range(1, col_pairs)) + grads[8, pair, 0]
            for pair in range(row_pairs)
        ]
        out[taps : taps + 1, :] = jnp.sum(sum(found[1:], found[0]), axis=0, keepdims=True)
        payload[pl.ds(base, taps + 1), lanes] = out[: taps + 1, :]
        return 0

    lax.fori_loop(first, last, one_tile, 0)


def tap_grads(spreads, grads, payload, first, last):
    rows, groups = spreads[0].shape[1:3]
    row_pairs, col_pairs = rows // 2, (groups - KERNEL + 1) // 2
    return pl.pallas_call(
        functools.partial(taps_kernel, first=first, last=last),
        in_specs=[in_vmem] * 6,
        out_specs=in_vmem,
        out_shape=shape_of(payload.shape),
        input_output_aliases={5: 0},
        scratch_shapes=[
            pltpu.VMEM((2, row_pairs + 3, 2 * col_pairs + 6, GROUPS, LANES), wide),
            pltpu.VMEM((9, row_pairs, col_pairs, GROUPS, LANES), wide),
            pltpu.VMEM((PRODUCTS, GROUPS, LANES), wide),
            pltpu.VMEM((TAPS_ROWS, LANES), wide),
        ],
        compiler_params=params(16),
        cost_estimate=cost(2 * (last - first)),
        name="tap_grads",
    )(*spreads, *grads, payload)


def finish_kernel(
    flag, own, other, weight_out, depth_out, depth_bias_out, bias_out, payload,
):
    part = own.shape[0]
    upper = flag[0] != 0
    mine, theirs = own[...].astype(wide), other[...].astype(wide)
    payload[:part, :] = jnp.where(upper, theirs, mine)
    payload[part:, :] = jnp.where(upper, mine, theirs)
    width = weight_out.shape[1]
    for first in range(0, weight_out.shape[0], width):
        weight_out[first : first + width, :] = payload[:width, first : first + width]
    for row_tap in range(KERNEL):
        start = width + row_tap * KERNEL
        depth_out[row_tap] = payload[start : start + KERNEL, :]
    taps = KERNEL * KERNEL
    depth_bias_out[...] = payload[width + taps, :]
    bias_out[...] = payload[width + taps + 1, :width]


def finish(flag, own, other, width):
    part, channels = own.shape
    return pl.pallas_call(
        finish_kernel,
        in_specs=[in_smem] + [in_vmem] * 2,
        out_specs=[in_vmem] * 4,
        out_shape=[
            shape_of((channels, width)),
            shape_of((KERNEL, KERNEL, channels)),
            shape_of((channels,)),
            shape_of((width,)),
        ],
        scratch_shapes=[pltpu.VMEM((2 * part, channels), wide)],
        compiler_params=params(8),
        cost_estimate=cost(1),
        name="finish",
    )(flag, own, other)


def body(
    features, depth_weight, depth_bias, reduce_weight, reduce_bias, class_weight, class_bias, labels
):
    together = lax.optimization_barrier
    block = features[0]
    rows, cols, channels = block.shape
    width = reduce_weight.shape[1]
    classes = class_bias.shape[0]
    count = rows * cols * lax.axis_size("sy") * lax.axis_size("sx")
    image_count = features.shape[0] * lax.axis_size("dp")

    flag = is_upper("sx", 1).astype(jnp.int32)[None]
    upper = is_upper("sx", 1)
    corner = 2 * (lax.axis_index("dp") & 1) + ((lax.axis_index("sx") & 2) >> 1)
    places = [corner ^ turn for turn in range(4)]
    block, flag, upper, places = together((block, flag, upper, places))
    bias_row = depth_bias[None]
    reduce_row = reduce_bias[None]
    left = next_along(block[:, cols - HALF :], "sx")
    right = back_along(block[:, :HALF], "sx")
    top = next_along(block[rows - HALF :], "sy")
    bottom = back_along(block[:HALF], "sy")
    spread, filters = spread_block(block, depth_weight)
    left, right, spread, filters = together((left, right, spread, filters))
    low, high, left, right, bias_row, reduce_row = together(
        (
            jnp.stack([left[rows - HALF :], right[rows - HALF :]]),
            jnp.stack([left[:HALF], right[:HALF]]),
            left,
            right,
            bias_row,
            reduce_row,
        )
    )
    corners_top = next_along(low, "sy")
    corners_bottom = back_along(high, "sy")
    spread, conv_in, before_in, feat_in, gram, colsum = conv_inner(
        spread, left, right, filters, bias_row, reduce_weight, reduce_row
    )
    spread_top, spread_bottom, conv_ed, before_ed, feat_ed, kept, sent = conv_edge(
        flag,
        spread,
        (top, bottom, corners_top, corners_bottom),
        filters,
        bias_row,
        reduce_weight,
        reduce_row,
        gram,
        colsum,
    )

    sums = kept + swap(sent, "sx", 1)
    sums, before_in, before_ed, conv_in, conv_ed = together(
        (sums, before_in, before_ed, conv_in, conv_ed)
    )
    gate_in, gate_ed, conv_turned, reduce_turned = prepare(
        before_in, before_ed, conv_in, conv_ed, reduce_weight
    )
    for shift in doublings("sx", 2):
        sums = exchange(sums, "sx", shift, wide)
    sums, gate_in, gate_ed, conv_turned, reduce_turned = together(
        (sums, gate_in, gate_ed, conv_turned, reduce_turned)
    )
    for shift in doublings("sy"):
        sums = exchange(sums, "sy", shift, wide)
    other = swap(sums, "sx", 1)

    root, payload, *grads = head(
        flag,
        labels,
        class_bias,
        sums,
        other,
        class_weight,
        (feat_in, feat_ed, gate_in, gate_ed, conv_turned, reduce_turned),
        count,
        image_count,
    )
    known = [root] + [swap(root, "dp", shift) for shift in range(1, lax.axis_size("dp"))]
    spreads = (spread, spread_top, spread_bottom)
    tiles = channels // LANES
    payload = tap_grads(spreads, grads, payload, 0, tiles - 1)
    payload, known = together((payload, known))
    payload = tap_grads(spreads, grads, payload, tiles - 1, tiles)

    part = payload.shape[0] // 2
    low, high = payload[:part], payload[part:]
    kept, sent = jnp.where(upper, high, low), jnp.where(upper, low, high)
    payload = kept + swap(sent.astype(narrow), "sx", 1).astype(wide)
    axes = ("dp", "sx")
    pairs = square_pairs(axes, (1, 2))
    payload = square_scatter(payload, axes, pairs, places, narrow)
    for shift in doublings("dp", 2):
        payload = exchange(payload, "dp", shift, narrow)
    payload = exchange_all(payload, "sy", narrow).astype(narrow)
    payload, known = together((payload, known))
    class_weight_grad = tree_sum(
        [part[width : width + classes, 0][:, None, None] * part[None, :width] for part in known]
    )
    totals = tree_sum([part[width:, 0] for part in known])
    class_bias_grad = totals[:classes]
    loss = totals[classes] / image_count
    payload = square_gather(payload, axes, pairs, places)
    other, class_weight_grad, class_bias_grad, loss = together(
        (swap(payload, "sx", 1), class_weight_grad, class_bias_grad, loss)
    )
    weight_grad, depth_grad, depth_bias_grad, bias_grad = finish(flag, payload, other, width)
    return (
        loss,
        depth_grad,
        depth_bias_grad,
        weight_grad,
        bias_grad,
        class_weight_grad,
        class_bias_grad,
    )


def solution(mesh):
    placed = (P("dp", "sy", "sx", None), P(), P(), P(), P(), P(), P(), P("dp"))
    return jax.shard_map(
        body,
        mesh=mesh,
        in_specs=placed,
        out_specs=(P(), P(), P(), P(), P(), P(), P()),
        check_vma=False,
    )
```

```python
import functools

import jax
import jax.numpy as jnp
from jax import lax
from jax.experimental import pallas as pl
from jax.experimental.pallas import tpu as pltpu
from jax.sharding import PartitionSpec as P

KERNEL = 7
HALF = KERNEL // 2
NEWTON_STEPS = 5
LANES = 128
GROUPS = 8
EDGE = 8
TAPS_ROWS = 64
SIDE = 4
FILL_ROWS = 4
PARTS = (4, 3, 4)

epsilon = 1e-05
loss_scale = 64.0
narrow = jnp.bfloat16
wide = jnp.float32


def params(megabytes):
    return pltpu.CompilerParams(vmem_limit_bytes=megabytes * 1024 * 1024)


def swap(value, axis, shift):
    count = lax.axis_size(axis)
    return lax.ppermute(value, axis, [(i, i ^ shift) for i in range(count)])


def is_upper(axis, shift):
    return (lax.axis_index(axis) & shift) != 0


def tree_sum(terms):
    while len(terms) > 1:
        terms = [terms[i] + terms[i + 1] for i in range(0, len(terms), 2)]
    return terms[0]


def exchange(value, axis, shift, sent_as):
    sent = value.astype(sent_as)
    return sent.astype(wide) + swap(sent, axis, shift).astype(wide)


def exchange_all(value, axis, sent_as):
    sent = value.astype(sent_as)
    moved = [sent] + [swap(sent, axis, shift) for shift in range(1, lax.axis_size(axis))]
    return tree_sum([part.astype(wide) for part in moved])


def square_pairs(axes, shifts):
    counts = [lax.axis_size(axis) for axis in axes]
    return {
        2 * first + second: [
            (i * counts[1] + j, (i ^ (first * shifts[0])) * counts[1] + (j ^ (second * shifts[1])))
            for i in range(counts[0])
            for j in range(counts[1])
        ]
        for first, second in ((0, 1), (1, 0), (1, 1))
    }


def square_scatter(value, axes, pairs, places, sent_as):
    pieces = value.reshape((4, value.shape[0] // 4) + value.shape[1:])

    def piece(turn):
        starts = (places[turn],) + (0,) * value.ndim
        sizes = (1,) + pieces.shape[1:]
        return lax.dynamic_slice(pieces, starts, sizes, allow_negative_indices=False)[0]

    moved = [
        lax.ppermute(piece(turn).astype(sent_as), axes, pairs[turn]).astype(wide)
        for turn in (1, 2, 3)
    ]
    return tree_sum([piece(0)] + moved)


def square_gather(value, axes, pairs, places):
    whole = jnp.zeros((4,) + value.shape, value.dtype)
    for turn in range(4):
        part = lax.ppermute(value, axes, pairs[turn]) if turn else value
        starts = (places[turn],) + (0,) * value.ndim
        whole = lax.dynamic_update_slice(whole, part[None], starts, allow_negative_indices=False)
    return whole.reshape((-1,) + value.shape[1:])


def doublings(axis, first=1):
    found = []
    shift = first
    while shift < lax.axis_size(axis):
        found.append(shift)
        shift *= 2
    return found


def next_along(value, axis):
    return lax.ppermute(value, axis, [(i, i + 1) for i in range(lax.axis_size(axis) - 1)])


def back_along(value, axis):
    return lax.ppermute(value, axis, [(i + 1, i) for i in range(lax.axis_size(axis) - 1)])


def spread_columns(source, target):
    for group in range(target.shape[0]):
        target[group] = source[pl.ds(EDGE - HALF + group, GROUPS, stride=GROUPS), :]


def fill_row(wide_row, middle, left, right):
    cols = middle.shape[0]
    wide_row[EDGE : EDGE + cols, :] = middle.astype(wide)
    wide_row[EDGE - HALF : EDGE, :] = left.astype(wide)
    wide_row[EDGE + cols : EDGE + cols + HALF, :] = right.astype(wide)


def lanes_of(tile):
    return pl.ds(pl.multiple_of(tile * LANES, LANES), LANES)


def part_starts():
    starts, total = {}, 0
    for row_part in range(3):
        for col_part in range(3):
            starts[row_part, col_part] = total
            total += PARTS[row_part] * PARTS[col_part]
    return starts, total


FILTERS, PRODUCTS = part_starts()


def part_taps(taps):
    even, odd = taps[0::2], taps[1::2]
    both = [a + b for a, b in zip(even, odd)] + even[len(odd) :]
    return even, odd, both


def spread_weights(weight_ref, filters, tile, lanes):
    rows = []
    for row_tap in range(KERNEL):
        row = [weight_ref[row_tap, tap : tap + 1, lanes] for tap in range(KERNEL)]
        rows.append([jnp.broadcast_to(tap, (GROUPS, LANES)) for tap in row])
    columns = [part_taps([rows[tap][col] for tap in range(KERNEL)]) for col in range(KERNEL)]
    for row_part, many in enumerate(PARTS):
        for row in range(many):
            line = [columns[col][row_part][row] for col in range(KERNEL)]
            for col_part, taps in enumerate(part_taps(line)):
                start = FILTERS[row_part, col_part] + row * PARTS[col_part]
                for col, value in enumerate(taps):
                    filters[tile, start + col] = value


def fill_parts(load, parts, row_pairs, groups):
    for pair in range(row_pairs):
        for group in range(groups):
            middle = load(2 * pair + 1, group)
            parts[0, pair, group] = load(2 * pair, group) - middle
            if pair < row_pairs - 1:
                parts[1, pair, group] = load(2 * pair + 2, group) - middle


def part_line(load, parts, row_part, col_part, pair, many):
    def value(group):
        return load(2 * pair + 1, group) if row_part == 2 else parts[row_part, pair, group]

    first = (0, 2, 1)[col_part]
    line = [value(2 * col + first) for col in range(many)]
    if col_part < 2:
        line = [side - value(2 * col + 1) for col, side in enumerate(line)]
    return line


def conv_rows(load, filters, tile, bias, steps, count, parts, products):
    row_pairs, col_pairs = count // 2, steps // 2
    fill_parts(load, parts, row_pairs + 3, 2 * col_pairs + 6)
    for row_part in range(3):
        for col_part in range(3):
            start = FILTERS[row_part, col_part]
            many_rows, many_cols = PARTS[row_part], PARTS[col_part]
            total = [[None] * col_pairs for _ in range(row_pairs)]
            for place in range(row_pairs + many_rows - 1):
                line = part_line(
                    load, parts, row_part, col_part, place, col_pairs + many_cols - 1
                )
                for row in range(row_pairs):
                    tap_row = place - row
                    if not 0 <= tap_row < many_rows:
                        continue
                    for tap_col in range(many_cols):
                        scale = filters[tile, start + tap_row * many_cols + tap_col]
                        for col in range(col_pairs):
                            term = line[col + tap_col] * scale
                            old = total[row][col]
                            total[row][col] = term if old is None else old + term
            for row in range(row_pairs):
                for col in range(col_pairs):
                    products[3 * row_part + col_part, row, col] = total[row][col]
    found = []
    for row in range(row_pairs):
        lines = [[], []]
        for col in range(col_pairs):
            values = [products[part, row, col] for part in range(9)]
            shared = [values[6] + values[8] + bias, values[7] + values[8] + bias]
            for row_part in range(2):
                for col_part in range(2):
                    own = values[3 * row_part + col_part] + values[3 * row_part + 2]
                    lines[row_part].append(own + shared[col_part])
        found += lines[0] + lines[1]
    return jnp.concatenate(found, axis=0).astype(narrow)


def parts_scratch(count, steps):
    row_pairs, col_pairs = count // 2, steps // 2
    return [
        pltpu.VMEM((2, row_pairs + 3, 2 * col_pairs + 6, GROUPS, LANES), wide),
        pltpu.VMEM((9, row_pairs, col_pairs, GROUPS, LANES), wide),
    ]


def reduce_part(conv_out, reduce_ref, reduce_bias_ref, before_out, feat_out):
    before = jnp.dot(conv_out[...], reduce_ref[...], preferred_element_type=wide)
    before = before + reduce_bias_ref[...]
    before_out[...] = before
    feat_out[...] = (before / (1.0 + jnp.exp(-before))).astype(narrow)
    feat = feat_out[...]
    gram = lax.dot_general(feat, feat, (((0,), (0,)), ((), ())), preferred_element_type=wide)
    return gram, jnp.sum(feat.astype(wide), axis=0, keepdims=True)


def inner_kernel(
    block, left, right, weight, bias, reduce_weight, reduce_bias,
    spread_out, filters, conv_out, before_out, feat_out, gram_out, colsum_out,
    wide_row, parts, products,
):
    rows, cols = block.shape[0], block.shape[1]
    steps = cols // GROUPS

    def one_tile(tile, _):
        lanes = lanes_of(tile)
        spread_weights(weight, filters, tile, lanes)
        start_value = jnp.broadcast_to(bias[0:1, lanes], (GROUPS, LANES))

        def fill(turn, _):
            for row in range(FILL_ROWS):
                row = turn * FILL_ROWS + row
                place = wide_row.at[row]
                fill_row(place, block[row, :, lanes], left[row, :, lanes], right[row, :, lanes])
                spread_columns(place, spread_out.at[tile, row])
            return 0

        lax.fori_loop(0, rows // FILL_ROWS, fill, 0)

        def load(row, group):
            return spread_out[tile, row + SIDE - HALF, group]

        conv_out[:, lanes] = conv_rows(
            load, filters, tile, start_value, steps, rows - 2 * SIDE, parts, products
        )
        return 0

    lax.fori_loop(0, spread_out.shape[0], one_tile, 0)
    gram_out[...], colsum_out[...] = reduce_part(
        conv_out, reduce_weight, reduce_bias, before_out, feat_out
    )


def edge_kernel(
    flag, spread_in, top, bottom, filters, bias, reduce_weight,
    reduce_bias, gram_in, colsum_in,
    spread_top, spread_bottom, conv_out, before_out, feat_out, kept_out, sent_out,
    wide_row, stage, parts, products, sums,
):
    rows, cols = spread_in.shape[1], wide_row.shape[1] - 2 * EDGE
    steps = cols // GROUPS

    def one_tile(tile, _):
        lanes = lanes_of(tile)
        start_value = jnp.broadcast_to(bias[0:1, lanes], (GROUPS, LANES))
        for side, (strip, spread) in enumerate(((top, spread_top), (bottom, spread_bottom))):
            stage[side] = strip[:, lanes].astype(wide)
            for row in range(HALF):
                place = wide_row.at[side * HALF + row]
                left = HALF * cols + row * HALF
                right = left + HALF * HALF
                fill_row(
                    place,
                    stage[side, row * cols : (row + 1) * cols, :],
                    stage[side, left : left + HALF, :],
                    stage[side, right : right + HALF, :],
                )
                spread_columns(place, spread.at[tile, row])

        def load_from(row):
            def load(row_tap, group):
                place = row + row_tap - HALF
                if place < 0:
                    return spread_top[tile, place + HALF, group]
                if place >= rows:
                    return spread_bottom[tile, place - rows, group]
                return spread_in[tile, place, group]

            return load

        for side, row in enumerate((0, rows - SIDE)):
            start = side * SIDE * cols
            conv_out[start : start + SIDE * cols, lanes] = conv_rows(
                load_from(row), filters, tile, start_value, steps, SIDE,
                parts.at[side], products.at[side],
            )
        return 0

    lax.fori_loop(0, spread_in.shape[0], one_tile, 0)
    gram, colsum = reduce_part(conv_out, reduce_weight, reduce_bias, before_out, feat_out)
    gram = gram + gram_in[...]
    colsum = colsum + colsum_in[...]
    half = gram.shape[0] // 2
    row = lax.broadcasted_iota(jnp.int32, (half, half), 0)
    col = lax.broadcasted_iota(jnp.int32, (half, half), 1)
    last_block = gram[half:, half:]
    diagonal = jnp.sum(jnp.where(row == col, last_block, 0.0), axis=0, keepdims=True)
    sums[:half, :half] = gram[:half, half:]
    sums[:half, half:] = jnp.where(row <= col, gram[:half, :half], last_block)
    sums[half : half + GROUPS, :] = jnp.broadcast_to(colsum, (GROUPS, 2 * half))
    sums[half + GROUPS :, :half] = jnp.broadcast_to(diagonal, (GROUPS, half))
    sums[half + GROUPS :, half:] = jnp.zeros((GROUPS, half), wide)
    part = kept_out.shape[0]
    keep_or_send(flag[0] != 0, sums[:part, :], sums[part:, :], kept_out, sent_out)


def keep_or_send(upper, low, high, kept_out, sent_out):
    kept_out[...] = jnp.where(upper, high, low)
    sent_out[...] = jnp.where(upper, low, high).astype(sent_out.dtype)


def edge_rows(rows):
    return list(range(SIDE)) + list(range(rows - SIDE, rows))


def shape_of(shape, dtype=wide):
    return jax.ShapeDtypeStruct(shape, dtype)


in_vmem = pl.BlockSpec(memory_space=pltpu.VMEM)
in_smem = pl.BlockSpec(memory_space=pltpu.SMEM)


def cost(microseconds):
    return pl.CostEstimate(
        flops=microseconds * 10**9, bytes_accessed=microseconds * 10**6, transcendentals=0
    )


def conv_inner(block, left, right, weight, bias, reduce_weight, reduce_bias):
    rows, cols, channels = block.shape
    width = reduce_weight.shape[1]
    tiles = channels // LANES
    steps = cols // GROUPS
    pixels = (rows - 2 * SIDE) * cols
    return pl.pallas_call(
        inner_kernel,
        in_specs=[in_vmem] * 7,
        out_specs=[in_vmem] * 7,
        out_shape=[
            shape_of((tiles, rows, steps + KERNEL - 1, GROUPS, LANES)),
            shape_of((tiles, PRODUCTS, GROUPS, LANES)),
            shape_of((pixels, channels), narrow),
            shape_of((pixels, width)),
            shape_of((pixels, width), narrow),
            shape_of((width, width)),
            shape_of((1, width)),
        ],
        scratch_shapes=[
            pltpu.VMEM((rows, cols + 2 * EDGE, LANES), wide),
            *parts_scratch(rows - 2 * SIDE, steps),
        ],
        compiler_params=params(24),
        cost_estimate=cost(10),
        name="conv_inner",
    )(block, left, right, weight, bias, reduce_weight, reduce_bias)


def conv_edge(flag, spread, halos, filters, bias, reduce_weight, reduce_bias, gram, colsum):
    tiles, rows, groups = spread.shape[:3]
    cols = (groups - KERNEL + 1) * GROUPS
    channels, width = reduce_weight.shape
    pixels = 2 * SIDE * cols
    parts, products = parts_scratch(SIDE, cols // GROUPS)
    side = (tiles, HALF, groups, GROUPS, LANES)
    sums_rows = width // 2 + 2 * GROUPS
    return pl.pallas_call(
        edge_kernel,
        in_specs=[in_smem] + [in_vmem] * 9,
        out_specs=[in_vmem] * 7,
        out_shape=[
            shape_of(side),
            shape_of(side),
            shape_of((pixels, channels), narrow),
            shape_of((pixels, width)),
            shape_of((pixels, width), narrow),
            shape_of((sums_rows // 2, width)),
            shape_of((sums_rows // 2, width)),
        ],
        scratch_shapes=[
            pltpu.VMEM((2 * HALF, cols + 2 * EDGE, LANES), wide),
            pltpu.VMEM((2,) + (halos[0].shape[0], LANES), wide),
            pltpu.VMEM((2,) + parts.shape, wide),
            pltpu.VMEM((2,) + products.shape, wide),
            pltpu.VMEM((sums_rows, width), wide),
        ],
        compiler_params=params(24),
        cost_estimate=cost(6),
        name="conv_edge",
    )(flag, spread, *halos, filters, bias, reduce_weight, reduce_bias, gram, colsum)


def split(value):
    high = value.astype(narrow)
    return high, (value - high.astype(wide)).astype(narrow)


def product(left, right):
    def dot(a, b):
        return jnp.dot(a, b, preferred_element_type=wide)

    return dot(left[0], right[0]) + (dot(left[0], right[1]) + dot(left[1], right[0]))


def square_root(current):
    size = current.shape[0]
    row = lax.broadcasted_iota(jnp.int32, (size, size), 0)
    col = lax.broadcasted_iota(jnp.int32, (size, size), 1)
    triple = jnp.where(row == col, 3.0, 0.0)
    factor = split(0.5 * (triple - current))
    current = split(current)
    trail = [(current, None, factor)]
    inverse = factor
    current = split(product(current, factor))
    for step in range(1, NEWTON_STEPS):
        factor = split(0.5 * (triple - product(inverse, current)))
        trail.append((current, inverse, factor))
        last = step == NEWTON_STEPS - 1
        if not last:
            inverse = split(product(factor, inverse))
        current = product(current, factor)
        if not last:
            current = split(current)
    return current, trail


def square_root_change(change, trail):
    first, _, factor = trail[0]
    move = split(change)
    factor_move = split(-0.5 * change)
    change = product(move, factor) + product(first, factor_move)
    inverse_move = factor_move
    for step in range(1, NEWTON_STEPS):
        current, inverse, factor = trail[step]
        move = split(change)
        factor_move = split(
            -0.5 * (product(inverse_move, current) + product(inverse, move))
        )
        change = product(move, factor) + product(current, factor_move)
        if step < NEWTON_STEPS - 1:
            inverse_move = split(product(factor_move, inverse) + product(factor, inverse_move))
    return change


def head_kernel(
    flag, label, class_bias, own, other, class_weight,
    feat_inner, feat_edge, gate_inner, gate_edge, conv_turned, reduce_turned,
    root_out, payload, conv_inner_out, conv_edge_out,
    sums, pre, *, count, image_count,
):
    width = root_out.shape[1]
    half = width // 2
    rows = own.shape[0]
    upper = flag[0] != 0
    mine, theirs = own[...], other[...]
    sums[:rows, :] = jnp.where(upper, theirs, mine)
    sums[rows:, :] = jnp.where(upper, mine, theirs)
    row = lax.broadcasted_iota(jnp.int32, (half, half), 0)
    col = lax.broadcasted_iota(jnp.int32, (half, half), 1)
    cross, mixed = sums[:half, :half], sums[:half, half:]
    turned = mixed.T
    first = jnp.where(row <= col, mixed, turned)
    diagonal = jnp.broadcast_to(sums[half + GROUPS : half + GROUPS + 1, :half], (half, half))
    last = jnp.where(row == col, diagonal, jnp.where(row > col, mixed, turned))
    gram = jnp.concatenate(
        [
            jnp.concatenate([first, cross], axis=1),
            jnp.concatenate([cross.T, last], axis=1),
        ],
        axis=0,
    )
    mean_row = sums[half : half + 1, :] / count
    mean_col = jnp.broadcast_to(mean_row, (width, width)).T
    sigma = gram / count - mean_col * mean_row
    row = lax.broadcasted_iota(jnp.int32, (width, width), 0)
    col = lax.broadcasted_iota(jnp.int32, (width, width), 1)
    diagonal = row == col
    trace_value = jnp.sum(jnp.where(diagonal, sigma, 0.0), keepdims=True) + epsilon
    root_scale = jnp.sqrt(trace_value)
    unit, trail = square_root(sigma / trace_value)
    root = root_scale * unit
    root_out[:width, :] = root

    classes = class_weight.shape[0]
    slots = root_out.shape[0] - width
    place = lax.broadcasted_iota(jnp.int32, (slots, 1), 0)
    bias = jnp.zeros((slots, 1), wide)
    for index in range(classes):
        bias = jnp.where(place == index, class_bias[index], bias)
    partial = [
        jnp.sum(class_weight[index].astype(wide) * root, axis=0, keepdims=True)
        for index in range(classes)
    ]
    partial.append(jnp.zeros((slots - classes, width), wide))
    logits = jnp.sum(jnp.concatenate(partial, axis=0), axis=1, keepdims=True) + bias
    onehot = jnp.where(place == label[0], 1.0, 0.0)
    soft = jnp.maximum(logits, 0.0) + jnp.log(1.0 + jnp.exp(-jnp.abs(logits)))
    share = 1.0 / (1.0 + jnp.exp(-logits))
    used = place < classes
    loss_part = jnp.sum(jnp.where(used, soft - onehot * logits, 0.0), keepdims=True)
    logit_grad = jnp.where(used, loss_scale * (share - onehot) / image_count, 0.0)
    root_out[width:, :] = jnp.broadcast_to(
        jnp.where(place == classes, loss_part, logit_grad), (slots, width)
    )
    across = lax.broadcasted_iota(jnp.int32, (slots, width), 1)
    facts = jnp.where(place == classes, loss_part, logit_grad)
    root_out[width + slots - 1 :, :] = jnp.sum(
        jnp.where(across == place, facts, 0.0), axis=0, keepdims=True
    )

    root_grad = jnp.zeros((width, width), wide)
    for index in range(classes):
        root_grad = root_grad + class_weight[index].astype(wide) * logit_grad[index : index + 1, :]
    root_grad = root_grad + root_grad.T
    change = square_root_change(root_scale * root_grad, trail)
    trace_grad = jnp.sum(root_grad * unit, keepdims=True) / (2.0 * root_scale) - jnp.sum(
        change * sigma, keepdims=True
    ) / (trace_value * trace_value)
    symmetric = (
        (change / trace_value + jnp.where(diagonal, trace_grad, 0.0)) / count
    ).astype(narrow)
    mean_term = jnp.sum(mean_col * symmetric.astype(wide), axis=0, keepdims=True)

    inner = feat_inner.shape[0]
    for feat, gate, start in ((feat_inner, gate_inner, 0), (feat_edge, gate_edge, inner)):
        grad = jnp.dot(feat[...], symmetric, preferred_element_type=wide) - mean_term
        pre[start : start + feat.shape[0], :] = (grad * gate[...]).astype(narrow)
    pre_grad = pre[...]
    payload[width:, :] = jnp.zeros((payload.shape[0] - width, payload.shape[1]), wide)
    taps = KERNEL * KERNEL
    payload[width + taps + 1 : width + taps + 2, :width] = jnp.sum(
        pre_grad.astype(wide), axis=0, keepdims=True
    )
    for first in range(0, conv_turned.shape[0], width):
        payload[:width, first : first + width] = jnp.dot(
            conv_turned[first : first + width, :], pre_grad, preferred_element_type=wide
        )
    for out, start in ((conv_inner_out, 0), (conv_edge_out, inner)):
        out[...] = jnp.dot(
            pre[start : start + out.shape[0], :], reduce_turned[...], preferred_element_type=wide
        ).astype(narrow)


def head(flag, label, class_bias, own, other, class_weight, prepared, count, image_count):
    feat_inner, feat_edge, gate_inner, gate_edge, conv_turned, reduce_turned = prepared
    width, channels = reduce_turned.shape
    inner, edge = feat_inner.shape[0], feat_edge.shape[0]
    slots = -(-(class_weight.shape[0] + 2) // GROUPS) * GROUPS
    return pl.pallas_call(
        functools.partial(head_kernel, count=count, image_count=image_count),
        in_specs=[in_smem] * 3 + [in_vmem] * 9,
        out_specs=[in_vmem] * 4,
        out_shape=[
            shape_of((width + slots, width)),
            shape_of((width + TAPS_ROWS, channels)),
            shape_of((inner, channels), narrow),
            shape_of((edge, channels), narrow),
        ],
        scratch_shapes=[
            pltpu.VMEM((2 * own.shape[0], width), wide),
            pltpu.VMEM((inner + edge, width), narrow),
        ],
        compiler_params=params(24),
        cost_estimate=cost(10),
        name="head",
    )(
        flag, label, class_bias, own, other, class_weight,
        feat_inner, feat_edge, gate_inner, gate_edge, conv_turned, reduce_turned,
    )


def prepare_kernel(
    before_inner, before_edge, conv_inner_in, conv_edge_in, reduce_weight,
    gate_inner, gate_edge, conv_turned, reduce_turned,
):
    for before, gate in ((before_inner, gate_inner), (before_edge, gate_edge)):
        value = before[...]
        share = 1.0 / (1.0 + jnp.exp(-value))
        gate[...] = share * (1.0 + value * (1.0 - share))
    inner = conv_inner_in.shape[0]
    conv_turned[:, :inner] = conv_inner_in[...].T
    conv_turned[:, inner:] = conv_edge_in[...].T
    reduce_turned[...] = reduce_weight[...].T


def prepare(before_inner, before_edge, conv_in, conv_ed, reduce_weight):
    channels, width = reduce_weight.shape
    inner, edge = before_inner.shape[0], before_edge.shape[0]
    return pl.pallas_call(
        prepare_kernel,
        in_specs=[in_vmem] * 5,
        out_specs=[in_vmem] * 4,
        out_shape=[
            shape_of((inner, width)),
            shape_of((edge, width)),
            shape_of((channels, inner + edge), narrow),
            shape_of((width, channels), narrow),
        ],
        compiler_params=params(16),
        cost_estimate=cost(1),
        name="prepare",
    )(before_inner, before_edge, conv_in, conv_ed, reduce_weight)


def taps_kernel(
    spread_in, spread_top, spread_bottom, grad_inner, grad_edge, payload_in, payload,
    parts, grads, products, out, *, first, last,
):
    rows = spread_in.shape[1]
    row_pairs, col_pairs = grads.shape[1:3]
    steps = 2 * col_pairs
    cols = steps * GROUPS
    order = edge_rows(rows)
    taps = KERNEL * KERNEL
    base = payload.shape[0] - TAPS_ROWS

    def one_tile(tile, _):
        lanes = lanes_of(tile)

        def grad_row(row):
            if row in order:
                source, place = grad_edge, order.index(row)
            else:
                source, place = grad_inner, row - SIDE
            values = source[place * cols : (place + 1) * cols, lanes].astype(wide)
            return [values[step * GROUPS : (step + 1) * GROUPS, :] for step in range(steps)]

        for pair in range(row_pairs):
            even, odd = grad_row(2 * pair), grad_row(2 * pair + 1)
            both = [a + b for a, b in zip(even, odd)]
            for row_part, line in enumerate((even, odd, both)):
                for col in range(col_pairs):
                    grads[3 * row_part, pair, col] = line[2 * col]
                    grads[3 * row_part + 1, pair, col] = line[2 * col + 1]
                    grads[3 * row_part + 2, pair, col] = line[2 * col] + line[2 * col + 1]

        def load(place, group):
            place = place - HALF
            if place < 0:
                return spread_top[tile, place + HALF, group]
            if place >= rows:
                return spread_bottom[tile, place - rows, group]
            return spread_in[tile, place, group]

        fill_parts(load, parts, row_pairs + 3, 2 * col_pairs + 6)
        for row_part in range(3):
            for col_part in range(3):
                part = 3 * row_part + col_part
                start = FILTERS[row_part, col_part]
                many_rows, many_cols = PARTS[row_part], PARTS[col_part]
                total = {}
                for place in range(row_pairs + many_rows - 1):
                    line = part_line(
                        load, parts, row_part, col_part, place, col_pairs + many_cols - 1
                    )
                    for tap_row in range(many_rows):
                        row = place - tap_row
                        if not 0 <= row < row_pairs:
                            continue
                        for col in range(col_pairs):
                            grad = grads[part, row, col]
                            for tap_col in range(many_cols):
                                term = line[col + tap_col] * grad
                                tap = tap_row * many_cols + tap_col
                                total[tap] = total[tap] + term if tap in total else term
                for tap, value in total.items():
                    products[start + tap] = value

        for row_tap in range(KERNEL):
            for col_tap in range(KERNEL):
                place = (row_tap // 2, col_tap // 2)
                found = None
                for row_part in (row_tap % 2, 2):
                    for col_part in (col_tap % 2, 2):
                        start = FILTERS[row_part, col_part]
                        value = products[start + place[0] * PARTS[col_part] + place[1]]
                        found = value if found is None else found + value
                tap = row_tap * KERNEL + col_tap
                out[tap : tap + 1, :] = jnp.sum(found, axis=0, keepdims=True)
        found = [
            sum(grads[8, pair, col] for col in range(1, col_pairs)) + grads[8, pair, 0]
            for pair in range(row_pairs)
        ]
        out[taps : taps + 1, :] = jnp.sum(sum(found[1:], found[0]), axis=0, keepdims=True)
        payload[pl.ds(base, taps + 1), lanes] = out[: taps + 1, :]
        return 0

    lax.fori_loop(first, last, one_tile, 0)


def tap_grads(spreads, grads, payload, first, last):
    rows, groups = spreads[0].shape[1:3]
    row_pairs, col_pairs = rows // 2, (groups - KERNEL + 1) // 2
    return pl.pallas_call(
        functools.partial(taps_kernel, first=first, last=last),
        in_specs=[in_vmem] * 6,
        out_specs=in_vmem,
        out_shape=shape_of(payload.shape),
        input_output_aliases={5: 0},
        scratch_shapes=[
            pltpu.VMEM((2, row_pairs + 3, 2 * col_pairs + 6, GROUPS, LANES), wide),
            pltpu.VMEM((9, row_pairs, col_pairs, GROUPS, LANES), wide),
            pltpu.VMEM((PRODUCTS, GROUPS, LANES), wide),
            pltpu.VMEM((TAPS_ROWS, LANES), wide),
        ],
        compiler_params=params(16),
        cost_estimate=cost(2 * (last - first)),
        name="tap_grads",
    )(*spreads, *grads, payload)


def finish_kernel(flag, own, other, *refs, image_count):
    known = refs[:-7]
    weight_out, depth_out, depth_bias_out, bias_out, class_bias_out, loss_out, payload = refs[-7:]
    part = own.shape[0]
    upper = flag[0] != 0
    mine, theirs = own[...].astype(wide), other[...].astype(wide)
    payload[:part, :] = jnp.where(upper, theirs, mine)
    payload[part:, :] = jnp.where(upper, mine, theirs)
    width = weight_out.shape[1]
    for first in range(0, weight_out.shape[0], width):
        weight_out[first : first + width, :] = payload[:width, first : first + width]
    for row_tap in range(KERNEL):
        start = width + row_tap * KERNEL
        depth_out[row_tap] = payload[start : start + KERNEL, :]
    taps = KERNEL * KERNEL
    depth_bias_out[...] = payload[width + taps, :]
    bias_out[...] = payload[width + taps + 1, :width]
    totals = tree_sum([part[part.shape[0] - 1 :, :] for part in known])
    classes = class_bias_out.shape[0]
    class_bias_out[...] = totals[0, :classes]
    across = lax.broadcasted_iota(jnp.int32, totals.shape, 1)
    loss_out[0] = jnp.sum(jnp.where(across == classes, totals, 0.0)) / image_count


def finish(flag, own, other, known, width, classes, image_count):
    part, channels = own.shape
    return pl.pallas_call(
        functools.partial(finish_kernel, image_count=image_count),
        in_specs=[in_smem] + [in_vmem] * (2 + len(known)),
        out_specs=[in_vmem] * 5 + [in_smem],
        out_shape=[
            shape_of((channels, width)),
            shape_of((KERNEL, KERNEL, channels)),
            shape_of((channels,)),
            shape_of((width,)),
            shape_of((classes,)),
            shape_of((1,)),
        ],
        scratch_shapes=[pltpu.VMEM((2 * part, channels), wide)],
        compiler_params=params(8),
        cost_estimate=cost(1),
        name="finish",
    )(flag, own, other, *known)


def edge_strip(block, left, right, rows):
    channels = block.shape[2]
    return jnp.concatenate([part[rows].reshape(-1, channels) for part in (block, left, right)])


def body(
    features, depth_weight, depth_bias, reduce_weight, reduce_bias, class_weight, class_bias, labels
):
    together = lax.optimization_barrier
    block = features[0]
    rows, cols, channels = block.shape
    width = reduce_weight.shape[1]
    classes = class_bias.shape[0]
    count = rows * cols * lax.axis_size("sy") * lax.axis_size("sx")
    image_count = features.shape[0] * lax.axis_size("dp")

    flag = is_upper("sx", 1).astype(jnp.int32)[None]
    upper = is_upper("sx", 1)
    corner = 2 * (lax.axis_index("dp") & 1) + ((lax.axis_index("sx") & 2) >> 1)
    places = [corner ^ turn for turn in range(4)]
    bias_row = depth_bias[None]
    reduce_row = reduce_bias[None]
    left = next_along(block[:, cols - HALF :], "sx")
    right = back_along(block[:, :HALF], "sx")
    low, high, left, right, flag, upper, places, bias_row, reduce_row = together(
        (
            edge_strip(block, left, right, slice(rows - HALF, rows)),
            edge_strip(block, left, right, slice(0, HALF)),
            left,
            right,
            flag,
            upper,
            places,
            bias_row,
            reduce_row,
        )
    )
    top = next_along(low, "sy")
    bottom = back_along(high, "sy")
    spread, filters, conv_in, before_in, feat_in, gram, colsum = conv_inner(
        block, left, right, depth_weight, bias_row, reduce_weight, reduce_row
    )
    spread_top, spread_bottom, conv_ed, before_ed, feat_ed, kept, sent = conv_edge(
        flag, spread, (top, bottom), filters, bias_row, reduce_weight, reduce_row, gram, colsum
    )

    sums = kept + swap(sent, "sx", 1)
    sums, before_in, before_ed, conv_in, conv_ed = together(
        (sums, before_in, before_ed, conv_in, conv_ed)
    )
    gate_in, gate_ed, conv_turned, reduce_turned = prepare(
        before_in, before_ed, conv_in, conv_ed, reduce_weight
    )
    for shift in doublings("sx", 2):
        sums = exchange(sums, "sx", shift, wide)
    sums, gate_in, gate_ed, conv_turned, reduce_turned = together(
        (sums, gate_in, gate_ed, conv_turned, reduce_turned)
    )
    for shift in doublings("sy"):
        sums = exchange(sums, "sy", shift, wide)
    other = swap(sums, "sx", 1)

    root, payload, *grads = head(
        flag,
        labels,
        class_bias,
        sums,
        other,
        class_weight,
        (feat_in, feat_ed, gate_in, gate_ed, conv_turned, reduce_turned),
        count,
        image_count,
    )
    known = [root] + [swap(root, "dp", shift) for shift in range(1, lax.axis_size("dp"))]
    spreads = (spread, spread_top, spread_bottom)
    tiles = channels // LANES
    payload = tap_grads(spreads, grads, payload, 0, tiles - 1)
    payload, known = together((payload, known))
    payload = tap_grads(spreads, grads, payload, tiles - 1, tiles)

    part = payload.shape[0] // 2
    low, high = payload[:part], payload[part:]
    kept, sent = jnp.where(upper, high, low), jnp.where(upper, low, high)
    payload = kept + swap(sent.astype(narrow), "sx", 1).astype(wide)
    axes = ("dp", "sx")
    pairs = square_pairs(axes, (1, 2))
    payload = square_scatter(payload, axes, pairs, places, narrow)
    for shift in doublings("dp", 2):
        payload = exchange(payload, "dp", shift, narrow)
    payload = exchange_all(payload, "sy", narrow).astype(narrow)
    payload, known = together((payload, known))
    class_weight_grad = tree_sum(
        [part[width : width + classes, 0][:, None, None] * part[None, :width] for part in known]
    )
    payload = square_gather(payload, axes, pairs, places)
    other, class_weight_grad = together((swap(payload, "sx", 1), class_weight_grad))
    weight_grad, depth_grad, depth_bias_grad, bias_grad, class_bias_grad, loss = finish(
        flag, payload, other, known, width, classes, image_count
    )
    return (
        loss[0],
        depth_grad,
        depth_bias_grad,
        weight_grad,
        bias_grad,
        class_weight_grad,
        class_bias_grad,
    )


def solution(mesh):
    placed = (P("dp", "sy", "sx", None), P(), P(), P(), P(), P(), P(), P("dp"))
    return jax.shard_map(
        body,
        mesh=mesh,
        in_specs=placed,
        out_specs=(P(), P(), P(), P(), P(), P(), P()),
        check_vma=False,
    )
```

```python
import functools

import jax
import jax.numpy as jnp
from jax import lax
from jax.experimental import pallas as pl
from jax.experimental.pallas import tpu as pltpu
from jax.sharding import PartitionSpec as P

KERNEL = 7
HALF = KERNEL // 2
NEWTON_STEPS = 5
LANES = 128
GROUPS = 8
EDGE = 8
TAPS_ROWS = 64
SIDE = 4
FILL_ROWS = 4
PARTS = (4, 3, 4)

epsilon = 1e-05
loss_scale = 64.0
narrow = jnp.bfloat16
wide = jnp.float32


def params(megabytes):
    return pltpu.CompilerParams(vmem_limit_bytes=megabytes * 1024 * 1024)


def swap(value, axis, shift):
    count = lax.axis_size(axis)
    return lax.ppermute(value, axis, [(i, i ^ shift) for i in range(count)])


def is_upper(axis, shift):
    return (lax.axis_index(axis) & shift) != 0


def tree_sum(terms):
    while len(terms) > 1:
        terms = [terms[i] + terms[i + 1] for i in range(0, len(terms), 2)]
    return terms[0]


def exchange(value, axis, shift, sent_as):
    sent = value.astype(sent_as)
    return sent.astype(wide) + swap(sent, axis, shift).astype(wide)


def square_pairs(axes, shifts):
    counts = [lax.axis_size(axis) for axis in axes]
    return {
        2 * first + second: [
            (i * counts[1] + j, (i ^ (first * shifts[0])) * counts[1] + (j ^ (second * shifts[1])))
            for i in range(counts[0])
            for j in range(counts[1])
        ]
        for first, second in ((0, 1), (1, 0), (1, 1))
    }


def square_scatter(value, axes, pairs, places, sent_as):
    pieces = value.reshape((4, value.shape[0] // 4) + value.shape[1:])

    def piece(turn):
        starts = (places[turn],) + (0,) * value.ndim
        sizes = (1,) + pieces.shape[1:]
        return lax.dynamic_slice(pieces, starts, sizes, allow_negative_indices=False)[0]

    moved = [
        lax.ppermute(piece(turn).astype(sent_as), axes, pairs[turn]).astype(wide)
        for turn in (1, 2, 3)
    ]
    return tree_sum([piece(0)] + moved)


def square_gather(value, axes, pairs, places):
    whole = jnp.zeros((4,) + value.shape, value.dtype)
    for turn in range(4):
        part = lax.ppermute(value, axes, pairs[turn]) if turn else value
        starts = (places[turn],) + (0,) * value.ndim
        whole = lax.dynamic_update_slice(whole, part[None], starts, allow_negative_indices=False)
    return whole.reshape((-1,) + value.shape[1:])


def doublings(axis, first=1):
    found = []
    shift = first
    while shift < lax.axis_size(axis):
        found.append(shift)
        shift *= 2
    return found


def next_along(value, axis):
    return lax.ppermute(value, axis, [(i, i + 1) for i in range(lax.axis_size(axis) - 1)])


def back_along(value, axis):
    return lax.ppermute(value, axis, [(i + 1, i) for i in range(lax.axis_size(axis) - 1)])


def spread_columns(source, target):
    for group in range(target.shape[0]):
        target[group] = source[pl.ds(EDGE - HALF + group, GROUPS, stride=GROUPS), :]


def fill_row(wide_row, middle, left, right):
    cols = middle.shape[0]
    wide_row[EDGE : EDGE + cols, :] = middle.astype(wide)
    wide_row[EDGE - HALF : EDGE, :] = left.astype(wide)
    wide_row[EDGE + cols : EDGE + cols + HALF, :] = right.astype(wide)


def lanes_of(tile):
    return pl.ds(pl.multiple_of(tile * LANES, LANES), LANES)


def part_starts():
    starts, total = {}, 0
    for row_part in range(3):
        for col_part in range(3):
            starts[row_part, col_part] = total
            total += PARTS[row_part] * PARTS[col_part]
    return starts, total


FILTERS, PRODUCTS = part_starts()


def part_taps(taps):
    even, odd = taps[0::2], taps[1::2]
    both = [a + b for a, b in zip(even, odd)] + even[len(odd) :]
    return even, odd, both


def spread_weights(weight_ref, filters, tile, lanes):
    rows = []
    for row_tap in range(KERNEL):
        row = [weight_ref[row_tap, tap : tap + 1, lanes] for tap in range(KERNEL)]
        rows.append([jnp.broadcast_to(tap, (GROUPS, LANES)) for tap in row])
    columns = [part_taps([rows[tap][col] for tap in range(KERNEL)]) for col in range(KERNEL)]
    for row_part, many in enumerate(PARTS):
        for row in range(many):
            line = [columns[col][row_part][row] for col in range(KERNEL)]
            for col_part, taps in enumerate(part_taps(line)):
                start = FILTERS[row_part, col_part] + row * PARTS[col_part]
                for col, value in enumerate(taps):
                    filters[tile, start + col] = value


def fill_parts(load, parts, row_pairs, groups):
    for pair in range(row_pairs):
        for group in range(groups):
            middle = load(2 * pair + 1, group)
            parts[0, pair, group] = load(2 * pair, group) - middle
            if pair < row_pairs - 1:
                parts[1, pair, group] = load(2 * pair + 2, group) - middle


def part_line(load, parts, row_part, col_part, pair, many):
    def value(group):
        return load(2 * pair + 1, group) if row_part == 2 else parts[row_part, pair, group]

    first = (0, 2, 1)[col_part]
    line = [value(2 * col + first) for col in range(many)]
    if col_part < 2:
        line = [side - value(2 * col + 1) for col, side in enumerate(line)]
    return line


def conv_rows(load, filters, tile, bias, steps, count, parts, products):
    row_pairs, col_pairs = count // 2, steps // 2
    fill_parts(load, parts, row_pairs + 3, 2 * col_pairs + 6)
    for row_part in range(3):
        for col_part in range(3):
            start = FILTERS[row_part, col_part]
            many_rows, many_cols = PARTS[row_part], PARTS[col_part]
            total = [[None] * col_pairs for _ in range(row_pairs)]
            for place in range(row_pairs + many_rows - 1):
                line = part_line(
                    load, parts, row_part, col_part, place, col_pairs + many_cols - 1
                )
                for row in range(row_pairs):
                    tap_row = place - row
                    if not 0 <= tap_row < many_rows:
                        continue
                    for tap_col in range(many_cols):
                        scale = filters[tile, start + tap_row * many_cols + tap_col]
                        for col in range(col_pairs):
                            term = line[col + tap_col] * scale
                            old = total[row][col]
                            total[row][col] = term if old is None else old + term
            for row in range(row_pairs):
                for col in range(col_pairs):
                    products[3 * row_part + col_part, row, col] = total[row][col]
    found = []
    for row in range(row_pairs):
        lines = [[], []]
        for col in range(col_pairs):
            values = [products[part, row, col] for part in range(9)]
            shared = [values[6] + values[8] + bias, values[7] + values[8] + bias]
            for row_part in range(2):
                for col_part in range(2):
                    own = values[3 * row_part + col_part] + values[3 * row_part + 2]
                    lines[row_part].append(own + shared[col_part])
        found += lines
    return found


def rounded(lines):
    return jnp.concatenate([part for line in lines for part in line], axis=0).astype(narrow)


def parts_scratch(count, steps):
    row_pairs, col_pairs = count // 2, steps // 2
    return [
        pltpu.VMEM((2, row_pairs + 3, 2 * col_pairs + 6, GROUPS, LANES), wide),
        pltpu.VMEM((9, row_pairs, col_pairs, GROUPS, LANES), wide),
    ]


def reduce_part(conv_out, reduce_ref, reduce_bias_ref, before_out, feat_out):
    before = jnp.dot(conv_out[...], reduce_ref[...], preferred_element_type=wide)
    before = before + reduce_bias_ref[...]
    before_out[...] = before
    feat_out[...] = (before / (1.0 + jnp.exp(-before))).astype(narrow)
    feat = feat_out[...]
    gram = lax.dot_general(feat, feat, (((0,), (0,)), ((), ())), preferred_element_type=wide)
    return gram, jnp.sum(feat.astype(wide), axis=0, keepdims=True)


def inner_kernel(
    block, left, right, weight, bias, reduce_weight, reduce_bias,
    spread_out, filters, conv_out, before_out, feat_out, gram_out, colsum_out, partial_out,
    wide_row, parts, products,
):
    rows, cols = block.shape[0], block.shape[1]
    steps = cols // GROUPS

    def one_tile(tile, _):
        lanes = lanes_of(tile)
        spread_weights(weight, filters, tile, lanes)
        start_value = jnp.broadcast_to(bias[0:1, lanes], (GROUPS, LANES))

        def fill(turn, _):
            for row in range(FILL_ROWS):
                row = turn * FILL_ROWS + row
                place = wide_row.at[row]
                fill_row(place, block[row, :, lanes], left[row, :, lanes], right[row, :, lanes])
                spread_columns(place, spread_out.at[tile, row])
            return 0

        lax.fori_loop(0, rows // FILL_ROWS, fill, 0)

        def load_from(first):
            def load(row, group):
                place = first + row - HALF
                if 0 <= place < rows:
                    return spread_out[tile, place, group]
                return jnp.zeros((GROUPS, LANES), wide)

            return load

        conv_out[:, lanes] = rounded(
            conv_rows(
                load_from(SIDE), filters, tile, start_value, steps, rows - 2 * SIDE, parts, products
            )
        )
        for side, first in enumerate((0, rows - SIDE)):
            lines = conv_rows(
                load_from(first), filters, tile, start_value, steps, SIDE, parts, products
            )
            for row, line in enumerate(lines):
                for step, value in enumerate(line):
                    partial_out[tile, side * SIDE + row, step] = value
        return 0

    lax.fori_loop(0, spread_out.shape[0], one_tile, 0)
    gram_out[...], colsum_out[...] = reduce_part(
        conv_out, reduce_weight, reduce_bias, before_out, feat_out
    )


def edge_kernel(
    flag, partial, top, bottom, filters, reduce_weight, reduce_bias, gram_in, colsum_in,
    spread_top, spread_bottom, conv_out, before_out, feat_out, kept_out, sent_out,
    wide_row, stage, sums,
):
    cols = wide_row.shape[1] - 2 * EDGE
    steps = cols // GROUPS

    def one_tile(tile, _):
        lanes = lanes_of(tile)
        for side, (strip, spread) in enumerate(((top, spread_top), (bottom, spread_bottom))):
            stage[side] = strip[:, lanes].astype(wide)
            for row in range(HALF):
                place = wide_row.at[side * HALF + row]
                left = HALF * cols + row * HALF
                right = left + HALF * HALF
                fill_row(
                    place,
                    stage[side, row * cols : (row + 1) * cols, :],
                    stage[side, left : left + HALF, :],
                    stage[side, right : right + HALF, :],
                )
                spread_columns(place, spread.at[tile, row])

        def filter_of(row_tap, col_tap):
            start = FILTERS[row_tap % 2, col_tap % 2]
            return filters[tile, start + row_tap // 2 * PARTS[col_tap % 2] + col_tap // 2]

        for side, spread in enumerate((spread_top, spread_bottom)):
            lines = [
                [partial[tile, side * SIDE + row, step] for step in range(steps)]
                for row in range(SIDE)
            ]
            for place in range(HALF):
                windows = [spread[tile, place, group] for group in range(steps + KERNEL - 1)]
                for row in range(SIDE):
                    row_tap = place - row if side == 0 else place + HALF + SIDE - row
                    if not 0 <= row_tap < KERNEL:
                        continue
                    for col_tap in range(KERNEL):
                        scale = filter_of(row_tap, col_tap)
                        for step in range(steps):
                            lines[row][step] = lines[row][step] + windows[step + col_tap] * scale
            start = side * SIDE * cols
            conv_out[start : start + SIDE * cols, lanes] = rounded(lines)
        return 0

    lax.fori_loop(0, partial.shape[0], one_tile, 0)
    gram, colsum = reduce_part(conv_out, reduce_weight, reduce_bias, before_out, feat_out)
    gram = gram + gram_in[...]
    colsum = colsum + colsum_in[...]
    half = gram.shape[0] // 2
    row = lax.broadcasted_iota(jnp.int32, (half, half), 0)
    col = lax.broadcasted_iota(jnp.int32, (half, half), 1)
    last_block = gram[half:, half:]
    diagonal = jnp.sum(jnp.where(row == col, last_block, 0.0), axis=0, keepdims=True)
    sums[:half, :half] = gram[:half, half:]
    sums[:half, half:] = jnp.where(row <= col, gram[:half, :half], last_block)
    sums[half : half + GROUPS, :] = jnp.broadcast_to(colsum, (GROUPS, 2 * half))
    sums[half + GROUPS :, :half] = jnp.broadcast_to(diagonal, (GROUPS, half))
    sums[half + GROUPS :, half:] = jnp.zeros((GROUPS, half), wide)
    part = kept_out.shape[0]
    keep_or_send(flag[0] != 0, sums[:part, :], sums[part:, :], kept_out, sent_out)


def keep_or_send(upper, low, high, kept_out, sent_out):
    kept_out[...] = jnp.where(upper, high, low)
    sent_out[...] = jnp.where(upper, low, high).astype(sent_out.dtype)


def edge_rows(rows):
    return list(range(SIDE)) + list(range(rows - SIDE, rows))


def shape_of(shape, dtype=wide):
    return jax.ShapeDtypeStruct(shape, dtype)


in_vmem = pl.BlockSpec(memory_space=pltpu.VMEM)
in_smem = pl.BlockSpec(memory_space=pltpu.SMEM)


def cost(microseconds):
    return pl.CostEstimate(
        flops=microseconds * 10**9, bytes_accessed=microseconds * 10**6, transcendentals=0
    )


def conv_inner(block, left, right, weight, bias, reduce_weight, reduce_bias):
    rows, cols, channels = block.shape
    width = reduce_weight.shape[1]
    tiles = channels // LANES
    steps = cols // GROUPS
    pixels = (rows - 2 * SIDE) * cols
    return pl.pallas_call(
        inner_kernel,
        in_specs=[in_vmem] * 7,
        out_specs=[in_vmem] * 8,
        out_shape=[
            shape_of((tiles, rows, steps + KERNEL - 1, GROUPS, LANES)),
            shape_of((tiles, PRODUCTS, GROUPS, LANES)),
            shape_of((pixels, channels), narrow),
            shape_of((pixels, width)),
            shape_of((pixels, width), narrow),
            shape_of((width, width)),
            shape_of((1, width)),
            shape_of((tiles, 2 * SIDE, steps, GROUPS, LANES)),
        ],
        scratch_shapes=[
            pltpu.VMEM((rows, cols + 2 * EDGE, LANES), wide),
            *parts_scratch(rows - 2 * SIDE, steps),
        ],
        compiler_params=params(24),
        cost_estimate=cost(10),
        name="conv_inner",
    )(block, left, right, weight, bias, reduce_weight, reduce_bias)


def conv_edge(flag, partial, halos, filters, reduce_weight, reduce_bias, gram, colsum):
    tiles, _, steps = partial.shape[:3]
    cols, groups = steps * GROUPS, steps + KERNEL - 1
    channels, width = reduce_weight.shape
    pixels = 2 * SIDE * cols
    side = (tiles, HALF, groups, GROUPS, LANES)
    sums_rows = width // 2 + 2 * GROUPS
    return pl.pallas_call(
        edge_kernel,
        in_specs=[in_smem] + [in_vmem] * 8,
        out_specs=[in_vmem] * 7,
        out_shape=[
            shape_of(side),
            shape_of(side),
            shape_of((pixels, channels), narrow),
            shape_of((pixels, width)),
            shape_of((pixels, width), narrow),
            shape_of((sums_rows // 2, width)),
            shape_of((sums_rows // 2, width)),
        ],
        scratch_shapes=[
            pltpu.VMEM((2 * HALF, cols + 2 * EDGE, LANES), wide),
            pltpu.VMEM((2,) + (halos[0].shape[0], LANES), wide),
            pltpu.VMEM((sums_rows, width), wide),
        ],
        compiler_params=params(24),
        cost_estimate=cost(6),
        name="conv_edge",
    )(flag, partial, *halos, filters, reduce_weight, reduce_bias, gram, colsum)


def split(value):
    high = value.astype(narrow)
    return high, (value - high.astype(wide)).astype(narrow)


def product(left, right):
    def dot(a, b):
        return jnp.dot(a, b, preferred_element_type=wide)

    return dot(left[0], right[0]) + (dot(left[0], right[1]) + dot(left[1], right[0]))


def square_root(current):
    size = current.shape[0]
    row = lax.broadcasted_iota(jnp.int32, (size, size), 0)
    col = lax.broadcasted_iota(jnp.int32, (size, size), 1)
    triple = jnp.where(row == col, 3.0, 0.0)
    factor = split(0.5 * (triple - current))
    current = split(current)
    trail = [(current, None, factor)]
    inverse = factor
    current = split(product(current, factor))
    for step in range(1, NEWTON_STEPS):
        factor = split(0.5 * (triple - product(inverse, current)))
        trail.append((current, inverse, factor))
        last = step == NEWTON_STEPS - 1
        if not last:
            inverse = split(product(factor, inverse))
        current = product(current, factor)
        if not last:
            current = split(current)
    return current, trail


def square_root_change(change, trail):
    first, _, factor = trail[0]
    move = split(change)
    factor_move = split(-0.5 * change)
    change = product(move, factor) + product(first, factor_move)
    inverse_move = factor_move
    for step in range(1, NEWTON_STEPS):
        current, inverse, factor = trail[step]
        move = split(change)
        factor_move = split(
            -0.5 * (product(inverse_move, current) + product(inverse, move))
        )
        change = product(move, factor) + product(current, factor_move)
        if step < NEWTON_STEPS - 1:
            inverse_move = split(product(factor_move, inverse) + product(factor, inverse_move))
    return change


def head_kernel(
    flag, label, class_bias, own, other, class_weight,
    feat_inner, feat_edge, gate_inner, gate_edge, conv_turned, reduce_turned,
    root_out, payload, conv_inner_out, conv_edge_out,
    sums, pre, *, count, image_count,
):
    width = root_out.shape[1]
    half = width // 2
    rows = own.shape[0]
    upper = flag[0] != 0
    mine, theirs = own[...], other[...]
    sums[:rows, :] = jnp.where(upper, theirs, mine)
    sums[rows:, :] = jnp.where(upper, mine, theirs)
    row = lax.broadcasted_iota(jnp.int32, (half, half), 0)
    col = lax.broadcasted_iota(jnp.int32, (half, half), 1)
    cross, mixed = sums[:half, :half], sums[:half, half:]
    turned = mixed.T
    first = jnp.where(row <= col, mixed, turned)
    diagonal = jnp.broadcast_to(sums[half + GROUPS : half + GROUPS + 1, :half], (half, half))
    last = jnp.where(row == col, diagonal, jnp.where(row > col, mixed, turned))
    gram = jnp.concatenate(
        [
            jnp.concatenate([first, cross], axis=1),
            jnp.concatenate([cross.T, last], axis=1),
        ],
        axis=0,
    )
    mean_row = sums[half : half + 1, :] / count
    mean_col = jnp.broadcast_to(mean_row, (width, width)).T
    sigma = gram / count - mean_col * mean_row
    row = lax.broadcasted_iota(jnp.int32, (width, width), 0)
    col = lax.broadcasted_iota(jnp.int32, (width, width), 1)
    diagonal = row == col
    trace_value = jnp.sum(jnp.where(diagonal, sigma, 0.0), keepdims=True) + epsilon
    root_scale = jnp.sqrt(trace_value)
    unit, trail = square_root(sigma / trace_value)
    root = root_scale * unit
    root_out[:width, :] = root

    classes = class_weight.shape[0]
    slots = root_out.shape[0] - width
    place = lax.broadcasted_iota(jnp.int32, (slots, 1), 0)
    bias = jnp.zeros((slots, 1), wide)
    for index in range(classes):
        bias = jnp.where(place == index, class_bias[index], bias)
    partial = [
        jnp.sum(class_weight[index].astype(wide) * root, axis=0, keepdims=True)
        for index in range(classes)
    ]
    partial.append(jnp.zeros((slots - classes, width), wide))
    logits = jnp.sum(jnp.concatenate(partial, axis=0), axis=1, keepdims=True) + bias
    onehot = jnp.where(place == label[0], 1.0, 0.0)
    soft = jnp.maximum(logits, 0.0) + jnp.log(1.0 + jnp.exp(-jnp.abs(logits)))
    share = 1.0 / (1.0 + jnp.exp(-logits))
    used = place < classes
    loss_part = jnp.sum(jnp.where(used, soft - onehot * logits, 0.0), keepdims=True)
    logit_grad = jnp.where(used, loss_scale * (share - onehot) / image_count, 0.0)
    root_out[width:, :] = jnp.broadcast_to(
        jnp.where(place == classes, loss_part, logit_grad), (slots, width)
    )
    across = lax.broadcasted_iota(jnp.int32, (slots, width), 1)
    facts = jnp.where(place == classes, loss_part, logit_grad)
    root_out[width + slots - 1 :, :] = jnp.sum(
        jnp.where(across == place, facts, 0.0), axis=0, keepdims=True
    )

    root_grad = jnp.zeros((width, width), wide)
    for index in range(classes):
        root_grad = root_grad + class_weight[index].astype(wide) * logit_grad[index : index + 1, :]
    root_grad = root_grad + root_grad.T
    change = square_root_change(root_scale * root_grad, trail)
    trace_grad = jnp.sum(root_grad * unit, keepdims=True) / (2.0 * root_scale) - jnp.sum(
        change * sigma, keepdims=True
    ) / (trace_value * trace_value)
    symmetric = (
        (change / trace_value + jnp.where(diagonal, trace_grad, 0.0)) / count
    ).astype(narrow)
    mean_term = jnp.sum(mean_col * symmetric.astype(wide), axis=0, keepdims=True)

    inner = feat_inner.shape[0]
    for feat, gate, start in ((feat_inner, gate_inner, 0), (feat_edge, gate_edge, inner)):
        grad = jnp.dot(feat[...], symmetric, preferred_element_type=wide) - mean_term
        pre[start : start + feat.shape[0], :] = (grad * gate[...]).astype(narrow)
    pre_grad = pre[...]
    payload[width:, :] = jnp.zeros((payload.shape[0] - width, payload.shape[1]), wide)
    taps = KERNEL * KERNEL
    payload[width + taps + 1 : width + taps + 2, :width] = jnp.sum(
        pre_grad.astype(wide), axis=0, keepdims=True
    )
    for first in range(0, conv_turned.shape[0], width):
        payload[:width, first : first + width] = jnp.dot(
            conv_turned[first : first + width, :], pre_grad, preferred_element_type=wide
        )
    for out, start in ((conv_inner_out, 0), (conv_edge_out, inner)):
        out[...] = jnp.dot(
            pre[start : start + out.shape[0], :], reduce_turned[...], preferred_element_type=wide
        ).astype(narrow)


def head(flag, label, class_bias, own, other, class_weight, prepared, count, image_count):
    feat_inner, feat_edge, gate_inner, gate_edge, conv_turned, reduce_turned = prepared
    width, channels = reduce_turned.shape
    inner, edge = feat_inner.shape[0], feat_edge.shape[0]
    slots = -(-(class_weight.shape[0] + 2) // GROUPS) * GROUPS
    return pl.pallas_call(
        functools.partial(head_kernel, count=count, image_count=image_count),
        in_specs=[in_smem] * 3 + [in_vmem] * 9,
        out_specs=[in_vmem] * 4,
        out_shape=[
            shape_of((width + slots, width)),
            shape_of((width + TAPS_ROWS, channels)),
            shape_of((inner, channels), narrow),
            shape_of((edge, channels), narrow),
        ],
        scratch_shapes=[
            pltpu.VMEM((2 * own.shape[0], width), wide),
            pltpu.VMEM((inner + edge, width), narrow),
        ],
        compiler_params=params(24),
        cost_estimate=cost(10),
        name="head",
    )(
        flag, label, class_bias, own, other, class_weight,
        feat_inner, feat_edge, gate_inner, gate_edge, conv_turned, reduce_turned,
    )


def prepare_kernel(
    before_inner, before_edge, conv_inner_in, conv_edge_in, reduce_weight,
    gate_inner, gate_edge, conv_turned, reduce_turned,
):
    for before, gate in ((before_inner, gate_inner), (before_edge, gate_edge)):
        value = before[...]
        share = 1.0 / (1.0 + jnp.exp(-value))
        gate[...] = share * (1.0 + value * (1.0 - share))
    inner = conv_inner_in.shape[0]
    conv_turned[:, :inner] = conv_inner_in[...].T
    conv_turned[:, inner:] = conv_edge_in[...].T
    reduce_turned[...] = reduce_weight[...].T


def prepare(before_inner, before_edge, conv_in, conv_ed, reduce_weight):
    channels, width = reduce_weight.shape
    inner, edge = before_inner.shape[0], before_edge.shape[0]
    return pl.pallas_call(
        prepare_kernel,
        in_specs=[in_vmem] * 5,
        out_specs=[in_vmem] * 4,
        out_shape=[
            shape_of((inner, width)),
            shape_of((edge, width)),
            shape_of((channels, inner + edge), narrow),
            shape_of((width, channels), narrow),
        ],
        compiler_params=params(16),
        cost_estimate=cost(1),
        name="prepare",
    )(before_inner, before_edge, conv_in, conv_ed, reduce_weight)


def taps_kernel(
    spread_in, spread_top, spread_bottom, grad_inner, grad_edge, payload_in, payload,
    parts, grads, products, out, *, first, last,
):
    rows = spread_in.shape[1]
    row_pairs, col_pairs = grads.shape[1:3]
    steps = 2 * col_pairs
    cols = steps * GROUPS
    order = edge_rows(rows)
    taps = KERNEL * KERNEL
    base = payload.shape[0] - TAPS_ROWS

    def one_tile(tile, _):
        lanes = lanes_of(tile)

        def grad_row(row):
            if row in order:
                source, place = grad_edge, order.index(row)
            else:
                source, place = grad_inner, row - SIDE
            values = source[place * cols : (place + 1) * cols, lanes].astype(wide)
            return [values[step * GROUPS : (step + 1) * GROUPS, :] for step in range(steps)]

        for pair in range(row_pairs):
            even, odd = grad_row(2 * pair), grad_row(2 * pair + 1)
            both = [a + b for a, b in zip(even, odd)]
            for row_part, line in enumerate((even, odd, both)):
                for col in range(col_pairs):
                    grads[3 * row_part, pair, col] = line[2 * col]
                    grads[3 * row_part + 1, pair, col] = line[2 * col + 1]
                    grads[3 * row_part + 2, pair, col] = line[2 * col] + line[2 * col + 1]

        def load(place, group):
            place = place - HALF
            if place < 0:
                return spread_top[tile, place + HALF, group]
            if place >= rows:
                return spread_bottom[tile, place - rows, group]
            return spread_in[tile, place, group]

        fill_parts(load, parts, row_pairs + 3, 2 * col_pairs + 6)
        for row_part in range(3):
            for col_part in range(3):
                part = 3 * row_part + col_part
                start = FILTERS[row_part, col_part]
                many_rows, many_cols = PARTS[row_part], PARTS[col_part]
                total = {}
                for place in range(row_pairs + many_rows - 1):
                    line = part_line(
                        load, parts, row_part, col_part, place, col_pairs + many_cols - 1
                    )
                    for tap_row in range(many_rows):
                        row = place - tap_row
                        if not 0 <= row < row_pairs:
                            continue
                        for col in range(col_pairs):
                            grad = grads[part, row, col]
                            for tap_col in range(many_cols):
                                term = line[col + tap_col] * grad
                                tap = tap_row * many_cols + tap_col
                                total[tap] = total[tap] + term if tap in total else term
                for tap, value in total.items():
                    products[start + tap] = value

        for row_tap in range(KERNEL):
            for col_tap in range(KERNEL):
                place = (row_tap // 2, col_tap // 2)
                found = None
                for row_part in (row_tap % 2, 2):
                    for col_part in (col_tap % 2, 2):
                        start = FILTERS[row_part, col_part]
                        value = products[start + place[0] * PARTS[col_part] + place[1]]
                        found = value if found is None else found + value
                tap = row_tap * KERNEL + col_tap
                out[tap : tap + 1, :] = jnp.sum(found, axis=0, keepdims=True)
        found = [
            sum(grads[8, pair, col] for col in range(1, col_pairs)) + grads[8, pair, 0]
            for pair in range(row_pairs)
        ]
        out[taps : taps + 1, :] = jnp.sum(sum(found[1:], found[0]), axis=0, keepdims=True)
        payload[pl.ds(base, taps + 1), lanes] = out[: taps + 1, :]
        return 0

    lax.fori_loop(first, last, one_tile, 0)


def tap_grads(spreads, grads, payload, first, last):
    rows, groups = spreads[0].shape[1:3]
    row_pairs, col_pairs = rows // 2, (groups - KERNEL + 1) // 2
    return pl.pallas_call(
        functools.partial(taps_kernel, first=first, last=last),
        in_specs=[in_vmem] * 6,
        out_specs=in_vmem,
        out_shape=shape_of(payload.shape),
        input_output_aliases={5: 0},
        scratch_shapes=[
            pltpu.VMEM((2, row_pairs + 3, 2 * col_pairs + 6, GROUPS, LANES), wide),
            pltpu.VMEM((9, row_pairs, col_pairs, GROUPS, LANES), wide),
            pltpu.VMEM((PRODUCTS, GROUPS, LANES), wide),
            pltpu.VMEM((TAPS_ROWS, LANES), wide),
        ],
        compiler_params=params(16),
        cost_estimate=cost(2 * (last - first)),
        name="tap_grads",
    )(*spreads, *grads, payload)


def finish_kernel(flag, own, other, *refs, image_count):
    known = refs[:-7]
    weight_out, depth_out, depth_bias_out, bias_out, class_bias_out, loss_out, payload = refs[-7:]
    part = own.shape[0]
    upper = flag[0] != 0
    mine, theirs = own[...].astype(wide), other[...].astype(wide)
    payload[:part, :] = jnp.where(upper, theirs, mine)
    payload[part:, :] = jnp.where(upper, mine, theirs)
    width = weight_out.shape[1]
    for first in range(0, weight_out.shape[0], width):
        weight_out[first : first + width, :] = payload[:width, first : first + width]
    for row_tap in range(KERNEL):
        start = width + row_tap * KERNEL
        depth_out[row_tap] = payload[start : start + KERNEL, :]
    taps = KERNEL * KERNEL
    depth_bias_out[...] = payload[width + taps, :]
    bias_out[...] = payload[width + taps + 1, :width]
    totals = tree_sum([part[part.shape[0] - 1 :, :] for part in known])
    classes = class_bias_out.shape[0]
    class_bias_out[...] = totals[0, :classes]
    across = lax.broadcasted_iota(jnp.int32, totals.shape, 1)
    loss_out[0] = jnp.sum(jnp.where(across == classes, totals, 0.0)) / image_count


def finish(flag, own, other, known, width, classes, image_count):
    part, channels = own.shape
    return pl.pallas_call(
        functools.partial(finish_kernel, image_count=image_count),
        in_specs=[in_smem] + [in_vmem] * (2 + len(known)),
        out_specs=[in_vmem] * 5 + [in_smem],
        out_shape=[
            shape_of((channels, width)),
            shape_of((KERNEL, KERNEL, channels)),
            shape_of((channels,)),
            shape_of((width,)),
            shape_of((classes,)),
            shape_of((1,)),
        ],
        scratch_shapes=[pltpu.VMEM((2 * part, channels), wide)],
        compiler_params=params(8),
        cost_estimate=cost(1),
        name="finish",
    )(flag, own, other, *known)


def edge_strip(block, left, right, rows):
    channels = block.shape[2]
    return jnp.concatenate([part[rows].reshape(-1, channels) for part in (block, left, right)])


def body(
    features, depth_weight, depth_bias, reduce_weight, reduce_bias, class_weight, class_bias, labels
):
    together = lax.optimization_barrier
    block = features[0]
    rows, cols, channels = block.shape
    width = reduce_weight.shape[1]
    classes = class_bias.shape[0]
    count = rows * cols * lax.axis_size("sy") * lax.axis_size("sx")
    image_count = features.shape[0] * lax.axis_size("dp")

    flag = is_upper("sx", 1).astype(jnp.int32)[None]
    upper = is_upper("sx", 1)
    corner = 2 * (lax.axis_index("dp") & 1) + ((lax.axis_index("sx") & 2) >> 1)
    places = [corner ^ turn for turn in range(4)]
    bias_row = depth_bias[None]
    reduce_row = reduce_bias[None]
    left = next_along(block[:, cols - HALF :], "sx")
    right = back_along(block[:, :HALF], "sx")
    low, high, left, right, flag, upper, places, bias_row, reduce_row = together(
        (
            edge_strip(block, left, right, slice(rows - HALF, rows)),
            edge_strip(block, left, right, slice(0, HALF)),
            left,
            right,
            flag,
            upper,
            places,
            bias_row,
            reduce_row,
        )
    )
    top = next_along(low, "sy")
    bottom = back_along(high, "sy")
    spread, filters, conv_in, before_in, feat_in, gram, colsum, partial = conv_inner(
        block, left, right, depth_weight, bias_row, reduce_weight, reduce_row
    )
    spread_top, spread_bottom, conv_ed, before_ed, feat_ed, kept, sent = conv_edge(
        flag, partial, (top, bottom), filters, reduce_weight, reduce_row, gram, colsum
    )

    sums = kept + swap(sent, "sx", 1)
    sums, before_in, before_ed, conv_in, conv_ed = together(
        (sums, before_in, before_ed, conv_in, conv_ed)
    )
    gate_in, gate_ed, conv_turned, reduce_turned = prepare(
        before_in, before_ed, conv_in, conv_ed, reduce_weight
    )
    for shift in doublings("sx", 2):
        sums = exchange(sums, "sx", shift, wide)
    sums, gate_in, gate_ed, conv_turned, reduce_turned = together(
        (sums, gate_in, gate_ed, conv_turned, reduce_turned)
    )
    for shift in doublings("sy"):
        sums = exchange(sums, "sy", shift, wide)
    other = swap(sums, "sx", 1)

    root, payload, *grads = head(
        flag,
        labels,
        class_bias,
        sums,
        other,
        class_weight,
        (feat_in, feat_ed, gate_in, gate_ed, conv_turned, reduce_turned),
        count,
        image_count,
    )
    known = [root] + [swap(root, "dp", shift) for shift in range(1, lax.axis_size("dp"))]
    spreads = (spread, spread_top, spread_bottom)
    tiles = channels // LANES
    payload = tap_grads(spreads, grads, payload, 0, tiles - 1)
    payload, known = together((payload, known))
    payload = tap_grads(spreads, grads, payload, tiles - 1, tiles)

    part = payload.shape[0] // 2
    low, high = payload[:part], payload[part:]
    kept, sent = jnp.where(upper, high, low), jnp.where(upper, low, high)
    payload = kept + swap(sent.astype(narrow), "sx", 1).astype(wide)
    axes = ("dp", "sx")
    pairs = square_pairs(axes, (1, 2))
    payload = square_scatter(payload, axes, pairs, places, narrow)
    for shift in doublings("dp", 2):
        payload = exchange(payload, "dp", shift, narrow)
    for shift in doublings("sy"):
        payload = exchange(payload, "sy", shift, narrow)
    payload = payload.astype(narrow)
    payload, known = together((payload, known))
    class_weight_grad = tree_sum(
        [part[width : width + classes, 0][:, None, None] * part[None, :width] for part in known]
    )
    payload, class_weight_grad = together(
        (square_gather(payload, axes, pairs, places), class_weight_grad)
    )
    other = swap(payload, "sx", 1)
    weight_grad, depth_grad, depth_bias_grad, bias_grad, class_bias_grad, loss = finish(
        flag, payload, other, known, width, classes, image_count
    )
    return (
        loss[0],
        depth_grad,
        depth_bias_grad,
        weight_grad,
        bias_grad,
        class_weight_grad,
        class_bias_grad,
    )


def solution(mesh):
    placed = (P("dp", "sy", "sx", None), P(), P(), P(), P(), P(), P(), P("dp"))
    return jax.shard_map(
        body,
        mesh=mesh,
        in_specs=placed,
        out_specs=(P(), P(), P(), P(), P(), P(), P()),
        check_vma=False,
    )
```

```python
import functools

import jax
import jax.numpy as jnp
from jax import lax
from jax.experimental import pallas as pl
from jax.experimental.pallas import tpu as pltpu
from jax.sharding import PartitionSpec as P

KERNEL = 7
HALF = KERNEL // 2
NEWTON_STEPS = 5
LANES = 128
GROUPS = 8
EDGE = 8
TAPS_ROWS = 64
SIDE = 4
FILL_ROWS = 4
PARTS = (4, 3, 4)

epsilon = 1e-05
loss_scale = 64.0
narrow = jnp.bfloat16
wide = jnp.float32


def params(megabytes):
    return pltpu.CompilerParams(vmem_limit_bytes=megabytes * 1024 * 1024)


def swap(value, axis, shift):
    count = lax.axis_size(axis)
    return lax.ppermute(value, axis, [(i, i ^ shift) for i in range(count)])


def is_upper(axis, shift):
    return (lax.axis_index(axis) & shift) != 0


def tree_sum(terms):
    while len(terms) > 1:
        terms = [terms[i] + terms[i + 1] for i in range(0, len(terms), 2)]
    return terms[0]


def exchange(value, axis, shift, sent_as):
    sent = value.astype(sent_as)
    return sent.astype(wide) + swap(sent, axis, shift).astype(wide)


def square_pairs(axes, shifts):
    counts = [lax.axis_size(axis) for axis in axes]
    return {
        2 * first + second: [
            (i * counts[1] + j, (i ^ (first * shifts[0])) * counts[1] + (j ^ (second * shifts[1])))
            for i in range(counts[0])
            for j in range(counts[1])
        ]
        for first, second in ((0, 1), (1, 0), (1, 1))
    }


def square_scatter(value, axes, pairs, places, sent_as):
    pieces = value.reshape((4, value.shape[0] // 4) + value.shape[1:])

    def piece(turn):
        starts = (places[turn],) + (0,) * value.ndim
        sizes = (1,) + pieces.shape[1:]
        return lax.dynamic_slice(pieces, starts, sizes, allow_negative_indices=False)[0]

    moved = [
        lax.ppermute(piece(turn).astype(sent_as), axes, pairs[turn]).astype(wide)
        for turn in (1, 2, 3)
    ]
    return tree_sum([piece(0)] + moved)


def square_gather(value, axes, pairs, places):
    whole = jnp.zeros((4,) + value.shape, value.dtype)
    for turn in range(4):
        part = lax.ppermute(value, axes, pairs[turn]) if turn else value
        starts = (places[turn],) + (0,) * value.ndim
        whole = lax.dynamic_update_slice(whole, part[None], starts, allow_negative_indices=False)
    return whole.reshape((-1,) + value.shape[1:])


def doublings(axis, first=1):
    found = []
    shift = first
    while shift < lax.axis_size(axis):
        found.append(shift)
        shift *= 2
    return found


def next_along(value, axis):
    return lax.ppermute(value, axis, [(i, i + 1) for i in range(lax.axis_size(axis) - 1)])


def back_along(value, axis):
    return lax.ppermute(value, axis, [(i + 1, i) for i in range(lax.axis_size(axis) - 1)])


def spread_columns(source, target):
    for group in range(target.shape[0]):
        target[group] = source[pl.ds(EDGE - HALF + group, GROUPS, stride=GROUPS), :]


def fill_row(wide_row, middle, left, right):
    cols = middle.shape[0]
    wide_row[EDGE : EDGE + cols, :] = middle.astype(wide)
    wide_row[EDGE - HALF : EDGE, :] = left.astype(wide)
    wide_row[EDGE + cols : EDGE + cols + HALF, :] = right.astype(wide)


def lanes_of(tile):
    return pl.ds(pl.multiple_of(tile * LANES, LANES), LANES)


def part_starts():
    starts, total = {}, 0
    for row_part in range(3):
        for col_part in range(3):
            starts[row_part, col_part] = total
            total += PARTS[row_part] * PARTS[col_part]
    return starts, total


FILTERS, PRODUCTS = part_starts()


def part_taps(taps):
    even, odd = taps[0::2], taps[1::2]
    both = [a + b for a, b in zip(even, odd)] + even[len(odd) :]
    return even, odd, both


def spread_weights(weight_ref, filters, tile, lanes):
    rows = []
    for row_tap in range(KERNEL):
        row = [weight_ref[row_tap, tap : tap + 1, lanes] for tap in range(KERNEL)]
        rows.append([jnp.broadcast_to(tap, (GROUPS, LANES)) for tap in row])
    columns = [part_taps([rows[tap][col] for tap in range(KERNEL)]) for col in range(KERNEL)]
    for row_part, many in enumerate(PARTS):
        for row in range(many):
            line = [columns[col][row_part][row] for col in range(KERNEL)]
            for col_part, taps in enumerate(part_taps(line)):
                start = FILTERS[row_part, col_part] + row * PARTS[col_part]
                for col, value in enumerate(taps):
                    filters[tile, start + col] = value


def fill_parts(load, parts, row_pairs, groups):
    for pair in range(row_pairs):
        for group in range(groups):
            middle = load(2 * pair + 1, group)
            parts[0, pair, group] = load(2 * pair, group) - middle
            if pair < row_pairs - 1:
                parts[1, pair, group] = load(2 * pair + 2, group) - middle


def part_line(load, parts, row_part, col_part, pair, many):
    def value(group):
        return load(2 * pair + 1, group) if row_part == 2 else parts[row_part, pair, group]

    first = (0, 2, 1)[col_part]
    line = [value(2 * col + first) for col in range(many)]
    if col_part < 2:
        line = [side - value(2 * col + 1) for col, side in enumerate(line)]
    return line


def conv_rows(load, filters, tile, bias, steps, count, parts, products):
    row_pairs, col_pairs = count // 2, steps // 2
    fill_parts(load, parts, row_pairs + 3, 2 * col_pairs + 6)
    for row_part in range(3):
        for col_part in range(3):
            start = FILTERS[row_part, col_part]
            many_rows, many_cols = PARTS[row_part], PARTS[col_part]
            total = [[None] * col_pairs for _ in range(row_pairs)]
            for place in range(row_pairs + many_rows - 1):
                line = part_line(
                    load, parts, row_part, col_part, place, col_pairs + many_cols - 1
                )
                for row in range(row_pairs):
                    tap_row = place - row
                    if not 0 <= tap_row < many_rows:
                        continue
                    for tap_col in range(many_cols):
                        scale = filters[tile, start + tap_row * many_cols + tap_col]
                        for col in range(col_pairs):
                            term = line[col + tap_col] * scale
                            old = total[row][col]
                            total[row][col] = term if old is None else old + term
            for row in range(row_pairs):
                for col in range(col_pairs):
                    products[3 * row_part + col_part, row, col] = total[row][col]
    found = []
    for row in range(row_pairs):
        lines = [[], []]
        for col in range(col_pairs):
            values = [products[part, row, col] for part in range(9)]
            shared = [values[6] + values[8] + bias, values[7] + values[8] + bias]
            for row_part in range(2):
                for col_part in range(2):
                    own = values[3 * row_part + col_part] + values[3 * row_part + 2]
                    lines[row_part].append(own + shared[col_part])
        found += lines
    return found


def rounded(lines):
    return jnp.concatenate([part for line in lines for part in line], axis=0).astype(narrow)


def parts_scratch(count, steps):
    row_pairs, col_pairs = count // 2, steps // 2
    return [
        pltpu.VMEM((2, row_pairs + 3, 2 * col_pairs + 6, GROUPS, LANES), wide),
        pltpu.VMEM((9, row_pairs, col_pairs, GROUPS, LANES), wide),
    ]


def reduce_part(conv_out, reduce_ref, reduce_bias_ref, before_out, feat_out):
    before = jnp.dot(conv_out[...], reduce_ref[...], preferred_element_type=wide)
    before = before + reduce_bias_ref[...]
    before_out[...] = before
    feat_out[...] = (before / (1.0 + jnp.exp(-before))).astype(narrow)
    feat = feat_out[...]
    gram = lax.dot_general(feat, feat, (((0,), (0,)), ((), ())), preferred_element_type=wide)
    return gram, jnp.sum(feat.astype(wide), axis=0, keepdims=True)


def inner_kernel(
    block, left, right, weight, bias, reduce_weight, reduce_bias,
    spread_out, filters, conv_out, before_out, feat_out, gram_out, colsum_out, partial_out,
    wide_row, parts, products,
):
    rows, cols = block.shape[0], block.shape[1]
    steps = cols // GROUPS

    def one_tile(tile, _):
        lanes = lanes_of(tile)
        spread_weights(weight, filters, tile, lanes)
        start_value = jnp.broadcast_to(bias[0:1, lanes], (GROUPS, LANES))

        def fill(turn, _):
            for row in range(FILL_ROWS):
                row = turn * FILL_ROWS + row
                place = wide_row.at[row]
                fill_row(place, block[row, :, lanes], left[row, :, lanes], right[row, :, lanes])
                spread_columns(place, spread_out.at[tile, row])
            return 0

        lax.fori_loop(0, rows // FILL_ROWS, fill, 0)

        def load_from(first):
            def load(row, group):
                place = first + row - HALF
                if 0 <= place < rows:
                    return spread_out[tile, place, group]
                return jnp.zeros((GROUPS, LANES), wide)

            return load

        conv_out[:, lanes] = rounded(
            conv_rows(
                load_from(SIDE), filters, tile, start_value, steps, rows - 2 * SIDE, parts, products
            )
        )
        for side, first in enumerate((0, rows - SIDE)):
            lines = conv_rows(
                load_from(first), filters, tile, start_value, steps, SIDE, parts, products
            )
            for row, line in enumerate(lines):
                for step, value in enumerate(line):
                    partial_out[tile, side * SIDE + row, step] = value
        return 0

    lax.fori_loop(0, spread_out.shape[0], one_tile, 0)
    gram_out[...], colsum_out[...] = reduce_part(
        conv_out, reduce_weight, reduce_bias, before_out, feat_out
    )


def edge_kernel(
    flag, partial, top, bottom, filters, reduce_weight, reduce_bias, gram_in, colsum_in,
    spread_top, spread_bottom, conv_out, before_out, feat_out, kept_out, sent_out,
    wide_row, stage, sums,
):
    cols = wide_row.shape[1] - 2 * EDGE
    steps = cols // GROUPS

    def one_tile(tile, _):
        lanes = lanes_of(tile)
        for side, (strip, spread) in enumerate(((top, spread_top), (bottom, spread_bottom))):
            stage[side] = strip[:, lanes].astype(wide)
            for row in range(HALF):
                place = wide_row.at[side * HALF + row]
                left = HALF * cols + row * HALF
                right = left + HALF * HALF
                fill_row(
                    place,
                    stage[side, row * cols : (row + 1) * cols, :],
                    stage[side, left : left + HALF, :],
                    stage[side, right : right + HALF, :],
                )
                spread_columns(place, spread.at[tile, row])

        def filter_of(row_tap, col_tap):
            start = FILTERS[row_tap % 2, col_tap % 2]
            return filters[tile, start + row_tap // 2 * PARTS[col_tap % 2] + col_tap // 2]

        for side, spread in enumerate((spread_top, spread_bottom)):
            lines = [
                [partial[tile, side * SIDE + row, step] for step in range(steps)]
                for row in range(SIDE)
            ]
            for place in range(HALF):
                windows = [spread[tile, place, group] for group in range(steps + KERNEL - 1)]
                for row in range(SIDE):
                    row_tap = place - row if side == 0 else place + HALF + SIDE - row
                    if not 0 <= row_tap < KERNEL:
                        continue
                    for col_tap in range(KERNEL):
                        scale = filter_of(row_tap, col_tap)
                        for step in range(steps):
                            lines[row][step] = lines[row][step] + windows[step + col_tap] * scale
            start = side * SIDE * cols
            conv_out[start : start + SIDE * cols, lanes] = rounded(lines)
        return 0

    lax.fori_loop(0, partial.shape[0], one_tile, 0)
    gram, colsum = reduce_part(conv_out, reduce_weight, reduce_bias, before_out, feat_out)
    gram = gram + gram_in[...]
    colsum = colsum + colsum_in[...]
    half = gram.shape[0] // 2
    row = lax.broadcasted_iota(jnp.int32, (half, half), 0)
    col = lax.broadcasted_iota(jnp.int32, (half, half), 1)
    last_block = gram[half:, half:]
    diagonal = jnp.sum(jnp.where(row == col, last_block, 0.0), axis=0, keepdims=True)
    sums[:half, :half] = gram[:half, half:]
    sums[:half, half:] = jnp.where(row <= col, gram[:half, :half], last_block)
    sums[half : half + GROUPS, :] = jnp.broadcast_to(colsum, (GROUPS, 2 * half))
    sums[half + GROUPS :, :half] = jnp.broadcast_to(diagonal, (GROUPS, half))
    sums[half + GROUPS :, half:] = jnp.zeros((GROUPS, half), wide)
    part = kept_out.shape[0]
    keep_or_send(flag[0] != 0, sums[:part, :], sums[part:, :], kept_out, sent_out)


def keep_or_send(upper, low, high, kept_out, sent_out):
    kept_out[...] = jnp.where(upper, high, low)
    sent_out[...] = jnp.where(upper, low, high).astype(sent_out.dtype)


def edge_rows(rows):
    return list(range(SIDE)) + list(range(rows - SIDE, rows))


def shape_of(shape, dtype=wide):
    return jax.ShapeDtypeStruct(shape, dtype)


in_vmem = pl.BlockSpec(memory_space=pltpu.VMEM)
in_smem = pl.BlockSpec(memory_space=pltpu.SMEM)


def cost(microseconds):
    return pl.CostEstimate(
        flops=microseconds * 10**9, bytes_accessed=microseconds * 10**6, transcendentals=0
    )


def conv_inner(block, left, right, weight, bias, reduce_weight, reduce_bias):
    rows, cols, channels = block.shape
    width = reduce_weight.shape[1]
    tiles = channels // LANES
    steps = cols // GROUPS
    pixels = (rows - 2 * SIDE) * cols
    return pl.pallas_call(
        inner_kernel,
        in_specs=[in_vmem] * 7,
        out_specs=[in_vmem] * 8,
        out_shape=[
            shape_of((tiles, rows, steps + KERNEL - 1, GROUPS, LANES)),
            shape_of((tiles, PRODUCTS, GROUPS, LANES)),
            shape_of((pixels, channels), narrow),
            shape_of((pixels, width)),
            shape_of((pixels, width), narrow),
            shape_of((width, width)),
            shape_of((1, width)),
            shape_of((tiles, 2 * SIDE, steps, GROUPS, LANES)),
        ],
        scratch_shapes=[
            pltpu.VMEM((rows, cols + 2 * EDGE, LANES), wide),
            *parts_scratch(rows - 2 * SIDE, steps),
        ],
        compiler_params=params(24),
        cost_estimate=cost(10),
        name="conv_inner",
    )(block, left, right, weight, bias, reduce_weight, reduce_bias)


def conv_edge(flag, partial, halos, filters, reduce_weight, reduce_bias, gram, colsum):
    tiles, _, steps = partial.shape[:3]
    cols, groups = steps * GROUPS, steps + KERNEL - 1
    channels, width = reduce_weight.shape
    pixels = 2 * SIDE * cols
    side = (tiles, HALF, groups, GROUPS, LANES)
    sums_rows = width // 2 + 2 * GROUPS
    return pl.pallas_call(
        edge_kernel,
        in_specs=[in_smem] + [in_vmem] * 8,
        out_specs=[in_vmem] * 7,
        out_shape=[
            shape_of(side),
            shape_of(side),
            shape_of((pixels, channels), narrow),
            shape_of((pixels, width)),
            shape_of((pixels, width), narrow),
            shape_of((sums_rows // 2, width)),
            shape_of((sums_rows // 2, width)),
        ],
        scratch_shapes=[
            pltpu.VMEM((2 * HALF, cols + 2 * EDGE, LANES), wide),
            pltpu.VMEM((2,) + (halos[0].shape[0], LANES), wide),
            pltpu.VMEM((sums_rows, width), wide),
        ],
        compiler_params=params(24),
        cost_estimate=cost(6),
        name="conv_edge",
    )(flag, partial, *halos, filters, reduce_weight, reduce_bias, gram, colsum)


def split(value):
    high = value.astype(narrow)
    return high, (value - high.astype(wide)).astype(narrow)


def product(left, right):
    def dot(a, b):
        return jnp.dot(a, b, preferred_element_type=wide)

    return dot(left[0], right[0]) + (dot(left[0], right[1]) + dot(left[1], right[0]))


def square_root(current):
    size = current.shape[0]
    row = lax.broadcasted_iota(jnp.int32, (size, size), 0)
    col = lax.broadcasted_iota(jnp.int32, (size, size), 1)
    triple = jnp.where(row == col, 3.0, 0.0)
    factor = split(0.5 * (triple - current))
    current = split(current)
    trail = [(current, None, factor)]
    inverse = factor
    current = split(product(current, factor))
    for step in range(1, NEWTON_STEPS):
        factor = split(0.5 * (triple - product(inverse, current)))
        trail.append((current, inverse, factor))
        last = step == NEWTON_STEPS - 1
        if not last:
            inverse = split(product(factor, inverse))
        current = product(current, factor)
        if not last:
            current = split(current)
    return current, trail


def square_root_change(change, trail):
    first, _, factor = trail[0]
    move = split(change)
    factor_move = split(-0.5 * change)
    change = product(move, factor) + product(first, factor_move)
    inverse_move = factor_move
    for step in range(1, NEWTON_STEPS):
        current, inverse, factor = trail[step]
        move = split(change)
        factor_move = split(
            -0.5 * (product(inverse_move, current) + product(inverse, move))
        )
        change = product(move, factor) + product(current, factor_move)
        if step < NEWTON_STEPS - 1:
            inverse_move = split(product(factor_move, inverse) + product(factor, inverse_move))
    return change


def head_kernel(
    flag, label, class_bias, own, other, class_weight,
    feat_inner, feat_edge, gate_inner, gate_edge,
    root_out, payload, pre,
    sums, *, count, image_count,
):
    width = root_out.shape[1]
    half = width // 2
    rows = own.shape[0]
    upper = flag[0] != 0
    mine, theirs = own[...], other[...]
    sums[:rows, :] = jnp.where(upper, theirs, mine)
    sums[rows:, :] = jnp.where(upper, mine, theirs)
    row = lax.broadcasted_iota(jnp.int32, (half, half), 0)
    col = lax.broadcasted_iota(jnp.int32, (half, half), 1)
    cross, mixed = sums[:half, :half], sums[:half, half:]
    turned = mixed.T
    first = jnp.where(row <= col, mixed, turned)
    diagonal = jnp.broadcast_to(sums[half + GROUPS : half + GROUPS + 1, :half], (half, half))
    last = jnp.where(row == col, diagonal, jnp.where(row > col, mixed, turned))
    gram = jnp.concatenate(
        [
            jnp.concatenate([first, cross], axis=1),
            jnp.concatenate([cross.T, last], axis=1),
        ],
        axis=0,
    )
    mean_row = sums[half : half + 1, :] / count
    mean_col = jnp.broadcast_to(mean_row, (width, width)).T
    sigma = gram / count - mean_col * mean_row
    row = lax.broadcasted_iota(jnp.int32, (width, width), 0)
    col = lax.broadcasted_iota(jnp.int32, (width, width), 1)
    diagonal = row == col
    trace_value = jnp.sum(jnp.where(diagonal, sigma, 0.0), keepdims=True) + epsilon
    root_scale = jnp.sqrt(trace_value)
    unit, trail = square_root(sigma / trace_value)
    root = root_scale * unit
    root_out[:width, :] = root

    classes = class_weight.shape[0]
    slots = root_out.shape[0] - width
    place = lax.broadcasted_iota(jnp.int32, (slots, 1), 0)
    bias = jnp.zeros((slots, 1), wide)
    for index in range(classes):
        bias = jnp.where(place == index, class_bias[index], bias)
    partial = [
        jnp.sum(class_weight[index].astype(wide) * root, axis=0, keepdims=True)
        for index in range(classes)
    ]
    partial.append(jnp.zeros((slots - classes, width), wide))
    logits = jnp.sum(jnp.concatenate(partial, axis=0), axis=1, keepdims=True) + bias
    onehot = jnp.where(place == label[0], 1.0, 0.0)
    soft = jnp.maximum(logits, 0.0) + jnp.log(1.0 + jnp.exp(-jnp.abs(logits)))
    share = 1.0 / (1.0 + jnp.exp(-logits))
    used = place < classes
    loss_part = jnp.sum(jnp.where(used, soft - onehot * logits, 0.0), keepdims=True)
    logit_grad = jnp.where(used, loss_scale * (share - onehot) / image_count, 0.0)
    root_out[width:, :] = jnp.broadcast_to(
        jnp.where(place == classes, loss_part, logit_grad), (slots, width)
    )
    across = lax.broadcasted_iota(jnp.int32, (slots, width), 1)
    facts = jnp.where(place == classes, loss_part, logit_grad)
    root_out[width + slots - 1 :, :] = jnp.sum(
        jnp.where(across == place, facts, 0.0), axis=0, keepdims=True
    )

    root_grad = jnp.zeros((width, width), wide)
    for index in range(classes):
        root_grad = root_grad + class_weight[index].astype(wide) * logit_grad[index : index + 1, :]
    root_grad = root_grad + root_grad.T
    change = square_root_change(root_scale * root_grad, trail)
    trace_grad = jnp.sum(root_grad * unit, keepdims=True) / (2.0 * root_scale) - jnp.sum(
        change * sigma, keepdims=True
    ) / (trace_value * trace_value)
    symmetric = (
        (change / trace_value + jnp.where(diagonal, trace_grad, 0.0)) / count
    ).astype(narrow)
    mean_term = jnp.sum(mean_col * symmetric.astype(wide), axis=0, keepdims=True)

    inner = feat_inner.shape[0]
    for feat, gate, start in ((feat_inner, gate_inner, 0), (feat_edge, gate_edge, inner)):
        grad = jnp.dot(feat[...], symmetric, preferred_element_type=wide) - mean_term
        pre[start : start + feat.shape[0], :] = (grad * gate[...]).astype(narrow)
    pre_grad = pre[...]
    payload[width:, :] = jnp.zeros((payload.shape[0] - width, payload.shape[1]), wide)
    taps = KERNEL * KERNEL
    payload[width + taps + 1 : width + taps + 2, :width] = jnp.sum(
        pre_grad.astype(wide), axis=0, keepdims=True
    )


def head(flag, label, class_bias, own, other, class_weight, prepared, channels, count, image_count):
    feat_inner, feat_edge = prepared[:2]
    width = feat_inner.shape[1]
    inner, edge = feat_inner.shape[0], feat_edge.shape[0]
    slots = -(-(class_weight.shape[0] + 2) // GROUPS) * GROUPS
    return pl.pallas_call(
        functools.partial(head_kernel, count=count, image_count=image_count),
        in_specs=[in_smem] * 3 + [in_vmem] * 7,
        out_specs=[in_vmem] * 3,
        out_shape=[
            shape_of((width + slots, width)),
            shape_of((width + TAPS_ROWS, channels)),
            shape_of((inner + edge, width), narrow),
        ],
        scratch_shapes=[pltpu.VMEM((2 * own.shape[0], width), wide)],
        compiler_params=params(24),
        cost_estimate=cost(10),
        name="head",
    )(flag, label, class_bias, own, other, class_weight, *prepared)


def prepare_kernel(
    before_inner, before_edge, conv_inner_in, conv_edge_in, reduce_weight,
    gate_inner, gate_edge, conv_turned, reduce_turned,
):
    for before, gate in ((before_inner, gate_inner), (before_edge, gate_edge)):
        value = before[...]
        share = 1.0 / (1.0 + jnp.exp(-value))
        gate[...] = share * (1.0 + value * (1.0 - share))
    inner = conv_inner_in.shape[0]
    conv_turned[:, :inner] = conv_inner_in[...].T
    conv_turned[:, inner:] = conv_edge_in[...].T
    reduce_turned[...] = reduce_weight[...].T


def prepare(before_inner, before_edge, conv_in, conv_ed, reduce_weight):
    channels, width = reduce_weight.shape
    inner, edge = before_inner.shape[0], before_edge.shape[0]
    return pl.pallas_call(
        prepare_kernel,
        in_specs=[in_vmem] * 5,
        out_specs=[in_vmem] * 4,
        out_shape=[
            shape_of((inner, width)),
            shape_of((edge, width)),
            shape_of((channels, inner + edge), narrow),
            shape_of((width, channels), narrow),
        ],
        compiler_params=params(16),
        cost_estimate=cost(1),
        name="prepare",
    )(before_inner, before_edge, conv_in, conv_ed, reduce_weight)


def taps_kernel(
    spread_in, spread_top, spread_bottom, pre, conv_turned, reduce_turned, payload_in, payload,
    parts, grads, products, out, conv_grad, *, first, last,
):
    rows = spread_in.shape[1]
    row_pairs, col_pairs = grads.shape[1:3]
    steps = 2 * col_pairs
    cols = steps * GROUPS
    order = edge_rows(rows)
    taps = KERNEL * KERNEL
    base = payload.shape[0] - TAPS_ROWS
    width = pre.shape[1]
    halves = width // LANES

    def fill_conv_grad(tile):
        product = jnp.dot(pre[...], reduce_turned[:, lanes_of(tile)], preferred_element_type=wide)
        conv_grad[tile % 2] = product.astype(narrow)

    fill_conv_grad(first)

    def one_tile(tile, _):
        lanes = lanes_of(tile)
        slot = tile % 2

        def grad_row(row):
            place = rows - 2 * SIDE + order.index(row) if row in order else row - SIDE
            values = conv_grad[slot, place * cols : (place + 1) * cols, :].astype(wide)
            return [values[step * GROUPS : (step + 1) * GROUPS, :] for step in range(steps)]

        for pair in range(row_pairs):
            even, odd = grad_row(2 * pair), grad_row(2 * pair + 1)
            both = [a + b for a, b in zip(even, odd)]
            for row_part, line in enumerate((even, odd, both)):
                for col in range(col_pairs):
                    grads[3 * row_part, pair, col] = line[2 * col]
                    grads[3 * row_part + 1, pair, col] = line[2 * col + 1]
                    grads[3 * row_part + 2, pair, col] = line[2 * col] + line[2 * col + 1]

        def load(place, group):
            place = place - HALF
            if place < 0:
                return spread_top[tile, place + HALF, group]
            if place >= rows:
                return spread_bottom[tile, place - rows, group]
            return spread_in[tile, place, group]

        fill_parts(load, parts, row_pairs + 3, 2 * col_pairs + 6)
        for row_part in range(3):
            for col_part in range(3):
                part = 3 * row_part + col_part
                start = FILTERS[row_part, col_part]
                many_rows, many_cols = PARTS[row_part], PARTS[col_part]
                total = {}
                for place in range(row_pairs + many_rows - 1):
                    line = part_line(
                        load, parts, row_part, col_part, place, col_pairs + many_cols - 1
                    )
                    for tap_row in range(many_rows):
                        row = place - tap_row
                        if not 0 <= row < row_pairs:
                            continue
                        for col in range(col_pairs):
                            grad = grads[part, row, col]
                            for tap_col in range(many_cols):
                                term = line[col + tap_col] * grad
                                tap = tap_row * many_cols + tap_col
                                total[tap] = total[tap] + term if tap in total else term
                for tap, value in total.items():
                    products[start + tap] = value

        for row_tap in range(KERNEL):
            for col_tap in range(KERNEL):
                place = (row_tap // 2, col_tap // 2)
                found = None
                for row_part in (row_tap % 2, 2):
                    for col_part in (col_tap % 2, 2):
                        start = FILTERS[row_part, col_part]
                        value = products[start + place[0] * PARTS[col_part] + place[1]]
                        found = value if found is None else found + value
                tap = row_tap * KERNEL + col_tap
                out[tap : tap + 1, :] = jnp.sum(found, axis=0, keepdims=True)
        found = [
            sum(grads[8, pair, col] for col in range(1, col_pairs)) + grads[8, pair, 0]
            for pair in range(row_pairs)
        ]
        out[taps : taps + 1, :] = jnp.sum(sum(found[1:], found[0]), axis=0, keepdims=True)
        payload[pl.ds(base, taps + 1), lanes] = out[: taps + 1, :]
        fill_conv_grad(jnp.minimum(tile + 1, last - 1))
        weight_rows = pl.ds(pl.multiple_of(tile % halves * LANES, LANES), LANES)
        weight_lanes = pl.ds(pl.multiple_of(tile // halves * width, width), width)
        payload[weight_rows, weight_lanes] = jnp.dot(
            conv_turned[pl.ds(pl.multiple_of(tile * LANES, LANES), LANES), :],
            pre[...],
            preferred_element_type=wide,
        )
        return 0

    lax.fori_loop(first, last, one_tile, 0)


def tap_grads(spreads, pre, conv_turned, reduce_turned, payload, first, last):
    rows, groups = spreads[0].shape[1:3]
    row_pairs, col_pairs = rows // 2, (groups - KERNEL + 1) // 2
    return pl.pallas_call(
        functools.partial(taps_kernel, first=first, last=last),
        in_specs=[in_vmem] * 7,
        out_specs=in_vmem,
        out_shape=shape_of(payload.shape),
        input_output_aliases={6: 0},
        scratch_shapes=[
            pltpu.VMEM((2, row_pairs + 3, 2 * col_pairs + 6, GROUPS, LANES), wide),
            pltpu.VMEM((9, row_pairs, col_pairs, GROUPS, LANES), wide),
            pltpu.VMEM((PRODUCTS, GROUPS, LANES), wide),
            pltpu.VMEM((TAPS_ROWS, LANES), wide),
            pltpu.VMEM((2, pre.shape[0], LANES), narrow),
        ],
        compiler_params=params(16),
        cost_estimate=cost(2 * (last - first)),
        name="tap_grads",
    )(*spreads, pre, conv_turned, reduce_turned, payload)


def finish_kernel(flag, own, other, *refs, image_count):
    known = refs[:-7]
    weight_out, depth_out, depth_bias_out, bias_out, class_bias_out, loss_out, payload = refs[-7:]
    part = own.shape[0]
    upper = flag[0] != 0
    mine, theirs = own[...].astype(wide), other[...].astype(wide)
    payload[:part, :] = jnp.where(upper, theirs, mine)
    payload[part:, :] = jnp.where(upper, mine, theirs)
    width = weight_out.shape[1]
    for first in range(0, weight_out.shape[0], width):
        weight_out[first : first + width, :] = payload[:width, first : first + width]
    for row_tap in range(KERNEL):
        start = width + row_tap * KERNEL
        depth_out[row_tap] = payload[start : start + KERNEL, :]
    taps = KERNEL * KERNEL
    depth_bias_out[...] = payload[width + taps, :]
    bias_out[...] = payload[width + taps + 1, :width]
    totals = tree_sum([part[part.shape[0] - 1 :, :] for part in known])
    classes = class_bias_out.shape[0]
    class_bias_out[...] = totals[0, :classes]
    across = lax.broadcasted_iota(jnp.int32, totals.shape, 1)
    loss_out[0] = jnp.sum(jnp.where(across == classes, totals, 0.0)) / image_count


def finish(flag, own, other, known, width, classes, image_count):
    part, channels = own.shape
    return pl.pallas_call(
        functools.partial(finish_kernel, image_count=image_count),
        in_specs=[in_smem] + [in_vmem] * (2 + len(known)),
        out_specs=[in_vmem] * 5 + [in_smem],
        out_shape=[
            shape_of((channels, width)),
            shape_of((KERNEL, KERNEL, channels)),
            shape_of((channels,)),
            shape_of((width,)),
            shape_of((classes,)),
            shape_of((1,)),
        ],
        scratch_shapes=[pltpu.VMEM((2 * part, channels), wide)],
        compiler_params=params(8),
        cost_estimate=cost(1),
        name="finish",
    )(flag, own, other, *known)


def edge_strip(block, left, right, rows):
    channels = block.shape[2]
    return jnp.concatenate([part[rows].reshape(-1, channels) for part in (block, left, right)])


def body(
    features, depth_weight, depth_bias, reduce_weight, reduce_bias, class_weight, class_bias, labels
):
    together = lax.optimization_barrier
    block = features[0]
    rows, cols, channels = block.shape
    width = reduce_weight.shape[1]
    classes = class_bias.shape[0]
    count = rows * cols * lax.axis_size("sy") * lax.axis_size("sx")
    image_count = features.shape[0] * lax.axis_size("dp")

    flag = is_upper("sx", 1).astype(jnp.int32)[None]
    upper = is_upper("sx", 1)
    corner = 2 * (lax.axis_index("dp") & 1) + ((lax.axis_index("sx") & 2) >> 1)
    places = [corner ^ turn for turn in range(4)]
    bias_row = depth_bias[None]
    reduce_row = reduce_bias[None]
    left = next_along(block[:, cols - HALF :], "sx")
    right = back_along(block[:, :HALF], "sx")
    low, high, left, right, flag, upper, places, bias_row, reduce_row = together(
        (
            edge_strip(block, left, right, slice(rows - HALF, rows)),
            edge_strip(block, left, right, slice(0, HALF)),
            left,
            right,
            flag,
            upper,
            places,
            bias_row,
            reduce_row,
        )
    )
    top = next_along(low, "sy")
    bottom = back_along(high, "sy")
    spread, filters, conv_in, before_in, feat_in, gram, colsum, partial = conv_inner(
        block, left, right, depth_weight, bias_row, reduce_weight, reduce_row
    )
    spread_top, spread_bottom, conv_ed, before_ed, feat_ed, kept, sent = conv_edge(
        flag, partial, (top, bottom), filters, reduce_weight, reduce_row, gram, colsum
    )

    sums = kept + swap(sent, "sx", 1)
    sums, before_in, before_ed, conv_in, conv_ed = together(
        (sums, before_in, before_ed, conv_in, conv_ed)
    )
    gate_in, gate_ed, conv_turned, reduce_turned = prepare(
        before_in, before_ed, conv_in, conv_ed, reduce_weight
    )
    for shift in doublings("sx", 2):
        sums = exchange(sums, "sx", shift, wide)
    sums, gate_in, gate_ed, conv_turned, reduce_turned = together(
        (sums, gate_in, gate_ed, conv_turned, reduce_turned)
    )
    for shift in doublings("sy"):
        sums = exchange(sums, "sy", shift, wide)
    other = swap(sums, "sx", 1)

    root, payload, pre = head(
        flag,
        labels,
        class_bias,
        sums,
        other,
        class_weight,
        (feat_in, feat_ed, gate_in, gate_ed),
        channels,
        count,
        image_count,
    )
    known = [root] + [swap(root, "dp", shift) for shift in range(1, lax.axis_size("dp"))]
    spreads = (spread, spread_top, spread_bottom)
    tiles = channels // LANES
    payload = tap_grads(spreads, pre, conv_turned, reduce_turned, payload, 0, tiles - 1)
    payload, known = together((payload, known))
    payload = tap_grads(spreads, pre, conv_turned, reduce_turned, payload, tiles - 1, tiles)

    part = payload.shape[0] // 2
    low, high = payload[:part], payload[part:]
    kept, sent = jnp.where(upper, high, low), jnp.where(upper, low, high)
    payload = kept + swap(sent.astype(narrow), "sx", 1).astype(wide)
    axes = ("dp", "sx")
    pairs = square_pairs(axes, (1, 2))
    payload = square_scatter(payload, axes, pairs, places, narrow)
    for shift in doublings("dp", 2):
        payload = exchange(payload, "dp", shift, narrow)
    for shift in doublings("sy"):
        payload = exchange(payload, "sy", shift, narrow)
    payload = payload.astype(narrow)
    payload, known = together((payload, known))
    class_weight_grad = tree_sum(
        [part[width : width + classes, 0][:, None, None] * part[None, :width] for part in known]
    )
    payload, class_weight_grad = together(
        (square_gather(payload, axes, pairs, places), class_weight_grad)
    )
    other = swap(payload, "sx", 1)
    weight_grad, depth_grad, depth_bias_grad, bias_grad, class_bias_grad, loss = finish(
        flag, payload, other, known, width, classes, image_count
    )
    return (
        loss[0],
        depth_grad,
        depth_bias_grad,
        weight_grad,
        bias_grad,
        class_weight_grad,
        class_bias_grad,
    )


def solution(mesh):
    placed = (P("dp", "sy", "sx", None), P(), P(), P(), P(), P(), P(), P("dp"))
    return jax.shard_map(
        body,
        mesh=mesh,
        in_specs=placed,
        out_specs=(P(), P(), P(), P(), P(), P(), P()),
        check_vma=False,
    )
```

```python
import functools

import jax
import jax.numpy as jnp
from jax import lax
from jax.experimental import pallas as pl
from jax.experimental.pallas import tpu as pltpu
from jax.sharding import PartitionSpec as P

KERNEL = 7
HALF = KERNEL // 2
NEWTON_STEPS = 5
LANES = 128
GROUPS = 8
EDGE = 8
TAPS_ROWS = 64
SIDE = 4
FILL_ROWS = 4
PARTS = (4, 3, 4)

epsilon = 1e-05
loss_scale = 64.0
narrow = jnp.bfloat16
wide = jnp.float32


def params(megabytes):
    return pltpu.CompilerParams(vmem_limit_bytes=megabytes * 1024 * 1024)


def swap(value, axis, shift):
    count = lax.axis_size(axis)
    return lax.ppermute(value, axis, [(i, i ^ shift) for i in range(count)])


def is_upper(axis, shift):
    return (lax.axis_index(axis) & shift) != 0


def tree_sum(terms):
    while len(terms) > 1:
        terms = [terms[i] + terms[i + 1] for i in range(0, len(terms), 2)]
    return terms[0]


def exchange(value, axis, shift, sent_as):
    sent = value.astype(sent_as)
    return sent.astype(wide) + swap(sent, axis, shift).astype(wide)


def square_pairs(axes, shifts):
    counts = [lax.axis_size(axis) for axis in axes]
    return {
        2 * first + second: [
            (i * counts[1] + j, (i ^ (first * shifts[0])) * counts[1] + (j ^ (second * shifts[1])))
            for i in range(counts[0])
            for j in range(counts[1])
        ]
        for first, second in ((0, 1), (1, 0), (1, 1))
    }


def square_scatter(value, axes, pairs, places, sent_as):
    pieces = value.reshape((4, value.shape[0] // 4) + value.shape[1:])

    def piece(turn):
        starts = (places[turn],) + (0,) * value.ndim
        sizes = (1,) + pieces.shape[1:]
        return lax.dynamic_slice(pieces, starts, sizes, allow_negative_indices=False)[0]

    moved = [
        lax.ppermute(piece(turn).astype(sent_as), axes, pairs[turn]).astype(wide)
        for turn in (1, 2, 3)
    ]
    return tree_sum([piece(0)] + moved)


def square_gather(value, axes, pairs, places):
    whole = jnp.zeros((4,) + value.shape, value.dtype)
    for turn in range(4):
        part = lax.ppermute(value, axes, pairs[turn]) if turn else value
        starts = (places[turn],) + (0,) * value.ndim
        whole = lax.dynamic_update_slice(whole, part[None], starts, allow_negative_indices=False)
    return whole.reshape((-1,) + value.shape[1:])


def doublings(axis, first=1):
    found = []
    shift = first
    while shift < lax.axis_size(axis):
        found.append(shift)
        shift *= 2
    return found


def next_along(value, axis):
    return lax.ppermute(value, axis, [(i, i + 1) for i in range(lax.axis_size(axis) - 1)])


def back_along(value, axis):
    return lax.ppermute(value, axis, [(i + 1, i) for i in range(lax.axis_size(axis) - 1)])


def spread_columns(source, target):
    for group in range(target.shape[0]):
        target[group] = source[pl.ds(EDGE - HALF + group, GROUPS, stride=GROUPS), :]


def fill_row(wide_row, middle, left, right):
    cols = middle.shape[0]
    wide_row[EDGE : EDGE + cols, :] = middle.astype(wide)
    wide_row[EDGE - HALF : EDGE, :] = left.astype(wide)
    wide_row[EDGE + cols : EDGE + cols + HALF, :] = right.astype(wide)


def lanes_of(tile):
    return pl.ds(pl.multiple_of(tile * LANES, LANES), LANES)


def part_starts():
    starts, total = {}, 0
    for row_part in range(3):
        for col_part in range(3):
            starts[row_part, col_part] = total
            total += PARTS[row_part] * PARTS[col_part]
    return starts, total


FILTERS, PRODUCTS = part_starts()


def part_taps(taps):
    even, odd = taps[0::2], taps[1::2]
    both = [a + b for a, b in zip(even, odd)] + even[len(odd) :]
    return even, odd, both


def spread_weights(weight_ref, filters, tile, lanes):
    rows = []
    for row_tap in range(KERNEL):
        row = [weight_ref[row_tap, tap : tap + 1, lanes] for tap in range(KERNEL)]
        rows.append([jnp.broadcast_to(tap, (GROUPS, LANES)) for tap in row])
    columns = [part_taps([rows[tap][col] for tap in range(KERNEL)]) for col in range(KERNEL)]
    for row_part, many in enumerate(PARTS):
        for row in range(many):
            line = [columns[col][row_part][row] for col in range(KERNEL)]
            for col_part, taps in enumerate(part_taps(line)):
                start = FILTERS[row_part, col_part] + row * PARTS[col_part]
                for col, value in enumerate(taps):
                    filters[tile, start + col] = value


def fill_parts(load, parts, row_pairs, groups):
    for pair in range(row_pairs):
        for group in range(groups):
            middle = load(2 * pair + 1, group)
            parts[0, pair, group] = load(2 * pair, group) - middle
            if pair < row_pairs - 1:
                parts[1, pair, group] = load(2 * pair + 2, group) - middle


def part_line(load, parts, row_part, col_part, pair, many):
    def value(group):
        return load(2 * pair + 1, group) if row_part == 2 else parts[row_part, pair, group]

    first = (0, 2, 1)[col_part]
    line = [value(2 * col + first) for col in range(many)]
    if col_part < 2:
        line = [side - value(2 * col + 1) for col, side in enumerate(line)]
    return line


def conv_rows(load, filters, tile, bias, steps, count, parts, products, skipped=()):
    row_pairs, col_pairs = count // 2, steps // 2
    fill_parts(load, parts, row_pairs + 3, 2 * col_pairs + 6)
    for row_part in range(3):
        for col_part in range(3):
            start = FILTERS[row_part, col_part]
            many_rows, many_cols = PARTS[row_part], PARTS[col_part]
            total = [[None] * col_pairs for _ in range(row_pairs)]
            for place in range(row_pairs + many_rows - 1):
                if (row_part, place) in skipped:
                    continue
                line = part_line(
                    load, parts, row_part, col_part, place, col_pairs + many_cols - 1
                )
                for row in range(row_pairs):
                    tap_row = place - row
                    if not 0 <= tap_row < many_rows:
                        continue
                    for tap_col in range(many_cols):
                        scale = filters[tile, start + tap_row * many_cols + tap_col]
                        for col in range(col_pairs):
                            term = line[col + tap_col] * scale
                            old = total[row][col]
                            total[row][col] = term if old is None else old + term
            for row in range(row_pairs):
                for col in range(col_pairs):
                    products[3 * row_part + col_part, row, col] = total[row][col]
    found = []
    for row in range(row_pairs):
        lines = [[], []]
        for col in range(col_pairs):
            values = [products[part, row, col] for part in range(9)]
            shared = [values[6] + values[8] + bias, values[7] + values[8] + bias]
            for row_part in range(2):
                for col_part in range(2):
                    own = values[3 * row_part + col_part] + values[3 * row_part + 2]
                    lines[row_part].append(own + shared[col_part])
        found += lines
    return found


def rounded(lines):
    return jnp.concatenate([part for line in lines for part in line], axis=0).astype(narrow)


def parts_scratch(count, steps):
    row_pairs, col_pairs = count // 2, steps // 2
    return [
        pltpu.VMEM((2, row_pairs + 3, 2 * col_pairs + 6, GROUPS, LANES), wide),
        pltpu.VMEM((9, row_pairs, col_pairs, GROUPS, LANES), wide),
    ]


def reduce_part(conv_out, reduce_ref, reduce_bias_ref, before_out, feat_out):
    before = jnp.dot(conv_out[...], reduce_ref[...], preferred_element_type=wide)
    before = before + reduce_bias_ref[...]
    before_out[...] = before
    feat_out[...] = (before / (1.0 + jnp.exp(-before))).astype(narrow)
    feat = feat_out[...]
    gram = lax.dot_general(feat, feat, (((0,), (0,)), ((), ())), preferred_element_type=wide)
    return gram, jnp.sum(feat.astype(wide), axis=0, keepdims=True)


def inner_kernel(
    block, left, right, weight, bias, reduce_weight, reduce_bias,
    spread_out, filters, conv_out, before_out, feat_out, gram_out, colsum_out, partial_out,
    wide_row, parts, products,
):
    rows, cols = block.shape[0], block.shape[1]
    steps = cols // GROUPS

    def one_tile(tile, _):
        lanes = lanes_of(tile)
        spread_weights(weight, filters, tile, lanes)
        start_value = jnp.broadcast_to(bias[0:1, lanes], (GROUPS, LANES))

        def fill(turn, _):
            for row in range(FILL_ROWS):
                row = turn * FILL_ROWS + row
                place = wide_row.at[row]
                fill_row(place, block[row, :, lanes], left[row, :, lanes], right[row, :, lanes])
                spread_columns(place, spread_out.at[tile, row])
            return 0

        lax.fori_loop(0, rows // FILL_ROWS, fill, 0)

        def load_from(first):
            def load(row, group):
                place = first + row - HALF
                if 0 <= place < rows:
                    return spread_out[tile, place, group]
                return jnp.zeros((GROUPS, LANES), wide)

            return load

        conv_out[:, lanes] = rounded(
            conv_rows(
                load_from(SIDE), filters, tile, start_value, steps, rows - 2 * SIDE, parts, products
            )
        )
        last = SIDE // 2 + 2
        beyond = (
            [(row_part, 0) for row_part in range(3)],
            [(0, last), (1, last - 1), (2, last)],
        )
        for side, first in enumerate((0, rows - SIDE)):
            lines = conv_rows(
                load_from(first), filters, tile, start_value, steps, SIDE, parts, products,
                beyond[side],
            )
            for row, line in enumerate(lines):
                for step, value in enumerate(line):
                    partial_out[tile, side * SIDE + row, step] = value
        return 0

    lax.fori_loop(0, spread_out.shape[0], one_tile, 0)
    gram_out[...], colsum_out[...] = reduce_part(
        conv_out, reduce_weight, reduce_bias, before_out, feat_out
    )


def edge_kernel(
    flag, partial, top, bottom, filters, reduce_weight, reduce_bias, gram_in, colsum_in,
    spread_top, spread_bottom, conv_out, before_out, feat_out, kept_out, sent_out,
    wide_row, stage, sums,
):
    cols = wide_row.shape[1] - 2 * EDGE
    steps = cols // GROUPS

    def one_tile(tile, _):
        lanes = lanes_of(tile)
        for side, (strip, spread) in enumerate(((top, spread_top), (bottom, spread_bottom))):
            stage[side] = strip[:, lanes].astype(wide)
            for row in range(HALF):
                place = wide_row.at[side * HALF + row]
                left = HALF * cols + row * HALF
                right = left + HALF * HALF
                fill_row(
                    place,
                    stage[side, row * cols : (row + 1) * cols, :],
                    stage[side, left : left + HALF, :],
                    stage[side, right : right + HALF, :],
                )
                spread_columns(place, spread.at[tile, row])

        def filter_of(row_tap, col_tap):
            start = FILTERS[row_tap % 2, col_tap % 2]
            return filters[tile, start + row_tap // 2 * PARTS[col_tap % 2] + col_tap // 2]

        for side, spread in enumerate((spread_top, spread_bottom)):
            lines = [
                [partial[tile, side * SIDE + row, step] for step in range(steps)]
                for row in range(SIDE)
            ]
            for place in range(HALF):
                windows = [spread[tile, place, group] for group in range(steps + KERNEL - 1)]
                for row in range(SIDE):
                    row_tap = place - row if side == 0 else place + HALF + SIDE - row
                    if not 0 <= row_tap < KERNEL:
                        continue
                    for col_tap in range(KERNEL):
                        scale = filter_of(row_tap, col_tap)
                        for step in range(steps):
                            lines[row][step] = lines[row][step] + windows[step + col_tap] * scale
            start = side * SIDE * cols
            conv_out[start : start + SIDE * cols, lanes] = rounded(lines)
        return 0

    lax.fori_loop(0, partial.shape[0], one_tile, 0)
    gram, colsum = reduce_part(conv_out, reduce_weight, reduce_bias, before_out, feat_out)
    gram = gram + gram_in[...]
    colsum = colsum + colsum_in[...]
    half = gram.shape[0] // 2
    row = lax.broadcasted_iota(jnp.int32, (half, half), 0)
    col = lax.broadcasted_iota(jnp.int32, (half, half), 1)
    last_block = gram[half:, half:]
    diagonal = jnp.sum(jnp.where(row == col, last_block, 0.0), axis=0, keepdims=True)
    sums[:half, :half] = gram[:half, half:]
    sums[:half, half:] = jnp.where(row <= col, gram[:half, :half], last_block)
    sums[half : half + GROUPS, :] = jnp.broadcast_to(colsum, (GROUPS, 2 * half))
    sums[half + GROUPS :, :half] = jnp.broadcast_to(diagonal, (GROUPS, half))
    sums[half + GROUPS :, half:] = jnp.zeros((GROUPS, half), wide)
    part = kept_out.shape[0]
    keep_or_send(flag[0] != 0, sums[:part, :], sums[part:, :], kept_out, sent_out)


def keep_or_send(upper, low, high, kept_out, sent_out):
    kept_out[...] = jnp.where(upper, high, low)
    sent_out[...] = jnp.where(upper, low, high).astype(sent_out.dtype)


def edge_rows(rows):
    return list(range(SIDE)) + list(range(rows - SIDE, rows))


def shape_of(shape, dtype=wide):
    return jax.ShapeDtypeStruct(shape, dtype)


in_vmem = pl.BlockSpec(memory_space=pltpu.VMEM)
in_smem = pl.BlockSpec(memory_space=pltpu.SMEM)


def cost(microseconds):
    return pl.CostEstimate(
        flops=microseconds * 10**9, bytes_accessed=microseconds * 10**6, transcendentals=0
    )


def conv_inner(block, left, right, weight, bias, reduce_weight, reduce_bias):
    rows, cols, channels = block.shape
    width = reduce_weight.shape[1]
    tiles = channels // LANES
    steps = cols // GROUPS
    pixels = (rows - 2 * SIDE) * cols
    return pl.pallas_call(
        inner_kernel,
        in_specs=[in_vmem] * 7,
        out_specs=[in_vmem] * 8,
        out_shape=[
            shape_of((tiles, rows, steps + KERNEL - 1, GROUPS, LANES)),
            shape_of((tiles, PRODUCTS, GROUPS, LANES)),
            shape_of((pixels, channels), narrow),
            shape_of((pixels, width)),
            shape_of((pixels, width), narrow),
            shape_of((width, width)),
            shape_of((1, width)),
            shape_of((tiles, 2 * SIDE, steps, GROUPS, LANES)),
        ],
        scratch_shapes=[
            pltpu.VMEM((rows, cols + 2 * EDGE, LANES), wide),
            *parts_scratch(rows - 2 * SIDE, steps),
        ],
        compiler_params=params(24),
        cost_estimate=cost(10),
        name="conv_inner",
    )(block, left, right, weight, bias, reduce_weight, reduce_bias)


def conv_edge(flag, partial, halos, filters, reduce_weight, reduce_bias, gram, colsum):
    tiles, _, steps = partial.shape[:3]
    cols, groups = steps * GROUPS, steps + KERNEL - 1
    channels, width = reduce_weight.shape
    pixels = 2 * SIDE * cols
    side = (tiles, HALF, groups, GROUPS, LANES)
    sums_rows = width // 2 + 2 * GROUPS
    return pl.pallas_call(
        edge_kernel,
        in_specs=[in_smem] + [in_vmem] * 8,
        out_specs=[in_vmem] * 7,
        out_shape=[
            shape_of(side),
            shape_of(side),
            shape_of((pixels, channels), narrow),
            shape_of((pixels, width)),
            shape_of((pixels, width), narrow),
            shape_of((sums_rows // 2, width)),
            shape_of((sums_rows // 2, width)),
        ],
        scratch_shapes=[
            pltpu.VMEM((2 * HALF, cols + 2 * EDGE, LANES), wide),
            pltpu.VMEM((2,) + (halos[0].shape[0], LANES), wide),
            pltpu.VMEM((sums_rows, width), wide),
        ],
        compiler_params=params(24),
        cost_estimate=cost(6),
        name="conv_edge",
    )(flag, partial, *halos, filters, reduce_weight, reduce_bias, gram, colsum)


def split(value):
    high = value.astype(narrow)
    return high, (value - high.astype(wide)).astype(narrow)


def product(left, right):
    def dot(a, b):
        return jnp.dot(a, b, preferred_element_type=wide)

    return dot(left[0], right[0]) + (dot(left[0], right[1]) + dot(left[1], right[0]))


def square_root(current):
    size = current.shape[0]
    row = lax.broadcasted_iota(jnp.int32, (size, size), 0)
    col = lax.broadcasted_iota(jnp.int32, (size, size), 1)
    triple = jnp.where(row == col, 3.0, 0.0)
    factor = split(0.5 * (triple - current))
    current = split(current)
    trail = [(current, None, factor)]
    inverse = factor
    current = split(product(current, factor))
    for step in range(1, NEWTON_STEPS):
        factor = split(0.5 * (triple - product(inverse, current)))
        trail.append((current, inverse, factor))
        last = step == NEWTON_STEPS - 1
        if not last:
            inverse = split(product(factor, inverse))
        current = product(current, factor)
        if not last:
            current = split(current)
    return current, trail


def square_root_change(change, trail):
    first, _, factor = trail[0]
    move = split(change)
    factor_move = split(-0.5 * change)
    change = product(move, factor) + product(first, factor_move)
    inverse_move = factor_move
    for step in range(1, NEWTON_STEPS):
        current, inverse, factor = trail[step]
        move = split(change)
        factor_move = split(
            -0.5 * (product(inverse_move, current) + product(inverse, move))
        )
        change = product(move, factor) + product(current, factor_move)
        if step < NEWTON_STEPS - 1:
            inverse_move = split(product(factor_move, inverse) + product(factor, inverse_move))
    return change


def head_kernel(
    flag, label, class_bias, own, other, class_weight,
    feat_inner, feat_edge, gate_inner, gate_edge, conv_turned, reduce_turned,
    root_out, payload, conv_inner_out, conv_edge_out,
    sums, pre, *, count, image_count,
):
    width = root_out.shape[1]
    half = width // 2
    rows = own.shape[0]
    upper = flag[0] != 0
    mine, theirs = own[...], other[...]
    sums[:rows, :] = jnp.where(upper, theirs, mine)
    sums[rows:, :] = jnp.where(upper, mine, theirs)
    row = lax.broadcasted_iota(jnp.int32, (half, half), 0)
    col = lax.broadcasted_iota(jnp.int32, (half, half), 1)
    cross, mixed = sums[:half, :half], sums[:half, half:]
    turned = mixed.T
    first = jnp.where(row <= col, mixed, turned)
    diagonal = jnp.broadcast_to(sums[half + GROUPS : half + GROUPS + 1, :half], (half, half))
    last = jnp.where(row == col, diagonal, jnp.where(row > col, mixed, turned))
    gram = jnp.concatenate(
        [
            jnp.concatenate([first, cross], axis=1),
            jnp.concatenate([cross.T, last], axis=1),
        ],
        axis=0,
    )
    mean_row = sums[half : half + 1, :] / count
    mean_col = jnp.broadcast_to(mean_row, (width, width)).T
    sigma = gram / count - mean_col * mean_row
    row = lax.broadcasted_iota(jnp.int32, (width, width), 0)
    col = lax.broadcasted_iota(jnp.int32, (width, width), 1)
    diagonal = row == col
    trace_value = jnp.sum(jnp.where(diagonal, sigma, 0.0), keepdims=True) + epsilon
    root_scale = jnp.sqrt(trace_value)
    unit, trail = square_root(sigma / trace_value)
    root = root_scale * unit
    root_out[:width, :] = root

    classes = class_weight.shape[0]
    slots = root_out.shape[0] - width
    place = lax.broadcasted_iota(jnp.int32, (slots, 1), 0)
    bias = jnp.zeros((slots, 1), wide)
    for index in range(classes):
        bias = jnp.where(place == index, class_bias[index], bias)
    partial = [
        jnp.sum(class_weight[index].astype(wide) * root, axis=0, keepdims=True)
        for index in range(classes)
    ]
    partial.append(jnp.zeros((slots - classes, width), wide))
    logits = jnp.sum(jnp.concatenate(partial, axis=0), axis=1, keepdims=True) + bias
    onehot = jnp.where(place == label[0], 1.0, 0.0)
    soft = jnp.maximum(logits, 0.0) + jnp.log(1.0 + jnp.exp(-jnp.abs(logits)))
    share = 1.0 / (1.0 + jnp.exp(-logits))
    used = place < classes
    loss_part = jnp.sum(jnp.where(used, soft - onehot * logits, 0.0), keepdims=True)
    logit_grad = jnp.where(used, loss_scale * (share - onehot) / image_count, 0.0)
    root_out[width:, :] = jnp.broadcast_to(
        jnp.where(place == classes, loss_part, logit_grad), (slots, width)
    )
    across = lax.broadcasted_iota(jnp.int32, (slots, width), 1)
    facts = jnp.where(place == classes, loss_part, logit_grad)
    root_out[width + slots - 1 :, :] = jnp.sum(
        jnp.where(across == place, facts, 0.0), axis=0, keepdims=True
    )

    root_grad = jnp.zeros((width, width), wide)
    for index in range(classes):
        root_grad = root_grad + class_weight[index].astype(wide) * logit_grad[index : index + 1, :]
    root_grad = root_grad + root_grad.T
    change = square_root_change(root_scale * root_grad, trail)
    trace_grad = jnp.sum(root_grad * unit, keepdims=True) / (2.0 * root_scale) - jnp.sum(
        change * sigma, keepdims=True
    ) / (trace_value * trace_value)
    symmetric = (
        (change / trace_value + jnp.where(diagonal, trace_grad, 0.0)) / count
    ).astype(narrow)
    mean_term = jnp.sum(mean_col * symmetric.astype(wide), axis=0, keepdims=True)

    inner = feat_inner.shape[0]
    for feat, gate, start in ((feat_inner, gate_inner, 0), (feat_edge, gate_edge, inner)):
        grad = jnp.dot(feat[...], symmetric, preferred_element_type=wide) - mean_term
        pre[start : start + feat.shape[0], :] = (grad * gate[...]).astype(narrow)
    pre_grad = pre[...]
    payload[width:, :] = jnp.zeros((payload.shape[0] - width, payload.shape[1]), wide)
    taps = KERNEL * KERNEL
    payload[width + taps + 1 : width + taps + 2, :width] = jnp.sum(
        pre_grad.astype(wide), axis=0, keepdims=True
    )
    for first in range(0, conv_turned.shape[0], width):
        payload[:width, first : first + width] = jnp.dot(
            conv_turned[first : first + width, :], pre_grad, preferred_element_type=wide
        )
    for out, start in ((conv_inner_out, 0), (conv_edge_out, inner)):
        out[...] = jnp.dot(
            pre[start : start + out.shape[0], :], reduce_turned[...], preferred_element_type=wide
        ).astype(narrow)


def head(flag, label, class_bias, own, other, class_weight, prepared, count, image_count):
    feat_inner, feat_edge, gate_inner, gate_edge, conv_turned, reduce_turned = prepared
    width, channels = reduce_turned.shape
    inner, edge = feat_inner.shape[0], feat_edge.shape[0]
    slots = -(-(class_weight.shape[0] + 2) // GROUPS) * GROUPS
    return pl.pallas_call(
        functools.partial(head_kernel, count=count, image_count=image_count),
        in_specs=[in_smem] * 3 + [in_vmem] * 9,
        out_specs=[in_vmem] * 4,
        out_shape=[
            shape_of((width + slots, width)),
            shape_of((width + TAPS_ROWS, channels)),
            shape_of((inner, channels), narrow),
            shape_of((edge, channels), narrow),
        ],
        scratch_shapes=[
            pltpu.VMEM((2 * own.shape[0], width), wide),
            pltpu.VMEM((inner + edge, width), narrow),
        ],
        compiler_params=params(24),
        cost_estimate=cost(10),
        name="head",
    )(
        flag, label, class_bias, own, other, class_weight,
        feat_inner, feat_edge, gate_inner, gate_edge, conv_turned, reduce_turned,
    )


def prepare_kernel(
    before_inner, before_edge, conv_inner_in, conv_edge_in, reduce_weight,
    gate_inner, gate_edge, conv_turned, reduce_turned,
):
    for before, gate in ((before_inner, gate_inner), (before_edge, gate_edge)):
        value = before[...]
        share = 1.0 / (1.0 + jnp.exp(-value))
        gate[...] = share * (1.0 + value * (1.0 - share))
    inner = conv_inner_in.shape[0]
    conv_turned[:, :inner] = conv_inner_in[...].T
    conv_turned[:, inner:] = conv_edge_in[...].T
    reduce_turned[...] = reduce_weight[...].T


def prepare(before_inner, before_edge, conv_in, conv_ed, reduce_weight):
    channels, width = reduce_weight.shape
    inner, edge = before_inner.shape[0], before_edge.shape[0]
    return pl.pallas_call(
        prepare_kernel,
        in_specs=[in_vmem] * 5,
        out_specs=[in_vmem] * 4,
        out_shape=[
            shape_of((inner, width)),
            shape_of((edge, width)),
            shape_of((channels, inner + edge), narrow),
            shape_of((width, channels), narrow),
        ],
        compiler_params=params(16),
        cost_estimate=cost(1),
        name="prepare",
    )(before_inner, before_edge, conv_in, conv_ed, reduce_weight)


def taps_kernel(
    spread_in, spread_top, spread_bottom, grad_inner, grad_edge, payload_in, payload,
    parts, grads, products, out, *, first, last,
):
    rows = spread_in.shape[1]
    row_pairs, col_pairs = grads.shape[1:3]
    steps = 2 * col_pairs
    cols = steps * GROUPS
    order = edge_rows(rows)
    taps = KERNEL * KERNEL
    base = payload.shape[0] - TAPS_ROWS

    def one_tile(tile, _):
        lanes = lanes_of(tile)

        def grad_row(row):
            if row in order:
                source, place = grad_edge, order.index(row)
            else:
                source, place = grad_inner, row - SIDE
            values = source[place * cols : (place + 1) * cols, lanes].astype(wide)
            return [values[step * GROUPS : (step + 1) * GROUPS, :] for step in range(steps)]

        for pair in range(row_pairs):
            even, odd = grad_row(2 * pair), grad_row(2 * pair + 1)
            both = [a + b for a, b in zip(even, odd)]
            for row_part, line in enumerate((even, odd, both)):
                for col in range(col_pairs):
                    grads[3 * row_part, pair, col] = line[2 * col]
                    grads[3 * row_part + 1, pair, col] = line[2 * col + 1]
                    grads[3 * row_part + 2, pair, col] = line[2 * col] + line[2 * col + 1]

        def load(place, group):
            place = place - HALF
            if place < 0:
                return spread_top[tile, place + HALF, group]
            if place >= rows:
                return spread_bottom[tile, place - rows, group]
            return spread_in[tile, place, group]

        fill_parts(load, parts, row_pairs + 3, 2 * col_pairs + 6)
        for row_part in range(3):
            for col_part in range(3):
                part = 3 * row_part + col_part
                start = FILTERS[row_part, col_part]
                many_rows, many_cols = PARTS[row_part], PARTS[col_part]
                total = {}
                for place in range(row_pairs + many_rows - 1):
                    line = part_line(
                        load, parts, row_part, col_part, place, col_pairs + many_cols - 1
                    )
                    for tap_row in range(many_rows):
                        row = place - tap_row
                        if not 0 <= row < row_pairs:
                            continue
                        for col in range(col_pairs):
                            grad = grads[part, row, col]
                            for tap_col in range(many_cols):
                                term = line[col + tap_col] * grad
                                tap = tap_row * many_cols + tap_col
                                total[tap] = total[tap] + term if tap in total else term
                for tap, value in total.items():
                    products[start + tap] = value

        for row_tap in range(KERNEL):
            for col_tap in range(KERNEL):
                place = (row_tap // 2, col_tap // 2)
                found = None
                for row_part in (row_tap % 2, 2):
                    for col_part in (col_tap % 2, 2):
                        start = FILTERS[row_part, col_part]
                        value = products[start + place[0] * PARTS[col_part] + place[1]]
                        found = value if found is None else found + value
                tap = row_tap * KERNEL + col_tap
                out[tap : tap + 1, :] = jnp.sum(found, axis=0, keepdims=True)
        found = [
            sum(grads[8, pair, col] for col in range(1, col_pairs)) + grads[8, pair, 0]
            for pair in range(row_pairs)
        ]
        out[taps : taps + 1, :] = jnp.sum(sum(found[1:], found[0]), axis=0, keepdims=True)
        payload[pl.ds(base, taps + 1), lanes] = out[: taps + 1, :]
        return 0

    lax.fori_loop(first, last, one_tile, 0)


def tap_grads(spreads, grads, payload, first, last):
    rows, groups = spreads[0].shape[1:3]
    row_pairs, col_pairs = rows // 2, (groups - KERNEL + 1) // 2
    return pl.pallas_call(
        functools.partial(taps_kernel, first=first, last=last),
        in_specs=[in_vmem] * 6,
        out_specs=in_vmem,
        out_shape=shape_of(payload.shape),
        input_output_aliases={5: 0},
        scratch_shapes=[
            pltpu.VMEM((2, row_pairs + 3, 2 * col_pairs + 6, GROUPS, LANES), wide),
            pltpu.VMEM((9, row_pairs, col_pairs, GROUPS, LANES), wide),
            pltpu.VMEM((PRODUCTS, GROUPS, LANES), wide),
            pltpu.VMEM((TAPS_ROWS, LANES), wide),
        ],
        compiler_params=params(16),
        cost_estimate=cost(2 * (last - first)),
        name="tap_grads",
    )(*spreads, *grads, payload)


def finish_kernel(flag, own, other, *refs, image_count):
    known = refs[:-7]
    weight_out, depth_out, depth_bias_out, bias_out, class_bias_out, loss_out, payload = refs[-7:]
    part = own.shape[0]
    upper = flag[0] != 0
    mine, theirs = own[...].astype(wide), other[...].astype(wide)
    payload[:part, :] = jnp.where(upper, theirs, mine)
    payload[part:, :] = jnp.where(upper, mine, theirs)
    width = weight_out.shape[1]
    for first in range(0, weight_out.shape[0], width):
        weight_out[first : first + width, :] = payload[:width, first : first + width]
    for row_tap in range(KERNEL):
        start = width + row_tap * KERNEL
        depth_out[row_tap] = payload[start : start + KERNEL, :]
    taps = KERNEL * KERNEL
    depth_bias_out[...] = payload[width + taps, :]
    bias_out[...] = payload[width + taps + 1, :width]
    totals = tree_sum([part[part.shape[0] - 1 :, :] for part in known])
    classes = class_bias_out.shape[0]
    class_bias_out[...] = totals[0, :classes]
    across = lax.broadcasted_iota(jnp.int32, totals.shape, 1)
    loss_out[0] = jnp.sum(jnp.where(across == classes, totals, 0.0)) / image_count


def finish(flag, own, other, known, width, classes, image_count):
    part, channels = own.shape
    return pl.pallas_call(
        functools.partial(finish_kernel, image_count=image_count),
        in_specs=[in_smem] + [in_vmem] * (2 + len(known)),
        out_specs=[in_vmem] * 5 + [in_smem],
        out_shape=[
            shape_of((channels, width)),
            shape_of((KERNEL, KERNEL, channels)),
            shape_of((channels,)),
            shape_of((width,)),
            shape_of((classes,)),
            shape_of((1,)),
        ],
        scratch_shapes=[pltpu.VMEM((2 * part, channels), wide)],
        compiler_params=params(8),
        cost_estimate=cost(1),
        name="finish",
    )(flag, own, other, *known)


def edge_strip(block, left, right, rows):
    channels = block.shape[2]
    return jnp.concatenate([part[rows].reshape(-1, channels) for part in (block, left, right)])


def body(
    features, depth_weight, depth_bias, reduce_weight, reduce_bias, class_weight, class_bias, labels
):
    together = lax.optimization_barrier
    block = features[0]
    rows, cols, channels = block.shape
    width = reduce_weight.shape[1]
    classes = class_bias.shape[0]
    count = rows * cols * lax.axis_size("sy") * lax.axis_size("sx")
    image_count = features.shape[0] * lax.axis_size("dp")

    flag = is_upper("sx", 1).astype(jnp.int32)[None]
    upper = is_upper("sx", 1)
    corner = 2 * (lax.axis_index("dp") & 1) + ((lax.axis_index("sx") & 2) >> 1)
    places = [corner ^ turn for turn in range(4)]
    bias_row = depth_bias[None]
    reduce_row = reduce_bias[None]
    left = next_along(block[:, cols - HALF :], "sx")
    right = back_along(block[:, :HALF], "sx")
    low, high, left, right, flag, upper, places, bias_row, reduce_row = together(
        (
            edge_strip(block, left, right, slice(rows - HALF, rows)),
            edge_strip(block, left, right, slice(0, HALF)),
            left,
            right,
            flag,
            upper,
            places,
            bias_row,
            reduce_row,
        )
    )
    top = next_along(low, "sy")
    bottom = back_along(high, "sy")
    spread, filters, conv_in, before_in, feat_in, gram, colsum, partial = conv_inner(
        block, left, right, depth_weight, bias_row, reduce_weight, reduce_row
    )
    spread_top, spread_bottom, conv_ed, before_ed, feat_ed, kept, sent = conv_edge(
        flag, partial, (top, bottom), filters, reduce_weight, reduce_row, gram, colsum
    )

    sums = kept + swap(sent, "sx", 1)
    sums, before_in, before_ed, conv_in, conv_ed = together(
        (sums, before_in, before_ed, conv_in, conv_ed)
    )
    gate_in, gate_ed, conv_turned, reduce_turned = prepare(
        before_in, before_ed, conv_in, conv_ed, reduce_weight
    )
    for shift in doublings("sx", 2):
        sums = exchange(sums, "sx", shift, wide)
    sums, gate_in, gate_ed, conv_turned, reduce_turned = together(
        (sums, gate_in, gate_ed, conv_turned, reduce_turned)
    )
    for shift in doublings("sy"):
        sums = exchange(sums, "sy", shift, wide)
    other = swap(sums, "sx", 1)

    root, payload, *grads = head(
        flag,
        labels,
        class_bias,
        sums,
        other,
        class_weight,
        (feat_in, feat_ed, gate_in, gate_ed, conv_turned, reduce_turned),
        count,
        image_count,
    )
    known = [root] + [swap(root, "dp", shift) for shift in range(1, lax.axis_size("dp"))]
    spreads = (spread, spread_top, spread_bottom)
    tiles = channels // LANES
    payload = tap_grads(spreads, grads, payload, 0, tiles - 1)
    payload, known = together((payload, known))
    payload = tap_grads(spreads, grads, payload, tiles - 1, tiles)

    part = payload.shape[0] // 2
    low, high = payload[:part], payload[part:]
    kept, sent = jnp.where(upper, high, low), jnp.where(upper, low, high)
    payload = kept + swap(sent.astype(narrow), "sx", 1).astype(wide)
    axes = ("dp", "sx")
    pairs = square_pairs(axes, (1, 2))
    payload = square_scatter(payload, axes, pairs, places, narrow)
    for shift in doublings("dp", 2):
        payload = exchange(payload, "dp", shift, narrow)
    for shift in doublings("sy"):
        payload = exchange(payload, "sy", shift, narrow)
    payload = payload.astype(narrow)
    payload, known = together((payload, known))
    class_weight_grad = tree_sum(
        [part[width : width + classes, 0][:, None, None] * part[None, :width] for part in known]
    )
    payload, class_weight_grad = together(
        (square_gather(payload, axes, pairs, places), class_weight_grad)
    )
    other = swap(payload, "sx", 1)
    weight_grad, depth_grad, depth_bias_grad, bias_grad, class_bias_grad, loss = finish(
        flag, payload, other, known, width, classes, image_count
    )
    return (
        loss[0],
        depth_grad,
        depth_bias_grad,
        weight_grad,
        bias_grad,
        class_weight_grad,
        class_bias_grad,
    )


def solution(mesh):
    placed = (P("dp", "sy", "sx", None), P(), P(), P(), P(), P(), P(), P("dp"))
    return jax.shard_map(
        body,
        mesh=mesh,
        in_specs=placed,
        out_specs=(P(), P(), P(), P(), P(), P(), P()),
        check_vma=False,
    )
```

```python
import functools

import jax
import jax.numpy as jnp
from jax import lax
from jax.experimental import pallas as pl
from jax.experimental.pallas import tpu as pltpu
from jax.sharding import PartitionSpec as P

KERNEL = 7
HALF = KERNEL // 2
NEWTON_STEPS = 5
LANES = 128
GROUPS = 8
EDGE = 8
TAPS_ROWS = 64
SIDE = 4
FILL_ROWS = 4
PARTS = (4, 3, 4)

epsilon = 1e-05
loss_scale = 64.0
narrow = jnp.bfloat16
wide = jnp.float32


def params(megabytes):
    return pltpu.CompilerParams(vmem_limit_bytes=megabytes * 1024 * 1024)


def swap(value, axis, shift):
    count = lax.axis_size(axis)
    return lax.ppermute(value, axis, [(i, i ^ shift) for i in range(count)])


def is_upper(axis, shift):
    return (lax.axis_index(axis) & shift) != 0


def tree_sum(terms):
    while len(terms) > 1:
        terms = [terms[i] + terms[i + 1] for i in range(0, len(terms), 2)]
    return terms[0]


def exchange(value, axis, shift, sent_as):
    sent = value.astype(sent_as)
    return sent.astype(wide) + swap(sent, axis, shift).astype(wide)


def square_pairs(axes, shifts):
    counts = [lax.axis_size(axis) for axis in axes]
    return {
        2 * first + second: [
            (i * counts[1] + j, (i ^ (first * shifts[0])) * counts[1] + (j ^ (second * shifts[1])))
            for i in range(counts[0])
            for j in range(counts[1])
        ]
        for first, second in ((0, 1), (1, 0), (1, 1))
    }


def square_scatter(value, axes, pairs, places, sent_as):
    pieces = value.reshape((4, value.shape[0] // 4) + value.shape[1:])

    def piece(turn):
        starts = (places[turn],) + (0,) * value.ndim
        sizes = (1,) + pieces.shape[1:]
        return lax.dynamic_slice(pieces, starts, sizes, allow_negative_indices=False)[0]

    moved = [
        lax.ppermute(piece(turn).astype(sent_as), axes, pairs[turn]).astype(wide)
        for turn in (1, 2, 3)
    ]
    return tree_sum([piece(0)] + moved)


def square_gather(value, axes, pairs, places):
    whole = jnp.zeros((4,) + value.shape, value.dtype)
    for turn in range(4):
        part = lax.ppermute(value, axes, pairs[turn]) if turn else value
        starts = (places[turn],) + (0,) * value.ndim
        whole = lax.dynamic_update_slice(whole, part[None], starts, allow_negative_indices=False)
    return whole.reshape((-1,) + value.shape[1:])


def doublings(axis, first=1):
    found = []
    shift = first
    while shift < lax.axis_size(axis):
        found.append(shift)
        shift *= 2
    return found


def next_along(value, axis):
    return lax.ppermute(value, axis, [(i, i + 1) for i in range(lax.axis_size(axis) - 1)])


def back_along(value, axis):
    return lax.ppermute(value, axis, [(i + 1, i) for i in range(lax.axis_size(axis) - 1)])


def spread_columns(source, target):
    for group in range(target.shape[0]):
        target[group] = source[pl.ds(EDGE - HALF + group, GROUPS, stride=GROUPS), :]


def fill_row(wide_row, middle, left, right):
    cols = middle.shape[0]
    wide_row[EDGE : EDGE + cols, :] = middle.astype(wide)
    wide_row[EDGE - HALF : EDGE, :] = left.astype(wide)
    wide_row[EDGE + cols : EDGE + cols + HALF, :] = right.astype(wide)


def lanes_of(tile):
    return pl.ds(pl.multiple_of(tile * LANES, LANES), LANES)


def part_starts():
    starts, total = {}, 0
    for row_part in range(3):
        for col_part in range(3):
            starts[row_part, col_part] = total
            total += PARTS[row_part] * PARTS[col_part]
    return starts, total


FILTERS, PRODUCTS = part_starts()


def part_taps(taps):
    even, odd = taps[0::2], taps[1::2]
    both = [a + b for a, b in zip(even, odd)] + even[len(odd) :]
    return even, odd, both


def spread_weights(weight_ref, filters, tile, lanes):
    rows = []
    for row_tap in range(KERNEL):
        row = [weight_ref[row_tap, tap : tap + 1, lanes] for tap in range(KERNEL)]
        rows.append([jnp.broadcast_to(tap, (GROUPS, LANES)) for tap in row])
    columns = [part_taps([rows[tap][col] for tap in range(KERNEL)]) for col in range(KERNEL)]
    for row_part, many in enumerate(PARTS):
        for row in range(many):
            line = [columns[col][row_part][row] for col in range(KERNEL)]
            for col_part, taps in enumerate(part_taps(line)):
                start = FILTERS[row_part, col_part] + row * PARTS[col_part]
                for col, value in enumerate(taps):
                    filters[tile, start + col] = value


def fill_parts(load, parts, row_pairs, groups):
    for pair in range(row_pairs):
        for group in range(groups):
            middle = load(2 * pair + 1, group)
            parts[0, pair, group] = load(2 * pair, group) - middle
            if pair < row_pairs - 1:
                parts[1, pair, group] = load(2 * pair + 2, group) - middle


def part_line(load, parts, row_part, col_part, pair, many):
    def value(group):
        return load(2 * pair + 1, group) if row_part == 2 else parts[row_part, pair, group]

    first = (0, 2, 1)[col_part]
    line = [value(2 * col + first) for col in range(many)]
    if col_part < 2:
        line = [side - value(2 * col + 1) for col, side in enumerate(line)]
    return line


def conv_rows(load, filters, tile, bias, steps, count, parts, products):
    row_pairs, col_pairs = count // 2, steps // 2
    fill_parts(load, parts, row_pairs + 3, 2 * col_pairs + 6)
    for row_part in range(3):
        for col_part in range(3):
            start = FILTERS[row_part, col_part]
            many_rows, many_cols = PARTS[row_part], PARTS[col_part]
            total = [[None] * col_pairs for _ in range(row_pairs)]
            for place in range(row_pairs + many_rows - 1):
                line = part_line(
                    load, parts, row_part, col_part, place, col_pairs + many_cols - 1
                )
                for row in range(row_pairs):
                    tap_row = place - row
                    if not 0 <= tap_row < many_rows:
                        continue
                    for tap_col in range(many_cols):
                        scale = filters[tile, start + tap_row * many_cols + tap_col]
                        for col in range(col_pairs):
                            term = line[col + tap_col] * scale
                            old = total[row][col]
                            total[row][col] = term if old is None else old + term
            for row in range(row_pairs):
                for col in range(col_pairs):
                    products[3 * row_part + col_part, row, col] = total[row][col]
    found = []
    for row in range(row_pairs):
        lines = [[], []]
        for col in range(col_pairs):
            values = [products[part, row, col] for part in range(9)]
            shared = [values[6] + values[8] + bias, values[7] + values[8] + bias]
            for row_part in range(2):
                for col_part in range(2):
                    own = values[3 * row_part + col_part] + values[3 * row_part + 2]
                    lines[row_part].append(own + shared[col_part])
        found += lines
    return found


def rounded(lines):
    return jnp.concatenate([part for line in lines for part in line], axis=0).astype(narrow)


def parts_scratch(count, steps):
    row_pairs, col_pairs = count // 2, steps // 2
    return [
        pltpu.VMEM((2, row_pairs + 3, 2 * col_pairs + 6, GROUPS, LANES), wide),
        pltpu.VMEM((9, row_pairs, col_pairs, GROUPS, LANES), wide),
    ]


def reduce_part(conv_out, reduce_ref, reduce_bias_ref, before_out, feat_out):
    before = jnp.dot(conv_out[...], reduce_ref[...], preferred_element_type=wide)
    before = before + reduce_bias_ref[...]
    before_out[...] = before
    feat_out[...] = (before / (1.0 + jnp.exp(-before))).astype(narrow)
    feat = feat_out[...]
    gram = lax.dot_general(feat, feat, (((0,), (0,)), ((), ())), preferred_element_type=wide)
    return gram, jnp.sum(feat.astype(wide), axis=0, keepdims=True)


def inner_kernel(
    block, left, right, weight, bias, reduce_weight, reduce_bias,
    spread_out, filters, conv_out, before_out, feat_out, gram_out, colsum_out, partial_out,
    wide_row, parts, products,
):
    rows, cols = block.shape[0], block.shape[1]
    steps = cols // GROUPS

    def one_tile(tile, _):
        lanes = lanes_of(tile)
        spread_weights(weight, filters, tile, lanes)
        start_value = jnp.broadcast_to(bias[0:1, lanes], (GROUPS, LANES))

        def fill(turn, _):
            for row in range(FILL_ROWS):
                row = turn * FILL_ROWS + row
                place = wide_row.at[row]
                fill_row(place, block[row, :, lanes], left[row, :, lanes], right[row, :, lanes])
                spread_columns(place, spread_out.at[tile, row])
            return 0

        lax.fori_loop(0, rows // FILL_ROWS, fill, 0)

        def load_from(first):
            def load(row, group):
                place = first + row - HALF
                if 0 <= place < rows:
                    return spread_out[tile, place, group]
                return jnp.zeros((GROUPS, LANES), wide)

            return load

        conv_out[:, lanes] = rounded(
            conv_rows(
                load_from(SIDE), filters, tile, start_value, steps, rows - 2 * SIDE, parts, products
            )
        )
        for side, first in enumerate((0, rows - SIDE)):
            lines = conv_rows(
                load_from(first), filters, tile, start_value, steps, SIDE, parts, products
            )
            for row, line in enumerate(lines):
                for step, value in enumerate(line):
                    partial_out[tile, side * SIDE + row, step] = value
        return 0

    lax.fori_loop(0, spread_out.shape[0], one_tile, 0)
    gram_out[...], colsum_out[...] = reduce_part(
        conv_out, reduce_weight, reduce_bias, before_out, feat_out
    )


def edge_kernel(
    flag, partial, top, bottom, filters, reduce_weight, reduce_bias, gram_in, colsum_in,
    spread_top, spread_bottom, conv_out, before_out, feat_out, kept_out, sent_out,
    wide_row, stage, sums,
):
    steps = partial.shape[2]
    cols = steps * GROUPS

    def one_tile(tile, _):
        lanes = lanes_of(tile)
        for side, (strip, spread) in enumerate(((top, spread_top), (bottom, spread_bottom))):
            stage[side] = strip[:, lanes].astype(wide)
            for row in range(HALF):
                place = wide_row.at[side * HALF + row]
                left = HALF * cols + row * HALF
                right = left + HALF * HALF
                fill_row(
                    place,
                    stage[side, row * cols : (row + 1) * cols, :],
                    stage[side, left : left + HALF, :],
                    stage[side, right : right + HALF, :],
                )
                spread_columns(place, spread.at[tile, row])

        def filter_of(row_tap, col_tap):
            start = FILTERS[row_tap % 2, col_tap % 2]
            return filters[tile, start + row_tap // 2 * PARTS[col_tap % 2] + col_tap // 2]

        for side, spread in enumerate((spread_top, spread_bottom)):
            lines = [
                [partial[tile, side * SIDE + row, step] for step in range(steps)]
                for row in range(SIDE)
            ]
            for place in range(HALF):
                windows = [spread[tile, place, group] for group in range(steps + KERNEL - 1)]
                for row in range(SIDE):
                    row_tap = place - row if side == 0 else place + HALF + SIDE - row
                    if not 0 <= row_tap < KERNEL:
                        continue
                    for col_tap in range(KERNEL):
                        scale = filter_of(row_tap, col_tap)
                        for step in range(steps):
                            lines[row][step] = lines[row][step] + windows[step + col_tap] * scale
            start = side * SIDE * cols
            conv_out[start : start + SIDE * cols, lanes] = rounded(lines)
        return 0

    lax.fori_loop(0, partial.shape[0], one_tile, 0)
    gram, colsum = reduce_part(conv_out, reduce_weight, reduce_bias, before_out, feat_out)
    gram = gram + gram_in[...]
    colsum = colsum + colsum_in[...]
    half = gram.shape[0] // 2
    row = lax.broadcasted_iota(jnp.int32, (half, half), 0)
    col = lax.broadcasted_iota(jnp.int32, (half, half), 1)
    last_block = gram[half:, half:]
    diagonal = jnp.sum(jnp.where(row == col, last_block, 0.0), axis=0, keepdims=True)
    sums[:half, :half] = gram[:half, half:]
    sums[:half, half:] = jnp.where(row <= col, gram[:half, :half], last_block)
    sums[half : half + GROUPS, :] = jnp.broadcast_to(colsum, (GROUPS, 2 * half))
    sums[half + GROUPS :, :half] = jnp.broadcast_to(diagonal, (GROUPS, half))
    sums[half + GROUPS :, half:] = jnp.zeros((GROUPS, half), wide)
    part = kept_out.shape[0]
    keep_or_send(flag[0] != 0, sums[:part, :], sums[part:, :], kept_out, sent_out)


def keep_or_send(upper, low, high, kept_out, sent_out):
    kept_out[...] = jnp.where(upper, high, low)
    sent_out[...] = jnp.where(upper, low, high).astype(sent_out.dtype)


def edge_rows(rows):
    return list(range(SIDE)) + list(range(rows - SIDE, rows))


def shape_of(shape, dtype=wide):
    return jax.ShapeDtypeStruct(shape, dtype)


in_vmem = pl.BlockSpec(memory_space=pltpu.VMEM)
in_smem = pl.BlockSpec(memory_space=pltpu.SMEM)


def cost(microseconds):
    return pl.CostEstimate(
        flops=microseconds * 10**9, bytes_accessed=microseconds * 10**6, transcendentals=0
    )


def conv_inner(block, left, right, weight, bias, reduce_weight, reduce_bias):
    rows, cols, channels = block.shape
    width = reduce_weight.shape[1]
    tiles = channels // LANES
    steps = cols // GROUPS
    pixels = (rows - 2 * SIDE) * cols
    return pl.pallas_call(
        inner_kernel,
        in_specs=[in_vmem] * 7,
        out_specs=[in_vmem] * 8,
        out_shape=[
            shape_of((tiles, rows, steps + KERNEL - 1, GROUPS, LANES)),
            shape_of((tiles, PRODUCTS, GROUPS, LANES)),
            shape_of((pixels, channels), narrow),
            shape_of((pixels, width)),
            shape_of((pixels, width), narrow),
            shape_of((width, width)),
            shape_of((1, width)),
            shape_of((tiles, 2 * SIDE, steps, GROUPS, LANES)),
        ],
        scratch_shapes=[
            pltpu.VMEM((rows, cols + 3 * EDGE, LANES), wide),
            *parts_scratch(rows - 2 * SIDE, steps),
        ],
        compiler_params=params(24),
        cost_estimate=cost(10),
        name="conv_inner",
    )(block, left, right, weight, bias, reduce_weight, reduce_bias)


def conv_edge(flag, partial, halos, filters, reduce_weight, reduce_bias, gram, colsum):
    tiles, _, steps = partial.shape[:3]
    cols, groups = steps * GROUPS, steps + KERNEL - 1
    channels, width = reduce_weight.shape
    pixels = 2 * SIDE * cols
    side = (tiles, HALF, groups, GROUPS, LANES)
    sums_rows = width // 2 + 2 * GROUPS
    return pl.pallas_call(
        edge_kernel,
        in_specs=[in_smem] + [in_vmem] * 8,
        out_specs=[in_vmem] * 7,
        out_shape=[
            shape_of(side),
            shape_of(side),
            shape_of((pixels, channels), narrow),
            shape_of((pixels, width)),
            shape_of((pixels, width), narrow),
            shape_of((sums_rows // 2, width)),
            shape_of((sums_rows // 2, width)),
        ],
        scratch_shapes=[
            pltpu.VMEM((2 * HALF, cols + 3 * EDGE, LANES), wide),
            pltpu.VMEM((2,) + (halos[0].shape[0], LANES), wide),
            pltpu.VMEM((sums_rows, width), wide),
        ],
        compiler_params=params(24),
        cost_estimate=cost(6),
        name="conv_edge",
    )(flag, partial, *halos, filters, reduce_weight, reduce_bias, gram, colsum)


def split(value):
    high = value.astype(narrow)
    return high, (value - high.astype(wide)).astype(narrow)


def product(left, right):
    def dot(a, b):
        return jnp.dot(a, b, preferred_element_type=wide)

    return dot(left[0], right[0]) + (dot(left[0], right[1]) + dot(left[1], right[0]))


def square_root(current):
    size = current.shape[0]
    row = lax.broadcasted_iota(jnp.int32, (size, size), 0)
    col = lax.broadcasted_iota(jnp.int32, (size, size), 1)
    triple = jnp.where(row == col, 3.0, 0.0)
    factor = split(0.5 * (triple - current))
    current = split(current)
    trail = [(current, None, factor)]
    inverse = factor
    current = split(product(current, factor))
    for step in range(1, NEWTON_STEPS):
        factor = split(0.5 * (triple - product(inverse, current)))
        trail.append((current, inverse, factor))
        last = step == NEWTON_STEPS - 1
        if not last:
            inverse = split(product(factor, inverse))
        current = product(current, factor)
        if not last:
            current = split(current)
    return current, trail


def square_root_change(change, trail):
    first, _, factor = trail[0]
    move = split(change)
    factor_move = split(-0.5 * change)
    change = product(move, factor) + product(first, factor_move)
    inverse_move = factor_move
    for step in range(1, NEWTON_STEPS):
        current, inverse, factor = trail[step]
        move = split(change)
        factor_move = split(
            -0.5 * (product(inverse_move, current) + product(inverse, move))
        )
        change = product(move, factor) + product(current, factor_move)
        if step < NEWTON_STEPS - 1:
            inverse_move = split(product(factor_move, inverse) + product(factor, inverse_move))
    return change


def head_kernel(
    flag, label, class_bias, own, other, class_weight,
    feat_inner, feat_edge, gate_inner, gate_edge, conv_turned, reduce_turned,
    root_out, payload, conv_inner_out, conv_edge_out,
    sums, pre, *, count, image_count,
):
    width = root_out.shape[1]
    half = width // 2
    rows = own.shape[0]
    upper = flag[0] != 0
    mine, theirs = own[...], other[...]
    sums[:rows, :] = jnp.where(upper, theirs, mine)
    sums[rows:, :] = jnp.where(upper, mine, theirs)
    row = lax.broadcasted_iota(jnp.int32, (half, half), 0)
    col = lax.broadcasted_iota(jnp.int32, (half, half), 1)
    cross, mixed = sums[:half, :half], sums[:half, half:]
    turned = mixed.T
    first = jnp.where(row <= col, mixed, turned)
    diagonal = jnp.broadcast_to(sums[half + GROUPS : half + GROUPS + 1, :half], (half, half))
    last = jnp.where(row == col, diagonal, jnp.where(row > col, mixed, turned))
    gram = jnp.concatenate(
        [
            jnp.concatenate([first, cross], axis=1),
            jnp.concatenate([cross.T, last], axis=1),
        ],
        axis=0,
    )
    mean_row = sums[half : half + 1, :] / count
    mean_col = jnp.broadcast_to(mean_row, (width, width)).T
    sigma = gram / count - mean_col * mean_row
    row = lax.broadcasted_iota(jnp.int32, (width, width), 0)
    col = lax.broadcasted_iota(jnp.int32, (width, width), 1)
    diagonal = row == col
    trace_value = jnp.sum(jnp.where(diagonal, sigma, 0.0), keepdims=True) + epsilon
    root_scale = jnp.sqrt(trace_value)
    unit, trail = square_root(sigma / trace_value)
    root = root_scale * unit
    root_out[:width, :] = root

    classes = class_weight.shape[0]
    slots = root_out.shape[0] - width
    place = lax.broadcasted_iota(jnp.int32, (slots, 1), 0)
    bias = jnp.zeros((slots, 1), wide)
    for index in range(classes):
        bias = jnp.where(place == index, class_bias[index], bias)
    partial = [
        jnp.sum(class_weight[index].astype(wide) * root, axis=0, keepdims=True)
        for index in range(classes)
    ]
    partial.append(jnp.zeros((slots - classes, width), wide))
    logits = jnp.sum(jnp.concatenate(partial, axis=0), axis=1, keepdims=True) + bias
    onehot = jnp.where(place == label[0], 1.0, 0.0)
    soft = jnp.maximum(logits, 0.0) + jnp.log(1.0 + jnp.exp(-jnp.abs(logits)))
    share = 1.0 / (1.0 + jnp.exp(-logits))
    used = place < classes
    loss_part = jnp.sum(jnp.where(used, soft - onehot * logits, 0.0), keepdims=True)
    logit_grad = jnp.where(used, loss_scale * (share - onehot) / image_count, 0.0)
    root_out[width:, :] = jnp.broadcast_to(
        jnp.where(place == classes, loss_part, logit_grad), (slots, width)
    )
    across = lax.broadcasted_iota(jnp.int32, (slots, width), 1)
    facts = jnp.where(place == classes, loss_part, logit_grad)
    root_out[width + slots - 1 :, :] = jnp.sum(
        jnp.where(across == place, facts, 0.0), axis=0, keepdims=True
    )

    root_grad = jnp.zeros((width, width), wide)
    for index in range(classes):
        root_grad = root_grad + class_weight[index].astype(wide) * logit_grad[index : index + 1, :]
    root_grad = root_grad + root_grad.T
    change = square_root_change(root_scale * root_grad, trail)
    trace_grad = jnp.sum(root_grad * unit, keepdims=True) / (2.0 * root_scale) - jnp.sum(
        change * sigma, keepdims=True
    ) / (trace_value * trace_value)
    symmetric = (
        (change / trace_value + jnp.where(diagonal, trace_grad, 0.0)) / count
    ).astype(narrow)
    mean_term = jnp.sum(mean_col * symmetric.astype(wide), axis=0, keepdims=True)

    inner = feat_inner.shape[0]
    for feat, gate, start in ((feat_inner, gate_inner, 0), (feat_edge, gate_edge, inner)):
        grad = jnp.dot(feat[...], symmetric, preferred_element_type=wide) - mean_term
        pre[start : start + feat.shape[0], :] = (grad * gate[...]).astype(narrow)
    pre_grad = pre[...]
    payload[width:, :] = jnp.zeros((payload.shape[0] - width, payload.shape[1]), wide)
    taps = KERNEL * KERNEL
    payload[width + taps + 1 : width + taps + 2, :width] = jnp.sum(
        pre_grad.astype(wide), axis=0, keepdims=True
    )
    for first in range(0, conv_turned.shape[0], width):
        payload[:width, first : first + width] = jnp.dot(
            conv_turned[first : first + width, :], pre_grad, preferred_element_type=wide
        )
    for out, start in ((conv_inner_out, 0), (conv_edge_out, inner)):
        out[...] = jnp.dot(
            pre[start : start + out.shape[0], :], reduce_turned[...], preferred_element_type=wide
        ).astype(narrow)


def head(flag, label, class_bias, own, other, class_weight, prepared, count, image_count):
    feat_inner, feat_edge, gate_inner, gate_edge, conv_turned, reduce_turned = prepared
    width, channels = reduce_turned.shape
    inner, edge = feat_inner.shape[0], feat_edge.shape[0]
    slots = -(-(class_weight.shape[0] + 2) // GROUPS) * GROUPS
    return pl.pallas_call(
        functools.partial(head_kernel, count=count, image_count=image_count),
        in_specs=[in_smem] * 3 + [in_vmem] * 9,
        out_specs=[in_vmem] * 4,
        out_shape=[
            shape_of((width + slots, width)),
            shape_of((width + TAPS_ROWS, channels)),
            shape_of((inner, channels), narrow),
            shape_of((edge, channels), narrow),
        ],
        scratch_shapes=[
            pltpu.VMEM((2 * own.shape[0], width), wide),
            pltpu.VMEM((inner + edge, width), narrow),
        ],
        compiler_params=params(24),
        cost_estimate=cost(10),
        name="head",
    )(
        flag, label, class_bias, own, other, class_weight,
        feat_inner, feat_edge, gate_inner, gate_edge, conv_turned, reduce_turned,
    )


def prepare_kernel(
    before_inner, before_edge, conv_inner_in, conv_edge_in, reduce_weight,
    gate_inner, gate_edge, conv_turned, reduce_turned,
):
    for before, gate in ((before_inner, gate_inner), (before_edge, gate_edge)):
        value = before[...]
        share = 1.0 / (1.0 + jnp.exp(-value))
        gate[...] = share * (1.0 + value * (1.0 - share))
    inner = conv_inner_in.shape[0]
    conv_turned[:, :inner] = conv_inner_in[...].T
    conv_turned[:, inner:] = conv_edge_in[...].T
    reduce_turned[...] = reduce_weight[...].T


def prepare(before_inner, before_edge, conv_in, conv_ed, reduce_weight):
    channels, width = reduce_weight.shape
    inner, edge = before_inner.shape[0], before_edge.shape[0]
    return pl.pallas_call(
        prepare_kernel,
        in_specs=[in_vmem] * 5,
        out_specs=[in_vmem] * 4,
        out_shape=[
            shape_of((inner, width)),
            shape_of((edge, width)),
            shape_of((channels, inner + edge), narrow),
            shape_of((width, channels), narrow),
        ],
        compiler_params=params(16),
        cost_estimate=cost(1),
        name="prepare",
    )(before_inner, before_edge, conv_in, conv_ed, reduce_weight)


def taps_kernel(
    spread_in, spread_top, spread_bottom, grad_inner, grad_edge, payload_in, payload,
    parts, grads, products, out, *, first, last,
):
    rows = spread_in.shape[1]
    row_pairs, col_pairs = grads.shape[1:3]
    steps = 2 * col_pairs
    cols = steps * GROUPS
    order = edge_rows(rows)
    taps = KERNEL * KERNEL
    base = payload.shape[0] - TAPS_ROWS

    def one_tile(tile, _):
        lanes = lanes_of(tile)

        def grad_row(row):
            if row in order:
                source, place = grad_edge, order.index(row)
            else:
                source, place = grad_inner, row - SIDE
            values = source[place * cols : (place + 1) * cols, lanes].astype(wide)
            return [values[step * GROUPS : (step + 1) * GROUPS, :] for step in range(steps)]

        for pair in range(row_pairs):
            even, odd = grad_row(2 * pair), grad_row(2 * pair + 1)
            both = [a + b for a, b in zip(even, odd)]
            for row_part, line in enumerate((even, odd, both)):
                for col in range(col_pairs):
                    grads[3 * row_part, pair, col] = line[2 * col]
                    grads[3 * row_part + 1, pair, col] = line[2 * col + 1]
                    grads[3 * row_part + 2, pair, col] = line[2 * col] + line[2 * col + 1]

        def load(place, group):
            place = place - HALF
            if place < 0:
                return spread_top[tile, place + HALF, group]
            if place >= rows:
                return spread_bottom[tile, place - rows, group]
            return spread_in[tile, place, group]

        fill_parts(load, parts, row_pairs + 3, 2 * col_pairs + 6)
        for row_part in range(3):
            for col_part in range(3):
                part = 3 * row_part + col_part
                start = FILTERS[row_part, col_part]
                many_rows, many_cols = PARTS[row_part], PARTS[col_part]
                total = {}
                for place in range(row_pairs + many_rows - 1):
                    line = part_line(
                        load, parts, row_part, col_part, place, col_pairs + many_cols - 1
                    )
                    for tap_row in range(many_rows):
                        row = place - tap_row
                        if not 0 <= row < row_pairs:
                            continue
                        for col in range(col_pairs):
                            grad = grads[part, row, col]
                            for tap_col in range(many_cols):
                                term = line[col + tap_col] * grad
                                tap = tap_row * many_cols + tap_col
                                total[tap] = total[tap] + term if tap in total else term
                for tap, value in total.items():
                    products[start + tap] = value

        for row_tap in range(KERNEL):
            for col_tap in range(KERNEL):
                place = (row_tap // 2, col_tap // 2)
                found = None
                for row_part in (row_tap % 2, 2):
                    for col_part in (col_tap % 2, 2):
                        start = FILTERS[row_part, col_part]
                        value = products[start + place[0] * PARTS[col_part] + place[1]]
                        found = value if found is None else found + value
                tap = row_tap * KERNEL + col_tap
                out[tap : tap + 1, :] = jnp.sum(found, axis=0, keepdims=True)
        found = [
            sum(grads[8, pair, col] for col in range(1, col_pairs)) + grads[8, pair, 0]
            for pair in range(row_pairs)
        ]
        out[taps : taps + 1, :] = jnp.sum(sum(found[1:], found[0]), axis=0, keepdims=True)
        payload[pl.ds(base, taps + 1), lanes] = out[: taps + 1, :]
        return 0

    lax.fori_loop(first, last, one_tile, 0)


def tap_grads(spreads, grads, payload, first, last):
    rows, groups = spreads[0].shape[1:3]
    row_pairs, col_pairs = rows // 2, (groups - KERNEL + 1) // 2
    return pl.pallas_call(
        functools.partial(taps_kernel, first=first, last=last),
        in_specs=[in_vmem] * 6,
        out_specs=in_vmem,
        out_shape=shape_of(payload.shape),
        input_output_aliases={5: 0},
        scratch_shapes=[
            pltpu.VMEM((2, row_pairs + 3, 2 * col_pairs + 6, GROUPS, LANES), wide),
            pltpu.VMEM((9, row_pairs, col_pairs, GROUPS, LANES), wide),
            pltpu.VMEM((PRODUCTS, GROUPS, LANES), wide),
            pltpu.VMEM((TAPS_ROWS, LANES), wide),
        ],
        compiler_params=params(16),
        cost_estimate=cost(2 * (last - first)),
        name="tap_grads",
    )(*spreads, *grads, payload)


def finish_kernel(flag, own, other, *refs, image_count):
    known = refs[:-7]
    weight_out, depth_out, depth_bias_out, bias_out, class_bias_out, loss_out, payload = refs[-7:]
    part = own.shape[0]
    upper = flag[0] != 0
    mine, theirs = own[...].astype(wide), other[...].astype(wide)
    payload[:part, :] = jnp.where(upper, theirs, mine)
    payload[part:, :] = jnp.where(upper, mine, theirs)
    width = weight_out.shape[1]
    for first in range(0, weight_out.shape[0], width):
        weight_out[first : first + width, :] = payload[:width, first : first + width]
    for row_tap in range(KERNEL):
        start = width + row_tap * KERNEL
        depth_out[row_tap] = payload[start : start + KERNEL, :]
    taps = KERNEL * KERNEL
    depth_bias_out[...] = payload[width + taps, :]
    bias_out[...] = payload[width + taps + 1, :width]
    totals = tree_sum([part[part.shape[0] - 1 :, :] for part in known])
    classes = class_bias_out.shape[0]
    class_bias_out[...] = totals[0, :classes]
    across = lax.broadcasted_iota(jnp.int32, totals.shape, 1)
    loss_out[0] = jnp.sum(jnp.where(across == classes, totals, 0.0)) / image_count


def finish(flag, own, other, known, width, classes, image_count):
    part, channels = own.shape
    return pl.pallas_call(
        functools.partial(finish_kernel, image_count=image_count),
        in_specs=[in_smem] + [in_vmem] * (2 + len(known)),
        out_specs=[in_vmem] * 5 + [in_smem],
        out_shape=[
            shape_of((channels, width)),
            shape_of((KERNEL, KERNEL, channels)),
            shape_of((channels,)),
            shape_of((width,)),
            shape_of((classes,)),
            shape_of((1,)),
        ],
        scratch_shapes=[pltpu.VMEM((2 * part, channels), wide)],
        compiler_params=params(8),
        cost_estimate=cost(1),
        name="finish",
    )(flag, own, other, *known)


def edge_strip(block, left, right, rows):
    channels = block.shape[2]
    return jnp.concatenate([part[rows].reshape(-1, channels) for part in (block, left, right)])


def body(
    features, depth_weight, depth_bias, reduce_weight, reduce_bias, class_weight, class_bias, labels
):
    together = lax.optimization_barrier
    block = features[0]
    rows, cols, channels = block.shape
    width = reduce_weight.shape[1]
    classes = class_bias.shape[0]
    count = rows * cols * lax.axis_size("sy") * lax.axis_size("sx")
    image_count = features.shape[0] * lax.axis_size("dp")

    flag = is_upper("sx", 1).astype(jnp.int32)[None]
    upper = is_upper("sx", 1)
    corner = 2 * (lax.axis_index("dp") & 1) + ((lax.axis_index("sx") & 2) >> 1)
    places = [corner ^ turn for turn in range(4)]
    bias_row = depth_bias[None]
    reduce_row = reduce_bias[None]
    left = next_along(block[:, cols - HALF :], "sx")
    right = back_along(block[:, :HALF], "sx")
    low, high, left, right, flag, upper, places, bias_row, reduce_row = together(
        (
            edge_strip(block, left, right, slice(rows - HALF, rows)),
            edge_strip(block, left, right, slice(0, HALF)),
            left,
            right,
            flag,
            upper,
            places,
            bias_row,
            reduce_row,
        )
    )
    top = next_along(low, "sy")
    bottom = back_along(high, "sy")
    spread, filters, conv_in, before_in, feat_in, gram, colsum, partial = conv_inner(
        block, left, right, depth_weight, bias_row, reduce_weight, reduce_row
    )
    spread_top, spread_bottom, conv_ed, before_ed, feat_ed, kept, sent = conv_edge(
        flag, partial, (top, bottom), filters, reduce_weight, reduce_row, gram, colsum
    )

    sums = kept + swap(sent, "sx", 1)
    sums, before_in, before_ed, conv_in, conv_ed = together(
        (sums, before_in, before_ed, conv_in, conv_ed)
    )
    gate_in, gate_ed, conv_turned, reduce_turned = prepare(
        before_in, before_ed, conv_in, conv_ed, reduce_weight
    )
    for shift in doublings("sx", 2):
        sums = exchange(sums, "sx", shift, wide)
    sums, gate_in, gate_ed, conv_turned, reduce_turned = together(
        (sums, gate_in, gate_ed, conv_turned, reduce_turned)
    )
    for shift in doublings("sy"):
        sums = exchange(sums, "sy", shift, wide)
    other = swap(sums, "sx", 1)

    root, payload, *grads = head(
        flag,
        labels,
        class_bias,
        sums,
        other,
        class_weight,
        (feat_in, feat_ed, gate_in, gate_ed, conv_turned, reduce_turned),
        count,
        image_count,
    )
    known = [root] + [swap(root, "dp", shift) for shift in range(1, lax.axis_size("dp"))]
    spreads = (spread, spread_top, spread_bottom)
    tiles = channels // LANES
    payload = tap_grads(spreads, grads, payload, 0, tiles - 1)
    payload, known = together((payload, known))
    payload = tap_grads(spreads, grads, payload, tiles - 1, tiles)

    part = payload.shape[0] // 2
    low, high = payload[:part], payload[part:]
    kept, sent = jnp.where(upper, high, low), jnp.where(upper, low, high)
    payload = kept + swap(sent.astype(narrow), "sx", 1).astype(wide)
    axes = ("dp", "sx")
    pairs = square_pairs(axes, (1, 2))
    payload = square_scatter(payload, axes, pairs, places, narrow)
    for shift in doublings("dp", 2):
        payload = exchange(payload, "dp", shift, narrow)
    for shift in doublings("sy"):
        payload = exchange(payload, "sy", shift, narrow)
    payload = payload.astype(narrow)
    payload, known = together((payload, known))
    class_weight_grad = tree_sum(
        [part[width : width + classes, 0][:, None, None] * part[None, :width] for part in known]
    )
    payload, class_weight_grad = together(
        (square_gather(payload, axes, pairs, places), class_weight_grad)
    )
    other = swap(payload, "sx", 1)
    weight_grad, depth_grad, depth_bias_grad, bias_grad, class_bias_grad, loss = finish(
        flag, payload, other, known, width, classes, image_count
    )
    return (
        loss[0],
        depth_grad,
        depth_bias_grad,
        weight_grad,
        bias_grad,
        class_weight_grad,
        class_bias_grad,
    )


def solution(mesh):
    placed = (P("dp", "sy", "sx", None), P(), P(), P(), P(), P(), P(), P("dp"))
    return jax.shard_map(
        body,
        mesh=mesh,
        in_specs=placed,
        out_specs=(P(), P(), P(), P(), P(), P(), P()),
        check_vma=False,
    )
```
